32 devices in a mesh: seq: 8 (over z, core), dp: 4 (over y, x).
Axes of the slice: x: 2, y: 2, z: 4, core: 2. Of those that a mesh axis runs over, the one named last changes fastest.
Arguments:
- hidden_in: bfloat16 [4, 1024, 1152], P('dp', 'seq'), may hold values from -6 to 6
- attn_norm: float32 [1152], P(('seq', 'dp')), may hold values from 0.1 to 1.9
- query_weight: bfloat16 [1152, 1152], P(('seq', 'dp')), may hold values from -0.1875 to 0.1875
- key_weight: bfloat16 [1152, 384], P(('seq', 'dp')), may hold values from -0.1875 to 0.1875
- value_weight: bfloat16 [1152, 384], P(('seq', 'dp')), may hold values from -0.1875 to 0.1875
- output_weight: bfloat16 [1152, 1152], P(('seq', 'dp')), may hold values from -1 to 1
- mlp_norm: float32 [1152], P(('seq', 'dp')), may hold values from 0.1 to 1.9
- gate_weight: bfloat16 [1152, 3072], P(('seq', 'dp')), may hold values from -0.1875 to 0.1875
- up_weight: bfloat16 [1152, 3072], P(('seq', 'dp')), may hold values from -0.1875 to 0.1875
- down_weight: bfloat16 [3072, 1152], P(('seq', 'dp')), may hold values from -0.109375 to 0.109375
- cotangent: bfloat16 [4, 1024, 1152], P('dp', 'seq'), may hold values from -6 to 6
- doc_starts: int32 [4, 8], replicated, may hold values from 0 to 1023, as said below
- keep_mask: int32 [4, 2], replicated, may hold values from 0 to 1, as said below
- keep_rate: float32 [2], replicated, may hold values from 0.5 to 0.9
- seq_order: int32 [4], replicated, may hold values from 0 to 3, each once
Outputs:
- block_output: bfloat16 [4, 1024, 1152], P('dp', 'seq')
- input_grad: float32 [4, 1024, 1152], P('dp', 'seq')
- grad_attn_norm: float32 [1152], P(('seq', 'dp'))
- grad_query: float32 [1152, 1152], P(('seq', 'dp'))
- grad_key: float32 [1152, 384], P(('seq', 'dp'))
- grad_value: float32 [1152, 384], P(('seq', 'dp'))
- grad_output: float32 [1152, 1152], P(('seq', 'dp'))
- grad_mlp_norm: float32 [1152], P(('seq', 'dp'))
- grad_gate: float32 [1152, 3072], P(('seq', 'dp'))
- grad_up: float32 [1152, 3072], P(('seq', 'dp'))
- grad_down: float32 [3072, 1152], P(('seq', 'dp'))
The draws below stay inside these ranges and needn't reach their ends.
Inputs may be any that keep to these rules, and one draw needn't show every extreme that they name: `doc_starts`: each row lists the starts of 8 documents of one sample in non-decreasing order, the first 0; equal starts are empty documents; every sample has a document of 640 tokens or more. `keep_mask`: column 0 is the attention branch, column 1 the feed-forward branch; column 0 holds both values. `seq_order`: each sample stands once.
All inputs are finite; a program needn't handle non-finite values.
Results may differ from the reference program's by a relative error of at most 0.035.
Values may be sent and summed in bfloat16 or wider, within the bound.
A program may use at most 192 MiB of HBM per device.

```python
import math
import jax
import jax.numpy as jnp
from jax import lax

D = 1152
H = 18
KV = 6
HD = 64
FF = 3072
NDOC = 8
LEN = 1024
SEQS = 4
LONGD = 640


def draw_doc_starts(key, part):
    key_list = jax.random.split(key, 2)
    long_begin = jax.random.randint(key_list[0], (SEQS, 1), 1, LEN - LONGD)
    free_draws = jax.random.randint(key_list[1], (SEQS, NDOC - 3), 1, LEN - LONGD)
    mapped = jnp.where(free_draws < long_begin, free_draws, free_draws + LONGD)
    zero_col = jnp.zeros((SEQS, 1), jnp.int32)
    joined = jnp.concatenate([zero_col, long_begin, long_begin + LONGD, mapped], axis=1)
    return jnp.sort(joined, axis=1).astype(jnp.int32)


def draw_keep_mask(key, part):
    key_list = jax.random.split(key, 4)
    coin_flips = jax.random.randint(key_list[0], (SEQS, 2), 0, 4)
    kept_flags = (coin_flips < 3).astype(jnp.int32)
    chosen_attn = jax.random.randint(key_list[1], (), 0, SEQS)
    chosen_mlp = jax.random.randint(key_list[2], (), 0, SEQS)
    dropped_attn = (chosen_attn + 1 + jax.random.randint(key_list[3], (), 0, SEQS - 1)) % SEQS
    index_row = jnp.arange(SEQS)
    attn_col = jnp.where(index_row == chosen_attn, 1, jnp.where(index_row == dropped_attn, 0, kept_flags[:, 0]))
    mlp_col = jnp.where(index_row == chosen_mlp, 1, kept_flags[:, 1])
    return jnp.stack([attn_col, mlp_col], axis=1).astype(jnp.int32)


def block_levels(rng, extent, pieces, least, largest):
    def one(position, blocks):
        draws = jax.random.uniform(jax.random.fold_in(jax.random.fold_in(rng, 6), position), (blocks,), jnp.float32, least / len(pieces), largest / len(pieces))
        return jnp.repeat(jnp.exp(draws), extent[position] // blocks).reshape((-1,) + (1,) * (len(extent) - position - 1))

    gain = one(*pieces[0])
    for cut in pieces[1:]:
        gain = gain * one(*cut)
    return gain


def centred(own_key, dims, width, most, pieces=(), held_as=jnp.bfloat16):
    gain = block_levels(own_key, dims, pieces, -0.22, 0.18) if pieces else 1.0
    values = jax.random.normal(own_key, dims, jnp.float32) * width * gain
    return jnp.minimum(jnp.maximum(values, -most), most).astype(held_as)


def setup_inputs(seed: int = 0) -> dict:
    arg_keys = jax.random.split(jax.random.key(seed), 16)
    return {
        "hidden_in": centred(arg_keys[0], (SEQS, LEN, D), 1.0, 6.0, ((0, 4), (1, 8))),
        "attn_norm": jnp.clip(1.0 + 0.18 * jax.random.normal(arg_keys[1], (D,), jnp.float32), 0.1, 1.9),
        "query_weight": centred(arg_keys[2], (D, H * HD), D ** -0.5, 0.1875, ((0, 32),)),
        "key_weight": centred(arg_keys[3], (D, KV * HD), D ** -0.5, 0.1875, ((0, 32),)),
        "value_weight": centred(arg_keys[4], (D, KV * HD), D ** -0.5, 0.1875, ((0, 32),)),
        "output_weight": centred(arg_keys[5], (H * HD, D), (H * HD // 32) ** -0.5, 1.0, ((0, 32),)),
        "mlp_norm": jnp.clip(1.0 + 0.18 * jax.random.normal(arg_keys[6], (D,), jnp.float32), 0.1, 1.9),
        "gate_weight": centred(arg_keys[7], (D, FF), D ** -0.5, 0.1875, ((0, 32),)),
        "up_weight": centred(arg_keys[8], (D, FF), D ** -0.5, 0.1875, ((0, 32),)),
        "down_weight": centred(arg_keys[9], (FF, D), FF ** -0.5, 0.109375, ((0, 32),)),
        "cotangent": centred(arg_keys[10], (SEQS, LEN, D), 1.0, 6.0, ((0, 4), (1, 8))),
        "doc_starts": draw_doc_starts(jax.random.fold_in(arg_keys[15], 71), 0),
        "keep_mask": draw_keep_mask(jax.random.fold_in(arg_keys[15], 71), 0),
        "keep_rate": jnp.clip(jax.random.uniform(arg_keys[13], (2,), jnp.float32, 0.5, 0.9), 0.5, 0.9),
        "seq_order": jax.random.permutation(arg_keys[14], SEQS).astype(jnp.int32),
    }


@jax.custom_vjp
def low(v):
    return lax.optimization_barrier(v.astype(jnp.bfloat16)).astype(jnp.float32)

@jax.custom_vjp
def low_back(v):
    return v

def low_keep(v):
    return (low(v), None)

def low_pass(kept, grad):
    return (grad,)

def back_keep(v):
    return (v, None)

def back_low(kept, grad):
    return (low(grad),)
low.defvjp(low_keep, low_pass)
low_back.defvjp(back_keep, back_low)
EPSILON = 1e-05
ROPE_BASE = 10000.0
MASKED = -1e+30

def rms_norm(values, gain_vec):
    return values * lax.rsqrt(lax.optimization_barrier(jnp.mean(values * values, axis=-1, keepdims=True)) + EPSILON) * gain_vec

def product(left_mat, right_mat):
    return jnp.dot(left_mat, right_mat, precision=lax.Precision.HIGHEST, preferred_element_type=jnp.float32)

def rotary(vectors, positions):
    half_size = vectors.shape[-1] // 2
    inverse_freq = ROPE_BASE ** (-2.0 * jnp.arange(half_size, dtype=jnp.float32) / vectors.shape[-1])
    angles = positions.astype(jnp.float32)[:, None] * inverse_freq[None, :]
    shape_out = (positions.shape[0],) + (1,) * (vectors.ndim - 2) + (half_size,)
    cosine = jnp.cos(angles).reshape(shape_out)
    sine_table = jnp.sin(angles).reshape(shape_out)
    first_half = vectors[..., :half_size]
    second_half = vectors[..., half_size:]
    return jnp.concatenate([first_half * cosine - second_half * sine_table, second_half * cosine + first_half * sine_table], axis=-1)

def attend_sequence(arguments):
    queries, keys, values, doc_ids = arguments
    block_rows = min(512, LEN)
    block_count = LEN // block_rows
    positions = jnp.arange(LEN)

    def one_block(inputs):
        query_block, block_pos, block_docs = inputs
        scores = jnp.einsum('tkgd,skd->kgts', query_block, keys, precision=lax.Precision.HIGHEST) / math.sqrt(HD)
        scores = low_back(scores)
        allowed = (positions[None, :] <= block_pos[:, None]) & (doc_ids[None, :] == block_docs[:, None])
        masked = jnp.where(allowed, scores, MASKED)
        peak = lax.optimization_barrier(jnp.max(masked, axis=-1, keepdims=True))
        expo = jnp.exp(masked - peak)
        probs = expo / lax.optimization_barrier(jnp.sum(expo, axis=-1, keepdims=True))
        return jnp.einsum('kgts,skd->tkgd', low(probs), values, precision=lax.Precision.HIGHEST)
    groups = H // KV
    result = lax.map(jax.checkpoint(one_block), (queries.reshape(block_count, block_rows, KV, groups, HD), positions.reshape(block_count, block_rows), doc_ids.reshape(block_count, block_rows)))
    return result.reshape(LEN, H * HD)

def reference(hidden_in, attn_norm, query_weight, key_weight, value_weight, output_weight, mlp_norm, gate_weight, up_weight, down_weight, cotangent, doc_starts, keep_mask, keep_rate, seq_order):
    sample_starts = doc_starts[seq_order]
    positions = jnp.arange(LEN)
    doc_ids = lax.optimization_barrier(jnp.sum((sample_starts[:, None, :] <= positions[None, :, None]).astype(jnp.int32), axis=2)) - 1
    keep_flags = keep_mask[seq_order].astype(jnp.float32)
    attn_scale = keep_flags[:, 0] / keep_rate[0]
    mlp_scale = keep_flags[:, 1] / keep_rate[1]
    groups = H // KV

    def block_forward(hidden, norm_one, weight_query, weight_key, weight_value, weight_output, norm_two, weight_gate, weight_up, weight_down):
        row_values = hidden.reshape(SEQS * LEN, D)
        seq_pos = jnp.tile(positions, SEQS)
        normed_first = low(rms_norm(row_values, norm_one))
        queries = low(rotary(low_back(product(normed_first, weight_query)).reshape(SEQS * LEN, KV, groups, HD), seq_pos))
        keys = low(rotary(low_back(product(normed_first, weight_key)).reshape(SEQS * LEN, KV, HD), seq_pos))
        values = low(low_back(product(normed_first, weight_value))).reshape(SEQS * LEN, KV, HD)
        attended = lax.map(attend_sequence, (queries.reshape(SEQS, LEN, KV, groups, HD), keys.reshape(SEQS, LEN, KV, HD), values.reshape(SEQS, LEN, KV, HD), doc_ids))
        attended = low(low_back(attended.reshape(SEQS * LEN, H * HD)))
        branch_attn = low_back(product(attended, weight_output)).reshape(SEQS, LEN, D)
        middle = hidden + attn_scale[:, None, None] * branch_attn
        normed_second = low(rms_norm(middle.reshape(SEQS * LEN, D), norm_two))
        gate_pre = low_back(product(normed_second, weight_gate))
        up_pre = low_back(product(normed_second, weight_up))
        activated = low(jax.nn.silu(gate_pre) * up_pre)
        branch_mlp = low_back(product(activated, weight_down)).reshape(SEQS, LEN, D)
        return middle + mlp_scale[:, None, None] * branch_mlp
    inputs = (hidden_in.astype(jnp.float32), attn_norm.astype(jnp.float32), query_weight.astype(jnp.float32), key_weight.astype(jnp.float32), value_weight.astype(jnp.float32), output_weight.astype(jnp.float32), mlp_norm.astype(jnp.float32), gate_weight.astype(jnp.float32), up_weight.astype(jnp.float32), down_weight.astype(jnp.float32))
    output, pullback = jax.vjp(block_forward, *inputs)
    gradients = pullback(cotangent.astype(jnp.float32))
    return (output.astype(jnp.bfloat16), gradients[0], gradients[1], gradients[2], gradients[3], gradients[4], gradients[5], gradients[6], gradients[7], gradients[8], gradients[9])
```

```python
import math

import jax
import jax.numpy as jnp
from jax import lax
from jax.sharding import PartitionSpec as P

H = 18
KV = 6
HD = 64


EPSILON = 1e-05
ROPE_BASE = 10000.0
MASKED = -1e30


def contract_rows(left_rows, right_rows):
    return lax.dot_general(
        left_rows, right_rows, (((0,), (0,)), ((), ())), preferred_element_type=jnp.float32
    )


def contract_cols(left_mat, right_mat):
    return lax.dot_general(
        left_mat, right_mat, (((1,), (1,)), ((), ())), preferred_element_type=jnp.float32
    )


def low(v):
    return v.astype(jnp.bfloat16)


def dot(a, b):
    return jnp.dot(a, b, preferred_element_type=jnp.float32)


def swap_halves(vectors):
    half = HD // 2
    return jnp.concatenate([vectors[..., half:], vectors[..., :half]], axis=-1)


def shards(
    hidden_in,
    attn_norm,
    query_weight,
    key_weight,
    value_weight,
    output_weight,
    mlp_norm,
    gate_weight,
    up_weight,
    down_weight,
    cotangent,
    doc_starts,
    keep_mask,
    keep_rate,
    seq_order,
):
    tok = hidden_in.shape[1]
    ns, nd = lax.axis_size("seq"), lax.axis_size("dp")
    length = tok * ns
    rows = query_weight.shape[0]
    ffr = down_weight.shape[0]
    dim = hidden_in.shape[2]
    groups = H // KV
    nq, nk = H * HD, KV * HD
    score_scale = 1.0 / math.sqrt(HD)
    me_s, me_d = lax.axis_index("seq"), lax.axis_index("dp")
    sample = jnp.sum(jnp.where(jnp.arange(nd) == me_d, seq_order, 0))
    pick = jnp.arange(nd) == sample
    doc_begin = jnp.sum(jnp.where(pick[:, None], doc_starts, 0), axis=0)
    keep_flags = jnp.sum(jnp.where(pick[:, None], keep_mask, 0), axis=0).astype(jnp.float32)
    attn_scale = keep_flags[0] / keep_rate[0]
    mlp_scale = keep_flags[1] / keep_rate[1]
    positions = me_s * tok + jnp.arange(tok)
    first = jnp.max(jnp.where(doc_begin[None, :] <= positions[:, None], doc_begin[None, :], 0), axis=1)
    gain_one, gain_two = attn_norm[:, None], mlp_norm[:, None]

    qkv_rows = low(jnp.concatenate([query_weight, key_weight, value_weight], axis=1).astype(jnp.float32) * gain_one)
    w_qkv = lax.all_gather(qkv_rows, ("seq", "dp"), axis=0, tiled=True)
    w_out = lax.all_gather(output_weight, ("seq", "dp"), axis=0, tiled=True)

    def split_hidden(w):
        w = low(w.astype(jnp.float32) * gain_two).reshape(rows, ns, nd, ffr)
        w = jnp.transpose(w, (0, 2, 1, 3)).reshape(rows, nd * ns * ffr)
        return w

    gu = jnp.concatenate(
        [split_hidden(gate_weight).reshape(rows, nd, -1), split_hidden(up_weight).reshape(rows, nd, -1)], axis=2
    )
    gu = lax.all_to_all(gu, "dp", split_axis=1, concat_axis=0, tiled=True).reshape(nd * rows, -1)
    w_gu = lax.all_gather(gu, "seq", axis=0, tiled=True)
    w_down = lax.all_gather(down_weight, "seq", axis=0, tiled=True)
    hid = w_down.shape[0]

    x = hidden_in[0].astype(jnp.float32)
    r_one = lax.rsqrt(jnp.mean(x * x, axis=-1, keepdims=True) + EPSILON)
    xn = low(x * r_one)
    qkv = dot(xn, w_qkv)
    inverse_freq = ROPE_BASE ** (-2.0 * jnp.arange(HD // 2, dtype=jnp.float32) / HD)
    angles = positions.astype(jnp.float32)[:, None] * inverse_freq[None, :]
    cosine = jnp.tile(jnp.cos(angles), (1, 2))[:, None, :]
    sine = jnp.concatenate([-jnp.sin(angles), jnp.sin(angles)], axis=1)[:, None, :]

    def turn(v):
        return v * cosine + swap_halves(v) * sine

    def turn_back(v):
        return v * cosine - swap_halves(v) * sine

    queries = low(turn(qkv[:, :nq].reshape(tok, H, HD))).reshape(tok, KV, groups, HD)
    keys = low(turn(qkv[:, nq : nq + nk].reshape(tok, KV, HD)))
    kv = jnp.concatenate([keys.reshape(tok, nk), low(qkv[:, nq + nk :])], axis=1)
    kv_all = lax.all_gather(kv, "seq", axis=0, tiled=True)
    k_all, v_all = kv_all[:, :nk].reshape(length, KV, HD), kv_all[:, nk:].reshape(length, KV, HD)
    key_pos = jnp.arange(length)
    allowed = (key_pos[None, :] <= positions[:, None]) & (key_pos[None, :] >= first[:, None])
    scores = jnp.einsum("tkgd,skd->kgts", queries, k_all, preferred_element_type=jnp.float32) * score_scale
    scores = jnp.where(allowed, scores, MASKED)
    expo = jnp.exp(scores - jnp.max(scores, axis=-1, keepdims=True))
    probs = low(expo / jnp.sum(expo, axis=-1, keepdims=True))
    attended = jnp.einsum("kgts,skd->tkgd", probs, v_all, preferred_element_type=jnp.float32)
    att = low(attended.reshape(tok, nq))
    middle = x + attn_scale * dot(att, w_out)
    r_two = lax.rsqrt(jnp.mean(middle * middle, axis=-1, keepdims=True) + EPSILON)
    mn = low(middle * r_two)

    cot = cotangent[0].astype(jnp.float32)
    side = lax.all_gather(jnp.concatenate([xn, low(mlp_scale * cot), att], axis=1), "dp", axis=0, tiled=True)
    xn_all, gd_all, att_all = side[:, :dim], side[:, dim : 2 * dim], side[:, 2 * dim :]
    mn_all = lax.all_gather(mn, "dp", axis=0, tiled=True)
    gate, up = dot(mn_all, w_gu[:, :hid]), dot(mn_all, w_gu[:, hid:])
    sig = jax.nn.sigmoid(gate)
    act_gate = gate * sig
    act = low(act_gate * up)
    g_act = contract_cols(gd_all, w_down)
    gg = low(g_act * up * (sig * (1.0 + gate * (1.0 - sig))))
    gu_in = low(g_act * act_gate)
    gboth = jnp.concatenate([gg, gu_in], axis=1)
    g_mn = lax.psum_scatter(low(contract_cols(gboth, w_gu)), "dp", scatter_dimension=0, tiled=True).astype(jnp.float32)
    branch = lax.psum_scatter(low(dot(act, w_down)), "dp", scatter_dimension=0, tiled=True).astype(jnp.float32)
    block_output = low(middle + mlp_scale * branch)[None]
    m_gu = lax.psum_scatter(low(contract_rows(mn_all, gboth)), "seq", scatter_dimension=0, tiled=True)
    m_down = lax.psum_scatter(low(contract_rows(act, gd_all)), "seq", scatter_dimension=0, tiled=True)

    def norm_back(e, v, r):
        return r * e - v * (r * r * r) * jnp.mean(e * v, axis=-1, keepdims=True)

    g_mid = cot + norm_back(g_mn, middle, r_two)
    gba = low(attn_scale * g_mid)
    g_att = low(contract_cols(gba, w_out)).reshape(tok, KV, groups, HD)
    g_probs = jnp.einsum("tkgd,skd->kgts", g_att, v_all, preferred_element_type=jnp.float32)
    delta = jnp.einsum("tkgd,tkgd->kgt", g_att.astype(jnp.float32), attended)
    g_scores = low(probs.astype(jnp.float32) * (g_probs - delta[..., None]))
    g_q = jnp.einsum("kgts,skd->tkgd", g_scores, k_all, preferred_element_type=jnp.float32) * score_scale
    g_k = jnp.einsum("kgts,tkgd->skd", g_scores, queries, preferred_element_type=jnp.float32) * score_scale
    g_v = jnp.einsum("kgts,tkgd->skd", probs, g_att, preferred_element_type=jnp.float32)
    g_kv = low(jnp.concatenate([g_k.reshape(length, nk), g_v.reshape(length, nk)], axis=1))
    g_kv = lax.psum_scatter(g_kv, "seq", scatter_dimension=0, tiled=True).astype(jnp.float32)
    g_q_in = low(turn_back(g_q.reshape(tok, H, HD))).reshape(tok, nq)
    g_k_in = low(turn_back(g_kv[:, :nk].reshape(tok, KV, HD))).reshape(tok, nk)
    g_qkv = jnp.concatenate([g_q_in, g_k_in, low(g_kv[:, nk:])], axis=1)
    g_xn = contract_cols(g_qkv, w_qkv)
    input_grad = (g_mid + norm_back(g_xn, x, r_one))[None]

    cut = jnp.concatenate([g_qkv.reshape(tok, nd, -1), gba.reshape(tok, nd, -1)], axis=2)
    wq = g_qkv.shape[1] // nd
    cut = lax.all_to_all(cut, "dp", split_axis=1, concat_axis=0, tiled=True).reshape(nd * tok, -1)
    m_att = jnp.concatenate([contract_rows(xn_all, cut[:, :wq]), contract_rows(att_all, cut[:, wq:])], axis=1)
    m_att = lax.psum_scatter(low(m_att), "seq", scatter_dimension=0, tiled=True)

    back = jnp.concatenate([m_gu, m_att], axis=1)
    back = lax.all_to_all(back.reshape(nd, rows, 1, -1), "dp", split_axis=0, concat_axis=2, tiled=True)
    back = back.reshape(rows, nd, -1).astype(jnp.float32)

    def whole_hidden(m):
        return jnp.transpose(m.reshape(rows, nd, ns, ffr), (0, 2, 1, 3)).reshape(rows, -1)

    m_gate, m_up = whole_hidden(back[:, :, :hid]), whole_hidden(back[:, :, hid : 2 * hid])
    m_qkv = back[:, :, 2 * hid : 2 * hid + wq].reshape(rows, -1)
    g_out = back[:, :, 2 * hid + wq :].reshape(rows, -1)

    def weigh(w, m):
        return jnp.sum(w.astype(jnp.float32) * m, axis=1)

    m_q, m_k, m_v = m_qkv[:, :nq], m_qkv[:, nq : nq + nk], m_qkv[:, nq + nk :]
    g_norm_one = weigh(query_weight, m_q) + weigh(key_weight, m_k) + weigh(value_weight, m_v)
    g_norm_two = weigh(gate_weight, m_gate) + weigh(up_weight, m_up)
    return (
        block_output,
        input_grad,
        g_norm_one,
        m_q * gain_one,
        m_k * gain_one,
        m_v * gain_one,
        g_out,
        g_norm_two,
        m_gate * gain_two,
        m_up * gain_two,
        m_down.astype(jnp.float32),
    )


def solution(mesh):
    placed = (
        P("dp", "seq", None),
        P(("seq", "dp")),
        P(("seq", "dp"), None),
        P(("seq", "dp"), None),
        P(("seq", "dp"), None),
        P(("seq", "dp"), None),
        P(("seq", "dp")),
        P(("seq", "dp"), None),
        P(("seq", "dp"), None),
        P(("seq", "dp"), None),
        P("dp", "seq", None),
        P(),
        P(),
        P(),
        P(),
    )
    return jax.shard_map(
        shards,
        mesh=mesh,
        in_specs=placed,
        out_specs=(
            P("dp", "seq", None),
            P("dp", "seq", None),
            P(("seq", "dp")),
            P(("seq", "dp"), None),
            P(("seq", "dp"), None),
            P(("seq", "dp"), None),
            P(("seq", "dp"), None),
            P(("seq", "dp")),
            P(("seq", "dp"), None),
            P(("seq", "dp"), None),
            P(("seq", "dp"), None),
        ),
        check_vma=False,
    )
```

```python
import math

import jax
import jax.numpy as jnp
from jax import lax
from jax.experimental import pallas as pl
from jax.experimental.pallas import tpu as pltpu
from jax.sharding import PartitionSpec as P

H = 18
KV = 6
HD = 64


EPSILON = 1e-05
ROPE_BASE = 10000.0
MASKED = -1e30


def contract_rows(left_rows, right_rows):
    return lax.dot_general(
        left_rows, right_rows, (((0,), (0,)), ((), ())), preferred_element_type=jnp.float32
    )


def contract_cols(left_mat, right_mat):
    return lax.dot_general(
        left_mat, right_mat, (((1,), (1,)), ((), ())), preferred_element_type=jnp.float32
    )


def low(v):
    return v.astype(jnp.bfloat16)


def dot(a, b):
    return jnp.dot(a, b, preferred_element_type=jnp.float32)


def swap_halves(vectors):
    half = HD // 2
    return jnp.concatenate([vectors[..., half:], vectors[..., :half]], axis=-1)


def shards(
    hidden_in,
    attn_norm,
    query_weight,
    key_weight,
    value_weight,
    output_weight,
    mlp_norm,
    gate_weight,
    up_weight,
    down_weight,
    cotangent,
    doc_starts,
    keep_mask,
    keep_rate,
    seq_order,
):
    tok = hidden_in.shape[1]
    ns, nd = lax.axis_size("seq"), lax.axis_size("dp")
    length = tok * ns
    rows = query_weight.shape[0]
    ffr = down_weight.shape[0]
    dim = hidden_in.shape[2]
    groups = H // KV
    nq, nk = H * HD, KV * HD
    score_scale = 1.0 / math.sqrt(HD)
    me_s, me_d = lax.axis_index("seq"), lax.axis_index("dp")
    sample = jnp.sum(jnp.where(jnp.arange(nd) == me_d, seq_order, 0))
    pick = jnp.arange(nd) == sample
    doc_begin = jnp.sum(jnp.where(pick[:, None], doc_starts, 0), axis=0)
    keep_flags = jnp.sum(jnp.where(pick[:, None], keep_mask, 0), axis=0).astype(jnp.float32)
    attn_scale = keep_flags[0] / keep_rate[0]
    mlp_scale = keep_flags[1] / keep_rate[1]
    positions = me_s * tok + jnp.arange(tok)
    first = jnp.max(jnp.where(doc_begin[None, :] <= positions[:, None], doc_begin[None, :], 0), axis=1)
    gain_one, gain_two = attn_norm[:, None], mlp_norm[:, None]

    qkv_rows = low(jnp.concatenate([query_weight, key_weight, value_weight], axis=1).astype(jnp.float32) * gain_one)
    w_qkv = lax.all_gather(qkv_rows, ("seq", "dp"), axis=0, tiled=True)
    w_out = lax.all_gather(output_weight, ("seq", "dp"), axis=0, tiled=True)

    def split_hidden(w):
        w = low(w.astype(jnp.float32) * gain_two).reshape(rows, ns, nd, ffr)
        w = jnp.transpose(w, (0, 2, 1, 3)).reshape(rows, nd * ns * ffr)
        return w

    gu = jnp.concatenate(
        [split_hidden(gate_weight).reshape(rows, nd, -1), split_hidden(up_weight).reshape(rows, nd, -1)], axis=2
    )
    gu = lax.all_to_all(gu, "dp", split_axis=1, concat_axis=0, tiled=True).reshape(nd * rows, -1)
    w_gu = lax.all_gather(gu, "seq", axis=0, tiled=True)
    w_down = lax.all_gather(down_weight, "seq", axis=0, tiled=True)
    hid = w_down.shape[0]

    x = hidden_in[0].astype(jnp.float32)
    r_one = lax.rsqrt(jnp.mean(x * x, axis=-1, keepdims=True) + EPSILON)
    xn = low(x * r_one)
    qkv = dot(xn, w_qkv)
    inverse_freq = ROPE_BASE ** (-2.0 * jnp.arange(HD // 2, dtype=jnp.float32) / HD)
    angles = positions.astype(jnp.float32)[:, None] * inverse_freq[None, :]
    cosine = jnp.tile(jnp.cos(angles), (1, 2))[:, None, :]
    sine = jnp.concatenate([-jnp.sin(angles), jnp.sin(angles)], axis=1)[:, None, :]

    def turn(v):
        return v * cosine + swap_halves(v) * sine

    def turn_back(v):
        return v * cosine - swap_halves(v) * sine

    queries = low(turn(qkv[:, :nq].reshape(tok, H, HD))).reshape(tok, KV, groups, HD)
    keys = low(turn(qkv[:, nq : nq + nk].reshape(tok, KV, HD)))
    kv = jnp.concatenate([keys.reshape(tok, nk), low(qkv[:, nq + nk :])], axis=1)
    kv_all = lax.all_gather(kv, "seq", axis=0, tiled=True)
    k_all, v_all = kv_all[:, :nk].reshape(length, KV, HD), kv_all[:, nk:].reshape(length, KV, HD)
    key_pos = jnp.arange(length)
    allowed = (key_pos[None, :] <= positions[:, None]) & (key_pos[None, :] >= first[:, None])
    scores = jnp.einsum("tkgd,skd->kgts", queries, k_all, preferred_element_type=jnp.float32) * score_scale
    scores = jnp.where(allowed, scores, MASKED)
    expo = jnp.exp(scores - jnp.max(scores, axis=-1, keepdims=True))
    probs = low(expo / jnp.sum(expo, axis=-1, keepdims=True))
    attended = jnp.einsum("kgts,skd->tkgd", probs, v_all, preferred_element_type=jnp.float32)
    att = low(attended.reshape(tok, nq))
    middle = x + attn_scale * dot(att, w_out)
    r_two = lax.rsqrt(jnp.mean(middle * middle, axis=-1, keepdims=True) + EPSILON)
    mn = low(middle * r_two)

    cot = cotangent[0].astype(jnp.float32)
    side = lax.all_gather(jnp.concatenate([xn, low(mlp_scale * cot), att], axis=1), "dp", axis=0, tiled=True)
    xn_all, gd_all, att_all = side[:, :dim], side[:, dim : 2 * dim], side[:, 2 * dim :]
    mn_all = lax.all_gather(mn, "dp", axis=0, tiled=True)
    gate, up = dot(mn_all, w_gu[:, :hid]), dot(mn_all, w_gu[:, hid:])
    sig = jax.nn.sigmoid(gate)
    act_gate = gate * sig
    act = low(act_gate * up)
    g_act = contract_cols(gd_all, w_down)
    gg = low(g_act * up * (sig * (1.0 + gate * (1.0 - sig))))
    gu_in = low(g_act * act_gate)
    gboth = jnp.concatenate([gg, gu_in], axis=1)
    g_mn = lax.psum_scatter(low(contract_cols(gboth, w_gu)), "dp", scatter_dimension=0, tiled=True).astype(jnp.float32)
    branch = lax.psum_scatter(low(dot(act, w_down)), "dp", scatter_dimension=0, tiled=True).astype(jnp.float32)
    block_output = low(middle + mlp_scale * branch)[None]
    m_gu = lax.psum_scatter(low(contract_rows(mn_all, gboth)), "seq", scatter_dimension=0, tiled=True)
    m_down = lax.psum_scatter(low(contract_rows(act, gd_all)), "seq", scatter_dimension=0, tiled=True)

    def norm_back(e, v, r):
        return r * e - v * (r * r * r) * jnp.mean(e * v, axis=-1, keepdims=True)

    g_mid = cot + norm_back(g_mn, middle, r_two)
    gba = low(attn_scale * g_mid)
    g_att = low(contract_cols(gba, w_out)).reshape(tok, KV, groups, HD)
    g_probs = jnp.einsum("tkgd,skd->kgts", g_att, v_all, preferred_element_type=jnp.float32)
    delta = jnp.einsum("tkgd,tkgd->kgt", g_att.astype(jnp.float32), attended)
    g_scores = low(probs.astype(jnp.float32) * (g_probs - delta[..., None]))
    g_q = jnp.einsum("kgts,skd->tkgd", g_scores, k_all, preferred_element_type=jnp.float32) * score_scale
    g_k = jnp.einsum("kgts,tkgd->skd", g_scores, queries, preferred_element_type=jnp.float32) * score_scale
    g_v = jnp.einsum("kgts,tkgd->skd", probs, g_att, preferred_element_type=jnp.float32)
    g_kv = low(jnp.concatenate([g_k.reshape(length, nk), g_v.reshape(length, nk)], axis=1))
    g_kv = lax.psum_scatter(g_kv, "seq", scatter_dimension=0, tiled=True).astype(jnp.float32)
    g_q_in = low(turn_back(g_q.reshape(tok, H, HD))).reshape(tok, nq)
    g_k_in = low(turn_back(g_kv[:, :nk].reshape(tok, KV, HD))).reshape(tok, nk)
    g_qkv = jnp.concatenate([g_q_in, g_k_in, low(g_kv[:, nk:])], axis=1)
    g_xn = contract_cols(g_qkv, w_qkv)
    input_grad = (g_mid + norm_back(g_xn, x, r_one))[None]

    cut = jnp.concatenate([g_qkv.reshape(tok, nd, -1), gba.reshape(tok, nd, -1)], axis=2)
    wq = g_qkv.shape[1] // nd
    cut = lax.all_to_all(cut, "dp", split_axis=1, concat_axis=0, tiled=True).reshape(nd * tok, -1)
    m_att = jnp.concatenate([contract_rows(xn_all, cut[:, :wq]), contract_rows(att_all, cut[:, wq:])], axis=1)
    m_att = lax.psum_scatter(low(m_att), "seq", scatter_dimension=0, tiled=True)

    back = jnp.concatenate([m_gu, m_att], axis=1)
    back = lax.all_to_all(back.reshape(nd, rows, 1, -1), "dp", split_axis=0, concat_axis=2, tiled=True)
    back = back.reshape(rows, nd, -1).astype(jnp.float32)

    def whole_hidden(m):
        return jnp.transpose(m.reshape(rows, nd, ns, ffr), (0, 2, 1, 3)).reshape(rows, -1)

    m_gate, m_up = whole_hidden(back[:, :, :hid]), whole_hidden(back[:, :, hid : 2 * hid])
    m_qkv = back[:, :, 2 * hid : 2 * hid + wq].reshape(rows, -1)
    g_out = back[:, :, 2 * hid + wq :].reshape(rows, -1)

    def weigh(w, m):
        return jnp.sum(w.astype(jnp.float32) * m, axis=1)

    m_q, m_k, m_v = m_qkv[:, :nq], m_qkv[:, nq : nq + nk], m_qkv[:, nq + nk :]
    g_norm_one = weigh(query_weight, m_q) + weigh(key_weight, m_k) + weigh(value_weight, m_v)
    g_norm_two = weigh(gate_weight, m_gate) + weigh(up_weight, m_up)
    return (
        block_output,
        input_grad,
        g_norm_one,
        m_q * gain_one,
        m_k * gain_one,
        m_v * gain_one,
        g_out,
        g_norm_two,
        m_gate * gain_two,
        m_up * gain_two,
        m_down.astype(jnp.float32),
    )


MESH = pl.DeviceIdType.MESH
LIMIT = 60 * 2**20
BF, F32 = jnp.bfloat16, jnp.float32


def dot_nn(a, b):
    return lax.dot_general(a, b, (((1,), (0,)), ((), ())), preferred_element_type=F32)


def dot_nt(a, b):
    return lax.dot_general(a, b, (((1,), (1,)), ((), ())), preferred_element_type=F32)


def dot_tn(a, b):
    return lax.dot_general(a, b, (((0,), (0,)), ((), ())), preferred_element_type=F32)


class Net:
    def __init__(self, sends, recvs):
        self.sends, self.recvs, self.count, self.open = sends, recvs, 0, []
        self.s, self.d = lax.axis_index("seq"), lax.axis_index("dp")
        self.z, self.c = lax.div(self.s, 2), lax.rem(self.s, 2)
        y, x = lax.div(self.d, 2), lax.rem(self.d, 2)
        self.plane = (y * 2 + 1 - x, (1 - y) * 2 + x, 3 - self.d)
        self.mate = self.at(self.z, 1 - self.c)

    def at(self, z, core):
        return {"seq": z * 2 + core, "dp": self.d}

    def across(self, kind):
        return {"seq": self.s, "dp": self.plane[kind]}

    def greet(self):
        barrier = pltpu.get_barrier_semaphore()
        peers = [self.mate] + [self.across(k) for k in range(3)]
        peers += [self.at(lax.rem(self.z + k, 4), self.c) for k in (1, 2, 3)]
        for peer in peers:
            pl.semaphore_signal(barrier, inc=1, device_id=peer, device_id_type=MESH)
        pl.semaphore_wait(barrier, len(peers))

    def copy(self, src, dst, send, recv, peer):
        return pltpu.make_async_remote_copy(
            src_ref=src,
            dst_ref=dst,
            send_sem=self.sends.at[send],
            recv_sem=self.recvs.at[recv],
            device_id=peer,
            device_id_type=MESH,
        )

    def push(self, src, dst, recv, peer, when=None):
        copy = self.copy(src, dst, self.count, recv, peer)
        self.count += 1
        if when is None:
            copy.start()
        else:
            pl.when(when)(copy.start)
        self.open.append((copy, when))

    def arrive(self, dst, recv, when=None):
        copy = self.copy(dst, dst, 0, recv, self.mate)
        if when is None:
            copy.wait_recv()
        else:
            pl.when(when)(copy.wait_recv)

    def finish(self):
        for copy, when in self.open:
            if when is None:
                copy.wait_send()
            else:
                pl.when(when)(copy.wait_send)
        self.open = []

    def order(self, step):
        if step == 0:
            return self.z
        table = ((1, 0, 3, 2), (2, 2, 1, 1), (3, 3, 0, 0))[step - 1]
        z = self.z
        return jnp.where(z == 0, table[0], jnp.where(z == 1, table[1], jnp.where(z == 2, table[2], table[3])))


class Chain:
    def __init__(self, net, block, base):
        self.net, self.block, self.base = net, block, base

    def start(self):
        net = self.net
        own = self.block(net.z, net.c)
        net.push(own, own, self.base + net.z, net.at(net.z + 1, net.c), net.z < 3)
        net.push(own, own, self.base + net.z, net.at(net.z - 1, net.c), net.z > 0)

    def step(self, k):
        net = self.net
        b = net.order(k)
        block = self.block(b, net.c)
        net.arrive(block, self.base + b)
        to = jnp.where(b < net.z, net.z + 1, net.z - 1)
        net.push(block, block, self.base + b, net.at(to, net.c), (to >= 0) & (to <= 3))


class Lines(Chain):
    def start(self):
        super().start()
        self.give(0)

    def give(self, k):
        net = self.net
        b = net.order(k)
        block = self.block(b, net.c)
        net.push(block, block, self.base + 4 + b, net.mate)

    def take(self):
        net = self.net
        for b in range(4):
            net.arrive(self.block(b, 1 - net.c), self.base + 4 + b)


class Slices(Chain):
    def __init__(self, net, full, rows, base):
        self.full, self.rows, self.half = full, rows, full.shape[2] // 2
        super().__init__(net, lambda z, core: self.part(net.d, z, core), base)

    def part(self, slot, z, core, cols=slice(None)):
        first = pl.multiple_of((z * 2 + core) * self.rows, 16)
        return self.full.at[slot, pl.ds(first, self.rows), cols]

    def spread(self, k):
        net = self.net
        b = net.order(k)
        block = self.part(net.d, b, net.c)
        net.push(block, block, self.base + 4 + b, net.across(0))
        net.push(block, block, self.base + 8 + b, net.across(1))
        net.push(block, block, self.base + 20 + b, net.mate)

    def pass_on(self, k):
        net = self.net
        b = net.order(k)
        for kind in (0, 1):
            block = self.part(net.plane[kind], b, net.c)
            net.arrive(block, self.base + 4 + 4 * kind + b)
            half = self.part(net.plane[kind], b, net.c, pl.ds(kind * self.half, self.half))
            net.push(half, half, self.base + 12 + 4 * kind + b, net.across(1 - kind))
            net.push(block, block, self.base + 24 + 4 * kind + b, net.mate)

    def corner(self, k):
        net = self.net
        b = net.order(k)
        for kind in (0, 1):
            half = self.part(net.plane[2], b, net.c, pl.ds(kind * self.half, self.half))
            net.arrive(half, self.base + 12 + 4 * kind + b)
        block = self.part(net.plane[2], b, net.c)
        net.push(block, block, self.base + 32 + b, net.mate)

    def take(self):
        net = self.net
        for b in range(4):
            net.arrive(self.part(net.d, b, 1 - net.c), self.base + 20 + b)
            for kind in range(3):
                net.arrive(self.part(net.plane[kind], b, 1 - net.c), self.base + 24 + 4 * kind + b)


def exchange(net, send, land, base):
    for kind in range(3):
        net.push(send.at[net.plane[kind]], land.at[net.d], base + kind, net.across(kind))
    land[net.d] = send[net.d]


def settle(net, land, wide, rows, base):
    for kind in range(3):
        net.arrive(land.at[net.plane[kind]], base + kind)
    for j in range(4):
        wide[pl.ds(j * rows, rows), : land.shape[2]] = land[j, :rows, :].astype(F32)


def share(net, full, base):
    for kind in range(3):
        net.push(full.at[net.d], full.at[net.d], base + kind, net.across(kind))


def shared(net, full, base):
    for kind in range(3):
        net.arrive(full.at[net.plane[kind]], base + kind)


def turned(tile, cosine, sine):
    lane = lax.broadcasted_iota(jnp.int32, tile.shape, 1)
    other = jnp.where(lax.rem(lane, HD) < HD // 2, pltpu.roll(tile, 128 - HD // 2, 1), pltpu.roll(tile, HD // 2, 1))
    return tile * cosine + other * sine


def front_kernel(
    x_in, cot_in, first_in, scale_in, cos_in, sin_in, att_send, gu_send, down,
    wa, wb, wgu, wd, xn_all, gd_all, mn_all, q_heads, k_heads, v_heads, probs, att, middle,
    att_land, gu_land, wide, kv_all, o_heads, bias, sends, recvs,
):
    net = Net(sends, recvs)
    tok, dim = x_in.shape[1], x_in.shape[2]
    rows = dim // 32
    blk = 4 * rows
    ffr = down.shape[0]
    d, z, c, s = net.d, net.z, net.c, net.s

    a = Slices(net, wa, blk, 16)
    b = Slices(net, wb, blk, 56)
    gu = Lines(net, lambda zz, core: wgu.at[pl.ds(pl.multiple_of((zz * 2 + core) * blk, 16), blk)], 96)
    dn = Lines(net, lambda zz, core: wd.at[pl.ds(pl.multiple_of((zz * 2 + core) * ffr, 16), ffr)], 104)
    kv = Lines(net, lambda zz, core: kv_all.at[zz * 2 + core], 112)

    net.greet()
    exchange(net, att_send, att_land, 0)
    x = x_in[0].astype(F32)
    xn = (x * lax.rsqrt(jnp.mean(x * x, axis=1, keepdims=True) + EPSILON)).astype(BF)
    xn_all[d] = xn
    gd_all[d] = (cot_in[0].astype(F32) * scale_in[1:2, 0:1]).astype(BF)
    wd[pl.ds(pl.multiple_of(s * ffr, 16), ffr), :] = down[...]
    settle(net, att_land, wide, rows, 0)
    own = pl.ds(pl.multiple_of(s * blk, 16), blk)
    wa[d, own, :] = wide[:, :512].astype(BF)
    wb[d, own, :] = wide[:, 512:768].astype(BF)
    a.start()
    a.spread(0)
    exchange(net, gu_send, gu_land, 3)
    dn.start()
    b.start()
    a.step(1)
    a.spread(1)
    a.pass_on(0)
    b.spread(0)
    a.step(2)
    a.spread(2)
    a.pass_on(1)
    a.corner(0)
    settle(net, gu_land, wide, rows, 3)
    wgu[own, :] = wide[...].astype(BF)
    gu.start()
    a.step(3)
    a.spread(3)
    a.pass_on(2)
    a.corner(1)
    b.step(1)
    b.spread(1)
    a.pass_on(3)
    a.corner(2)
    b.step(2)
    b.spread(2)
    a.corner(3)
    a.take()

    cosine, sine = cos_in[...], sin_in[...]
    for j in range(4):
        part = dot_nn(xn, wa[j])
        for i in range(4):
            t = 4 * j + i
            if t == 15:
                continue
            tile = part[:, 128 * i : 128 * i + 128]
            if t < 12:
                tile = turned(tile, cosine, sine)
            if t < 9:
                tile = (tile * (1.0 / math.sqrt(HD))).astype(BF)
                q_heads[2 * t] = tile[:, :HD]
                q_heads[2 * t + 1] = tile[:, HD:]
            else:
                kv_all[s, :, pl.ds(128 * (t - 9), 128)] = tile.astype(BF)
    kv.start()
    share(net, gd_all, 8)
    b.step(3)
    b.spread(3)

    position = s * tok + lax.broadcasted_iota(jnp.int32, (tok, 1), 0)
    key = lax.broadcasted_iota(jnp.int32, bias.shape, 1)
    bias[...] = jnp.where((key <= position) & (key >= first_in[:, 0:1]), 0.0, MASKED)

    for k in range(3):
        b.pass_on(k)
    b.corner(0)
    b.corner(1)
    for k in (1, 2, 3):
        kv.step(k)
        kv.give(k)
        if k == 1:
            dn.step(1)
            dn.give(1)
            b.pass_on(3)
        if k == 2:
            gu.step(1)
            gu.give(1)
            b.corner(2)
    kv.take()
    share(net, xn_all, 11)
    for j in range(8):
        for k in range(KV):
            k_heads[k, pl.ds(tok * j, tok), :] = kv_all[j, :, HD * k : HD * k + HD]
            v_heads[k, pl.ds(tok * j, tok), :] = kv_all[j, :, HD * (KV + k) : HD * (KV + k) + HD]

    def head(h, carry):
        k = lax.div(h, H // KV)
        score = dot_nt(q_heads[h], k_heads[k]) + bias[...]
        expo = jnp.exp(score - jnp.max(score, axis=1, keepdims=True))
        p = (expo / jnp.sum(expo, axis=1, keepdims=True)).astype(BF)
        probs[h] = p
        o_heads[h] = dot_nn(p, v_heads[k])
        return carry

    lax.fori_loop(0, 6, head, 0)
    dn.step(2)
    dn.give(2)
    b.corner(3)
    b.take()
    lax.fori_loop(6, 12, head, 0)
    gu.step(2)
    gu.give(2)
    lax.fori_loop(12, 18, head, 0)
    for j in range(H // 2):
        att[:, 128 * j : 128 * j + 128] = jnp.concatenate([o_heads[2 * j], o_heads[2 * j + 1]], axis=1).astype(BF)
    full = att[...]
    branch = [dot_nn(full, wb[j]) for j in range(4)] + [dot_nn(full, wa[3, :, 384:])]
    mid = x_in[0].astype(F32) + scale_in[0:1, 0:1] * jnp.concatenate(branch, axis=1)
    middle[...] = mid
    mn_all[d] = (mid * lax.rsqrt(jnp.mean(mid * mid, axis=1, keepdims=True) + EPSILON)).astype(BF)
    share(net, mn_all, 120)
    dn.step(3)
    dn.give(3)
    gu.step(3)
    gu.give(3)
    shared(net, gd_all, 8)
    shared(net, xn_all, 11)
    dn.take()
    gu.take()
    shared(net, mn_all, 120)
    net.finish()


def front(x, cot, first, scale, cosine, sine, att_send, gu_send, down):
    tok, dim = x.shape[1:]
    ns = 8
    length = tok * ns
    hid = down.shape[0] * ns
    vm = pl.BlockSpec(memory_space=pltpu.VMEM)
    outs = [
        ((4, dim, 512), BF),
        ((4, dim, 256), BF),
        ((dim, 2 * hid), BF),
        ((hid, dim), BF),
        ((4, tok, dim), BF),
        ((4, tok, dim), BF),
        ((4, tok, dim), BF),
        ((H, tok, HD), BF),
        ((KV, length, HD), BF),
        ((KV, length, HD), BF),
        ((H, tok, length), BF),
        ((tok, H * HD), BF),
        ((tok, dim), F32),
    ]
    return pl.pallas_call(
        front_kernel,
        out_shape=[jax.ShapeDtypeStruct(*o) for o in outs],
        in_specs=[vm] * 9,
        out_specs=[vm] * len(outs),
        scratch_shapes=[
            pltpu.VMEM(att_send.shape, BF),
            pltpu.VMEM(gu_send.shape, BF),
            pltpu.VMEM((dim // 8, 2 * hid), F32),
            pltpu.VMEM((ns, tok, 2 * KV * HD), BF),
            pltpu.VMEM((H, tok, HD), F32),
            pltpu.VMEM((tok, length), F32),
            pltpu.SemaphoreType.DMA((160,)),
            pltpu.SemaphoreType.DMA((128,)),
        ],
        compiler_params=pltpu.CompilerParams(collective_id=0, has_side_effects=True, vmem_limit_bytes=LIMIT),
        name="k_front",
    )(x, cot, first, scale, cosine, sine, att_send, gu_send, down)


def shards_by_kernels(
    hidden_in,
    attn_norm,
    query_weight,
    key_weight,
    value_weight,
    output_weight,
    mlp_norm,
    gate_weight,
    up_weight,
    down_weight,
    cotangent,
    doc_starts,
    keep_mask,
    keep_rate,
    seq_order,
):
    tok = hidden_in.shape[1]
    ns, nd = lax.axis_size("seq"), lax.axis_size("dp")
    length = tok * ns
    rows = query_weight.shape[0]
    ffr = down_weight.shape[0]
    dim = hidden_in.shape[2]
    groups = H // KV
    nq, nk = H * HD, KV * HD
    score_scale = 1.0 / math.sqrt(HD)
    me_s, me_d = lax.axis_index("seq"), lax.axis_index("dp")
    sample = jnp.sum(jnp.where(jnp.arange(nd) == me_d, seq_order, 0))
    pick = jnp.arange(nd) == sample
    doc_begin = jnp.sum(jnp.where(pick[:, None], doc_starts, 0), axis=0)
    keep_flags = jnp.sum(jnp.where(pick[:, None], keep_mask, 0), axis=0).astype(jnp.float32)
    attn_scale = keep_flags[0] / keep_rate[0]
    mlp_scale = keep_flags[1] / keep_rate[1]
    positions = me_s * tok + jnp.arange(tok)
    first = jnp.max(jnp.where(doc_begin[None, :] <= positions[:, None], doc_begin[None, :], 0), axis=1)
    gain_one, gain_two = attn_norm[:, None], mlp_norm[:, None]

    qkv_rows = low(jnp.concatenate([query_weight, key_weight, value_weight], axis=1).astype(jnp.float32) * gain_one)
    def split_hidden(w):
        w = low(w.astype(jnp.float32) * gain_two).reshape(rows, ns, nd, ffr)
        w = jnp.transpose(w, (0, 2, 1, 3)).reshape(rows, nd * ns * ffr)
        return w

    gu = jnp.concatenate(
        [split_hidden(gate_weight).reshape(rows, nd, -1), split_hidden(up_weight).reshape(rows, nd, -1)], axis=2
    )
    att_send = jnp.stack(
        [jnp.concatenate([qkv_rows[:, 512 * j : 512 * j + 512], output_weight[:, 256 * j : 256 * j + 256]], axis=1) for j in range(3)]
        + [jnp.concatenate([qkv_rows[:, 1536:], output_weight[:, 1024:], output_weight[:, 768:1024]], axis=1)]
    )
    pad = ((0, 0), (0, -rows % 16), (0, 0))
    x = hidden_in[0].astype(jnp.float32)
    r_one = lax.rsqrt(jnp.mean(x * x, axis=-1, keepdims=True) + EPSILON)
    inverse_freq = ROPE_BASE ** (-2.0 * jnp.arange(HD // 2, dtype=jnp.float32) / HD)
    angles = positions.astype(jnp.float32)[:, None] * inverse_freq[None, :]
    cosine = jnp.tile(jnp.cos(angles), (1, 4))
    sine = jnp.tile(jnp.concatenate([-jnp.sin(angles), jnp.sin(angles)], axis=1), (1, 2))
    scale = jnp.broadcast_to(jnp.stack([attn_scale, mlp_scale])[:, None], (2, 128))
    firsts = jnp.broadcast_to(first[:, None], (tok, 128))
    wa, wb, w_gu, w_down, xn_all, gd_all, mn_all, queries, k_all, v_all, probs, att, middle = front(
        hidden_in, cotangent, firsts, scale, cosine, sine, jnp.pad(att_send, pad), jnp.pad(jnp.transpose(gu, (1, 0, 2)), pad), down_weight
    )
    w_qkv = jnp.concatenate([wa[0], wa[1], wa[2], wa[3][:, :384]], axis=1)
    w_out = jnp.concatenate([wb[0], wb[1], wb[2], wb[3], wa[3][:, 384:]], axis=1)
    hid = w_down.shape[0]
    r_two = lax.rsqrt(jnp.mean(middle * middle, axis=-1, keepdims=True) + EPSILON)
    cosine, sine = cosine[:, None, :HD], sine[:, None, :HD]
    queries = jnp.transpose(queries, (1, 0, 2)).reshape(tok, KV, groups, HD)
    k_all, v_all = jnp.transpose(k_all, (1, 0, 2)), jnp.transpose(v_all, (1, 0, 2))
    probs = probs.reshape(KV, groups, tok, length)
    xn_all, gd_all, mn_all = xn_all.reshape(4 * tok, dim), gd_all.reshape(4 * tok, dim), mn_all.reshape(4 * tok, dim)

    def turn_back(v):
        return v * cosine - swap_halves(v) * sine

    cot = cotangent[0].astype(jnp.float32)
    att_all = lax.all_gather(att, "dp", axis=0, tiled=True)
    gate, up = dot(mn_all, w_gu[:, :hid]), dot(mn_all, w_gu[:, hid:])
    sig = jax.nn.sigmoid(gate)
    act_gate = gate * sig
    act = low(act_gate * up)
    g_act = contract_cols(gd_all, w_down)
    gg = low(g_act * up * (sig * (1.0 + gate * (1.0 - sig))))
    gu_in = low(g_act * act_gate)
    gboth = jnp.concatenate([gg, gu_in], axis=1)
    g_mn = lax.psum_scatter(low(contract_cols(gboth, w_gu)), "dp", scatter_dimension=0, tiled=True).astype(jnp.float32)
    branch = lax.psum_scatter(low(dot(act, w_down)), "dp", scatter_dimension=0, tiled=True).astype(jnp.float32)
    block_output = low(middle + mlp_scale * branch)[None]
    m_gu = lax.psum_scatter(low(contract_rows(mn_all, gboth)), "seq", scatter_dimension=0, tiled=True)
    m_down = lax.psum_scatter(low(contract_rows(act, gd_all)), "seq", scatter_dimension=0, tiled=True)

    def norm_back(e, v, r):
        return r * e - v * (r * r * r) * jnp.mean(e * v, axis=-1, keepdims=True)

    g_mid = cot + norm_back(g_mn, middle, r_two)
    gba = low(attn_scale * g_mid)
    g_att = low(contract_cols(gba, w_out)).reshape(tok, KV, groups, HD)
    g_probs = jnp.einsum("tkgd,skd->kgts", g_att, v_all, preferred_element_type=jnp.float32)
    delta = jnp.sum(probs.astype(jnp.float32) * g_probs, axis=-1)
    g_scores = low(probs.astype(jnp.float32) * (g_probs - delta[..., None]))
    g_q = jnp.einsum("kgts,skd->tkgd", g_scores, k_all, preferred_element_type=jnp.float32) * score_scale
    g_k = jnp.einsum("kgts,tkgd->skd", g_scores, queries, preferred_element_type=jnp.float32)
    g_v = jnp.einsum("kgts,tkgd->skd", probs, g_att, preferred_element_type=jnp.float32)
    g_kv = low(jnp.concatenate([g_k.reshape(length, nk), g_v.reshape(length, nk)], axis=1))
    g_kv = lax.psum_scatter(g_kv, "seq", scatter_dimension=0, tiled=True).astype(jnp.float32)
    g_q_in = low(turn_back(g_q.reshape(tok, H, HD))).reshape(tok, nq)
    g_k_in = low(turn_back(g_kv[:, :nk].reshape(tok, KV, HD))).reshape(tok, nk)
    g_qkv = jnp.concatenate([g_q_in, g_k_in, low(g_kv[:, nk:])], axis=1)
    g_xn = contract_cols(g_qkv, w_qkv)
    input_grad = (g_mid + norm_back(g_xn, x, r_one))[None]

    cut = jnp.concatenate([g_qkv.reshape(tok, nd, -1), gba.reshape(tok, nd, -1)], axis=2)
    wq = g_qkv.shape[1] // nd
    cut = lax.all_to_all(cut, "dp", split_axis=1, concat_axis=0, tiled=True).reshape(nd * tok, -1)
    m_att = jnp.concatenate([contract_rows(xn_all, cut[:, :wq]), contract_rows(att_all, cut[:, wq:])], axis=1)
    m_att = lax.psum_scatter(low(m_att), "seq", scatter_dimension=0, tiled=True)

    back = jnp.concatenate([m_gu, m_att], axis=1)
    back = lax.all_to_all(back.reshape(nd, rows, 1, -1), "dp", split_axis=0, concat_axis=2, tiled=True)
    back = back.reshape(rows, nd, -1).astype(jnp.float32)

    def whole_hidden(m):
        return jnp.transpose(m.reshape(rows, nd, ns, ffr), (0, 2, 1, 3)).reshape(rows, -1)

    m_gate, m_up = whole_hidden(back[:, :, :hid]), whole_hidden(back[:, :, hid : 2 * hid])
    m_qkv = back[:, :, 2 * hid : 2 * hid + wq].reshape(rows, -1)
    g_out = back[:, :, 2 * hid + wq :].reshape(rows, -1)

    def weigh(w, m):
        return jnp.sum(w.astype(jnp.float32) * m, axis=1)

    m_q, m_k, m_v = m_qkv[:, :nq], m_qkv[:, nq : nq + nk], m_qkv[:, nq + nk :]
    g_norm_one = weigh(query_weight, m_q) + weigh(key_weight, m_k) + weigh(value_weight, m_v)
    g_norm_two = weigh(gate_weight, m_gate) + weigh(up_weight, m_up)
    return (
        block_output,
        input_grad,
        g_norm_one,
        m_q * gain_one,
        m_k * gain_one,
        m_v * gain_one,
        g_out,
        g_norm_two,
        m_gate * gain_two,
        m_up * gain_two,
        m_down.astype(jnp.float32),
    )


def solution(mesh):
    placed = (
        P("dp", "seq", None),
        P(("seq", "dp")),
        P(("seq", "dp"), None),
        P(("seq", "dp"), None),
        P(("seq", "dp"), None),
        P(("seq", "dp"), None),
        P(("seq", "dp")),
        P(("seq", "dp"), None),
        P(("seq", "dp"), None),
        P(("seq", "dp"), None),
        P("dp", "seq", None),
        P(),
        P(),
        P(),
        P(),
    )
    fits = mesh.shape["seq"] == 8 and mesh.shape["dp"] == 4
    return jax.shard_map(
        shards_by_kernels if fits else shards,
        mesh=mesh,
        in_specs=placed,
        out_specs=(
            P("dp", "seq", None),
            P("dp", "seq", None),
            P(("seq", "dp")),
            P(("seq", "dp"), None),
            P(("seq", "dp"), None),
            P(("seq", "dp"), None),
            P(("seq", "dp"), None),
            P(("seq", "dp")),
            P(("seq", "dp"), None),
            P(("seq", "dp"), None),
            P(("seq", "dp"), None),
        ),
        check_vma=False,
    )
```

```python
import math

import jax
import jax.numpy as jnp
from jax import lax
from jax.experimental import pallas as pl
from jax.experimental.pallas import tpu as pltpu
from jax.sharding import PartitionSpec as P

H = 18
KV = 6
HD = 64


EPSILON = 1e-05
ROPE_BASE = 10000.0
MASKED = -1e30


def contract_rows(left_rows, right_rows):
    return lax.dot_general(
        left_rows, right_rows, (((0,), (0,)), ((), ())), preferred_element_type=jnp.float32
    )


def contract_cols(left_mat, right_mat):
    return lax.dot_general(
        left_mat, right_mat, (((1,), (1,)), ((), ())), preferred_element_type=jnp.float32
    )


def low(v):
    return v.astype(jnp.bfloat16)


def dot(a, b):
    return jnp.dot(a, b, preferred_element_type=jnp.float32)


def swap_halves(vectors):
    half = HD // 2
    return jnp.concatenate([vectors[..., half:], vectors[..., :half]], axis=-1)


def shards(
    hidden_in,
    attn_norm,
    query_weight,
    key_weight,
    value_weight,
    output_weight,
    mlp_norm,
    gate_weight,
    up_weight,
    down_weight,
    cotangent,
    doc_starts,
    keep_mask,
    keep_rate,
    seq_order,
):
    tok = hidden_in.shape[1]
    ns, nd = lax.axis_size("seq"), lax.axis_size("dp")
    length = tok * ns
    rows = query_weight.shape[0]
    ffr = down_weight.shape[0]
    dim = hidden_in.shape[2]
    groups = H // KV
    nq, nk = H * HD, KV * HD
    score_scale = 1.0 / math.sqrt(HD)
    me_s, me_d = lax.axis_index("seq"), lax.axis_index("dp")
    sample = jnp.sum(jnp.where(jnp.arange(nd) == me_d, seq_order, 0))
    pick = jnp.arange(nd) == sample
    doc_begin = jnp.sum(jnp.where(pick[:, None], doc_starts, 0), axis=0)
    keep_flags = jnp.sum(jnp.where(pick[:, None], keep_mask, 0), axis=0).astype(jnp.float32)
    attn_scale = keep_flags[0] / keep_rate[0]
    mlp_scale = keep_flags[1] / keep_rate[1]
    positions = me_s * tok + jnp.arange(tok)
    first = jnp.max(jnp.where(doc_begin[None, :] <= positions[:, None], doc_begin[None, :], 0), axis=1)
    gain_one, gain_two = attn_norm[:, None], mlp_norm[:, None]

    qkv_rows = low(jnp.concatenate([query_weight, key_weight, value_weight], axis=1).astype(jnp.float32) * gain_one)
    w_qkv = lax.all_gather(qkv_rows, ("seq", "dp"), axis=0, tiled=True)
    w_out = lax.all_gather(output_weight, ("seq", "dp"), axis=0, tiled=True)

    def split_hidden(w):
        w = low(w.astype(jnp.float32) * gain_two).reshape(rows, ns, nd, ffr)
        w = jnp.transpose(w, (0, 2, 1, 3)).reshape(rows, nd * ns * ffr)
        return w

    gu = jnp.concatenate(
        [split_hidden(gate_weight).reshape(rows, nd, -1), split_hidden(up_weight).reshape(rows, nd, -1)], axis=2
    )
    gu = lax.all_to_all(gu, "dp", split_axis=1, concat_axis=0, tiled=True).reshape(nd * rows, -1)
    w_gu = lax.all_gather(gu, "seq", axis=0, tiled=True)
    w_down = lax.all_gather(down_weight, "seq", axis=0, tiled=True)
    hid = w_down.shape[0]

    x = hidden_in[0].astype(jnp.float32)
    r_one = lax.rsqrt(jnp.mean(x * x, axis=-1, keepdims=True) + EPSILON)
    xn = low(x * r_one)
    qkv = dot(xn, w_qkv)
    inverse_freq = ROPE_BASE ** (-2.0 * jnp.arange(HD // 2, dtype=jnp.float32) / HD)
    angles = positions.astype(jnp.float32)[:, None] * inverse_freq[None, :]
    cosine = jnp.tile(jnp.cos(angles), (1, 2))[:, None, :]
    sine = jnp.concatenate([-jnp.sin(angles), jnp.sin(angles)], axis=1)[:, None, :]

    def turn(v):
        return v * cosine + swap_halves(v) * sine

    def turn_back(v):
        return v * cosine - swap_halves(v) * sine

    queries = low(turn(qkv[:, :nq].reshape(tok, H, HD))).reshape(tok, KV, groups, HD)
    keys = low(turn(qkv[:, nq : nq + nk].reshape(tok, KV, HD)))
    kv = jnp.concatenate([keys.reshape(tok, nk), low(qkv[:, nq + nk :])], axis=1)
    kv_all = lax.all_gather(kv, "seq", axis=0, tiled=True)
    k_all, v_all = kv_all[:, :nk].reshape(length, KV, HD), kv_all[:, nk:].reshape(length, KV, HD)
    key_pos = jnp.arange(length)
    allowed = (key_pos[None, :] <= positions[:, None]) & (key_pos[None, :] >= first[:, None])
    scores = jnp.einsum("tkgd,skd->kgts", queries, k_all, preferred_element_type=jnp.float32) * score_scale
    scores = jnp.where(allowed, scores, MASKED)
    expo = jnp.exp(scores - jnp.max(scores, axis=-1, keepdims=True))
    probs = low(expo / jnp.sum(expo, axis=-1, keepdims=True))
    attended = jnp.einsum("kgts,skd->tkgd", probs, v_all, preferred_element_type=jnp.float32)
    att = low(attended.reshape(tok, nq))
    middle = x + attn_scale * dot(att, w_out)
    r_two = lax.rsqrt(jnp.mean(middle * middle, axis=-1, keepdims=True) + EPSILON)
    mn = low(middle * r_two)

    cot = cotangent[0].astype(jnp.float32)
    side = lax.all_gather(jnp.concatenate([xn, low(mlp_scale * cot), att], axis=1), "dp", axis=0, tiled=True)
    xn_all, gd_all, att_all = side[:, :dim], side[:, dim : 2 * dim], side[:, 2 * dim :]
    mn_all = lax.all_gather(mn, "dp", axis=0, tiled=True)
    gate, up = dot(mn_all, w_gu[:, :hid]), dot(mn_all, w_gu[:, hid:])
    sig = jax.nn.sigmoid(gate)
    act_gate = gate * sig
    act = low(act_gate * up)
    g_act = contract_cols(gd_all, w_down)
    gg = low(g_act * up * (sig * (1.0 + gate * (1.0 - sig))))
    gu_in = low(g_act * act_gate)
    gboth = jnp.concatenate([gg, gu_in], axis=1)
    g_mn = lax.psum_scatter(low(contract_cols(gboth, w_gu)), "dp", scatter_dimension=0, tiled=True).astype(jnp.float32)
    branch = lax.psum_scatter(low(dot(act, w_down)), "dp", scatter_dimension=0, tiled=True).astype(jnp.float32)
    block_output = low(middle + mlp_scale * branch)[None]
    m_gu = lax.psum_scatter(low(contract_rows(mn_all, gboth)), "seq", scatter_dimension=0, tiled=True)
    m_down = lax.psum_scatter(low(contract_rows(act, gd_all)), "seq", scatter_dimension=0, tiled=True)

    def norm_back(e, v, r):
        return r * e - v * (r * r * r) * jnp.mean(e * v, axis=-1, keepdims=True)

    g_mid = cot + norm_back(g_mn, middle, r_two)
    gba = low(attn_scale * g_mid)
    g_att = low(contract_cols(gba, w_out)).reshape(tok, KV, groups, HD)
    g_probs = jnp.einsum("tkgd,skd->kgts", g_att, v_all, preferred_element_type=jnp.float32)
    delta = jnp.einsum("tkgd,tkgd->kgt", g_att.astype(jnp.float32), attended)
    g_scores = low(probs.astype(jnp.float32) * (g_probs - delta[..., None]))
    g_q = jnp.einsum("kgts,skd->tkgd", g_scores, k_all, preferred_element_type=jnp.float32) * score_scale
    g_k = jnp.einsum("kgts,tkgd->skd", g_scores, queries, preferred_element_type=jnp.float32) * score_scale
    g_v = jnp.einsum("kgts,tkgd->skd", probs, g_att, preferred_element_type=jnp.float32)
    g_kv = low(jnp.concatenate([g_k.reshape(length, nk), g_v.reshape(length, nk)], axis=1))
    g_kv = lax.psum_scatter(g_kv, "seq", scatter_dimension=0, tiled=True).astype(jnp.float32)
    g_q_in = low(turn_back(g_q.reshape(tok, H, HD))).reshape(tok, nq)
    g_k_in = low(turn_back(g_kv[:, :nk].reshape(tok, KV, HD))).reshape(tok, nk)
    g_qkv = jnp.concatenate([g_q_in, g_k_in, low(g_kv[:, nk:])], axis=1)
    g_xn = contract_cols(g_qkv, w_qkv)
    input_grad = (g_mid + norm_back(g_xn, x, r_one))[None]

    cut = jnp.concatenate([g_qkv.reshape(tok, nd, -1), gba.reshape(tok, nd, -1)], axis=2)
    wq = g_qkv.shape[1] // nd
    cut = lax.all_to_all(cut, "dp", split_axis=1, concat_axis=0, tiled=True).reshape(nd * tok, -1)
    m_att = jnp.concatenate([contract_rows(xn_all, cut[:, :wq]), contract_rows(att_all, cut[:, wq:])], axis=1)
    m_att = lax.psum_scatter(low(m_att), "seq", scatter_dimension=0, tiled=True)

    back = jnp.concatenate([m_gu, m_att], axis=1)
    back = lax.all_to_all(back.reshape(nd, rows, 1, -1), "dp", split_axis=0, concat_axis=2, tiled=True)
    back = back.reshape(rows, nd, -1).astype(jnp.float32)

    def whole_hidden(m):
        return jnp.transpose(m.reshape(rows, nd, ns, ffr), (0, 2, 1, 3)).reshape(rows, -1)

    m_gate, m_up = whole_hidden(back[:, :, :hid]), whole_hidden(back[:, :, hid : 2 * hid])
    m_qkv = back[:, :, 2 * hid : 2 * hid + wq].reshape(rows, -1)
    g_out = back[:, :, 2 * hid + wq :].reshape(rows, -1)

    def weigh(w, m):
        return jnp.sum(w.astype(jnp.float32) * m, axis=1)

    m_q, m_k, m_v = m_qkv[:, :nq], m_qkv[:, nq : nq + nk], m_qkv[:, nq + nk :]
    g_norm_one = weigh(query_weight, m_q) + weigh(key_weight, m_k) + weigh(value_weight, m_v)
    g_norm_two = weigh(gate_weight, m_gate) + weigh(up_weight, m_up)
    return (
        block_output,
        input_grad,
        g_norm_one,
        m_q * gain_one,
        m_k * gain_one,
        m_v * gain_one,
        g_out,
        g_norm_two,
        m_gate * gain_two,
        m_up * gain_two,
        m_down.astype(jnp.float32),
    )


MESH = pl.DeviceIdType.MESH
LIMIT = 60 * 2**20
BF, F32 = jnp.bfloat16, jnp.float32


def dot_nn(a, b):
    return lax.dot_general(a, b, (((1,), (0,)), ((), ())), preferred_element_type=F32)


def dot_nt(a, b):
    return lax.dot_general(a, b, (((1,), (1,)), ((), ())), preferred_element_type=F32)


def dot_tn(a, b):
    return lax.dot_general(a, b, (((0,), (0,)), ((), ())), preferred_element_type=F32)


class Net:
    def __init__(self, sends, recvs):
        self.sends, self.recvs, self.count, self.open, self.used = sends, recvs, 0, [], 0
        self.s, self.d = lax.axis_index("seq"), lax.axis_index("dp")
        self.z, self.c = lax.div(self.s, 2), lax.rem(self.s, 2)
        y, x = lax.div(self.d, 2), lax.rem(self.d, 2)
        self.plane = (y * 2 + 1 - x, (1 - y) * 2 + x, 3 - self.d)
        self.mate = self.at(self.z, 1 - self.c)

    def room(self, count):
        base = self.used
        self.used += count
        return base

    def at(self, z, core):
        return {"seq": z * 2 + core, "dp": self.d}

    def across(self, kind):
        return {"seq": self.s, "dp": self.plane[kind]}

    def greet(self):
        barrier = pltpu.get_barrier_semaphore()
        peers = [self.mate] + [self.across(k) for k in range(3)]
        peers += [self.at(lax.rem(self.z + k, 4), self.c) for k in (1, 2, 3)]
        for peer in peers:
            pl.semaphore_signal(barrier, inc=1, device_id=peer, device_id_type=MESH)
        pl.semaphore_wait(barrier, len(peers))

    def copy(self, src, dst, send, recv, peer):
        return pltpu.make_async_remote_copy(
            src_ref=src,
            dst_ref=dst,
            send_sem=self.sends.at[send],
            recv_sem=self.recvs.at[recv],
            device_id=peer,
            device_id_type=MESH,
        )

    def push(self, src, dst, recv, peer, when=None):
        copy = self.copy(src, dst, self.count, recv, peer)
        self.count += 1
        if when is None:
            copy.start()
        else:
            pl.when(when)(copy.start)
        self.open.append((copy, when))

    def arrive(self, dst, recv, when=None):
        copy = self.copy(dst, dst, 0, recv, self.mate)
        if when is None:
            copy.wait_recv()
        else:
            pl.when(when)(copy.wait_recv)

    def finish(self):
        for copy, when in self.open:
            if when is None:
                copy.wait_send()
            else:
                pl.when(when)(copy.wait_send)
        self.open = []

    def order(self, step):
        if step == 0:
            return self.z
        table = ((1, 0, 3, 2), (2, 2, 1, 1), (3, 3, 0, 0))[step - 1]
        z = self.z
        return jnp.where(z == 0, table[0], jnp.where(z == 1, table[1], jnp.where(z == 2, table[2], table[3])))


class Chain:
    def __init__(self, net, block, room=4):
        self.net, self.block, self.base = net, block, net.room(room)

    def start(self):
        net = self.net
        own = self.block(net.z, net.c)
        net.push(own, own, self.base + net.z, net.at(net.z + 1, net.c), net.z < 3)
        net.push(own, own, self.base + net.z, net.at(net.z - 1, net.c), net.z > 0)

    def step(self, k):
        net = self.net
        b = net.order(k)
        block = self.block(b, net.c)
        net.arrive(block, self.base + b)
        to = jnp.where(b < net.z, net.z + 1, net.z - 1)
        net.push(block, block, self.base + b, net.at(to, net.c), (to >= 0) & (to <= 3))


class Lines(Chain):
    def __init__(self, net, block):
        super().__init__(net, block, 8)

    def start(self):
        super().start()
        self.give(0)

    def give(self, k):
        net = self.net
        b = net.order(k)
        block = self.block(b, net.c)
        net.push(block, block, self.base + 4 + b, net.mate)

    def take(self):
        net = self.net
        for b in range(4):
            net.arrive(self.block(b, 1 - net.c), self.base + 4 + b)


class Slices(Chain):
    def __init__(self, net, full, rows):
        self.full, self.rows, self.half = full, rows, rows // 32 * 16
        super().__init__(net, lambda z, core: self.part(net.d, z, core), 36)

    def part(self, slot, z, core, half=None):
        first = pl.multiple_of((z * 2 + core) * self.rows, 16)
        if half is None:
            return self.full.at[slot, pl.ds(first, self.rows)]
        if half == 0:
            return self.full.at[slot, pl.ds(first, self.half)]
        return self.full.at[slot, pl.ds(pl.multiple_of(first + self.half, 16), self.rows - self.half)]

    def spread(self, k):
        net = self.net
        b = net.order(k)
        block = self.part(net.d, b, net.c)
        net.push(block, block, self.base + 4 + b, net.across(0))
        net.push(block, block, self.base + 8 + b, net.across(1))
        net.push(block, block, self.base + 20 + b, net.mate)

    def pass_on(self, k):
        net = self.net
        b = net.order(k)
        for kind in (0, 1):
            block = self.part(net.plane[kind], b, net.c)
            net.arrive(block, self.base + 4 + 4 * kind + b)
            half = self.part(net.plane[kind], b, net.c, kind)
            net.push(half, half, self.base + 12 + 4 * kind + b, net.across(1 - kind))
            net.push(block, block, self.base + 24 + 4 * kind + b, net.mate)

    def corner(self, k):
        net = self.net
        b = net.order(k)
        for kind in (0, 1):
            half = self.part(net.plane[2], b, net.c, kind)
            net.arrive(half, self.base + 12 + 4 * kind + b)
        block = self.part(net.plane[2], b, net.c)
        net.push(block, block, self.base + 32 + b, net.mate)

    def take(self):
        net = self.net
        for b in range(4):
            net.arrive(self.part(net.d, b, 1 - net.c), self.base + 20 + b)
            for kind in range(3):
                net.arrive(self.part(net.plane[kind], b, 1 - net.c), self.base + 24 + 4 * kind + b)


class Plane:
    def __init__(self, net, full):
        self.net, self.full, self.base = net, full, net.room(4)
        self.half = full.shape[1] // 2

    def start(self):
        net = self.net
        own = self.full.at[net.d]
        for kind in (0, 1):
            net.push(own, own, self.base + kind, net.across(kind))

    def pass_on(self):
        net = self.net
        for kind in (0, 1):
            net.arrive(self.full.at[net.plane[kind]], self.base + kind)
            half = self.full.at[net.plane[kind], pl.ds(kind * self.half, self.half)]
            net.push(half, half, self.base + 2 + kind, net.across(1 - kind))

    def take(self):
        net = self.net
        for kind in (0, 1):
            net.arrive(self.full.at[net.plane[2], pl.ds(kind * self.half, self.half)], self.base + 2 + kind)


class Spread:
    def __init__(self, net, send, land):
        self.net, self.send, self.land, self.base = net, send, land, net.room(3)

    def start(self):
        net = self.net
        for kind in (2, 0, 1):
            net.push(self.send(net.plane[kind]), self.land(net.d), self.base + kind, net.across(kind))

    def take(self):
        for kind in range(3):
            self.net.arrive(self.land(self.net.plane[kind]), self.base + kind)


class ToMate:
    def __init__(self, net, send, land):
        self.net, self.send, self.land, self.base = net, send, land, net.room(1)

    def start(self):
        self.net.push(self.send, self.land, self.base, self.net.mate)

    def take(self):
        self.net.arrive(self.land, self.base)


class ToOwners:
    def __init__(self, net, part, land, down=False):
        self.net, self.part, self.land, self.down, self.base = net, part, land, down, net.room(3)

    def start(self):
        net = self.net
        for k in (3, 2, 1):
            to = lax.rem(net.z - k + 4, 4)
            net.push(self.part(to), self.land(k - 1), self.base + k - 1, net.at(to, net.c), (net.z >= k) if self.down else None)

    def take(self):
        net = self.net
        for k in (1, 2, 3):
            net.arrive(self.land(k - 1), self.base + k - 1, (net.z + k <= 3) if self.down else None)


class ChainSum:
    def __init__(self, net, part, land, add):
        self.net, self.part, self.land, self.add, self.base = net, part, land, add, net.room(6)

    def hop(self, i):
        net, z = self.net, net_z(self.net)

        @pl.when((i < z) & (z < 3))
        def _():
            net.arrive(self.land(i), self.base + i)
            self.add(i, i)

        net.push(self.part(i), self.land(i), self.base + i, net.at(z - 1, net.c), i < z)

        @pl.when((3 - i > z) & (z > 0))
        def _():
            net.arrive(self.land(4 - i), self.base + 3 + i)
            self.add(3 - i, 4 - i)

        net.push(self.part(3 - i), self.land(4 - i), self.base + 3 + i, net.at(z + 1, net.c), 3 - i > z)

    def own(self):
        net, z = self.net, net_z(self.net)

        @pl.when(z < 3)
        def _():
            net.arrive(self.land(z), self.base + z)
            self.add(z, z)

        @pl.when(z > 0)
        def _():
            net.arrive(self.land(1 + z), self.base + 6 - z)
            self.add(z, 1 + z)


def net_z(net):
    return net.z


def settle(land, wide, rows):
    for j in range(4):
        wide[pl.ds(j * rows, rows), : land.shape[2]] = land[j, :rows, :].astype(F32)


def turned(tile, cosine, sine):
    lane = lax.broadcasted_iota(jnp.int32, tile.shape, 1)
    other = jnp.where(lax.rem(lane, HD) < HD // 2, pltpu.roll(tile, 128 - HD // 2, 1), pltpu.roll(tile, HD // 2, 1))
    return tile * cosine + other * sine


def own_rows(index, rows):
    return pl.ds(pl.multiple_of(index * rows, 16), rows)


def norm_scale(v):
    return lax.rsqrt(jnp.mean(v * v, axis=1, keepdims=True) + EPSILON)


def norm_pull(e, v):
    r = norm_scale(v)
    return r * e - v * (r * r * r) * jnp.mean(e * v, axis=1, keepdims=True)


def joined(heads, j, tok):
    groups = H // KV
    pair = [heads[h // groups, tok * (h % groups) : tok * (h % groups) + tok, :] for h in (2 * j, 2 * j + 1)]
    return jnp.concatenate(pair, axis=1)


def plane_sum(net, send, land):
    total = send[net.d].astype(F32)
    for kind in range(3):
        total = total + land[net.plane[kind]].astype(F32)
    return total


def layer_kernel(
    x_in, cot_in, first_in, scale_in, cos_in, sin_in, att_send, gu_send, down,
    block_out, input_grad, back_gu, back_att, back_down,
    att_land, gu_land, wide, qkv_land, kv_all, o_heads, bias, wa, wb, wgu, wd,
    xn_all, gd_all, mn_all, att_all, q_heads, k_heads, v_heads, probs, middle, act, gboth, turn_x, turn_n, turn_a,
    gn_send, gn_land, br_send, br_land, gu_mate, gu_zone, dn_mate, dn_zone, gmid, do_heads, dkv, kv_mate, kv_zone, kv_tot,
    cut_land, ma_mate, ma_zone, gx_land, sends, recvs,
):
    net = Net(sends, recvs)
    tok, dim = x_in.shape[1], x_in.shape[2]
    rows = dim // 32
    blk = 4 * rows
    ffr = down.shape[0]
    hid = 8 * ffr
    d, z, c, s = net.d, net.z, net.c, net.s
    span, length = 4 * tok, 8 * tok
    groups = H // KV
    qkv_send = cut_send = act.reshape(4, tok, hid)
    gx_send, gs_heads = gd_all, gboth
    m_att = wb.reshape(4, 4, 2, blk, 384)

    a2a_att = Spread(net, lambda j: att_send.at[j], lambda j: att_land.at[j])
    a2a_gu = Spread(net, lambda j: gu_send.at[j], lambda j: gu_land.at[j])
    a2a_qkv = Spread(net, lambda j: qkv_send.at[j, :, pl.ds(0, 512)], lambda j: qkv_land.at[j])
    a = Lines(net, lambda zz, core: wa.at[own_rows(zz * 2 + core, blk)])
    b = Slices(net, wb, blk)
    gu = Lines(net, lambda zz, core: wgu.at[zz, core])
    dn = Lines(net, lambda zz, core: wd.at[zz, core])
    kv = Lines(net, lambda zz, core: kv_all.at[zz, core])
    xs = Plane(net, xn_all)
    gs = Plane(net, gd_all)
    ms = Plane(net, mn_all)
    ats = Plane(net, att_all)

    net.greet()
    a2a_att.start()
    att_land[d] = att_send[d]
    x = x_in[0].astype(F32)
    xn_all[d] = (x * norm_scale(x)).astype(BF)
    xs.start()
    a2a_gu.start()
    gu_land[d] = gu_send[d]
    gd_all[d] = (cot_in[0].astype(F32) * scale_in[1:2, 0:1]).astype(BF)
    wd[z, c] = down[...]
    a2a_att.take()
    settle(att_land, wide, rows)
    own = own_rows(s, blk)
    wa[own, :] = wide[:, :512].astype(BF)
    wb[d, own, :] = wide[:, 384:768].astype(BF)
    a.start()
    a.step(1)
    a.give(1)
    dn.start()
    xs.pass_on()
    a.step(2)
    a.give(2)
    b.start()
    a.step(3)
    a.give(3)
    a2a_gu.take()
    settle(gu_land, wide, rows)
    wgu[z, c] = wide[...].astype(BF)
    gu.start()
    xs.take()
    a.take()

    cosine, sine = cos_in[...], sin_in[...]
    eighth = 1.0 / math.sqrt(HD)
    for j in range(4):
        part = dot_nn(xn_all[j], wa[...])
        for i in range(4):
            tile = part[:, 128 * i : 128 * i + 128]
            spun = turned(tile, cosine, sine)
            if i < 2:
                tile = spun * eighth
            elif i == 2:
                tile = jnp.where(d < 2, spun, tile)
            else:
                tile = jnp.where(d == 0, spun, jnp.where(d == 2, spun * eighth, tile))
            qkv_send[j, :, 128 * i : 128 * i + 128] = tile.astype(BF)
    a2a_qkv.start()
    qkv_land[d] = qkv_send[d, :, :512]
    b.spread(0)
    b.step(1)
    b.spread(1)
    a2a_qkv.take()
    places = [(0, 256), (0, 384), (1, 256), (1, 384), (2, 256), (3, 256)]
    for i, (j, col) in enumerate(places):
        kv_all[z, c, :, 128 * i : 128 * i + 128] = qkv_land[j, :, col : col + 128]
    kv.start()
    gs.start()
    for t in range(9):
        j, col = (t // 2, (t % 2) * 128) if t < 8 else (2, 384)
        for h in (2 * t, 2 * t + 1):
            at = col + HD * (h % 2)
            q_heads[h // groups, tok * (h % groups) : tok * (h % groups) + tok, :] = qkv_land[j, :, at : at + HD]
    position = s * tok + lax.broadcasted_iota(jnp.int32, (tok, 1), 0)
    key = lax.broadcasted_iota(jnp.int32, bias.shape, 1)
    bias[...] = jnp.where((key <= position) & (key >= first_in[:, 0:1]), 0.0, MASKED)

    kv.step(1)
    kv.give(1)
    b.step(2)
    b.spread(2)
    kv.step(2)
    kv.give(2)
    b.step(3)
    b.spread(3)
    b.pass_on(0)
    b.pass_on(1)
    kv.step(3)
    kv.give(3)
    dn.step(1)
    gu.step(1)
    gs.pass_on()
    b.pass_on(2)
    b.corner(0)
    b.corner(1)
    kv.take()
    for j in range(8):
        for k in range(KV):
            k_heads[k, pl.ds(tok * j, tok), :] = kv_all[j // 2, j % 2, :, HD * k : HD * k + HD]
            v_heads[k, pl.ds(tok * j, tok), :] = kv_all[j // 2, j % 2, :, HD * (KV + k) : HD * (KV + k) + HD]

    def head(h, carry):
        k = lax.div(h, groups)
        mine = pl.ds(pl.multiple_of(lax.rem(h, groups) * tok, tok), tok)
        score = dot_nt(q_heads[k, mine, :], k_heads[k]) + bias[...]
        expo = jnp.exp(score - jnp.max(score, axis=1, keepdims=True))
        p = (expo / jnp.sum(expo, axis=1, keepdims=True)).astype(BF)
        probs[k, mine, :] = p
        o_heads[k, mine, :] = dot_nn(p, v_heads[k])
        return carry

    lax.fori_loop(0, 6, head, 0)
    b.pass_on(3)
    b.corner(2)
    lax.fori_loop(6, 12, head, 0)
    b.corner(3)
    dn.step(2)
    gu.step(2)
    lax.fori_loop(12, 18, head, 0)
    b.take()
    for j in range(H // 2):
        att_all[d, :, 128 * j : 128 * j + 128] = joined(o_heads, j, tok).astype(BF)
    full = att_all[d]
    branch = [dot_nn(full, wb[j, :, 128:]) for j in range(4)] + [dot_nn(full, wb[3, :, :128])]
    mid = x_in[0].astype(F32) + scale_in[0:1, 0:1] * jnp.concatenate(branch, axis=1)
    middle[...] = mid
    mn_all[d] = (mid * norm_scale(mid)).astype(BF)
    gs.take()
    ms.start()
    for k in (1, 2):
        dn.give(k)
        gu.give(k)
    dn.step(3)
    dn.give(3)
    ms.pass_on()
    gu.step(3)
    gu.give(3)
    ms.take()
    dn.take()
    gu.take()
    net.finish()
    ats.start()

    def by_cols(send, land, width):
        return [
            Spread(
                net,
                lambda j, n=n: send.at[j, :, pl.ds(width * n, width)],
                lambda j, n=n: land.at[j, :, pl.ds(width * n, width)],
            )
            for n in range(dim // width)
        ]

    gn, br, gx = by_cols(gn_send, gn_land, 384), by_cols(br_send, br_land, dim), by_cols(gx_send, gx_land, 384)
    wgu_flat, wd_flat = wgu.reshape(dim, 2 * hid), wd.reshape(hid, dim)
    other = 1 - c
    gu_pair = [
        ToMate(net, wgu.at[:, other, :, pl.ds(256 * n, 256)], gu_mate.at[:, :, pl.ds(256 * n, 256)]) for n in range(2 * hid // 256)
    ]
    dn_pair = [ToMate(net, wd.at[:, other, :, pl.ds(384 * n, 384)], dn_mate.at[:, :, pl.ds(384 * n, 384)]) for n in range(3)]

    for n in range(hid // 256):
        cols, ups = pl.ds(256 * n, 256), pl.ds(hid + 256 * n, 256)
        normed = mn_all[...].reshape(span, dim)
        gate = dot_nn(normed, wgu_flat[:, cols])
        up = dot_nn(normed, wgu_flat[:, ups])
        g_act = dot_nt(gd_all[...].reshape(span, dim), wd_flat[cols, :])
        sig = jax.nn.sigmoid(gate)
        swish = gate * sig
        act[:, cols] = (swish * up).astype(BF)
        gboth[:, cols] = (g_act * up * (sig * (1.0 + gate * (1.0 - sig)))).astype(BF)
        gboth[:, ups] = (g_act * swish).astype(BF)
    for n in range(3):
        part = dot_nt(gboth[...], wgu_flat[384 * n : 384 * n + 384, :]).astype(BF)
        gn_send[:, :, 384 * n : 384 * n + 384] = part.reshape(4, tok, 384)
        gn[n].start()
    for n in range(3):
        part = dot_nn(act[...], wd_flat[:, 384 * n : 384 * n + 384]).astype(BF)
        br_send[:, :, 384 * n : 384 * n + 384] = part.reshape(4, tok, 384)
    br[0].start()
    turn_x[...] = mn_all[...].reshape(span, dim).T
    turn_a[...] = act[...].T
    for n in range(2 * hid // 256):
        wgu_flat[:, 256 * n : 256 * n + 256] = dot_nn(turn_x[...], gboth[:, 256 * n : 256 * n + 256]).astype(BF)
        gu_pair[n].start()
    for n in range(3):
        cols = pl.ds(384 * n, 384)
        wd_flat[:, cols] = dot_nn(turn_a[...], gd_all[:, :, cols].reshape(span, 384)).astype(BF)
        dn_pair[n].start()

    def add_gu(block, slot):
        wgu[block, c] = (wgu[block, c].astype(F32) + gu_zone[slot].astype(F32)).astype(BF)

    def add_dn(block, slot):
        wd[block, c] = (wd[block, c].astype(F32) + dn_zone[slot].astype(F32)).astype(BF)

    gu_sum = ChainSum(net, lambda zz: wgu.at[zz, c], lambda k: gu_zone.at[k], add_gu)
    dn_sum = ChainSum(net, lambda zz: wd.at[zz, c], lambda k: dn_zone.at[k], add_dn)
    ats.pass_on()
    for pair in gu_pair:
        pair.take()
    for k in range(4):
        wgu[k, c] = (wgu[k, c].astype(F32) + gu_mate[k].astype(F32)).astype(BF)
    for pair in dn_pair:
        pair.take()
    for k in range(4):
        wd[k, c] = (wd[k, c].astype(F32) + dn_mate[k].astype(F32)).astype(BF)
    gu_sum.hop(0)
    dn_sum.hop(0)

    for n in range(3):
        gn[n].take()
    mid = middle[...]
    g_mid = cot_in[0].astype(F32) + norm_pull(plane_sum(net, gn_send, gn_land), mid)
    gmid[...] = g_mid
    gba = (scale_in[0:1, 0:1] * g_mid).astype(BF)
    for j in range(4):
        cut_send[j, :, 512:768] = gba[:, 256 * j : 256 * j + 256]
    cut_send[3, :, 384:512] = gba[:, 1024:1152]
    cut = lambda cols: Spread(net, lambda j: cut_send.at[j, :, cols], lambda j: cut_land.at[j, :, cols])
    cut_o, cut_q, cut_l = cut(pl.ds(512, 256)), cut(pl.ds(0, 256)), cut(pl.ds(256, 256))
    cut_o.start()
    cut_land[d, :, 512:768] = cut_send[d, :, 512:768]
    g_att = dot_nt(gba[:, 1024:1152], wb[3, :, :128])
    for j in range(4):
        g_att = g_att + dot_nt(gba[:, 256 * j : 256 * j + 256], wb[j, :, 128:])
    for h in range(H):
        do_heads[h // groups, tok * (h % groups) : tok * (h % groups) + tok, :] = g_att[:, HD * h : HD * h + HD].astype(BF)
    gu_sum.hop(1)
    dn_sum.hop(1)

    kv_pair = [ToMate(net, dkv.at[n, :, other], kv_mate.at[n]) for n in range(2)]
    kv_sum = [ToOwners(net, lambda zz, n=n: dkv.at[n, zz, c], lambda k, n=n: kv_zone.at[n, k], True) for n in range(2)]

    def pull(k, carry):
        for g in range(groups):
            mine = pl.ds(tok * g, tok)
            p = probs[k, mine, :].astype(F32)
            t = p * dot_nt(do_heads[k, mine, :], v_heads[k])
            ds = (t - p * jnp.sum(t, axis=1, keepdims=True)).astype(BF)
            gs_heads[mine, :length] = ds
            o_heads[k, mine, :] = dot_nn(ds, k_heads[k]) * eighth
        half, kk = lax.div(k, 3), lax.rem(k, 3)
        for i, (left, right) in enumerate(((q_heads[k], gs_heads[: groups * tok, :length]), (do_heads[k], probs[k]))):
            turned_grad = dot_tn(left, right).astype(BF)
            at = pl.ds(pl.multiple_of(192 * i + HD * kk, HD), HD)
            for j in range(8):
                dkv[half, j // 2, j % 2, at, :] = turned_grad[:, tok * j : tok * j + tok]
        return carry

    def pair_sum(n):
        kv_pair[n].take()
        for k in range(4):
            dkv[n, k, c] = (dkv[n, k, c].astype(F32) + kv_mate[n, k].astype(F32)).astype(BF)
        kv_sum[n].start()

    def grads(p, parts):
        at = 0
        for part in parts:
            wb[p, :, at : at + part.shape[1]] = part.astype(BF)
            at += part.shape[1]
        pair = ToMate(net, m_att.at[p, :, other, :, quarter], ma_mate.at[p])
        pair.start()
        return pair

    def grads_sum(p, pair):
        pair.take()
        for k in range(4):
            m_att[p, k, c, :, quarter] = (m_att[p, k, c, :, quarter].astype(F32) + ma_mate[p, k].astype(F32)).astype(BF)
        out = ToOwners(net, lambda zz: m_att.at[p, zz, c, :, quarter], lambda k: ma_zone.at[p, k])
        out.start()
        return out

    def grads_back(p, out):
        cols = pl.ds(256 * p, 256)
        out.take()
        total = m_att[p, z, c, :, quarter].astype(F32)
        for k in range(3):
            total = total + ma_zone[p, k].astype(F32)
        wide[:, : total.shape[1]] = total
        for j in range(4):
            att_land[j, :rows, cols] = wide[pl.ds(j * rows, rows), : total.shape[1]].astype(BF)
        spread = Spread(net, lambda j: att_land.at[j, :, cols], lambda j: back_att.at[j, :, cols])
        spread.start()
        back_att[d, :, cols] = att_land[d, :, cols]
        return spread

    q_cols, l_cols, o_cols = pl.ds(0, 256), pl.ds(256, 256), pl.ds(512, 256)
    quarter = pl.ds(0, 256)
    lax.fori_loop(0, 3, pull, 0)
    kv_pair[0].start()
    ats.take()
    cut_o.take()
    turn_x[...] = att_all[...].reshape(span, dim).T
    pair_o = grads(2, [dot_nn(turn_x[...], cut_land[:, :, o_cols].reshape(span, 256))])
    pair_sum(0)
    lax.fori_loop(3, 6, pull, 0)
    kv_pair[1].start()
    for t in range(9):
        j, col = (t // 2, (t % 2) * 128) if t < 8 else (2, 384)
        cut_send[j, :, col : col + 128] = turned(joined(o_heads, t, tok), cosine, -sine).astype(BF)
    cut_q.start()
    cut_land[d, :, q_cols] = cut_send[d, :, q_cols]
    pair_sum(1)
    gu_sum.hop(2)
    dn_sum.hop(2)
    sum_o = grads_sum(2, pair_o)
    turn_n[...] = xn_all[...].reshape(span, dim).T
    cut_q.take()
    pair_q = grads(0, [dot_nn(turn_n[...], cut_land[:, :, q_cols].reshape(span, 256))])
    br[0].take()
    block_out[0] = (middle[...] + scale_in[1:2, 0:1] * plane_sum(net, br_send, br_land)).astype(BF)
    sum_q = grads_sum(0, pair_q)

    for n in range(2):
        kv_sum[n].take()
        kv_tot[n] = dkv[n, z, c].astype(F32)
        for k in (1, 2, 3):

            @pl.when(z + k <= 3)
            def _(n=n, k=k):
                kv_tot[n] += kv_zone[n, k - 1].astype(F32)

    keys = jnp.concatenate([kv_tot[0, :192, :], kv_tot[1, :192, :]], axis=0).T
    vals = jnp.concatenate([kv_tot[0, 192:, :], kv_tot[1, 192:, :]], axis=0).T
    late = [turned(keys[:, 128 * i : 128 * i + 128], cosine, -sine) for i in range(3)] + [vals[:, 128 * i : 128 * i + 128] for i in range(3)]
    for tile, (j, col) in zip(late, places):
        cut_send[j, :, col : col + 128] = tile.astype(BF)
    cut_l.start()
    cut_land[d, :, l_cols] = cut_send[d, :, l_cols]
    cut_l.take()
    last = cut_land[:, :, 384:512].reshape(span, 128)
    cuts = cut_land[:, :, :512].reshape(span, 512)
    lane = lax.broadcasted_iota(jnp.int32, cuts.shape, 1)
    cuts = jnp.where((d == 3) & (lane >= 384), jnp.zeros_like(cuts), cuts)
    for n in range(3):
        part = dot_nt(cuts, wa[384 * n : 384 * n + 384, :]).astype(BF)
        gx_send[:, :, 384 * n : 384 * n + 384] = part.reshape(4, tok, 384)
        gx[n].start()
    second = jnp.where(d == 3, dot_nn(turn_x[...], last), dot_nn(turn_n[...], last))
    pair_l = grads(1, [dot_nn(turn_n[...], cut_land[:, :, 256:384].reshape(span, 128)), second])
    sum_l = grads_sum(1, pair_l)
    back_o = grads_back(2, sum_o)
    back_q = grads_back(0, sum_q)
    gu_sum.own()
    dn_sum.own()
    back_down[...] = wd[z, c]
    wide[...] = wgu[z, c].astype(F32)
    for j in range(4):
        gu_land[j, :rows, :] = wide[pl.ds(j * rows, rows), :].astype(BF)
    back_g = Spread(net, lambda j: gu_land.at[j], lambda j: back_gu.at[j])
    back_g.start()
    back_gu[d] = gu_land[d]
    back_l = grads_back(1, sum_l)
    for n in range(3):
        gx[n].take()
    input_grad[0] = gmid[...] + norm_pull(plane_sum(net, gx_send, gx_land), x_in[0].astype(F32))
    for spread in (back_o, back_q, back_g, back_l):
        spread.take()
    net.finish()


def layer(x, cot, first, scale, cosine, sine, att_send, gu_send, down):
    tok, dim = x.shape[1:]
    ns = 8
    length = tok * ns
    ffr = down.shape[0]
    hid = ffr * ns
    blk = dim // ns
    span = 4 * tok
    vm = pl.BlockSpec(memory_space=pltpu.VMEM)
    outs = [
        ((1, tok, dim), BF),
        ((1, tok, dim), F32),
        (gu_send.shape, BF),
        (att_send.shape, BF),
        (down.shape, BF),
    ]
    plane = ((4, tok, dim), BF)
    wide_cut = ((4, tok, 512), BF)
    three = ((KV, 3 * tok, HD), BF)
    scratch = [
        (att_send.shape, BF),
        (gu_send.shape, BF),
        ((blk, 2 * hid), F32),
        wide_cut,
        ((4, 2, tok, 2 * KV * HD), BF),
        ((KV, 3 * tok, HD), F32),
        ((tok, length), F32),
        ((dim, 512), BF),
        ((4, dim, 384), BF),
        ((4, 2, blk, 2 * hid), BF),
        ((4, 2, ffr, dim), BF),
        plane,
        plane,
        plane,
        plane,
        three,
        ((KV, length, HD), BF),
        ((KV, length, HD), BF),
        ((KV, 3 * tok, length), BF),
        ((tok, dim), F32),
        ((span, hid), BF),
        ((span, 2 * hid), BF),
        ((dim, span), BF),
        ((dim, span), BF),
        ((hid, span), BF),
        plane,
        plane,
        plane,
        plane,
        ((4, blk, 2 * hid), BF),
        ((5, blk, 2 * hid), BF),
        ((4, ffr, dim), BF),
        ((5, ffr, dim), BF),
        ((tok, dim), F32),
        three,
        ((2, 4, 2, 384, tok), BF),
        ((2, 4, 384, tok), BF),
        ((2, 3, 384, tok), BF),
        ((2, 384, tok), F32),
        ((4, tok, 768), BF),
        ((3, 4, blk, 256), BF),
        ((3, 3, blk, 256), BF),
        plane,
    ]
    return pl.pallas_call(
        layer_kernel,
        out_shape=[jax.ShapeDtypeStruct(*o) for o in outs],
        in_specs=[vm] * 9,
        out_specs=[vm] * len(outs),
        scratch_shapes=[pltpu.VMEM(*t) for t in scratch] + [pltpu.SemaphoreType.DMA((320,)), pltpu.SemaphoreType.DMA((256,))],
        compiler_params=pltpu.CompilerParams(collective_id=0, has_side_effects=True, vmem_limit_bytes=LIMIT),
        name="k_layer",
    )(x, cot, first, scale, cosine, sine, att_send, gu_send, down)


def shards_by_kernel(
    hidden_in,
    attn_norm,
    query_weight,
    key_weight,
    value_weight,
    output_weight,
    mlp_norm,
    gate_weight,
    up_weight,
    down_weight,
    cotangent,
    doc_starts,
    keep_mask,
    keep_rate,
    seq_order,
):
    tok = hidden_in.shape[1]
    ns, nd = lax.axis_size("seq"), lax.axis_size("dp")
    length = tok * ns
    rows = query_weight.shape[0]
    ffr = down_weight.shape[0]
    dim = hidden_in.shape[2]
    groups = H // KV
    nq, nk = H * HD, KV * HD
    score_scale = 1.0 / math.sqrt(HD)
    me_s, me_d = lax.axis_index("seq"), lax.axis_index("dp")
    sample = jnp.sum(jnp.where(jnp.arange(nd) == me_d, seq_order, 0))
    pick = jnp.arange(nd) == sample
    doc_begin = jnp.sum(jnp.where(pick[:, None], doc_starts, 0), axis=0)
    keep_flags = jnp.sum(jnp.where(pick[:, None], keep_mask, 0), axis=0).astype(jnp.float32)
    attn_scale = keep_flags[0] / keep_rate[0]
    mlp_scale = keep_flags[1] / keep_rate[1]
    positions = me_s * tok + jnp.arange(tok)
    first = jnp.max(jnp.where(doc_begin[None, :] <= positions[:, None], doc_begin[None, :], 0), axis=1)
    gain_one, gain_two = attn_norm[:, None], mlp_norm[:, None]

    qkv_rows = low(jnp.concatenate([query_weight, key_weight, value_weight], axis=1).astype(jnp.float32) * gain_one)
    def split_hidden(w):
        w = low(w.astype(jnp.float32) * gain_two).reshape(rows, ns, nd, ffr)
        w = jnp.transpose(w, (0, 2, 1, 3)).reshape(rows, nd * ns * ffr)
        return w

    gu = jnp.concatenate(
        [split_hidden(gate_weight).reshape(rows, nd, -1), split_hidden(up_weight).reshape(rows, nd, -1)], axis=2
    )
    late = [(9, 10), (11, 12), (13, 8), (14, None)]
    tiles = []
    for j in range(4):
        first_late, second_late = late[j]
        qkv_tile = lambda t: qkv_rows[:, 128 * t : 128 * t + 128]
        second = output_weight[:, 1024:] if second_late is None else qkv_tile(second_late)
        tiles.append(
            jnp.concatenate(
                [qkv_rows[:, 256 * j : 256 * j + 256], qkv_tile(first_late), second, output_weight[:, 256 * j : 256 * j + 256]], axis=1
            )
        )
    att_send = jnp.stack(tiles)
    pad = ((0, 0), (0, -rows % 16), (0, 0))
    inverse_freq = ROPE_BASE ** (-2.0 * jnp.arange(HD // 2, dtype=jnp.float32) / HD)
    angles = positions.astype(jnp.float32)[:, None] * inverse_freq[None, :]
    cosine = jnp.tile(jnp.cos(angles), (1, 4))
    sine = jnp.tile(jnp.concatenate([-jnp.sin(angles), jnp.sin(angles)], axis=1), (1, 2))
    scale = jnp.broadcast_to(jnp.stack([attn_scale, mlp_scale])[:, None], (2, 128))
    firsts = jnp.broadcast_to(first[:, None], (tok, 128))
    block_output, input_grad, back_gu, back_att, m_down = layer(
        hidden_in, cotangent, firsts, scale, cosine, sine, jnp.pad(att_send, pad), jnp.pad(jnp.transpose(gu, (1, 0, 2)), pad), down_weight
    )
    hid = ns * ffr
    back_gu = jnp.transpose(back_gu[:, :rows].astype(jnp.float32), (1, 0, 2))
    m_att = jnp.transpose(back_att[:, :rows].astype(jnp.float32), (1, 0, 2))

    def whole_hidden(m):
        return jnp.transpose(m.reshape(rows, nd, ns, ffr), (0, 2, 1, 3)).reshape(rows, -1)

    m_gate, m_up = whole_hidden(back_gu[:, :, :hid]), whole_hidden(back_gu[:, :, hid:])
    tiles = [None] * 15
    for j in range(4):
        tiles[2 * j], tiles[2 * j + 1] = m_att[:, j, :128], m_att[:, j, 128:256]
        tiles[late[j][0]] = m_att[:, j, 256:384]
        if late[j][1] is not None:
            tiles[late[j][1]] = m_att[:, j, 384:512]
    m_qkv = jnp.concatenate(tiles, axis=1)
    g_out = jnp.concatenate([m_att[:, j, 512:] for j in range(4)] + [m_att[:, 3, 384:512]], axis=1)

    def weigh(w, m):
        return jnp.sum(w.astype(jnp.float32) * m, axis=1)

    m_q, m_k, m_v = m_qkv[:, :nq], m_qkv[:, nq : nq + nk], m_qkv[:, nq + nk :]
    g_norm_one = weigh(query_weight, m_q) + weigh(key_weight, m_k) + weigh(value_weight, m_v)
    g_norm_two = weigh(gate_weight, m_gate) + weigh(up_weight, m_up)
    return (
        block_output,
        input_grad,
        g_norm_one,
        m_q * gain_one,
        m_k * gain_one,
        m_v * gain_one,
        g_out,
        g_norm_two,
        m_gate * gain_two,
        m_up * gain_two,
        m_down.astype(jnp.float32),
    )


def solution(mesh):
    placed = (
        P("dp", "seq", None),
        P(("seq", "dp")),
        P(("seq", "dp"), None),
        P(("seq", "dp"), None),
        P(("seq", "dp"), None),
        P(("seq", "dp"), None),
        P(("seq", "dp")),
        P(("seq", "dp"), None),
        P(("seq", "dp"), None),
        P(("seq", "dp"), None),
        P("dp", "seq", None),
        P(),
        P(),
        P(),
        P(),
    )
    fits = mesh.shape["seq"] == 8 and mesh.shape["dp"] == 4
    return jax.shard_map(
        shards_by_kernel if fits else shards,
        mesh=mesh,
        in_specs=placed,
        out_specs=(
            P("dp", "seq", None),
            P("dp", "seq", None),
            P(("seq", "dp")),
            P(("seq", "dp"), None),
            P(("seq", "dp"), None),
            P(("seq", "dp"), None),
            P(("seq", "dp"), None),
            P(("seq", "dp")),
            P(("seq", "dp"), None),
            P(("seq", "dp"), None),
            P(("seq", "dp"), None),
        ),
        check_vma=False,
    )
```

```python
import math

import jax
import jax.numpy as jnp
from jax import lax
from jax.experimental import pallas as pl
from jax.experimental.pallas import tpu as pltpu
from jax.sharding import PartitionSpec as P

H = 18
KV = 6
HD = 64


EPSILON = 1e-05
ROPE_BASE = 10000.0
MASKED = -1e30


def contract_rows(left_rows, right_rows):
    return lax.dot_general(
        left_rows, right_rows, (((0,), (0,)), ((), ())), preferred_element_type=jnp.float32
    )


def contract_cols(left_mat, right_mat):
    return lax.dot_general(
        left_mat, right_mat, (((1,), (1,)), ((), ())), preferred_element_type=jnp.float32
    )


def low(v):
    return v.astype(jnp.bfloat16)


def dot(a, b):
    return jnp.dot(a, b, preferred_element_type=jnp.float32)


def swap_halves(vectors):
    half = HD // 2
    return jnp.concatenate([vectors[..., half:], vectors[..., :half]], axis=-1)


def shards(
    hidden_in,
    attn_norm,
    query_weight,
    key_weight,
    value_weight,
    output_weight,
    mlp_norm,
    gate_weight,
    up_weight,
    down_weight,
    cotangent,
    doc_starts,
    keep_mask,
    keep_rate,
    seq_order,
):
    tok = hidden_in.shape[1]
    ns, nd = lax.axis_size("seq"), lax.axis_size("dp")
    length = tok * ns
    rows = query_weight.shape[0]
    ffr = down_weight.shape[0]
    dim = hidden_in.shape[2]
    groups = H // KV
    nq, nk = H * HD, KV * HD
    score_scale = 1.0 / math.sqrt(HD)
    me_s, me_d = lax.axis_index("seq"), lax.axis_index("dp")
    sample = jnp.sum(jnp.where(jnp.arange(nd) == me_d, seq_order, 0))
    pick = jnp.arange(nd) == sample
    doc_begin = jnp.sum(jnp.where(pick[:, None], doc_starts, 0), axis=0)
    keep_flags = jnp.sum(jnp.where(pick[:, None], keep_mask, 0), axis=0).astype(jnp.float32)
    attn_scale = keep_flags[0] / keep_rate[0]
    mlp_scale = keep_flags[1] / keep_rate[1]
    positions = me_s * tok + jnp.arange(tok)
    first = jnp.max(jnp.where(doc_begin[None, :] <= positions[:, None], doc_begin[None, :], 0), axis=1)
    gain_one, gain_two = attn_norm[:, None], mlp_norm[:, None]

    qkv_rows = low(jnp.concatenate([query_weight, key_weight, value_weight], axis=1).astype(jnp.float32) * gain_one)
    w_qkv = lax.all_gather(qkv_rows, ("seq", "dp"), axis=0, tiled=True)
    w_out = lax.all_gather(output_weight, ("seq", "dp"), axis=0, tiled=True)

    def split_hidden(w):
        w = low(w.astype(jnp.float32) * gain_two).reshape(rows, ns, nd, ffr)
        w = jnp.transpose(w, (0, 2, 1, 3)).reshape(rows, nd * ns * ffr)
        return w

    gu = jnp.concatenate(
        [split_hidden(gate_weight).reshape(rows, nd, -1), split_hidden(up_weight).reshape(rows, nd, -1)], axis=2
    )
    gu = lax.all_to_all(gu, "dp", split_axis=1, concat_axis=0, tiled=True).reshape(nd * rows, -1)
    w_gu = lax.all_gather(gu, "seq", axis=0, tiled=True)
    w_down = lax.all_gather(down_weight, "seq", axis=0, tiled=True)
    hid = w_down.shape[0]

    x = hidden_in[0].astype(jnp.float32)
    r_one = lax.rsqrt(jnp.mean(x * x, axis=-1, keepdims=True) + EPSILON)
    xn = low(x * r_one)
    qkv = dot(xn, w_qkv)
    inverse_freq = ROPE_BASE ** (-2.0 * jnp.arange(HD // 2, dtype=jnp.float32) / HD)
    angles = positions.astype(jnp.float32)[:, None] * inverse_freq[None, :]
    cosine = jnp.tile(jnp.cos(angles), (1, 2))[:, None, :]
    sine = jnp.concatenate([-jnp.sin(angles), jnp.sin(angles)], axis=1)[:, None, :]

    def turn(v):
        return v * cosine + swap_halves(v) * sine

    def turn_back(v):
        return v * cosine - swap_halves(v) * sine

    queries = low(turn(qkv[:, :nq].reshape(tok, H, HD))).reshape(tok, KV, groups, HD)
    keys = low(turn(qkv[:, nq : nq + nk].reshape(tok, KV, HD)))
    kv = jnp.concatenate([keys.reshape(tok, nk), low(qkv[:, nq + nk :])], axis=1)
    kv_all = lax.all_gather(kv, "seq", axis=0, tiled=True)
    k_all, v_all = kv_all[:, :nk].reshape(length, KV, HD), kv_all[:, nk:].reshape(length, KV, HD)
    key_pos = jnp.arange(length)
    allowed = (key_pos[None, :] <= positions[:, None]) & (key_pos[None, :] >= first[:, None])
    scores = jnp.einsum("tkgd,skd->kgts", queries, k_all, preferred_element_type=jnp.float32) * score_scale
    scores = jnp.where(allowed, scores, MASKED)
    expo = jnp.exp(scores - jnp.max(scores, axis=-1, keepdims=True))
    probs = low(expo / jnp.sum(expo, axis=-1, keepdims=True))
    attended = jnp.einsum("kgts,skd->tkgd", probs, v_all, preferred_element_type=jnp.float32)
    att = low(attended.reshape(tok, nq))
    middle = x + attn_scale * dot(att, w_out)
    r_two = lax.rsqrt(jnp.mean(middle * middle, axis=-1, keepdims=True) + EPSILON)
    mn = low(middle * r_two)

    cot = cotangent[0].astype(jnp.float32)
    side = lax.all_gather(jnp.concatenate([xn, low(mlp_scale * cot), att], axis=1), "dp", axis=0, tiled=True)
    xn_all, gd_all, att_all = side[:, :dim], side[:, dim : 2 * dim], side[:, 2 * dim :]
    mn_all = lax.all_gather(mn, "dp", axis=0, tiled=True)
    gate, up = dot(mn_all, w_gu[:, :hid]), dot(mn_all, w_gu[:, hid:])
    sig = jax.nn.sigmoid(gate)
    act_gate = gate * sig
    act = low(act_gate * up)
    g_act = contract_cols(gd_all, w_down)
    gg = low(g_act * up * (sig * (1.0 + gate * (1.0 - sig))))
    gu_in = low(g_act * act_gate)
    gboth = jnp.concatenate([gg, gu_in], axis=1)
    g_mn = lax.psum_scatter(low(contract_cols(gboth, w_gu)), "dp", scatter_dimension=0, tiled=True).astype(jnp.float32)
    branch = lax.psum_scatter(low(dot(act, w_down)), "dp", scatter_dimension=0, tiled=True).astype(jnp.float32)
    block_output = low(middle + mlp_scale * branch)[None]
    m_gu = lax.psum_scatter(low(contract_rows(mn_all, gboth)), "seq", scatter_dimension=0, tiled=True)
    m_down = lax.psum_scatter(low(contract_rows(act, gd_all)), "seq", scatter_dimension=0, tiled=True)

    def norm_back(e, v, r):
        return r * e - v * (r * r * r) * jnp.mean(e * v, axis=-1, keepdims=True)

    g_mid = cot + norm_back(g_mn, middle, r_two)
    gba = low(attn_scale * g_mid)
    g_att = low(contract_cols(gba, w_out)).reshape(tok, KV, groups, HD)
    g_probs = jnp.einsum("tkgd,skd->kgts", g_att, v_all, preferred_element_type=jnp.float32)
    delta = jnp.einsum("tkgd,tkgd->kgt", g_att.astype(jnp.float32), attended)
    g_scores = low(probs.astype(jnp.float32) * (g_probs - delta[..., None]))
    g_q = jnp.einsum("kgts,skd->tkgd", g_scores, k_all, preferred_element_type=jnp.float32) * score_scale
    g_k = jnp.einsum("kgts,tkgd->skd", g_scores, queries, preferred_element_type=jnp.float32) * score_scale
    g_v = jnp.einsum("kgts,tkgd->skd", probs, g_att, preferred_element_type=jnp.float32)
    g_kv = low(jnp.concatenate([g_k.reshape(length, nk), g_v.reshape(length, nk)], axis=1))
    g_kv = lax.psum_scatter(g_kv, "seq", scatter_dimension=0, tiled=True).astype(jnp.float32)
    g_q_in = low(turn_back(g_q.reshape(tok, H, HD))).reshape(tok, nq)
    g_k_in = low(turn_back(g_kv[:, :nk].reshape(tok, KV, HD))).reshape(tok, nk)
    g_qkv = jnp.concatenate([g_q_in, g_k_in, low(g_kv[:, nk:])], axis=1)
    g_xn = contract_cols(g_qkv, w_qkv)
    input_grad = (g_mid + norm_back(g_xn, x, r_one))[None]

    cut = jnp.concatenate([g_qkv.reshape(tok, nd, -1), gba.reshape(tok, nd, -1)], axis=2)
    wq = g_qkv.shape[1] // nd
    cut = lax.all_to_all(cut, "dp", split_axis=1, concat_axis=0, tiled=True).reshape(nd * tok, -1)
    m_att = jnp.concatenate([contract_rows(xn_all, cut[:, :wq]), contract_rows(att_all, cut[:, wq:])], axis=1)
    m_att = lax.psum_scatter(low(m_att), "seq", scatter_dimension=0, tiled=True)

    back = jnp.concatenate([m_gu, m_att], axis=1)
    back = lax.all_to_all(back.reshape(nd, rows, 1, -1), "dp", split_axis=0, concat_axis=2, tiled=True)
    back = back.reshape(rows, nd, -1).astype(jnp.float32)

    def whole_hidden(m):
        return jnp.transpose(m.reshape(rows, nd, ns, ffr), (0, 2, 1, 3)).reshape(rows, -1)

    m_gate, m_up = whole_hidden(back[:, :, :hid]), whole_hidden(back[:, :, hid : 2 * hid])
    m_qkv = back[:, :, 2 * hid : 2 * hid + wq].reshape(rows, -1)
    g_out = back[:, :, 2 * hid + wq :].reshape(rows, -1)

    def weigh(w, m):
        return jnp.sum(w.astype(jnp.float32) * m, axis=1)

    m_q, m_k, m_v = m_qkv[:, :nq], m_qkv[:, nq : nq + nk], m_qkv[:, nq + nk :]
    g_norm_one = weigh(query_weight, m_q) + weigh(key_weight, m_k) + weigh(value_weight, m_v)
    g_norm_two = weigh(gate_weight, m_gate) + weigh(up_weight, m_up)
    return (
        block_output,
        input_grad,
        g_norm_one,
        m_q * gain_one,
        m_k * gain_one,
        m_v * gain_one,
        g_out,
        g_norm_two,
        m_gate * gain_two,
        m_up * gain_two,
        m_down.astype(jnp.float32),
    )


MESH = pl.DeviceIdType.MESH
LIMIT = 60 * 2**20
BF, F32 = jnp.bfloat16, jnp.float32


def dot_nn(a, b):
    return lax.dot_general(a, b, (((1,), (0,)), ((), ())), preferred_element_type=F32)


def dot_nt(a, b):
    return lax.dot_general(a, b, (((1,), (1,)), ((), ())), preferred_element_type=F32)


def dot_tn(a, b):
    return lax.dot_general(a, b, (((0,), (0,)), ((), ())), preferred_element_type=F32)


class Net:
    def __init__(self, sends, recvs):
        self.sends, self.recvs, self.count, self.open, self.used = sends, recvs, 0, [], 0
        self.s, self.d = lax.axis_index("seq"), lax.axis_index("dp")
        self.z, self.c = lax.div(self.s, 2), lax.rem(self.s, 2)
        y, x = lax.div(self.d, 2), lax.rem(self.d, 2)
        self.plane = (y * 2 + 1 - x, (1 - y) * 2 + x, 3 - self.d)
        self.mate = self.at(self.z, 1 - self.c)

    def room(self, count):
        base = self.used
        self.used += count
        return base

    def at(self, z, core):
        return {"seq": z * 2 + core, "dp": self.d}

    def across(self, kind):
        return {"seq": self.s, "dp": self.plane[kind]}

    def greet(self):
        barrier = pltpu.get_barrier_semaphore()
        peers = [self.mate] + [self.across(k) for k in range(3)]
        peers += [self.at(lax.rem(self.z + k, 4), self.c) for k in (1, 2, 3)]
        for peer in peers:
            pl.semaphore_signal(barrier, inc=1, device_id=peer, device_id_type=MESH)
        pl.semaphore_wait(barrier, len(peers))

    def copy(self, src, dst, send, recv, peer):
        return pltpu.make_async_remote_copy(
            src_ref=src,
            dst_ref=dst,
            send_sem=self.sends.at[send],
            recv_sem=self.recvs.at[recv],
            device_id=peer,
            device_id_type=MESH,
        )

    def push(self, src, dst, recv, peer, when=None):
        copy = self.copy(src, dst, self.count, recv, peer)
        self.count += 1
        if when is None:
            copy.start()
        else:
            pl.when(when)(copy.start)
        self.open.append((copy, when))

    def arrive(self, dst, recv, when=None):
        copy = self.copy(dst, dst, 0, recv, self.mate)
        if when is None:
            copy.wait_recv()
        else:
            pl.when(when)(copy.wait_recv)

    def finish(self, upto=None):
        upto = len(self.open) if upto is None else upto
        for copy, when in self.open[:upto]:
            if when is None:
                copy.wait_send()
            else:
                pl.when(when)(copy.wait_send)
        self.open = self.open[upto:]

    def order(self, step):
        if step == 0:
            return self.z
        table = ((1, 0, 3, 2), (2, 2, 1, 1), (3, 3, 0, 0))[step - 1]
        z = self.z
        return jnp.where(z == 0, table[0], jnp.where(z == 1, table[1], jnp.where(z == 2, table[2], table[3])))


class Chain:
    def __init__(self, net, block, room=4):
        self.net, self.block, self.base = net, block, net.room(room)

    def start(self):
        net = self.net
        own = self.block(net.z, net.c)
        net.push(own, own, self.base + net.z, net.at(net.z + 1, net.c), net.z < 3)
        net.push(own, own, self.base + net.z, net.at(net.z - 1, net.c), net.z > 0)

    def step(self, k):
        net = self.net
        b = net.order(k)
        block = self.block(b, net.c)
        net.arrive(block, self.base + b)
        to = jnp.where(b < net.z, net.z + 1, net.z - 1)
        net.push(block, block, self.base + b, net.at(to, net.c), (to >= 0) & (to <= 3))


class Lines(Chain):
    def __init__(self, net, block):
        super().__init__(net, block, 8)

    def start(self):
        super().start()
        self.give(0)

    def give(self, k):
        net = self.net
        b = net.order(k)
        block = self.block(b, net.c)
        net.push(block, block, self.base + 4 + b, net.mate)

    def take(self):
        net = self.net
        for b in range(4):
            net.arrive(self.block(b, 1 - net.c), self.base + 4 + b)


class Slices(Chain):
    def __init__(self, net, full, rows):
        self.full, self.rows, self.half = full, rows, rows // 32 * 16
        super().__init__(net, lambda z, core: self.part(net.d, z, core), 36)

    def part(self, slot, z, core, half=None):
        first = pl.multiple_of((z * 2 + core) * self.rows, 16)
        if half is None:
            return self.full.at[slot, pl.ds(first, self.rows)]
        if half == 0:
            return self.full.at[slot, pl.ds(first, self.half)]
        return self.full.at[slot, pl.ds(pl.multiple_of(first + self.half, 16), self.rows - self.half)]

    def spread(self, k):
        net = self.net
        b = net.order(k)
        block = self.part(net.d, b, net.c)
        net.push(block, block, self.base + 4 + b, net.across(0))
        net.push(block, block, self.base + 8 + b, net.across(1))
        net.push(block, block, self.base + 20 + b, net.mate)

    def pass_on(self, k):
        net = self.net
        b = net.order(k)
        for kind in (0, 1):
            block = self.part(net.plane[kind], b, net.c)
            net.arrive(block, self.base + 4 + 4 * kind + b)
            half = self.part(net.plane[kind], b, net.c, kind)
            net.push(half, half, self.base + 12 + 4 * kind + b, net.across(1 - kind))
            net.push(block, block, self.base + 24 + 4 * kind + b, net.mate)

    def corner(self, k):
        net = self.net
        b = net.order(k)
        for kind in (0, 1):
            half = self.part(net.plane[2], b, net.c, kind)
            net.arrive(half, self.base + 12 + 4 * kind + b)
        block = self.part(net.plane[2], b, net.c)
        net.push(block, block, self.base + 32 + b, net.mate)

    def take(self):
        net = self.net
        for b in range(4):
            net.arrive(self.part(net.d, b, 1 - net.c), self.base + 20 + b)
            for kind in range(3):
                net.arrive(self.part(net.plane[kind], b, 1 - net.c), self.base + 24 + 4 * kind + b)


class Plane:
    def __init__(self, net, full):
        self.net, self.full, self.base = net, full, net.room(4)
        self.half = full.shape[1] // 2

    def start(self):
        net = self.net
        own = self.full.at[net.d]
        for kind in (0, 1):
            net.push(own, own, self.base + kind, net.across(kind))

    def pass_on(self):
        net = self.net
        for kind in (0, 1):
            net.arrive(self.full.at[net.plane[kind]], self.base + kind)
            half = self.full.at[net.plane[kind], pl.ds(kind * self.half, self.half)]
            net.push(half, half, self.base + 2 + kind, net.across(1 - kind))

    def take(self):
        net = self.net
        for kind in (0, 1):
            net.arrive(self.full.at[net.plane[2], pl.ds(kind * self.half, self.half)], self.base + 2 + kind)


class Spread:
    def __init__(self, net, send, land):
        self.net, self.send, self.land, self.base = net, send, land, net.room(3)

    def start(self):
        net = self.net
        for kind in (2, 0, 1):
            net.push(self.send(net.plane[kind]), self.land(net.d), self.base + kind, net.across(kind))

    def take(self):
        for kind in range(3):
            self.net.arrive(self.land(self.net.plane[kind]), self.base + kind)


class ToMate:
    def __init__(self, net, send, land):
        self.net, self.send, self.land, self.base = net, send, land, net.room(1)

    def start(self):
        self.net.push(self.send, self.land, self.base, self.net.mate)

    def take(self):
        self.net.arrive(self.land, self.base)


class ToOwners:
    def __init__(self, net, part, land, down=False):
        self.net, self.part, self.land, self.down, self.base = net, part, land, down, net.room(3)

    def start(self):
        net = self.net
        for k in (3, 2, 1):
            to = lax.rem(net.z - k + 4, 4)
            net.push(self.part(to), self.land(k - 1), self.base + k - 1, net.at(to, net.c), (net.z >= k) if self.down else None)

    def take(self):
        net = self.net
        for k in (1, 2, 3):
            net.arrive(self.land(k - 1), self.base + k - 1, (net.z + k <= 3) if self.down else None)


class ChainSum:
    def __init__(self, net, part, land, add):
        self.net, self.part, self.land, self.add, self.base = net, part, land, add, net.room(6)

    def stage(self, k):
        net, z = self.net, self.net.z
        i = k - 3 + z
        valid = (i >= 0) & (i < z)
        i = jnp.clip(i, 0, 3)

        @pl.when(valid & (z < 3))
        def _():
            net.arrive(self.land(i), self.base + i)
            self.add(i, i)

        net.push(self.part(i), self.land(i), self.base + i, net.at(z - 1, net.c), valid)
        j = k - z
        valid = (j >= 0) & (3 - j > z)
        j = jnp.clip(j, 0, 3)

        @pl.when(valid & (z > 0))
        def _():
            net.arrive(self.land(4 - j), self.base + 3 + j)
            self.add(3 - j, 4 - j)

        net.push(self.part(3 - j), self.land(4 - j), self.base + 3 + j, net.at(z + 1, net.c), valid)

    def own(self):
        net, z = self.net, self.net.z

        @pl.when(z < 3)
        def _():
            net.arrive(self.land(z), self.base + z)
            self.add(z, z)

        @pl.when(z > 0)
        def _():
            net.arrive(self.land(1 + z), self.base + 6 - z)
            self.add(z, 1 + z)


def settle(land, wide, rows):
    for j in range(4):
        wide[pl.ds(j * rows, rows), : land.shape[2]] = land[j, :rows, :].astype(F32)


def turned(tile, cosine, sine):
    lane = lax.broadcasted_iota(jnp.int32, tile.shape, 1)
    other = jnp.where(lax.rem(lane, HD) < HD // 2, pltpu.roll(tile, 128 - HD // 2, 1), pltpu.roll(tile, HD // 2, 1))
    return tile * cosine + other * sine


def own_rows(index, rows):
    return pl.ds(pl.multiple_of(index * rows, 16), rows)


def norm_scale(v):
    return lax.rsqrt(jnp.mean(v * v, axis=1, keepdims=True) + EPSILON)


def norm_pull(e, v):
    r = norm_scale(v)
    return r * e - v * (r * r * r) * jnp.mean(e * v, axis=1, keepdims=True)


def joined(heads, j, tok):
    groups = H // KV
    pair = [heads[h // groups, tok * (h % groups) : tok * (h % groups) + tok, :] for h in (2 * j, 2 * j + 1)]
    return jnp.concatenate(pair, axis=1)


def plane_sum(net, send, land):
    total = send[net.d].astype(F32)
    for kind in range(3):
        total = total + land[net.plane[kind]].astype(F32)
    return total


def layer_kernel(
    x_in, cot_in, first_in, scale_in, cos_in, sin_in, att_send, gu_send, down,
    block_out, input_grad, back_gu, back_att, back_down,
    att_land, gu_land, wide, qkv_land, kv_all, o_heads, bias, wa, wb, wgu, wd,
    xn_all, gd_all, mn_all, att_all, q_heads, k_heads, v_heads, probs, middle, act, gboth, turn_x, turn_n, turn_a,
    gn_send, gn_land, br_send, br_land, gu_mate, gu_zone, dn_mate, dn_zone, gmid, do_heads, dkv, kv_mate, kv_zone, kv_tot,
    cut_land, ma_mate, ma_zone, gx_land, sends, recvs,
):
    net = Net(sends, recvs)
    tok, dim = x_in.shape[1], x_in.shape[2]
    rows = dim // 32
    blk = 4 * rows
    ffr = down.shape[0]
    hid = 8 * ffr
    d, z, c, s = net.d, net.z, net.c, net.s
    span, length = 4 * tok, 8 * tok
    groups = H // KV
    qkv_send = cut_send = act.reshape(4, tok, hid)
    gx_send, gs_heads = gd_all, gboth
    m_att = wb.reshape(4, 4, 2, blk, 384)

    a2a_att = Spread(net, lambda j: att_send.at[j], lambda j: att_land.at[j])
    a2a_gu = Spread(net, lambda j: gu_send.at[j], lambda j: gu_land.at[j])
    a2a_qkv = Spread(net, lambda j: qkv_send.at[j, :, pl.ds(0, 512)], lambda j: qkv_land.at[j])
    a = Lines(net, lambda zz, core: wa.at[own_rows(zz * 2 + core, blk)])
    b = Slices(net, wb, blk)
    gu = Lines(net, lambda zz, core: wgu.at[zz, core])
    dn = Lines(net, lambda zz, core: wd.at[zz, core])
    kv = Lines(net, lambda zz, core: kv_all.at[zz, core])
    xs = Plane(net, xn_all)
    gs = Plane(net, gd_all)
    ms = Plane(net, mn_all)
    ats = Plane(net, att_all)

    net.greet()
    a2a_att.start()
    att_land[d] = att_send[d]
    x = x_in[0].astype(F32)
    xn_all[d] = (x * norm_scale(x)).astype(BF)
    xs.start()
    a2a_gu.start()
    gu_land[d] = gu_send[d]
    gd_all[d] = (cot_in[0].astype(F32) * scale_in[1:2, 0:1]).astype(BF)
    wd[z, c] = down[...]
    a2a_att.take()
    settle(att_land, wide, rows)
    own = own_rows(s, blk)
    wa[own, :] = wide[:, :512].astype(BF)
    wb[d, own, :] = wide[:, 384:768].astype(BF)
    a.start()
    a.step(1)
    a.give(1)
    dn.start()
    xs.pass_on()
    a.step(2)
    a.give(2)
    b.start()
    a.step(3)
    a.give(3)
    a2a_gu.take()
    settle(gu_land, wide, rows)
    wgu[z, c] = wide[...].astype(BF)
    gu.start()
    xs.take()
    a.take()

    cosine, sine = cos_in[...], sin_in[...]
    eighth = 1.0 / math.sqrt(HD)
    for j in range(4):
        part = dot_nn(xn_all[j], wa[...])
        for i in range(4):
            tile = part[:, 128 * i : 128 * i + 128]
            spun = turned(tile, cosine, sine)
            if i < 2:
                tile = spun * eighth
            elif i == 2:
                tile = jnp.where(d < 2, spun, tile)
            else:
                tile = jnp.where(d == 0, spun, jnp.where(d == 2, spun * eighth, tile))
            qkv_send[j, :, 128 * i : 128 * i + 128] = tile.astype(BF)
    a2a_qkv.start()
    early = len(net.open)
    qkv_land[d] = qkv_send[d, :, :512]
    b.spread(0)
    b.step(1)
    b.spread(1)
    a2a_qkv.take()
    places = [(0, 256), (0, 384), (1, 256), (1, 384), (2, 256), (3, 256)]
    for i, (j, col) in enumerate(places):
        kv_all[z, c, :, 128 * i : 128 * i + 128] = qkv_land[j, :, col : col + 128]
    kv.start()
    gs.start()
    for t in range(9):
        j, col = (t // 2, (t % 2) * 128) if t < 8 else (2, 384)
        for h in (2 * t, 2 * t + 1):
            at = col + HD * (h % 2)
            q_heads[h // groups, tok * (h % groups) : tok * (h % groups) + tok, :] = qkv_land[j, :, at : at + HD]
    position = s * tok + lax.broadcasted_iota(jnp.int32, (tok, 1), 0)
    key = lax.broadcasted_iota(jnp.int32, bias.shape, 1)
    bias[...] = jnp.where((key <= position) & (key >= first_in[:, 0:1]), 0.0, MASKED)

    kv.step(1)
    kv.give(1)
    b.step(2)
    b.spread(2)
    kv.step(2)
    kv.give(2)
    b.step(3)
    b.spread(3)
    b.pass_on(0)
    b.pass_on(1)
    kv.step(3)
    kv.give(3)
    dn.step(1)
    gu.step(1)
    gs.pass_on()
    b.pass_on(2)
    b.corner(0)
    b.corner(1)
    kv.take()
    for j in range(8):
        for k in range(KV):
            k_heads[k, pl.ds(tok * j, tok), :] = kv_all[j // 2, j % 2, :, HD * k : HD * k + HD]
            v_heads[k, pl.ds(tok * j, tok), :] = kv_all[j // 2, j % 2, :, HD * (KV + k) : HD * (KV + k) + HD]

    def head(h, carry):
        k = lax.div(h, groups)
        mine = pl.ds(pl.multiple_of(lax.rem(h, groups) * tok, tok), tok)
        score = dot_nt(q_heads[k, mine, :], k_heads[k]) + bias[...]
        expo = jnp.exp(score - jnp.max(score, axis=1, keepdims=True))
        p = (expo / jnp.sum(expo, axis=1, keepdims=True)).astype(BF)
        probs[k, mine, :] = p
        o_heads[k, mine, :] = dot_nn(p, v_heads[k])
        return carry

    lax.fori_loop(0, 6, head, 0)
    b.pass_on(3)
    b.corner(2)
    lax.fori_loop(6, 12, head, 0)
    b.corner(3)
    dn.step(2)
    gu.step(2)
    lax.fori_loop(12, 18, head, 0)
    b.take()
    for j in range(H // 2):
        att_all[d, :, 128 * j : 128 * j + 128] = joined(o_heads, j, tok).astype(BF)
    full = att_all[d]
    branch = [dot_nn(full, wb[j, :, 128:]) for j in range(4)] + [dot_nn(full, wb[3, :, :128])]
    mid = x_in[0].astype(F32) + scale_in[0:1, 0:1] * jnp.concatenate(branch, axis=1)
    middle[...] = mid
    mn_all[d] = (mid * norm_scale(mid)).astype(BF)
    gs.take()
    ms.start()
    for k in (1, 2):
        dn.give(k)
        gu.give(k)
    dn.step(3)
    dn.give(3)
    ms.pass_on()
    gu.step(3)
    gu.give(3)
    ms.take()
    dn.take()
    gu.take()
    net.finish(early)
    sent = len(net.open)
    ats.start()

    def by_cols(send, land, width):
        return [
            Spread(
                net,
                lambda j, n=n: send.at[j, :, pl.ds(width * n, width)],
                lambda j, n=n: land.at[j, :, pl.ds(width * n, width)],
            )
            for n in range(dim // width)
        ]

    gn, br, gx = by_cols(gn_send, gn_land, 384), by_cols(br_send, br_land, dim), by_cols(gx_send, gx_land, 384)
    wgu_flat, wd_flat = wgu.reshape(dim, 2 * hid), wd.reshape(hid, dim)
    other = 1 - c
    gu_pair = [
        ToMate(net, wgu.at[:, other, :, pl.ds(256 * n, 256)], gu_mate.at[:, :, pl.ds(256 * n, 256)]) for n in range(2 * hid // 256)
    ]
    dn_pair = [ToMate(net, wd.at[:, other, :, pl.ds(384 * n, 384)], dn_mate.at[:, :, pl.ds(384 * n, 384)]) for n in range(3)]

    for n in range(hid // 256):
        cols, ups = pl.ds(256 * n, 256), pl.ds(hid + 256 * n, 256)
        normed = mn_all[...].reshape(span, dim)
        gate = dot_nn(normed, wgu_flat[:, cols])
        up = dot_nn(normed, wgu_flat[:, ups])
        g_act = dot_nt(gd_all[...].reshape(span, dim), wd_flat[cols, :])
        sig = jax.nn.sigmoid(gate)
        swish = gate * sig
        act[:, cols] = (swish * up).astype(BF)
        gboth[:, cols] = (g_act * up * (sig * (1.0 + gate * (1.0 - sig)))).astype(BF)
        gboth[:, ups] = (g_act * swish).astype(BF)
    for n in range(3):
        part = dot_nt(gboth[...], wgu_flat[384 * n : 384 * n + 384, :]).astype(BF)
        gn_send[:, :, 384 * n : 384 * n + 384] = part.reshape(4, tok, 384)
        gn[n].start()
    for n in range(3):
        part = dot_nn(act[...], wd_flat[:, 384 * n : 384 * n + 384]).astype(BF)
        br_send[:, :, 384 * n : 384 * n + 384] = part.reshape(4, tok, 384)
    turn_x[...] = mn_all[...].reshape(span, dim).T
    turn_a[...] = act[...].T
    net.finish(sent)
    for n in range(2 * hid // 256):
        wgu_flat[:, 256 * n : 256 * n + 256] = dot_nn(turn_x[...], gboth[:, 256 * n : 256 * n + 256]).astype(BF)
        gu_pair[n].start()
    for n in range(3):
        cols = pl.ds(384 * n, 384)
        wd_flat[:, cols] = dot_nn(turn_a[...], gd_all[:, :, cols].reshape(span, 384)).astype(BF)
        dn_pair[n].start()
    br[0].start()

    def add_gu(block, slot):
        wgu[block, c] = (wgu[block, c].astype(F32) + gu_zone[slot].astype(F32)).astype(BF)

    def add_dn(block, slot):
        wd[block, c] = (wd[block, c].astype(F32) + dn_zone[slot].astype(F32)).astype(BF)

    gu_sum = ChainSum(net, lambda zz: wgu.at[zz, c], lambda k: gu_zone.at[k], add_gu)
    dn_sum = ChainSum(net, lambda zz: wd.at[zz, c], lambda k: dn_zone.at[k], add_dn)
    ats.pass_on()
    for pair in gu_pair:
        pair.take()
    for k in range(4):
        wgu[k, c] = (wgu[k, c].astype(F32) + gu_mate[k].astype(F32)).astype(BF)
    gu_sum.stage(0)
    for pair in dn_pair:
        pair.take()
    for k in range(4):
        wd[k, c] = (wd[k, c].astype(F32) + dn_mate[k].astype(F32)).astype(BF)
    dn_sum.stage(0)

    for n in range(3):
        gn[n].take()
    mid = middle[...]
    g_mid = cot_in[0].astype(F32) + norm_pull(plane_sum(net, gn_send, gn_land), mid)
    gmid[...] = g_mid
    gba = (scale_in[0:1, 0:1] * g_mid).astype(BF)
    for j in range(4):
        cut_send[j, :, 512:768] = gba[:, 256 * j : 256 * j + 256]
    cut_send[3, :, 384:512] = gba[:, 1024:1152]
    cut = lambda cols: Spread(net, lambda j: cut_send.at[j, :, cols], lambda j: cut_land.at[j, :, cols])
    cut_o, cut_q, cut_l = cut(pl.ds(512, 256)), cut(pl.ds(0, 256)), cut(pl.ds(256, 256))
    cut_o.start()
    cut_land[d, :, 512:768] = cut_send[d, :, 512:768]
    g_att = dot_nt(gba[:, 1024:1152], wb[3, :, :128])
    for j in range(4):
        g_att = g_att + dot_nt(gba[:, 256 * j : 256 * j + 256], wb[j, :, 128:])
    for h in range(H):
        do_heads[h // groups, tok * (h % groups) : tok * (h % groups) + tok, :] = g_att[:, HD * h : HD * h + HD].astype(BF)
    gu_sum.stage(1)

    kv_pair = [ToMate(net, dkv.at[n, :, other], kv_mate.at[n]) for n in range(2)]
    kv_sum = [ToOwners(net, lambda zz, n=n: dkv.at[n, zz, c], lambda k, n=n: kv_zone.at[n, k], True) for n in range(2)]

    def pull(k, carry):
        for g in range(groups):
            mine = pl.ds(tok * g, tok)
            p = probs[k, mine, :].astype(F32)
            t = p * dot_nt(do_heads[k, mine, :], v_heads[k])
            ds = (t - p * jnp.sum(t, axis=1, keepdims=True)).astype(BF)
            gs_heads[mine, :length] = ds
            o_heads[k, mine, :] = dot_nn(ds, k_heads[k]) * eighth
        half, kk = lax.div(k, 3), lax.rem(k, 3)
        for i, (left, right) in enumerate(((q_heads[k], gs_heads[: groups * tok, :length]), (do_heads[k], probs[k]))):
            turned_grad = dot_tn(left, right).astype(BF)
            at = pl.ds(pl.multiple_of(192 * i + HD * kk, HD), HD)
            for j in range(8):
                dkv[half, j // 2, j % 2, at, :] = turned_grad[:, tok * j : tok * j + tok]
        return carry

    def pair_sum(n):
        kv_pair[n].take()
        for k in range(4):
            dkv[n, k, c] = (dkv[n, k, c].astype(F32) + kv_mate[n, k].astype(F32)).astype(BF)
        kv_sum[n].start()

    def grads(p, parts):
        at = 0
        for part in parts:
            wb[p, :, at : at + part.shape[1]] = part.astype(BF)
            at += part.shape[1]
        pair = ToMate(net, m_att.at[p, :, other, :, quarter], ma_mate.at[p])
        pair.start()
        return pair

    def grads_sum(p, pair):
        pair.take()
        for k in range(4):
            m_att[p, k, c, :, quarter] = (m_att[p, k, c, :, quarter].astype(F32) + ma_mate[p, k].astype(F32)).astype(BF)
        out = ToOwners(net, lambda zz: m_att.at[p, zz, c, :, quarter], lambda k: ma_zone.at[p, k])
        out.start()
        return out

    def grads_back(p, out):
        cols = pl.ds(256 * p, 256)
        out.take()
        total = m_att[p, z, c, :, quarter].astype(F32)
        for k in range(3):
            total = total + ma_zone[p, k].astype(F32)
        wide[:, : total.shape[1]] = total
        for j in range(4):
            att_land[j, :rows, cols] = wide[pl.ds(j * rows, rows), : total.shape[1]].astype(BF)
        spread = Spread(net, lambda j: att_land.at[j, :, cols], lambda j: back_att.at[j, :, cols])
        spread.start()
        back_att[d, :, cols] = att_land[d, :, cols]
        return spread

    q_cols, l_cols, o_cols = pl.ds(0, 256), pl.ds(256, 256), pl.ds(512, 256)
    quarter = pl.ds(0, 256)
    lax.fori_loop(0, 3, pull, 0)
    kv_pair[0].start()
    ats.take()
    cut_o.take()
    turn_x[...] = att_all[...].reshape(span, dim).T
    pair_sum(0)
    lax.fori_loop(3, 6, pull, 0)
    kv_pair[1].start()
    for t in range(9):
        j, col = (t // 2, (t % 2) * 128) if t < 8 else (2, 384)
        cut_send[j, :, col : col + 128] = turned(joined(o_heads, t, tok), cosine, -sine).astype(BF)
    cut_q.start()
    cut_land[d, :, q_cols] = cut_send[d, :, q_cols]
    pair_sum(1)
    pair_o = grads(2, [dot_nn(turn_x[...], cut_land[:, :, o_cols].reshape(span, 256))])
    turn_n[...] = xn_all[...].reshape(span, dim).T
    br[0].take()
    block_out[0] = (middle[...] + scale_in[1:2, 0:1] * plane_sum(net, br_send, br_land)).astype(BF)
    cut_q.take()
    pair_q = grads(0, [dot_nn(turn_n[...], cut_land[:, :, q_cols].reshape(span, 256))])
    dn_sum.stage(1)

    for n in range(2):
        kv_sum[n].take()
        kv_tot[n] = dkv[n, z, c].astype(F32)
        for k in (1, 2, 3):

            @pl.when(z + k <= 3)
            def _(n=n, k=k):
                kv_tot[n] += kv_zone[n, k - 1].astype(F32)

    keys = jnp.concatenate([kv_tot[0, :192, :], kv_tot[1, :192, :]], axis=0).T
    vals = jnp.concatenate([kv_tot[0, 192:, :], kv_tot[1, 192:, :]], axis=0).T
    late = [turned(keys[:, 128 * i : 128 * i + 128], cosine, -sine) for i in range(3)] + [vals[:, 128 * i : 128 * i + 128] for i in range(3)]
    for tile, (j, col) in zip(late, places):
        cut_send[j, :, col : col + 128] = tile.astype(BF)
    cut_l.start()
    cut_land[d, :, l_cols] = cut_send[d, :, l_cols]
    gu_sum.stage(2)
    sum_o = grads_sum(2, pair_o)
    cut_l.take()
    last = cut_land[:, :, 384:512].reshape(span, 128)
    cuts = cut_land[:, :, :512].reshape(span, 512)
    lane = lax.broadcasted_iota(jnp.int32, cuts.shape, 1)
    cuts = jnp.where((d == 3) & (lane >= 384), jnp.zeros_like(cuts), cuts)
    for n in range(3):
        part = dot_nt(cuts, wa[384 * n : 384 * n + 384, :]).astype(BF)
        gx_send[:, :, 384 * n : 384 * n + 384] = part.reshape(4, tok, 384)
        gx[n].start()
    second = jnp.where(d == 3, dot_nn(turn_x[...], last), dot_nn(turn_n[...], last))
    pair_l = grads(1, [dot_nn(turn_n[...], cut_land[:, :, 256:384].reshape(span, 128)), second])
    sum_l = grads_sum(1, pair_l)
    sum_q = grads_sum(0, pair_q)
    dn_sum.stage(2)
    back_o = grads_back(2, sum_o)
    gu_sum.own()
    wide[...] = wgu[z, c].astype(F32)
    for j in range(4):
        gu_land[j, :rows, :] = wide[pl.ds(j * rows, rows), :].astype(BF)
    back_g = Spread(net, lambda j: gu_land.at[j], lambda j: back_gu.at[j])
    back_g.start()
    back_gu[d] = gu_land[d]
    back_l = grads_back(1, sum_l)
    back_q = grads_back(0, sum_q)
    for n in range(3):
        gx[n].take()
    input_grad[0] = gmid[...] + norm_pull(plane_sum(net, gx_send, gx_land), x_in[0].astype(F32))
    dn_sum.own()
    back_down[...] = wd[z, c]
    for spread in (back_o, back_q, back_g, back_l):
        spread.take()
    net.finish()


def layer(x, cot, first, scale, cosine, sine, att_send, gu_send, down):
    tok, dim = x.shape[1:]
    ns = 8
    length = tok * ns
    ffr = down.shape[0]
    hid = ffr * ns
    blk = dim // ns
    span = 4 * tok
    vm = pl.BlockSpec(memory_space=pltpu.VMEM)
    outs = [
        ((1, tok, dim), BF),
        ((1, tok, dim), F32),
        (gu_send.shape, BF),
        (att_send.shape, BF),
        (down.shape, BF),
    ]
    plane = ((4, tok, dim), BF)
    wide_cut = ((4, tok, 512), BF)
    three = ((KV, 3 * tok, HD), BF)
    scratch = [
        (att_send.shape, BF),
        (gu_send.shape, BF),
        ((blk, 2 * hid), F32),
        wide_cut,
        ((4, 2, tok, 2 * KV * HD), BF),
        ((KV, 3 * tok, HD), F32),
        ((tok, length), F32),
        ((dim, 512), BF),
        ((4, dim, 384), BF),
        ((4, 2, blk, 2 * hid), BF),
        ((4, 2, ffr, dim), BF),
        plane,
        plane,
        plane,
        plane,
        three,
        ((KV, length, HD), BF),
        ((KV, length, HD), BF),
        ((KV, 3 * tok, length), BF),
        ((tok, dim), F32),
        ((span, hid), BF),
        ((span, 2 * hid), BF),
        ((dim, span), BF),
        ((dim, span), BF),
        ((hid, span), BF),
        plane,
        plane,
        plane,
        plane,
        ((4, blk, 2 * hid), BF),
        ((5, blk, 2 * hid), BF),
        ((4, ffr, dim), BF),
        ((5, ffr, dim), BF),
        ((tok, dim), F32),
        three,
        ((2, 4, 2, 384, tok), BF),
        ((2, 4, 384, tok), BF),
        ((2, 3, 384, tok), BF),
        ((2, 384, tok), F32),
        ((4, tok, 768), BF),
        ((3, 4, blk, 256), BF),
        ((3, 3, blk, 256), BF),
        plane,
    ]
    return pl.pallas_call(
        layer_kernel,
        out_shape=[jax.ShapeDtypeStruct(*o) for o in outs],
        in_specs=[vm] * 9,
        out_specs=[vm] * len(outs),
        scratch_shapes=[pltpu.VMEM(*t) for t in scratch] + [pltpu.SemaphoreType.DMA((320,)), pltpu.SemaphoreType.DMA((256,))],
        compiler_params=pltpu.CompilerParams(collective_id=0, has_side_effects=True, vmem_limit_bytes=LIMIT),
        name="k_layer",
    )(x, cot, first, scale, cosine, sine, att_send, gu_send, down)


def shards_by_kernel(
    hidden_in,
    attn_norm,
    query_weight,
    key_weight,
    value_weight,
    output_weight,
    mlp_norm,
    gate_weight,
    up_weight,
    down_weight,
    cotangent,
    doc_starts,
    keep_mask,
    keep_rate,
    seq_order,
):
    tok = hidden_in.shape[1]
    ns, nd = lax.axis_size("seq"), lax.axis_size("dp")
    length = tok * ns
    rows = query_weight.shape[0]
    ffr = down_weight.shape[0]
    dim = hidden_in.shape[2]
    groups = H // KV
    nq, nk = H * HD, KV * HD
    score_scale = 1.0 / math.sqrt(HD)
    me_s, me_d = lax.axis_index("seq"), lax.axis_index("dp")
    sample = jnp.sum(jnp.where(jnp.arange(nd) == me_d, seq_order, 0))
    pick = jnp.arange(nd) == sample
    doc_begin = jnp.sum(jnp.where(pick[:, None], doc_starts, 0), axis=0)
    keep_flags = jnp.sum(jnp.where(pick[:, None], keep_mask, 0), axis=0).astype(jnp.float32)
    attn_scale = keep_flags[0] / keep_rate[0]
    mlp_scale = keep_flags[1] / keep_rate[1]
    positions = me_s * tok + jnp.arange(tok)
    first = jnp.max(jnp.where(doc_begin[None, :] <= positions[:, None], doc_begin[None, :], 0), axis=1)
    gain_one, gain_two = attn_norm[:, None], mlp_norm[:, None]

    qkv_rows = low(jnp.concatenate([query_weight, key_weight, value_weight], axis=1).astype(jnp.float32) * gain_one)
    def split_hidden(w):
        w = low(w.astype(jnp.float32) * gain_two).reshape(rows, ns, nd, ffr)
        w = jnp.transpose(w, (0, 2, 1, 3)).reshape(rows, nd * ns * ffr)
        return w

    gu = jnp.concatenate(
        [split_hidden(gate_weight).reshape(rows, nd, -1), split_hidden(up_weight).reshape(rows, nd, -1)], axis=2
    )
    late = [(9, 10), (11, 12), (13, 8), (14, None)]
    tiles = []
    for j in range(4):
        first_late, second_late = late[j]
        qkv_tile = lambda t: qkv_rows[:, 128 * t : 128 * t + 128]
        second = output_weight[:, 1024:] if second_late is None else qkv_tile(second_late)
        tiles.append(
            jnp.concatenate(
                [qkv_rows[:, 256 * j : 256 * j + 256], qkv_tile(first_late), second, output_weight[:, 256 * j : 256 * j + 256]], axis=1
            )
        )
    att_send = jnp.stack(tiles)
    pad = ((0, 0), (0, -rows % 16), (0, 0))
    inverse_freq = ROPE_BASE ** (-2.0 * jnp.arange(HD // 2, dtype=jnp.float32) / HD)
    angles = positions.astype(jnp.float32)[:, None] * inverse_freq[None, :]
    cosine = jnp.tile(jnp.cos(angles), (1, 4))
    sine = jnp.tile(jnp.concatenate([-jnp.sin(angles), jnp.sin(angles)], axis=1), (1, 2))
    scale = jnp.broadcast_to(jnp.stack([attn_scale, mlp_scale])[:, None], (2, 128))
    firsts = jnp.broadcast_to(first[:, None], (tok, 128))
    block_output, input_grad, back_gu, back_att, m_down = layer(
        hidden_in, cotangent, firsts, scale, cosine, sine, jnp.pad(att_send, pad), jnp.pad(jnp.transpose(gu, (1, 0, 2)), pad), down_weight
    )
    hid = ns * ffr
    back_gu = jnp.transpose(back_gu[:, :rows].astype(jnp.float32), (1, 0, 2))
    m_att = jnp.transpose(back_att[:, :rows].astype(jnp.float32), (1, 0, 2))

    def whole_hidden(m):
        return jnp.transpose(m.reshape(rows, nd, ns, ffr), (0, 2, 1, 3)).reshape(rows, -1)

    m_gate, m_up = whole_hidden(back_gu[:, :, :hid]), whole_hidden(back_gu[:, :, hid:])
    tiles = [None] * 15
    for j in range(4):
        tiles[2 * j], tiles[2 * j + 1] = m_att[:, j, :128], m_att[:, j, 128:256]
        tiles[late[j][0]] = m_att[:, j, 256:384]
        if late[j][1] is not None:
            tiles[late[j][1]] = m_att[:, j, 384:512]
    m_qkv = jnp.concatenate(tiles, axis=1)
    g_out = jnp.concatenate([m_att[:, j, 512:] for j in range(4)] + [m_att[:, 3, 384:512]], axis=1)

    def weigh(w, m):
        return jnp.sum(w.astype(jnp.float32) * m, axis=1)

    m_q, m_k, m_v = m_qkv[:, :nq], m_qkv[:, nq : nq + nk], m_qkv[:, nq + nk :]
    g_norm_one = weigh(query_weight, m_q) + weigh(key_weight, m_k) + weigh(value_weight, m_v)
    g_norm_two = weigh(gate_weight, m_gate) + weigh(up_weight, m_up)
    return (
        block_output,
        input_grad,
        g_norm_one,
        m_q * gain_one,
        m_k * gain_one,
        m_v * gain_one,
        g_out,
        g_norm_two,
        m_gate * gain_two,
        m_up * gain_two,
        m_down.astype(jnp.float32),
    )


def solution(mesh):
    placed = (
        P("dp", "seq", None),
        P(("seq", "dp")),
        P(("seq", "dp"), None),
        P(("seq", "dp"), None),
        P(("seq", "dp"), None),
        P(("seq", "dp"), None),
        P(("seq", "dp")),
        P(("seq", "dp"), None),
        P(("seq", "dp"), None),
        P(("seq", "dp"), None),
        P("dp", "seq", None),
        P(),
        P(),
        P(),
        P(),
    )
    fits = mesh.shape["seq"] == 8 and mesh.shape["dp"] == 4
    return jax.shard_map(
        shards_by_kernel if fits else shards,
        mesh=mesh,
        in_specs=placed,
        out_specs=(
            P("dp", "seq", None),
            P("dp", "seq", None),
            P(("seq", "dp")),
            P(("seq", "dp"), None),
            P(("seq", "dp"), None),
            P(("seq", "dp"), None),
            P(("seq", "dp"), None),
            P(("seq", "dp")),
            P(("seq", "dp"), None),
            P(("seq", "dp"), None),
            P(("seq", "dp"), None),
        ),
        check_vma=False,
    )
```

```python
import math

import jax
import jax.numpy as jnp
from jax import lax
from jax.experimental import pallas as pl
from jax.experimental.pallas import tpu as pltpu
from jax.sharding import PartitionSpec as P

H = 18
KV = 6
HD = 64


EPSILON = 1e-05
ROPE_BASE = 10000.0
MASKED = -1e30


def contract_rows(left_rows, right_rows):
    return lax.dot_general(
        left_rows, right_rows, (((0,), (0,)), ((), ())), preferred_element_type=jnp.float32
    )


def contract_cols(left_mat, right_mat):
    return lax.dot_general(
        left_mat, right_mat, (((1,), (1,)), ((), ())), preferred_element_type=jnp.float32
    )


def low(v):
    return v.astype(jnp.bfloat16)


def dot(a, b):
    return jnp.dot(a, b, preferred_element_type=jnp.float32)


def swap_halves(vectors):
    half = HD // 2
    return jnp.concatenate([vectors[..., half:], vectors[..., :half]], axis=-1)


def shards(
    hidden_in,
    attn_norm,
    query_weight,
    key_weight,
    value_weight,
    output_weight,
    mlp_norm,
    gate_weight,
    up_weight,
    down_weight,
    cotangent,
    doc_starts,
    keep_mask,
    keep_rate,
    seq_order,
):
    tok = hidden_in.shape[1]
    ns, nd = lax.axis_size("seq"), lax.axis_size("dp")
    length = tok * ns
    rows = query_weight.shape[0]
    ffr = down_weight.shape[0]
    dim = hidden_in.shape[2]
    groups = H // KV
    nq, nk = H * HD, KV * HD
    score_scale = 1.0 / math.sqrt(HD)
    me_s, me_d = lax.axis_index("seq"), lax.axis_index("dp")
    sample = jnp.sum(jnp.where(jnp.arange(nd) == me_d, seq_order, 0))
    pick = jnp.arange(nd) == sample
    doc_begin = jnp.sum(jnp.where(pick[:, None], doc_starts, 0), axis=0)
    keep_flags = jnp.sum(jnp.where(pick[:, None], keep_mask, 0), axis=0).astype(jnp.float32)
    attn_scale = keep_flags[0] / keep_rate[0]
    mlp_scale = keep_flags[1] / keep_rate[1]
    positions = me_s * tok + jnp.arange(tok)
    first = jnp.max(jnp.where(doc_begin[None, :] <= positions[:, None], doc_begin[None, :], 0), axis=1)
    gain_one, gain_two = attn_norm[:, None], mlp_norm[:, None]

    qkv_rows = low(jnp.concatenate([query_weight, key_weight, value_weight], axis=1).astype(jnp.float32) * gain_one)
    w_qkv = lax.all_gather(qkv_rows, ("seq", "dp"), axis=0, tiled=True)
    w_out = lax.all_gather(output_weight, ("seq", "dp"), axis=0, tiled=True)

    def split_hidden(w):
        w = low(w.astype(jnp.float32) * gain_two).reshape(rows, ns, nd, ffr)
        w = jnp.transpose(w, (0, 2, 1, 3)).reshape(rows, nd * ns * ffr)
        return w

    gu = jnp.concatenate(
        [split_hidden(gate_weight).reshape(rows, nd, -1), split_hidden(up_weight).reshape(rows, nd, -1)], axis=2
    )
    gu = lax.all_to_all(gu, "dp", split_axis=1, concat_axis=0, tiled=True).reshape(nd * rows, -1)
    w_gu = lax.all_gather(gu, "seq", axis=0, tiled=True)
    w_down = lax.all_gather(down_weight, "seq", axis=0, tiled=True)
    hid = w_down.shape[0]

    x = hidden_in[0].astype(jnp.float32)
    r_one = lax.rsqrt(jnp.mean(x * x, axis=-1, keepdims=True) + EPSILON)
    xn = low(x * r_one)
    qkv = dot(xn, w_qkv)
    inverse_freq = ROPE_BASE ** (-2.0 * jnp.arange(HD // 2, dtype=jnp.float32) / HD)
    angles = positions.astype(jnp.float32)[:, None] * inverse_freq[None, :]
    cosine = jnp.tile(jnp.cos(angles), (1, 2))[:, None, :]
    sine = jnp.concatenate([-jnp.sin(angles), jnp.sin(angles)], axis=1)[:, None, :]

    def turn(v):
        return v * cosine + swap_halves(v) * sine

    def turn_back(v):
        return v * cosine - swap_halves(v) * sine

    queries = low(turn(qkv[:, :nq].reshape(tok, H, HD))).reshape(tok, KV, groups, HD)
    keys = low(turn(qkv[:, nq : nq + nk].reshape(tok, KV, HD)))
    kv = jnp.concatenate([keys.reshape(tok, nk), low(qkv[:, nq + nk :])], axis=1)
    kv_all = lax.all_gather(kv, "seq", axis=0, tiled=True)
    k_all, v_all = kv_all[:, :nk].reshape(length, KV, HD), kv_all[:, nk:].reshape(length, KV, HD)
    key_pos = jnp.arange(length)
    allowed = (key_pos[None, :] <= positions[:, None]) & (key_pos[None, :] >= first[:, None])
    scores = jnp.einsum("tkgd,skd->kgts", queries, k_all, preferred_element_type=jnp.float32) * score_scale
    scores = jnp.where(allowed, scores, MASKED)
    expo = jnp.exp(scores - jnp.max(scores, axis=-1, keepdims=True))
    probs = low(expo / jnp.sum(expo, axis=-1, keepdims=True))
    attended = jnp.einsum("kgts,skd->tkgd", probs, v_all, preferred_element_type=jnp.float32)
    att = low(attended.reshape(tok, nq))
    middle = x + attn_scale * dot(att, w_out)
    r_two = lax.rsqrt(jnp.mean(middle * middle, axis=-1, keepdims=True) + EPSILON)
    mn = low(middle * r_two)

    cot = cotangent[0].astype(jnp.float32)
    side = lax.all_gather(jnp.concatenate([xn, low(mlp_scale * cot), att], axis=1), "dp", axis=0, tiled=True)
    xn_all, gd_all, att_all = side[:, :dim], side[:, dim : 2 * dim], side[:, 2 * dim :]
    mn_all = lax.all_gather(mn, "dp", axis=0, tiled=True)
    gate, up = dot(mn_all, w_gu[:, :hid]), dot(mn_all, w_gu[:, hid:])
    sig = jax.nn.sigmoid(gate)
    act_gate = gate * sig
    act = low(act_gate * up)
    g_act = contract_cols(gd_all, w_down)
    gg = low(g_act * up * (sig * (1.0 + gate * (1.0 - sig))))
    gu_in = low(g_act * act_gate)
    gboth = jnp.concatenate([gg, gu_in], axis=1)
    g_mn = lax.psum_scatter(low(contract_cols(gboth, w_gu)), "dp", scatter_dimension=0, tiled=True).astype(jnp.float32)
    branch = lax.psum_scatter(low(dot(act, w_down)), "dp", scatter_dimension=0, tiled=True).astype(jnp.float32)
    block_output = low(middle + mlp_scale * branch)[None]
    m_gu = lax.psum_scatter(low(contract_rows(mn_all, gboth)), "seq", scatter_dimension=0, tiled=True)
    m_down = lax.psum_scatter(low(contract_rows(act, gd_all)), "seq", scatter_dimension=0, tiled=True)

    def norm_back(e, v, r):
        return r * e - v * (r * r * r) * jnp.mean(e * v, axis=-1, keepdims=True)

    g_mid = cot + norm_back(g_mn, middle, r_two)
    gba = low(attn_scale * g_mid)
    g_att = low(contract_cols(gba, w_out)).reshape(tok, KV, groups, HD)
    g_probs = jnp.einsum("tkgd,skd->kgts", g_att, v_all, preferred_element_type=jnp.float32)
    delta = jnp.einsum("tkgd,tkgd->kgt", g_att.astype(jnp.float32), attended)
    g_scores = low(probs.astype(jnp.float32) * (g_probs - delta[..., None]))
    g_q = jnp.einsum("kgts,skd->tkgd", g_scores, k_all, preferred_element_type=jnp.float32) * score_scale
    g_k = jnp.einsum("kgts,tkgd->skd", g_scores, queries, preferred_element_type=jnp.float32) * score_scale
    g_v = jnp.einsum("kgts,tkgd->skd", probs, g_att, preferred_element_type=jnp.float32)
    g_kv = low(jnp.concatenate([g_k.reshape(length, nk), g_v.reshape(length, nk)], axis=1))
    g_kv = lax.psum_scatter(g_kv, "seq", scatter_dimension=0, tiled=True).astype(jnp.float32)
    g_q_in = low(turn_back(g_q.reshape(tok, H, HD))).reshape(tok, nq)
    g_k_in = low(turn_back(g_kv[:, :nk].reshape(tok, KV, HD))).reshape(tok, nk)
    g_qkv = jnp.concatenate([g_q_in, g_k_in, low(g_kv[:, nk:])], axis=1)
    g_xn = contract_cols(g_qkv, w_qkv)
    input_grad = (g_mid + norm_back(g_xn, x, r_one))[None]

    cut = jnp.concatenate([g_qkv.reshape(tok, nd, -1), gba.reshape(tok, nd, -1)], axis=2)
    wq = g_qkv.shape[1] // nd
    cut = lax.all_to_all(cut, "dp", split_axis=1, concat_axis=0, tiled=True).reshape(nd * tok, -1)
    m_att = jnp.concatenate([contract_rows(xn_all, cut[:, :wq]), contract_rows(att_all, cut[:, wq:])], axis=1)
    m_att = lax.psum_scatter(low(m_att), "seq", scatter_dimension=0, tiled=True)

    back = jnp.concatenate([m_gu, m_att], axis=1)
    back = lax.all_to_all(back.reshape(nd, rows, 1, -1), "dp", split_axis=0, concat_axis=2, tiled=True)
    back = back.reshape(rows, nd, -1).astype(jnp.float32)

    def whole_hidden(m):
        return jnp.transpose(m.reshape(rows, nd, ns, ffr), (0, 2, 1, 3)).reshape(rows, -1)

    m_gate, m_up = whole_hidden(back[:, :, :hid]), whole_hidden(back[:, :, hid : 2 * hid])
    m_qkv = back[:, :, 2 * hid : 2 * hid + wq].reshape(rows, -1)
    g_out = back[:, :, 2 * hid + wq :].reshape(rows, -1)

    def weigh(w, m):
        return jnp.sum(w.astype(jnp.float32) * m, axis=1)

    m_q, m_k, m_v = m_qkv[:, :nq], m_qkv[:, nq : nq + nk], m_qkv[:, nq + nk :]
    g_norm_one = weigh(query_weight, m_q) + weigh(key_weight, m_k) + weigh(value_weight, m_v)
    g_norm_two = weigh(gate_weight, m_gate) + weigh(up_weight, m_up)
    return (
        block_output,
        input_grad,
        g_norm_one,
        m_q * gain_one,
        m_k * gain_one,
        m_v * gain_one,
        g_out,
        g_norm_two,
        m_gate * gain_two,
        m_up * gain_two,
        m_down.astype(jnp.float32),
    )


MESH = pl.DeviceIdType.MESH
LIMIT = 60 * 2**20
BF, F32 = jnp.bfloat16, jnp.float32


def dot_nn(a, b):
    return lax.dot_general(a, b, (((1,), (0,)), ((), ())), preferred_element_type=F32)


def dot_nt(a, b):
    return lax.dot_general(a, b, (((1,), (1,)), ((), ())), preferred_element_type=F32)


def dot_tn(a, b):
    return lax.dot_general(a, b, (((0,), (0,)), ((), ())), preferred_element_type=F32)


class Net:
    def __init__(self, sends, recvs):
        self.sends, self.recvs, self.count, self.open, self.used = sends, recvs, 0, [], 0
        self.s, self.d = lax.axis_index("seq"), lax.axis_index("dp")
        self.z, self.c = lax.div(self.s, 2), lax.rem(self.s, 2)
        y, x = lax.div(self.d, 2), lax.rem(self.d, 2)
        self.plane = (y * 2 + 1 - x, (1 - y) * 2 + x, 3 - self.d)
        self.mate = self.at(self.z, 1 - self.c)

    def room(self, count):
        base = self.used
        self.used += count
        return base

    def at(self, z, core):
        return {"seq": z * 2 + core, "dp": self.d}

    def across(self, kind):
        return {"seq": self.s, "dp": self.plane[kind]}

    def greet(self):
        barrier = pltpu.get_barrier_semaphore()
        peers = [self.mate] + [self.across(k) for k in range(3)]
        peers += [self.at(lax.rem(self.z + k, 4), self.c) for k in (1, 2, 3)]
        for peer in peers:
            pl.semaphore_signal(barrier, inc=1, device_id=peer, device_id_type=MESH)

    def greeted(self):
        pl.semaphore_wait(pltpu.get_barrier_semaphore(), 7)

    def copy(self, src, dst, send, recv, peer):
        return pltpu.make_async_remote_copy(
            src_ref=src,
            dst_ref=dst,
            send_sem=self.sends.at[send],
            recv_sem=self.recvs.at[recv],
            device_id=peer,
            device_id_type=MESH,
        )

    def push(self, src, dst, recv, peer, when=None):
        copy = self.copy(src, dst, self.count, recv, peer)
        self.count += 1
        if when is None:
            copy.start()
        else:
            pl.when(when)(copy.start)
        self.open.append((copy, when))

    def arrive(self, dst, recv, when=None):
        copy = self.copy(dst, dst, 0, recv, self.mate)
        if when is None:
            copy.wait_recv()
        else:
            pl.when(when)(copy.wait_recv)

    def finish(self, upto=None):
        upto = len(self.open) if upto is None else upto
        for copy, when in self.open[:upto]:
            if when is None:
                copy.wait_send()
            else:
                pl.when(when)(copy.wait_send)
        self.open = self.open[upto:]

    def order(self, step):
        if step == 0:
            return self.z
        table = ((1, 0, 3, 2), (2, 2, 1, 1), (3, 3, 0, 0))[step - 1]
        z = self.z
        return jnp.where(z == 0, table[0], jnp.where(z == 1, table[1], jnp.where(z == 2, table[2], table[3])))


class Chain:
    def __init__(self, net, block, room=4):
        self.net, self.block, self.base = net, block, net.room(room)

    def start(self):
        net = self.net
        own = self.block(net.z, net.c)
        net.push(own, own, self.base + net.z, net.at(net.z + 1, net.c), net.z < 3)
        net.push(own, own, self.base + net.z, net.at(net.z - 1, net.c), net.z > 0)

    def step(self, k):
        net = self.net
        b = net.order(k)
        block = self.block(b, net.c)
        net.arrive(block, self.base + b)
        to = jnp.where(b < net.z, net.z + 1, net.z - 1)
        net.push(block, block, self.base + b, net.at(to, net.c), (to >= 0) & (to <= 3))


class Lines(Chain):
    def __init__(self, net, block):
        super().__init__(net, block, 8)

    def start(self):
        super().start()
        self.give(0)

    def give(self, k):
        net = self.net
        b = net.order(k)
        block = self.block(b, net.c)
        net.push(block, block, self.base + 4 + b, net.mate)

    def take(self):
        net = self.net
        for b in range(4):
            net.arrive(self.block(b, 1 - net.c), self.base + 4 + b)


class Slices(Chain):
    def __init__(self, net, full, rows):
        self.full, self.rows, self.half = full, rows, rows // 32 * 16
        super().__init__(net, lambda z, core: self.part(net.d, z, core), 36)

    def part(self, slot, z, core, half=None):
        first = pl.multiple_of((z * 2 + core) * self.rows, 16)
        if half is None:
            return self.full.at[slot, pl.ds(first, self.rows)]
        if half == 0:
            return self.full.at[slot, pl.ds(first, self.half)]
        return self.full.at[slot, pl.ds(pl.multiple_of(first + self.half, 16), self.rows - self.half)]

    def spread(self, k):
        net = self.net
        b = net.order(k)
        block = self.part(net.d, b, net.c)
        net.push(block, block, self.base + 4 + b, net.across(0))
        net.push(block, block, self.base + 8 + b, net.across(1))
        net.push(block, block, self.base + 20 + b, net.mate)

    def pass_on(self, k):
        net = self.net
        b = net.order(k)
        for kind in (0, 1):
            block = self.part(net.plane[kind], b, net.c)
            net.arrive(block, self.base + 4 + 4 * kind + b)
            half = self.part(net.plane[kind], b, net.c, kind)
            net.push(half, half, self.base + 12 + 4 * kind + b, net.across(1 - kind))
            net.push(block, block, self.base + 24 + 4 * kind + b, net.mate)

    def corner(self, k):
        net = self.net
        b = net.order(k)
        for kind in (0, 1):
            half = self.part(net.plane[2], b, net.c, kind)
            net.arrive(half, self.base + 12 + 4 * kind + b)
        block = self.part(net.plane[2], b, net.c)
        net.push(block, block, self.base + 32 + b, net.mate)

    def take(self):
        net = self.net
        for b in range(4):
            net.arrive(self.part(net.d, b, 1 - net.c), self.base + 20 + b)
            for kind in range(3):
                net.arrive(self.part(net.plane[kind], b, 1 - net.c), self.base + 24 + 4 * kind + b)


class Plane:
    def __init__(self, net, full):
        self.net, self.full, self.base = net, full, net.room(4)
        self.half = full.shape[1] // 2

    def start(self):
        net = self.net
        own = self.full.at[net.d]
        for kind in (0, 1):
            net.push(own, own, self.base + kind, net.across(kind))

    def pass_on(self):
        net = self.net
        for kind in (0, 1):
            net.arrive(self.full.at[net.plane[kind]], self.base + kind)
            half = self.full.at[net.plane[kind], pl.ds(kind * self.half, self.half)]
            net.push(half, half, self.base + 2 + kind, net.across(1 - kind))

    def take(self):
        net = self.net
        for kind in (0, 1):
            net.arrive(self.full.at[net.plane[2], pl.ds(kind * self.half, self.half)], self.base + 2 + kind)


class Spread:
    def __init__(self, net, send, land):
        self.net, self.send, self.land, self.base = net, send, land, net.room(3)

    def start(self):
        net = self.net
        for kind in (2, 0, 1):
            net.push(self.send(net.plane[kind]), self.land(net.d), self.base + kind, net.across(kind))

    def take(self):
        for kind in range(3):
            self.net.arrive(self.land(self.net.plane[kind]), self.base + kind)


class ToMate:
    def __init__(self, net, send, land):
        self.net, self.send, self.land, self.base = net, send, land, net.room(1)

    def start(self):
        self.net.push(self.send, self.land, self.base, self.net.mate)

    def take(self):
        self.net.arrive(self.land, self.base)


class ToOwners:
    def __init__(self, net, part, land, down=False):
        self.net, self.part, self.land, self.down, self.base = net, part, land, down, net.room(3)

    def start(self):
        net = self.net
        for k in (3, 2, 1):
            to = lax.rem(net.z - k + 4, 4)
            net.push(self.part(to), self.land(k - 1), self.base + k - 1, net.at(to, net.c), (net.z >= k) if self.down else None)

    def take(self):
        net = self.net
        for k in (1, 2, 3):
            net.arrive(self.land(k - 1), self.base + k - 1, (net.z + k <= 3) if self.down else None)


class ChainSum:
    def __init__(self, net, part, land, add):
        self.net, self.part, self.land, self.add, self.base = net, part, land, add, net.room(6)

    def stage(self, k):
        net, z = self.net, self.net.z
        i = k - 3 + z
        valid = (i >= 0) & (i < z)
        i = jnp.clip(i, 0, 3)

        @pl.when(valid & (z < 3))
        def _():
            net.arrive(self.land(i), self.base + i)
            self.add(i, i)

        net.push(self.part(i), self.land(i), self.base + i, net.at(z - 1, net.c), valid)
        j = k - z
        valid = (j >= 0) & (3 - j > z)
        j = jnp.clip(j, 0, 3)

        @pl.when(valid & (z > 0))
        def _():
            net.arrive(self.land(4 - j), self.base + 3 + j)
            self.add(3 - j, 4 - j)

        net.push(self.part(3 - j), self.land(4 - j), self.base + 3 + j, net.at(z + 1, net.c), valid)

    def own(self):
        net, z = self.net, self.net.z

        @pl.when(z < 3)
        def _():
            net.arrive(self.land(z), self.base + z)
            self.add(z, z)

        @pl.when(z > 0)
        def _():
            net.arrive(self.land(1 + z), self.base + 6 - z)
            self.add(z, 1 + z)


def settle(land, wide, rows):
    for j in range(4):
        wide[pl.ds(j * rows, rows), : land.shape[2]] = land[j, :rows, :].astype(F32)


def turned(tile, cosine, sine):
    lane = lax.broadcasted_iota(jnp.int32, tile.shape, 1)
    other = jnp.where(lax.rem(lane, HD) < HD // 2, pltpu.roll(tile, 128 - HD // 2, 1), pltpu.roll(tile, HD // 2, 1))
    return tile * cosine + other * sine


def own_rows(index, rows):
    return pl.ds(pl.multiple_of(index * rows, 16), rows)


def norm_scale(v):
    return lax.rsqrt(jnp.mean(v * v, axis=1, keepdims=True) + EPSILON)


def norm_pull(e, v):
    r = norm_scale(v)
    return r * e - v * (r * r * r) * jnp.mean(e * v, axis=1, keepdims=True)


def joined(heads, j, tok):
    groups = H // KV
    pair = [heads[h // groups, tok * (h % groups) : tok * (h % groups) + tok, :] for h in (2 * j, 2 * j + 1)]
    return jnp.concatenate(pair, axis=1)


def plane_sum(net, send, land):
    total = send[net.d].astype(F32)
    for kind in range(3):
        total = total + land[net.plane[kind]].astype(F32)
    return total


LATE = ((9, 10), (11, 12), (13, 8), (14, None))


def column(row):
    n = row.shape[1]
    same = lax.broadcasted_iota(jnp.int32, (n, n), 0) == lax.broadcasted_iota(jnp.int32, (n, n), 1)
    return jnp.sum(jnp.where(same, row, 0.0), axis=1, keepdims=True)


def row_of(col):
    n = col.shape[0]
    same = lax.broadcasted_iota(jnp.int32, (n, n), 0) == lax.broadcasted_iota(jnp.int32, (n, n), 1)
    return jnp.sum(jnp.where(same, col, 0.0), axis=0, keepdims=True)


def layer_kernel(
    x_in, cot_in, query, key_w, value, output, gate_w, up_w, down, gain_one, gain_two, freq,
    doc_starts, keep_mask, keep_rate, seq_order,
    block_out, input_grad, back_gu, back_att, back_down,
    att_send, gu_send, att_land, gu_land, wide, qkv_land, kv_all, o_heads, bias, wa, wb, wgu, wd,
    xn_all, gd_all, mn_all, att_all, q_heads, k_heads, v_heads, probs, middle, act, gboth, turn_x, turn_n, turn_a,
    gn_send, gn_land, br_send, br_land, gu_mate, gu_zone, dn_mate, dn_zone, gmid, do_heads, dkv, kv_mate, kv_zone, kv_tot,
    cut_land, ma_mate, ma_zone, gx_land, sends, recvs,
):
    net = Net(sends, recvs)
    tok, dim = x_in.shape[1], x_in.shape[2]
    rows = dim // 32
    blk = 4 * rows
    ffr = down.shape[0]
    hid = 8 * ffr
    d, z, c, s = net.d, net.z, net.c, net.s
    span, length = 4 * tok, 8 * tok
    groups = H // KV
    qkv_send = cut_send = act.reshape(4, tok, hid)
    gx_send, gs_heads = gd_all, gboth
    m_att = wb.reshape(4, 4, 2, blk, 384)

    a2a_att = Spread(net, lambda j: att_send.at[j], lambda j: att_land.at[j])
    a2a_gu = Spread(net, lambda j: gu_send.at[j], lambda j: gu_land.at[j])
    a2a_qkv = Spread(net, lambda j: qkv_send.at[j, :, pl.ds(0, 512)], lambda j: qkv_land.at[j])
    a = Lines(net, lambda zz, core: wa.at[own_rows(zz * 2 + core, blk)])
    b = Slices(net, wb, blk)
    gu = Lines(net, lambda zz, core: wgu.at[zz, core])
    dn = Lines(net, lambda zz, core: wd.at[zz, core])
    kv = Lines(net, lambda zz, core: kv_all.at[zz, core])
    xs = Plane(net, xn_all)
    gs = Plane(net, gd_all)
    ms = Plane(net, mn_all)
    ats = Plane(net, att_all)

    net.greet()
    first_gain = column(gain_one[...])
    zero = jnp.zeros((att_send.shape[1] - rows, 128), BF)
    weights = (query, key_w, value)

    def qkv_tile(t):
        ref, t = (query, t) if t < 9 else (key_w, t - 9) if t < 12 else (value, t - 12)
        return (ref[:, 128 * t : 128 * t + 128].astype(F32) * first_gain).astype(BF)

    for j in range(4):
        tiles = [qkv_tile(2 * j), qkv_tile(2 * j + 1), qkv_tile(LATE[j][0])]
        tiles.append(output[:, 1024:1152] if LATE[j][1] is None else qkv_tile(LATE[j][1]))
        tiles += [output[:, 256 * j : 256 * j + 128], output[:, 256 * j + 128 : 256 * j + 256]]
        for i, tile in enumerate(tiles):
            att_send[j, :rows, 128 * i : 128 * i + 128] = tile
            att_send[j, rows:, 128 * i : 128 * i + 128] = zero
    net.greeted()
    a2a_att.start()
    att_land[d] = att_send[d]
    x = x_in[0].astype(F32)
    xn_all[d] = (x * norm_scale(x)).astype(BF)
    xs.start()
    second_gain = column(gain_two[...])
    for i, ref in enumerate((gate_w, up_w)):
        scaled = ref[...].astype(F32) * second_gain
        for j in range(4):
            part = [scaled[:, ffr * (4 * k + j) : ffr * (4 * k + j) + ffr] for k in range(8)]
            gu_send[j, :rows, hid * i : hid * i + hid] = jnp.concatenate(part, axis=1).astype(BF)
            gu_send[j, rows:, hid * i : hid * i + hid] = jnp.zeros((gu_send.shape[1] - rows, hid), BF)
    a2a_gu.start()
    gu_land[d] = gu_send[d]
    sample = seq_order[d]
    scale_attn, scale_mlp = [
        jnp.full((1, 1), keep_mask[sample, i].astype(F32), F32) / jnp.full((1, 1), keep_rate[i], F32) for i in range(2)
    ]
    gd_all[d] = (cot_in[0].astype(F32) * scale_mlp).astype(BF)
    wd[z, c] = down[...]
    position = s * tok + lax.broadcasted_iota(jnp.int32, (tok, 1), 0)
    angle = position.astype(F32) * freq[...]
    lane = lax.broadcasted_iota(jnp.int32, angle.shape, 1)
    cosine, sine = jnp.cos(angle), jnp.where(lax.rem(lane, HD) < HD // 2, -jnp.sin(angle), jnp.sin(angle))
    a2a_att.take()
    settle(att_land, wide, rows)
    own = own_rows(s, blk)
    wa[own, :] = wide[:, :512].astype(BF)
    wb[d, own, :] = wide[:, 384:768].astype(BF)
    a.start()
    a.step(1)
    a.give(1)
    dn.start()
    xs.pass_on()
    a.step(2)
    a.give(2)
    b.start()
    a.step(3)
    a.give(3)
    a2a_gu.take()
    settle(gu_land, wide, rows)
    wgu[z, c] = wide[...].astype(BF)
    gu.start()
    xs.take()
    a.take()

    eighth = 1.0 / math.sqrt(HD)
    for j in range(4):
        part = dot_nn(xn_all[j], wa[...])
        for i in range(4):
            tile = part[:, 128 * i : 128 * i + 128]
            spun = turned(tile, cosine, sine)
            if i < 2:
                tile = spun * eighth
            elif i == 2:
                tile = jnp.where(d < 2, spun, tile)
            else:
                tile = jnp.where(d == 0, spun, jnp.where(d == 2, spun * eighth, tile))
            qkv_send[j, :, 128 * i : 128 * i + 128] = tile.astype(BF)
    a2a_qkv.start()
    early = len(net.open)
    qkv_land[d] = qkv_send[d, :, :512]
    b.spread(0)
    b.step(1)
    b.spread(1)
    a2a_qkv.take()
    places = [(0, 256), (0, 384), (1, 256), (1, 384), (2, 256), (3, 256)]
    for i, (j, col) in enumerate(places):
        kv_all[z, c, :, 128 * i : 128 * i + 128] = qkv_land[j, :, col : col + 128]
    kv.start()
    gs.start()
    for t in range(9):
        j, col = (t // 2, (t % 2) * 128) if t < 8 else (2, 384)
        for h in (2 * t, 2 * t + 1):
            at = col + HD * (h % 2)
            q_heads[h // groups, tok * (h % groups) : tok * (h % groups) + tok, :] = qkv_land[j, :, at : at + HD]
    first = jnp.zeros((tok, 1), jnp.int32)
    for j in range(doc_starts.shape[1]):
        start = doc_starts[sample, j]
        first = jnp.where(position >= start, jnp.maximum(first, start), first)
    key = lax.broadcasted_iota(jnp.int32, bias.shape, 1)
    bias[...] = jnp.where((key <= position) & (key >= first), 0.0, MASKED)

    kv.step(1)
    kv.give(1)
    b.step(2)
    b.spread(2)
    kv.step(2)
    kv.give(2)
    b.step(3)
    b.spread(3)
    b.pass_on(0)
    b.pass_on(1)
    kv.step(3)
    kv.give(3)
    dn.step(1)
    gu.step(1)
    gs.pass_on()
    b.pass_on(2)
    b.corner(0)
    b.corner(1)
    kv.take()
    for j in range(8):
        for k in range(KV):
            k_heads[k, pl.ds(tok * j, tok), :] = kv_all[j // 2, j % 2, :, HD * k : HD * k + HD]
            v_heads[k, pl.ds(tok * j, tok), :] = kv_all[j // 2, j % 2, :, HD * (KV + k) : HD * (KV + k) + HD]

    def head(h, carry):
        k = lax.div(h, groups)
        mine = pl.ds(pl.multiple_of(lax.rem(h, groups) * tok, tok), tok)
        score = dot_nt(q_heads[k, mine, :], k_heads[k]) + bias[...]
        expo = jnp.exp(score - jnp.max(score, axis=1, keepdims=True))
        p = (expo / jnp.sum(expo, axis=1, keepdims=True)).astype(BF)
        probs[k, mine, :] = p
        o_heads[k, mine, :] = dot_nn(p, v_heads[k])
        return carry

    lax.fori_loop(0, 6, head, 0)
    b.pass_on(3)
    b.corner(2)
    lax.fori_loop(6, 12, head, 0)
    b.corner(3)
    dn.step(2)
    gu.step(2)
    lax.fori_loop(12, 18, head, 0)
    b.take()
    for j in range(H // 2):
        att_all[d, :, 128 * j : 128 * j + 128] = joined(o_heads, j, tok).astype(BF)
    full = att_all[d]
    branch = [dot_nn(full, wb[j, :, 128:]) for j in range(4)] + [dot_nn(full, wb[3, :, :128])]
    mid = x_in[0].astype(F32) + scale_attn * jnp.concatenate(branch, axis=1)
    middle[...] = mid
    mn_all[d] = (mid * norm_scale(mid)).astype(BF)
    gs.take()
    ms.start()
    for k in (1, 2):
        dn.give(k)
        gu.give(k)
    dn.step(3)
    dn.give(3)
    ms.pass_on()
    gu.step(3)
    gu.give(3)
    ms.take()
    dn.take()
    gu.take()
    net.finish(early)
    sent = len(net.open)
    ats.start()

    def by_cols(send, land, width):
        return [
            Spread(
                net,
                lambda j, n=n: send.at[j, :, pl.ds(width * n, width)],
                lambda j, n=n: land.at[j, :, pl.ds(width * n, width)],
            )
            for n in range(dim // width)
        ]

    gn, br, gx = by_cols(gn_send, gn_land, 384), by_cols(br_send, br_land, dim), by_cols(gx_send, gx_land, 384)
    wgu_flat, wd_flat = wgu.reshape(dim, 2 * hid), wd.reshape(hid, dim)
    other = 1 - c
    gu_pair = [
        ToMate(net, wgu.at[:, other, :, pl.ds(256 * n, 256)], gu_mate.at[:, :, pl.ds(256 * n, 256)]) for n in range(2 * hid // 256)
    ]
    dn_pair = [ToMate(net, wd.at[:, other, :, pl.ds(384 * n, 384)], dn_mate.at[:, :, pl.ds(384 * n, 384)]) for n in range(3)]

    for n in range(hid // 256):
        cols, ups = pl.ds(256 * n, 256), pl.ds(hid + 256 * n, 256)
        normed = mn_all[...].reshape(span, dim)
        gate = dot_nn(normed, wgu_flat[:, cols])
        up = dot_nn(normed, wgu_flat[:, ups])
        g_act = dot_nt(gd_all[...].reshape(span, dim), wd_flat[cols, :])
        sig = jax.nn.sigmoid(gate)
        swish = gate * sig
        act[:, cols] = (swish * up).astype(BF)
        gboth[:, cols] = (g_act * up * (sig * (1.0 + gate * (1.0 - sig)))).astype(BF)
        gboth[:, ups] = (g_act * swish).astype(BF)
    for n in range(3):
        part = dot_nt(gboth[...], wgu_flat[384 * n : 384 * n + 384, :]).astype(BF)
        gn_send[:, :, 384 * n : 384 * n + 384] = part.reshape(4, tok, 384)
        gn[n].start()
    for n in range(3):
        part = dot_nn(act[...], wd_flat[:, 384 * n : 384 * n + 384]).astype(BF)
        br_send[:, :, 384 * n : 384 * n + 384] = part.reshape(4, tok, 384)
    turn_x[...] = mn_all[...].reshape(span, dim).T
    turn_a[...] = act[...].T
    net.finish(sent)
    for n in range(2 * hid // 256):
        wgu_flat[:, 256 * n : 256 * n + 256] = dot_nn(turn_x[...], gboth[:, 256 * n : 256 * n + 256]).astype(BF)
        gu_pair[n].start()
    for n in range(3):
        cols = pl.ds(384 * n, 384)
        wd_flat[:, cols] = dot_nn(turn_a[...], gd_all[:, :, cols].reshape(span, 384)).astype(BF)
        dn_pair[n].start()
    br[0].start()

    def add_gu(block, slot):
        wgu[block, c] = (wgu[block, c].astype(F32) + gu_zone[slot].astype(F32)).astype(BF)

    def add_dn(block, slot):
        wd[block, c] = (wd[block, c].astype(F32) + dn_zone[slot].astype(F32)).astype(BF)

    gu_sum = ChainSum(net, lambda zz: wgu.at[zz, c], lambda k: gu_zone.at[k], add_gu)
    dn_sum = ChainSum(net, lambda zz: wd.at[zz, c], lambda k: dn_zone.at[k], add_dn)
    ats.pass_on()
    for pair in gu_pair:
        pair.take()
    for k in range(4):
        wgu[k, c] = (wgu[k, c].astype(F32) + gu_mate[k].astype(F32)).astype(BF)
    gu_sum.stage(0)
    for pair in dn_pair:
        pair.take()
    for k in range(4):
        wd[k, c] = (wd[k, c].astype(F32) + dn_mate[k].astype(F32)).astype(BF)
    dn_sum.stage(0)

    for n in range(3):
        gn[n].take()
    mid = middle[...]
    g_mid = cot_in[0].astype(F32) + norm_pull(plane_sum(net, gn_send, gn_land), mid)
    gmid[...] = g_mid
    gba = (scale_attn * g_mid).astype(BF)
    for j in range(4):
        cut_send[j, :, 512:768] = gba[:, 256 * j : 256 * j + 256]
    cut_send[3, :, 384:512] = gba[:, 1024:1152]
    cut = lambda cols: Spread(net, lambda j: cut_send.at[j, :, cols], lambda j: cut_land.at[j, :, cols])
    cut_o, cut_q, cut_l = cut(pl.ds(512, 256)), cut(pl.ds(0, 256)), cut(pl.ds(256, 256))
    cut_o.start()
    cut_land[d, :, 512:768] = cut_send[d, :, 512:768]
    g_att = dot_nt(gba[:, 1024:1152], wb[3, :, :128])
    for j in range(4):
        g_att = g_att + dot_nt(gba[:, 256 * j : 256 * j + 256], wb[j, :, 128:])
    for h in range(H):
        do_heads[h // groups, tok * (h % groups) : tok * (h % groups) + tok, :] = g_att[:, HD * h : HD * h + HD].astype(BF)
    gu_sum.stage(1)

    kv_pair = [ToMate(net, dkv.at[n, :, other], kv_mate.at[n]) for n in range(2)]
    kv_sum = [ToOwners(net, lambda zz, n=n: dkv.at[n, zz, c], lambda k, n=n: kv_zone.at[n, k], True) for n in range(2)]

    def pull(k, carry):
        for g in range(groups):
            mine = pl.ds(tok * g, tok)
            p = probs[k, mine, :].astype(F32)
            t = p * dot_nt(do_heads[k, mine, :], v_heads[k])
            ds = (t - p * jnp.sum(t, axis=1, keepdims=True)).astype(BF)
            gs_heads[mine, :length] = ds
            o_heads[k, mine, :] = dot_nn(ds, k_heads[k]) * eighth
        half, kk = lax.div(k, 3), lax.rem(k, 3)
        for i, (left, right) in enumerate(((q_heads[k], gs_heads[: groups * tok, :length]), (do_heads[k], probs[k]))):
            turned_grad = dot_tn(left, right).astype(BF)
            at = pl.ds(pl.multiple_of(192 * i + HD * kk, HD), HD)
            for j in range(8):
                dkv[half, j // 2, j % 2, at, :] = turned_grad[:, tok * j : tok * j + tok]
        return carry

    def pair_sum(n):
        kv_pair[n].take()
        for k in range(4):
            dkv[n, k, c] = (dkv[n, k, c].astype(F32) + kv_mate[n, k].astype(F32)).astype(BF)
        kv_sum[n].start()

    def grads(p, parts):
        at = 0
        for part in parts:
            wb[p, :, at : at + part.shape[1]] = part.astype(BF)
            at += part.shape[1]
        pair = ToMate(net, m_att.at[p, :, other, :, quarter], ma_mate.at[p])
        pair.start()
        return pair

    def grads_sum(p, pair):
        pair.take()
        for k in range(4):
            m_att[p, k, c, :, quarter] = (m_att[p, k, c, :, quarter].astype(F32) + ma_mate[p, k].astype(F32)).astype(BF)
        out = ToOwners(net, lambda zz: m_att.at[p, zz, c, :, quarter], lambda k: ma_zone.at[p, k])
        out.start()
        return out

    def grads_back(p, out):
        cols = pl.ds(256 * p, 256)
        out.take()
        total = m_att[p, z, c, :, quarter].astype(F32)
        for k in range(3):
            total = total + ma_zone[p, k].astype(F32)
        wide[:, : total.shape[1]] = total
        for j in range(4):
            att_land[j, :rows, cols] = wide[pl.ds(j * rows, rows), : total.shape[1]].astype(BF)
        spread = Spread(net, lambda j: att_land.at[j, :, cols], lambda j: back_att.at[j, :, cols])
        spread.start()
        back_att[d, :, cols] = att_land[d, :, cols]
        return spread

    q_cols, l_cols, o_cols = pl.ds(0, 256), pl.ds(256, 256), pl.ds(512, 256)
    quarter = pl.ds(0, 256)
    lax.fori_loop(0, 3, pull, 0)
    kv_pair[0].start()
    ats.take()
    cut_o.take()
    turn_x[...] = att_all[...].reshape(span, dim).T
    pair_sum(0)
    lax.fori_loop(3, 6, pull, 0)
    kv_pair[1].start()
    for t in range(9):
        j, col = (t // 2, (t % 2) * 128) if t < 8 else (2, 384)
        cut_send[j, :, col : col + 128] = turned(joined(o_heads, t, tok), cosine, -sine).astype(BF)
    cut_q.start()
    cut_land[d, :, q_cols] = cut_send[d, :, q_cols]
    pair_sum(1)
    pair_o = grads(2, [dot_nn(turn_x[...], cut_land[:, :, o_cols].reshape(span, 256))])
    turn_n[...] = xn_all[...].reshape(span, dim).T
    br[0].take()
    block_out[0] = (middle[...] + scale_mlp * plane_sum(net, br_send, br_land)).astype(BF)
    cut_q.take()
    pair_q = grads(0, [dot_nn(turn_n[...], cut_land[:, :, q_cols].reshape(span, 256))])
    dn_sum.stage(1)

    for n in range(2):
        kv_sum[n].take()
        kv_tot[n] = dkv[n, z, c].astype(F32)
        for k in (1, 2, 3):

            @pl.when(z + k <= 3)
            def _(n=n, k=k):
                kv_tot[n] += kv_zone[n, k - 1].astype(F32)

    keys = jnp.concatenate([kv_tot[0, :192, :], kv_tot[1, :192, :]], axis=0).T
    vals = jnp.concatenate([kv_tot[0, 192:, :], kv_tot[1, 192:, :]], axis=0).T
    late = [turned(keys[:, 128 * i : 128 * i + 128], cosine, -sine) for i in range(3)] + [vals[:, 128 * i : 128 * i + 128] for i in range(3)]
    for tile, (j, col) in zip(late, places):
        cut_send[j, :, col : col + 128] = tile.astype(BF)
    cut_l.start()
    cut_land[d, :, l_cols] = cut_send[d, :, l_cols]
    gu_sum.stage(2)
    sum_o = grads_sum(2, pair_o)
    cut_l.take()
    last = cut_land[:, :, 384:512].reshape(span, 128)
    cuts = cut_land[:, :, :512].reshape(span, 512)
    lane = lax.broadcasted_iota(jnp.int32, cuts.shape, 1)
    cuts = jnp.where((d == 3) & (lane >= 384), jnp.zeros_like(cuts), cuts)
    for n in range(3):
        part = dot_nt(cuts, wa[384 * n : 384 * n + 384, :]).astype(BF)
        gx_send[:, :, 384 * n : 384 * n + 384] = part.reshape(4, tok, 384)
        gx[n].start()
    second = jnp.where(d == 3, dot_nn(turn_x[...], last), dot_nn(turn_n[...], last))
    pair_l = grads(1, [dot_nn(turn_n[...], cut_land[:, :, 256:384].reshape(span, 128)), second])
    sum_l = grads_sum(1, pair_l)
    sum_q = grads_sum(0, pair_q)
    dn_sum.stage(2)
    back_o = grads_back(2, sum_o)
    gu_sum.own()
    wide[...] = wgu[z, c].astype(F32)
    for j in range(4):
        gu_land[j, :rows, :] = wide[pl.ds(j * rows, rows), :].astype(BF)
    back_g = Spread(net, lambda j: gu_land.at[j], lambda j: back_gu.at[j])
    back_g.start()
    back_gu[d] = gu_land[d]
    back_l = grads_back(1, sum_l)
    back_q = grads_back(0, sum_q)
    for n in range(3):
        gx[n].take()
    input_grad[0] = gmid[...] + norm_pull(plane_sum(net, gx_send, gx_land), x_in[0].astype(F32))
    dn_sum.own()
    back_down[...] = wd[z, c]
    for spread in (back_o, back_q, back_g, back_l):
        spread.take()
    net.finish()


def layer(x, cot, weights, down, gains, freq, doc_starts, keep_mask, keep_rate, seq_order):
    tok, dim = x.shape[1:]
    ns = 8
    length = tok * ns
    ffr = down.shape[0]
    hid = ffr * ns
    blk = dim // ns
    span = 4 * tok
    vm = pl.BlockSpec(memory_space=pltpu.VMEM)
    sm = pl.BlockSpec(memory_space=pltpu.SMEM)
    padded = blk // 4 + -(blk // 4) % 16
    att_pack, gu_pack = ((4, padded, 768), BF), ((4, padded, 2 * hid), BF)
    outs = [((1, tok, dim), BF), ((1, tok, dim), F32), gu_pack, att_pack, (down.shape, BF)]
    plane = ((4, tok, dim), BF)
    wide_cut = ((4, tok, 512), BF)
    three = ((KV, 3 * tok, HD), BF)
    scratch = [
        att_pack,
        gu_pack,
        att_pack,
        gu_pack,
        ((blk, 2 * hid), F32),
        wide_cut,
        ((4, 2, tok, 2 * KV * HD), BF),
        ((KV, 3 * tok, HD), F32),
        ((tok, length), F32),
        ((dim, 512), BF),
        ((4, dim, 384), BF),
        ((4, 2, blk, 2 * hid), BF),
        ((4, 2, ffr, dim), BF),
        plane,
        plane,
        plane,
        plane,
        three,
        ((KV, length, HD), BF),
        ((KV, length, HD), BF),
        ((KV, 3 * tok, length), BF),
        ((tok, dim), F32),
        ((span, hid), BF),
        ((span, 2 * hid), BF),
        ((dim, span), BF),
        ((dim, span), BF),
        ((hid, span), BF),
        plane,
        plane,
        plane,
        plane,
        ((4, blk, 2 * hid), BF),
        ((5, blk, 2 * hid), BF),
        ((4, ffr, dim), BF),
        ((5, ffr, dim), BF),
        ((tok, dim), F32),
        three,
        ((2, 4, 2, 384, tok), BF),
        ((2, 4, 384, tok), BF),
        ((2, 3, 384, tok), BF),
        ((2, 384, tok), F32),
        ((4, tok, 768), BF),
        ((3, 4, blk, 256), BF),
        ((3, 3, blk, 256), BF),
        plane,
    ]
    return pl.pallas_call(
        layer_kernel,
        out_shape=[jax.ShapeDtypeStruct(*o) for o in outs],
        in_specs=[vm] * 12 + [sm] * 4,
        out_specs=[vm] * len(outs),
        scratch_shapes=[pltpu.VMEM(*t) for t in scratch] + [pltpu.SemaphoreType.DMA((320,)), pltpu.SemaphoreType.DMA((256,))],
        compiler_params=pltpu.CompilerParams(collective_id=0, has_side_effects=True, vmem_limit_bytes=LIMIT),
        name="k_layer",
    )(x, cot, *weights, down, *gains, freq, doc_starts, keep_mask, keep_rate, seq_order)


def grads_kernel(
    query, key_w, value, gate_w, up_w, gain_one, gain_two, block_in, input_in, back_gu, back_att, back_down,
    block_out, input_out, norm_one, g_query, g_key, g_value, g_output, norm_two, g_gate, g_up, g_down,
):
    rows, ffr = query.shape[0], back_down.shape[0]
    hid = 8 * ffr
    block_out[...] = block_in[...]
    input_out[...] = input_in[...]
    g_down[...] = back_down[...].astype(F32)
    gain = column(gain_one[...])
    total = jnp.zeros((rows, 128), F32)
    for j in range(4):
        for i, t in enumerate((2 * j, 2 * j + 1, LATE[j][0], LATE[j][1])):
            m = back_att[j, :rows, 128 * i : 128 * i + 128].astype(F32)
            if t is None:
                g_output[:, 1024:1152] = m
                continue
            w, g, t = (query, g_query, t) if t < 9 else (key_w, g_key, t - 9) if t < 12 else (value, g_value, t - 12)
            cols = slice(128 * t, 128 * t + 128)
            total = total + w[:, cols].astype(F32) * m
            g[:, cols] = m * gain
        g_output[:, 256 * j : 256 * j + 256] = back_att[j, :rows, 512:768].astype(F32)
    norm_one[...] = row_of(jnp.sum(total, axis=1, keepdims=True))
    gain = column(gain_two[...])
    total = jnp.zeros((rows, 4 * ffr), F32)
    for i, (w, g) in enumerate(((gate_w, g_gate), (up_w, g_up))):
        parts = [back_gu[j, :rows, hid * i : hid * i + hid].astype(F32) for j in range(4)]
        for k in range(8):
            m = jnp.concatenate([part[:, ffr * k : ffr * k + ffr] for part in parts], axis=1)
            cols = slice(4 * ffr * k, 4 * ffr * k + 4 * ffr)
            total = total + w[:, cols].astype(F32) * m
            g[:, cols] = m * gain
    norm_two[...] = row_of(jnp.sum(total, axis=1, keepdims=True))


def gradients(query, key_w, value, output, gate_w, up_w, gains, results):
    block, grad, back_gu, back_att, back_down = results
    shapes = [grad.shape, gains[0].shape] + [w.shape for w in (query, key_w, value, output)]
    shapes += [gains[1].shape, gate_w.shape, up_w.shape, back_down.shape]
    vm = pl.BlockSpec(memory_space=pltpu.VMEM)
    return pl.pallas_call(
        grads_kernel,
        out_shape=[jax.ShapeDtypeStruct(block.shape, BF)] + [jax.ShapeDtypeStruct(t, F32) for t in shapes],
        in_specs=[vm] * 12,
        out_specs=[vm] * 11,
        name="k_grads",
    )(query, key_w, value, gate_w, up_w, *gains, block, grad, back_gu, back_att, back_down)


def shards_by_kernel(
    hidden_in,
    attn_norm,
    query_weight,
    key_weight,
    value_weight,
    output_weight,
    mlp_norm,
    gate_weight,
    up_weight,
    down_weight,
    cotangent,
    doc_starts,
    keep_mask,
    keep_rate,
    seq_order,
):
    rows = query_weight.shape[0]
    freq = ROPE_BASE ** (-2.0 * jnp.arange(HD // 2, dtype=F32) / HD)
    freq = jnp.tile(freq, 128 // freq.shape[0])[None]
    gains = (attn_norm.reshape(1, rows), mlp_norm.reshape(1, rows))
    weights = (query_weight, key_weight, value_weight, output_weight, gate_weight, up_weight)
    results = layer(
        hidden_in, cotangent, weights, down_weight, gains, freq, doc_starts, keep_mask, keep_rate, seq_order
    )
    outs = list(gradients(*weights, gains, results))
    outs[2], outs[7] = outs[2].reshape(rows), outs[7].reshape(rows)
    return tuple(outs)


def solution(mesh):
    placed = (
        P("dp", "seq", None),
        P(("seq", "dp")),
        P(("seq", "dp"), None),
        P(("seq", "dp"), None),
        P(("seq", "dp"), None),
        P(("seq", "dp"), None),
        P(("seq", "dp")),
        P(("seq", "dp"), None),
        P(("seq", "dp"), None),
        P(("seq", "dp"), None),
        P("dp", "seq", None),
        P(),
        P(),
        P(),
        P(),
    )
    fits = mesh.shape["seq"] == 8 and mesh.shape["dp"] == 4
    return jax.shard_map(
        shards_by_kernel if fits else shards,
        mesh=mesh,
        in_specs=placed,
        out_specs=(
            P("dp", "seq", None),
            P("dp", "seq", None),
            P(("seq", "dp")),
            P(("seq", "dp"), None),
            P(("seq", "dp"), None),
            P(("seq", "dp"), None),
            P(("seq", "dp"), None),
            P(("seq", "dp")),
            P(("seq", "dp"), None),
            P(("seq", "dp"), None),
            P(("seq", "dp"), None),
        ),
        check_vma=False,
    )
```

```python
import math

import jax
import jax.numpy as jnp
from jax import lax
from jax.experimental import pallas as pl
from jax.experimental.pallas import tpu as pltpu
from jax.sharding import PartitionSpec as P

H = 18
KV = 6
HD = 64


EPSILON = 1e-05
ROPE_BASE = 10000.0
MASKED = -1e30


def contract_rows(left_rows, right_rows):
    return lax.dot_general(
        left_rows, right_rows, (((0,), (0,)), ((), ())), preferred_element_type=jnp.float32
    )


def contract_cols(left_mat, right_mat):
    return lax.dot_general(
        left_mat, right_mat, (((1,), (1,)), ((), ())), preferred_element_type=jnp.float32
    )


def low(v):
    return v.astype(jnp.bfloat16)


def dot(a, b):
    return jnp.dot(a, b, preferred_element_type=jnp.float32)


def swap_halves(vectors):
    half = HD // 2
    return jnp.concatenate([vectors[..., half:], vectors[..., :half]], axis=-1)


def shards(
    hidden_in,
    attn_norm,
    query_weight,
    key_weight,
    value_weight,
    output_weight,
    mlp_norm,
    gate_weight,
    up_weight,
    down_weight,
    cotangent,
    doc_starts,
    keep_mask,
    keep_rate,
    seq_order,
):
    tok = hidden_in.shape[1]
    ns, nd = lax.axis_size("seq"), lax.axis_size("dp")
    length = tok * ns
    rows = query_weight.shape[0]
    ffr = down_weight.shape[0]
    dim = hidden_in.shape[2]
    groups = H // KV
    nq, nk = H * HD, KV * HD
    score_scale = 1.0 / math.sqrt(HD)
    me_s, me_d = lax.axis_index("seq"), lax.axis_index("dp")
    sample = jnp.sum(jnp.where(jnp.arange(nd) == me_d, seq_order, 0))
    pick = jnp.arange(nd) == sample
    doc_begin = jnp.sum(jnp.where(pick[:, None], doc_starts, 0), axis=0)
    keep_flags = jnp.sum(jnp.where(pick[:, None], keep_mask, 0), axis=0).astype(jnp.float32)
    attn_scale = keep_flags[0] / keep_rate[0]
    mlp_scale = keep_flags[1] / keep_rate[1]
    positions = me_s * tok + jnp.arange(tok)
    first = jnp.max(jnp.where(doc_begin[None, :] <= positions[:, None], doc_begin[None, :], 0), axis=1)
    gain_one, gain_two = attn_norm[:, None], mlp_norm[:, None]

    qkv_rows = low(jnp.concatenate([query_weight, key_weight, value_weight], axis=1).astype(jnp.float32) * gain_one)
    w_qkv = lax.all_gather(qkv_rows, ("seq", "dp"), axis=0, tiled=True)
    w_out = lax.all_gather(output_weight, ("seq", "dp"), axis=0, tiled=True)

    def split_hidden(w):
        w = low(w.astype(jnp.float32) * gain_two).reshape(rows, ns, nd, ffr)
        w = jnp.transpose(w, (0, 2, 1, 3)).reshape(rows, nd * ns * ffr)
        return w

    gu = jnp.concatenate(
        [split_hidden(gate_weight).reshape(rows, nd, -1), split_hidden(up_weight).reshape(rows, nd, -1)], axis=2
    )
    gu = lax.all_to_all(gu, "dp", split_axis=1, concat_axis=0, tiled=True).reshape(nd * rows, -1)
    w_gu = lax.all_gather(gu, "seq", axis=0, tiled=True)
    w_down = lax.all_gather(down_weight, "seq", axis=0, tiled=True)
    hid = w_down.shape[0]

    x = hidden_in[0].astype(jnp.float32)
    r_one = lax.rsqrt(jnp.mean(x * x, axis=-1, keepdims=True) + EPSILON)
    xn = low(x * r_one)
    qkv = dot(xn, w_qkv)
    inverse_freq = ROPE_BASE ** (-2.0 * jnp.arange(HD // 2, dtype=jnp.float32) / HD)
    angles = positions.astype(jnp.float32)[:, None] * inverse_freq[None, :]
    cosine = jnp.tile(jnp.cos(angles), (1, 2))[:, None, :]
    sine = jnp.concatenate([-jnp.sin(angles), jnp.sin(angles)], axis=1)[:, None, :]

    def turn(v):
        return v * cosine + swap_halves(v) * sine

    def turn_back(v):
        return v * cosine - swap_halves(v) * sine

    queries = low(turn(qkv[:, :nq].reshape(tok, H, HD))).reshape(tok, KV, groups, HD)
    keys = low(turn(qkv[:, nq : nq + nk].reshape(tok, KV, HD)))
    kv = jnp.concatenate([keys.reshape(tok, nk), low(qkv[:, nq + nk :])], axis=1)
    kv_all = lax.all_gather(kv, "seq", axis=0, tiled=True)
    k_all, v_all = kv_all[:, :nk].reshape(length, KV, HD), kv_all[:, nk:].reshape(length, KV, HD)
    key_pos = jnp.arange(length)
    allowed = (key_pos[None, :] <= positions[:, None]) & (key_pos[None, :] >= first[:, None])
    scores = jnp.einsum("tkgd,skd->kgts", queries, k_all, preferred_element_type=jnp.float32) * score_scale
    scores = jnp.where(allowed, scores, MASKED)
    expo = jnp.exp(scores - jnp.max(scores, axis=-1, keepdims=True))
    probs = low(expo / jnp.sum(expo, axis=-1, keepdims=True))
    attended = jnp.einsum("kgts,skd->tkgd", probs, v_all, preferred_element_type=jnp.float32)
    att = low(attended.reshape(tok, nq))
    middle = x + attn_scale * dot(att, w_out)
    r_two = lax.rsqrt(jnp.mean(middle * middle, axis=-1, keepdims=True) + EPSILON)
    mn = low(middle * r_two)

    cot = cotangent[0].astype(jnp.float32)
    side = lax.all_gather(jnp.concatenate([xn, low(mlp_scale * cot), att], axis=1), "dp", axis=0, tiled=True)
    xn_all, gd_all, att_all = side[:, :dim], side[:, dim : 2 * dim], side[:, 2 * dim :]
    mn_all = lax.all_gather(mn, "dp", axis=0, tiled=True)
    gate, up = dot(mn_all, w_gu[:, :hid]), dot(mn_all, w_gu[:, hid:])
    sig = jax.nn.sigmoid(gate)
    act_gate = gate * sig
    act = low(act_gate * up)
    g_act = contract_cols(gd_all, w_down)
    gg = low(g_act * up * (sig * (1.0 + gate * (1.0 - sig))))
    gu_in = low(g_act * act_gate)
    gboth = jnp.concatenate([gg, gu_in], axis=1)
    g_mn = lax.psum_scatter(low(contract_cols(gboth, w_gu)), "dp", scatter_dimension=0, tiled=True).astype(jnp.float32)
    branch = lax.psum_scatter(low(dot(act, w_down)), "dp", scatter_dimension=0, tiled=True).astype(jnp.float32)
    block_output = low(middle + mlp_scale * branch)[None]
    m_gu = lax.psum_scatter(low(contract_rows(mn_all, gboth)), "seq", scatter_dimension=0, tiled=True)
    m_down = lax.psum_scatter(low(contract_rows(act, gd_all)), "seq", scatter_dimension=0, tiled=True)

    def norm_back(e, v, r):
        return r * e - v * (r * r * r) * jnp.mean(e * v, axis=-1, keepdims=True)

    g_mid = cot + norm_back(g_mn, middle, r_two)
    gba = low(attn_scale * g_mid)
    g_att = low(contract_cols(gba, w_out)).reshape(tok, KV, groups, HD)
    g_probs = jnp.einsum("tkgd,skd->kgts", g_att, v_all, preferred_element_type=jnp.float32)
    delta = jnp.einsum("tkgd,tkgd->kgt", g_att.astype(jnp.float32), attended)
    g_scores = low(probs.astype(jnp.float32) * (g_probs - delta[..., None]))
    g_q = jnp.einsum("kgts,skd->tkgd", g_scores, k_all, preferred_element_type=jnp.float32) * score_scale
    g_k = jnp.einsum("kgts,tkgd->skd", g_scores, queries, preferred_element_type=jnp.float32) * score_scale
    g_v = jnp.einsum("kgts,tkgd->skd", probs, g_att, preferred_element_type=jnp.float32)
    g_kv = low(jnp.concatenate([g_k.reshape(length, nk), g_v.reshape(length, nk)], axis=1))
    g_kv = lax.psum_scatter(g_kv, "seq", scatter_dimension=0, tiled=True).astype(jnp.float32)
    g_q_in = low(turn_back(g_q.reshape(tok, H, HD))).reshape(tok, nq)
    g_k_in = low(turn_back(g_kv[:, :nk].reshape(tok, KV, HD))).reshape(tok, nk)
    g_qkv = jnp.concatenate([g_q_in, g_k_in, low(g_kv[:, nk:])], axis=1)
    g_xn = contract_cols(g_qkv, w_qkv)
    input_grad = (g_mid + norm_back(g_xn, x, r_one))[None]

    cut = jnp.concatenate([g_qkv.reshape(tok, nd, -1), gba.reshape(tok, nd, -1)], axis=2)
    wq = g_qkv.shape[1] // nd
    cut = lax.all_to_all(cut, "dp", split_axis=1, concat_axis=0, tiled=True).reshape(nd * tok, -1)
    m_att = jnp.concatenate([contract_rows(xn_all, cut[:, :wq]), contract_rows(att_all, cut[:, wq:])], axis=1)
    m_att = lax.psum_scatter(low(m_att), "seq", scatter_dimension=0, tiled=True)

    back = jnp.concatenate([m_gu, m_att], axis=1)
    back = lax.all_to_all(back.reshape(nd, rows, 1, -1), "dp", split_axis=0, concat_axis=2, tiled=True)
    back = back.reshape(rows, nd, -1).astype(jnp.float32)

    def whole_hidden(m):
        return jnp.transpose(m.reshape(rows, nd, ns, ffr), (0, 2, 1, 3)).reshape(rows, -1)

    m_gate, m_up = whole_hidden(back[:, :, :hid]), whole_hidden(back[:, :, hid : 2 * hid])
    m_qkv = back[:, :, 2 * hid : 2 * hid + wq].reshape(rows, -1)
    g_out = back[:, :, 2 * hid + wq :].reshape(rows, -1)

    def weigh(w, m):
        return jnp.sum(w.astype(jnp.float32) * m, axis=1)

    m_q, m_k, m_v = m_qkv[:, :nq], m_qkv[:, nq : nq + nk], m_qkv[:, nq + nk :]
    g_norm_one = weigh(query_weight, m_q) + weigh(key_weight, m_k) + weigh(value_weight, m_v)
    g_norm_two = weigh(gate_weight, m_gate) + weigh(up_weight, m_up)
    return (
        block_output,
        input_grad,
        g_norm_one,
        m_q * gain_one,
        m_k * gain_one,
        m_v * gain_one,
        g_out,
        g_norm_two,
        m_gate * gain_two,
        m_up * gain_two,
        m_down.astype(jnp.float32),
    )


MESH = pl.DeviceIdType.MESH
LIMIT = 60 * 2**20
BF, F32 = jnp.bfloat16, jnp.float32


def dot_nn(a, b):
    return lax.dot_general(a, b, (((1,), (0,)), ((), ())), preferred_element_type=F32)


def dot_nt(a, b):
    return lax.dot_general(a, b, (((1,), (1,)), ((), ())), preferred_element_type=F32)


def dot_tn(a, b):
    return lax.dot_general(a, b, (((0,), (0,)), ((), ())), preferred_element_type=F32)


class Net:
    def __init__(self, sends, recvs):
        self.sends, self.recvs, self.count, self.open, self.used = sends, recvs, 0, [], 0
        self.s, self.d = lax.axis_index("seq"), lax.axis_index("dp")
        self.z, self.c = lax.div(self.s, 2), lax.rem(self.s, 2)
        y, x = lax.div(self.d, 2), lax.rem(self.d, 2)
        self.plane = (y * 2 + 1 - x, (1 - y) * 2 + x, 3 - self.d)
        self.mate = self.at(self.z, 1 - self.c)

    def room(self, count):
        base = self.used
        self.used += count
        return base

    def at(self, z, core):
        return {"seq": z * 2 + core, "dp": self.d}

    def across(self, kind):
        return {"seq": self.s, "dp": self.plane[kind]}

    def greet(self):
        barrier = pltpu.get_barrier_semaphore()
        peers = [self.mate] + [self.across(k) for k in range(3)]
        peers += [self.at(lax.rem(self.z + k, 4), self.c) for k in (1, 2, 3)]
        for peer in peers:
            pl.semaphore_signal(barrier, inc=1, device_id=peer, device_id_type=MESH)

    def greeted(self):
        pl.semaphore_wait(pltpu.get_barrier_semaphore(), 7)

    def copy(self, src, dst, send, recv, peer):
        return pltpu.make_async_remote_copy(
            src_ref=src,
            dst_ref=dst,
            send_sem=self.sends.at[send],
            recv_sem=self.recvs.at[recv],
            device_id=peer,
            device_id_type=MESH,
        )

    def push(self, owner, src, dst, recv, peer, when=None):
        copy = self.copy(src, dst, self.count, recv, peer)
        self.count += 1
        if when is None:
            copy.start()
        else:
            pl.when(when)(copy.start)
        self.open.append((copy, when, owner))

    def arrive(self, dst, recv, when=None):
        copy = self.copy(dst, dst, 0, recv, self.mate)
        if when is None:
            copy.wait_recv()
        else:
            pl.when(when)(copy.wait_recv)

    def finish(self, *owners):
        kept = []
        for copy, when, owner in self.open:
            if owners and owner not in owners:
                kept.append((copy, when, owner))
            elif when is None:
                copy.wait_send()
            else:
                pl.when(when)(copy.wait_send)
        self.open = kept

    def order(self, step):
        if step == 0:
            return self.z
        table = ((1, 0, 3, 2), (2, 2, 1, 1), (3, 3, 0, 0))[step - 1]
        z = self.z
        return jnp.where(z == 0, table[0], jnp.where(z == 1, table[1], jnp.where(z == 2, table[2], table[3])))


class Chain:
    def __init__(self, net, block, room=4):
        self.net, self.block, self.base = net, block, net.room(room)

    def start(self):
        net = self.net
        own = self.block(net.z, net.c)
        net.push(self, own, own, self.base + net.z, net.at(net.z + 1, net.c), net.z < 3)
        net.push(self, own, own, self.base + net.z, net.at(net.z - 1, net.c), net.z > 0)

    def step(self, k):
        net = self.net
        b = net.order(k)
        block = self.block(b, net.c)
        net.arrive(block, self.base + b)
        to = jnp.where(b < net.z, net.z + 1, net.z - 1)
        net.push(self, block, block, self.base + b, net.at(to, net.c), (to >= 0) & (to <= 3))


class Lines(Chain):
    def __init__(self, net, block):
        super().__init__(net, block, 8)

    def start(self):
        super().start()
        self.give(0)

    def onward(self, b):
        to = jnp.where(b < self.net.z, self.net.z + 1, self.net.z - 1)
        return to, (to >= 0) & (to <= 3)

    def step(self, k):
        net = self.net
        b = net.order(k)
        block = self.block(b, net.c)
        to, on = self.onward(b)
        net.arrive(block, self.base + b, on)
        net.push(self, block, block, self.base + b, net.at(to, net.c), on)

    def give(self, k):
        net = self.net
        b = net.order(k)
        block = self.block(b, net.c)
        if k:
            net.arrive(block, self.base + b, jnp.logical_not(self.onward(b)[1]))
        net.push(self, block, block, self.base + 4 + b, net.mate)

    def take(self):
        net = self.net
        for b in range(4):
            net.arrive(self.block(b, 1 - net.c), self.base + 4 + b)


class Rising(Lines):
    def start(self):
        net = self.net
        own = self.block(net.z, net.c)
        net.push(self, own, own, self.base + net.z, net.at(net.z + 1, net.c), net.z < 3)
        net.push(self, own, own, self.base + 4 + net.z, net.mate)

    def step(self, k):
        net = self.net
        b = jnp.maximum(net.z - k, 0)
        block = self.block(b, net.c)
        net.arrive(block, self.base + b, net.z >= k)
        net.push(self, block, block, self.base + b, net.at(net.z + 1, net.c), (net.z >= k) & (net.z < 3))
        net.push(self, block, block, self.base + 4 + b, net.mate, net.z >= k)

    def take(self):
        net = self.net
        for b in range(4):
            net.arrive(self.block(b, 1 - net.c), self.base + 4 + b, net.z >= b)


class Slices(Chain):
    def __init__(self, net, full, rows):
        self.full, self.rows, self.half = full, rows, rows // 32 * 16
        super().__init__(net, lambda z, core: self.part(net.d, z, core), 36)

    def part(self, slot, z, core, half=None):
        first = pl.multiple_of((z * 2 + core) * self.rows, 16)
        if half is None:
            return self.full.at[slot, pl.ds(first, self.rows)]
        if half == 0:
            return self.full.at[slot, pl.ds(first, self.half)]
        return self.full.at[slot, pl.ds(pl.multiple_of(first + self.half, 16), self.rows - self.half)]

    def spread(self, k):
        net = self.net
        b = net.order(k)
        block = self.part(net.d, b, net.c)
        net.push(self, block, block, self.base + 4 + b, net.across(0))
        net.push(self, block, block, self.base + 8 + b, net.across(1))
        net.push(self, block, block, self.base + 20 + b, net.mate)

    def pass_on(self, k):
        net = self.net
        b = net.order(k)
        for kind in (0, 1):
            block = self.part(net.plane[kind], b, net.c)
            net.arrive(block, self.base + 4 + 4 * kind + b)
            half = self.part(net.plane[kind], b, net.c, kind)
            net.push(self, half, half, self.base + 12 + 4 * kind + b, net.across(1 - kind))
            net.push(self, block, block, self.base + 24 + 4 * kind + b, net.mate)

    def corner(self, k):
        net = self.net
        b = net.order(k)
        for kind in (0, 1):
            half = self.part(net.plane[2], b, net.c, kind)
            net.arrive(half, self.base + 12 + 4 * kind + b)
        block = self.part(net.plane[2], b, net.c)
        net.push(self, block, block, self.base + 32 + b, net.mate)

    def take(self):
        net = self.net
        for b in range(4):
            net.arrive(self.part(net.d, b, 1 - net.c), self.base + 20 + b)
            for kind in range(3):
                net.arrive(self.part(net.plane[kind], b, 1 - net.c), self.base + 24 + 4 * kind + b)


class Plane:
    def __init__(self, net, full):
        self.net, self.full, self.base = net, full, net.room(4)
        self.half = full.shape[1] // 2

    def start(self):
        net = self.net
        own = self.full.at[net.d]
        for kind in (0, 1):
            net.push(self, own, own, self.base + kind, net.across(kind))

    def pass_on(self):
        net = self.net
        for kind in (0, 1):
            net.arrive(self.full.at[net.plane[kind]], self.base + kind)
            half = self.full.at[net.plane[kind], pl.ds(kind * self.half, self.half)]
            net.push(self, half, half, self.base + 2 + kind, net.across(1 - kind))

    def take(self):
        net = self.net
        for kind in (0, 1):
            net.arrive(self.full.at[net.plane[2], pl.ds(kind * self.half, self.half)], self.base + 2 + kind)


class Spread:
    def __init__(self, net, send, land):
        self.net, self.send, self.land, self.base = net, send, land, net.room(3)

    def start(self):
        net = self.net
        for kind in (2, 0, 1):
            net.push(self, self.send(net.plane[kind]), self.land(net.d), self.base + kind, net.across(kind))

    def take(self):
        for kind in range(3):
            self.net.arrive(self.land(self.net.plane[kind]), self.base + kind)


class ToMate:
    def __init__(self, net, send, land):
        self.net, self.send, self.land, self.base = net, send, land, net.room(1)

    def start(self):
        self.net.push(self, self.send, self.land, self.base, self.net.mate)

    def take(self):
        self.net.arrive(self.land, self.base)


class ToOwners:
    def __init__(self, net, part, land, down=False):
        self.net, self.part, self.land, self.down, self.base = net, part, land, down, net.room(3)

    def start(self):
        net = self.net
        for k in (3, 2, 1):
            to = lax.rem(net.z - k + 4, 4)
            net.push(self, self.part(to), self.land(k - 1), self.base + k - 1, net.at(to, net.c), (net.z >= k) if self.down else None)

    def take(self):
        net = self.net
        for k in (1, 2, 3):
            net.arrive(self.land(k - 1), self.base + k - 1, (net.z + k <= 3) if self.down else None)


class ChainSum:
    def __init__(self, net, part, land, add):
        self.net, self.part, self.land, self.add, self.base = net, part, land, add, net.room(6)

    def stage(self, k):
        net, z = self.net, self.net.z
        i = k - 3 + z
        valid = (i >= 0) & (i < z)
        i = jnp.clip(i, 0, 3)

        @pl.when(valid & (z < 3))
        def _():
            net.arrive(self.land(i), self.base + i)
            self.add(i, i)

        net.push(self, self.part(i), self.land(i), self.base + i, net.at(z - 1, net.c), valid)
        j = k - z
        valid = (j >= 0) & (3 - j > z)
        j = jnp.clip(j, 0, 3)

        @pl.when(valid & (z > 0))
        def _():
            net.arrive(self.land(4 - j), self.base + 3 + j)
            self.add(3 - j, 4 - j)

        net.push(self, self.part(3 - j), self.land(4 - j), self.base + 3 + j, net.at(z + 1, net.c), valid)

    def own(self):
        net, z = self.net, self.net.z

        @pl.when(z < 3)
        def _():
            net.arrive(self.land(z), self.base + z)
            self.add(z, z)

        @pl.when(z > 0)
        def _():
            net.arrive(self.land(1 + z), self.base + 6 - z)
            self.add(z, 1 + z)


def settle(land, wide, rows, cols=slice(None)):
    for j in range(4):
        wide[pl.ds(j * rows, rows), :] = land[j, :rows, cols].astype(F32)
    return wide[...].astype(BF)


def unsettle(block, wide, land, rows, cols):
    wide[:, : block.shape[1]] = block
    for j in range(4):
        land[j, :rows, cols] = wide[pl.ds(j * rows, rows), : block.shape[1]].astype(BF)


def turned(tile, cosine, sine):
    lane = lax.broadcasted_iota(jnp.int32, tile.shape, 1)
    other = jnp.where(lax.rem(lane, HD) < HD // 2, pltpu.roll(tile, 128 - HD // 2, 1), pltpu.roll(tile, HD // 2, 1))
    return tile * cosine + other * sine


def own_rows(index, rows):
    return pl.ds(pl.multiple_of(index * rows, 16), rows)


def norm_scale(v):
    return lax.rsqrt(jnp.mean(v * v, axis=1, keepdims=True) + EPSILON)


def norm_pull(e, v):
    r = norm_scale(v)
    return r * e - v * (r * r * r) * jnp.mean(e * v, axis=1, keepdims=True)


def joined(heads, j, tok):
    groups = H // KV
    pair = [heads[h // groups, tok * (h % groups) : tok * (h % groups) + tok, :] for h in (2 * j, 2 * j + 1)]
    return jnp.concatenate(pair, axis=1)


def plane_sum(net, send, land):
    total = send[net.d].astype(F32)
    for kind in range(3):
        total = total + land[net.plane[kind]].astype(F32)
    return total


LATE = ((9, 10), (11, 12), (13, 8), (14, None))


def column(row):
    n = row.shape[1]
    same = lax.broadcasted_iota(jnp.int32, (n, n), 0) == lax.broadcasted_iota(jnp.int32, (n, n), 1)
    return jnp.sum(jnp.where(same, row, 0.0), axis=1, keepdims=True)


def row_of(col):
    n = col.shape[0]
    same = lax.broadcasted_iota(jnp.int32, (n, n), 0) == lax.broadcasted_iota(jnp.int32, (n, n), 1)
    return jnp.sum(jnp.where(same, col, 0.0), axis=0, keepdims=True)


def layer_kernel(
    x_in, cot_in, query, key_w, value, output, gate_w, up_w, down, gain_one, gain_two, freq,
    doc_starts, keep_mask, keep_rate, seq_order,
    block_out, input_grad, back_gu, back_att, back_down,
    att_land, gu_land, wide, qkv_land, kv_all, o_heads, bias, wa, wb, wgu, wd,
    xn_all, gd_all, mn_all, att_all, q_heads, k_heads, v_heads, probs, middle, act, gboth, turn_x, turn_n, turn_a,
    gn_send, gn_land, br_send, br_land, gu_mate, gu_zone, dn_mate, dn_zone, gmid, do_heads, dkv, kv_mate, kv_zone, kv_tot,
    cut_land, ma_mate, ma_zone, gx_land, sends, recvs,
):
    net = Net(sends, recvs)
    tok, dim = x_in.shape[1], x_in.shape[2]
    rows = dim // 32
    blk = 4 * rows
    ffr = down.shape[0]
    hid, quad = 8 * ffr, 4 * ffr
    d, z, c, s = net.d, net.z, net.c, net.s
    span, length = 4 * tok, 8 * tok
    groups = H // KV
    padded = att_land.shape[1]
    att_send = qkv_send = cut_send = act.reshape(4, tok, hid)
    gu_send = gboth.reshape(4, tok, 2 * hid)
    gx_send, gs_heads = gd_all, gboth
    m_att = wb.reshape(4, 4, 2, blk, 384)

    first_cols, late_cols = pl.ds(0, 256), pl.ds(256, 256)
    a2a_att = Spread(net, lambda j: att_send.at[j, pl.ds(0, padded)], lambda j: att_land.at[j])
    a2a_gu = Spread(net, lambda j: gu_send.at[j, pl.ds(0, padded)], lambda j: gu_land.at[j])
    a2a_qkv = [
        Spread(net, lambda j, cols=cols: qkv_send.at[j, :, cols], lambda j, cols=cols: qkv_land.at[j, :, cols])
        for cols in (late_cols, first_cols)
    ]
    a = [Lines(net, lambda zz, core, cols=cols: wa.at[own_rows(zz * 2 + core, blk), cols]) for cols in (late_cols, first_cols)]
    b = Slices(net, wb, blk)
    gu = [Lines(net, lambda zz, core, h=h: wgu.at[zz, core, :, pl.ds(hid * h, hid)]) for h in range(2)]
    dn = Lines(net, lambda zz, core: wd.at[zz, core])
    kv = Rising(net, lambda zz, core: kv_all.at[zz, core])
    xs = Plane(net, xn_all)
    gs = Plane(net, gd_all)
    ms = Plane(net, mn_all)
    ats = Plane(net, att_all)

    kv_all[...] = jnp.zeros_like(kv_all)
    net.greet()
    first_gain = column(gain_one[...])
    zero = jnp.zeros((padded - rows, 128), BF)
    weights = (query, key_w, value)

    def qkv_tile(t):
        ref, t = (query, t) if t < 9 else (key_w, t - 9) if t < 12 else (value, t - 12)
        return (ref[:, 128 * t : 128 * t + 128].astype(F32) * first_gain).astype(BF)

    for j in range(4):
        tiles = [qkv_tile(2 * j), qkv_tile(2 * j + 1), qkv_tile(LATE[j][0])]
        tiles.append(output[:, 1024:1152] if LATE[j][1] is None else qkv_tile(LATE[j][1]))
        tiles += [output[:, 256 * j : 256 * j + 128], output[:, 256 * j + 128 : 256 * j + 256]]
        for i, tile in enumerate(tiles):
            att_send[j, :rows, 128 * i : 128 * i + 128] = tile
            att_send[j, rows:padded, 128 * i : 128 * i + 128] = zero
    net.greeted()
    a2a_att.start()
    att_land[d] = att_send[d, :padded, :]
    x = x_in[0].astype(F32)
    xn_all[d] = (x * norm_scale(x)).astype(BF)
    xs.start()
    second_gain = column(gain_two[...])
    for i, ref in enumerate((gate_w, up_w)):
        scaled = ref[...].astype(F32) * second_gain
        for j in range(4):
            for h in range(2):
                part = [scaled[:, ffr * (4 * k + j) : ffr * (4 * k + j) + ffr] for k in range(4 * h, 4 * h + 4)]
                cols = slice(hid * h + quad * i, hid * h + quad * i + quad)
                gu_send[j, :rows, cols] = jnp.concatenate(part, axis=1).astype(BF)
                gu_send[j, rows:padded, cols] = jnp.zeros((padded - rows, quad), BF)
    gu_land[d] = gu_send[d, :padded, :]
    sample = seq_order[d]
    scale_attn, scale_mlp = [
        jnp.full((1, 1), keep_mask[sample, i].astype(F32), F32) / jnp.full((1, 1), keep_rate[i], F32) for i in range(2)
    ]
    gd_all[d] = (cot_in[0].astype(F32) * scale_mlp).astype(BF)
    wd[z, c] = down[...]
    position = s * tok + lax.broadcasted_iota(jnp.int32, (tok, 1), 0)
    angle = position.astype(F32) * freq[...]
    lane = lax.broadcasted_iota(jnp.int32, angle.shape, 1)
    cosine, sine = jnp.cos(angle), jnp.where(lax.rem(lane, HD) < HD // 2, -jnp.sin(angle), jnp.sin(angle))
    a2a_att.take()
    own = own_rows(s, blk)
    packed = settle(att_land, wide, rows)
    wa[own, :] = packed[:, :512]
    wb[d, own, :] = packed[:, 384:]
    for line in a:
        line.start()
    for k in (1, 2, 3):
        for line in a:
            line.step(k)
        for line in a:
            line.give(k)
        if k == 1:
            xs.pass_on()
            a2a_gu.start()
    b.start()
    dn.start()
    xs.take()
    a[0].take()

    eighth = 1.0 / math.sqrt(HD)

    def project(cols, kinds):
        part = dot_nn(xn_all[...].reshape(span, dim), wa[:, cols])
        for j in range(4):
            for i, kind in enumerate(kinds):
                tile = part[tok * j : tok * j + tok, 128 * i : 128 * i + 128]
                spun = turned(tile, cosine, sine)
                if kind == 1:
                    tile = jnp.where(d < 2, spun, tile)
                elif kind == 2:
                    tile = jnp.where(d == 0, spun, jnp.where(d == 2, spun * eighth, tile))
                else:
                    tile = spun * eighth
                qkv_send[j, :, pl.ds(cols.start + 128 * i, 128)] = tile.astype(BF)

    net.finish(a2a_att)
    project(late_cols, (1, 2))
    a2a_qkv[0].start()
    a[1].take()
    project(first_cols, (0, 0))
    a2a_qkv[1].start()
    qkv_land[d] = qkv_send[d, :, :512]
    b.spread(0)
    b.step(1)
    b.spread(1)
    a2a_qkv[0].take()
    places = [(0, 256), (0, 384), (1, 256), (1, 384), (2, 256), (3, 256)]
    for i, (j, col) in enumerate(places):
        kv_all[z, c, :, 128 * i : 128 * i + 128] = qkv_land[j, :, col : col + 128]
    kv.start()
    b.step(2)
    b.spread(2)
    a2a_gu.take()
    for h in range(2):
        wgu[z, c, :, hid * h : hid * h + hid] = settle(gu_land, wide, rows, slice(hid * h, hid * h + hid))
    b.step(3)
    b.spread(3)
    gu[0].start()
    b.pass_on(0)
    b.pass_on(1)
    a2a_qkv[1].take()
    gs.start()
    for t in range(9):
        j, col = (t // 2, (t % 2) * 128) if t < 8 else (2, 384)
        for h in (2 * t, 2 * t + 1):
            at = col + HD * (h % 2)
            q_heads[h // groups, tok * (h % groups) : tok * (h % groups) + tok, :] = qkv_land[j, :, at : at + HD]
    first = jnp.zeros((tok, 1), jnp.int32)
    for j in range(doc_starts.shape[1]):
        start = doc_starts[sample, j]
        first = jnp.where(position >= start, jnp.maximum(first, start), first)
    key = lax.broadcasted_iota(jnp.int32, bias.shape, 1)
    bias[...] = jnp.where((key <= position) & (key >= first), 0.0, MASKED)

    kv.step(1)
    kv.step(2)
    b.pass_on(2)
    b.pass_on(3)
    b.corner(0)
    b.corner(1)
    kv.step(3)
    dn.step(1)
    kv.take()
    for j in range(8):
        for k in range(KV):
            k_heads[k, pl.ds(tok * j, tok), :] = kv_all[j // 2, j % 2, :, HD * k : HD * k + HD]
            v_heads[k, pl.ds(tok * j, tok), :] = kv_all[j // 2, j % 2, :, HD * (KV + k) : HD * (KV + k) + HD]

    def head(h, carry):
        k = lax.div(h, groups)
        mine = pl.ds(pl.multiple_of(lax.rem(h, groups) * tok, tok), tok)
        score = dot_nt(q_heads[k, mine, :], k_heads[k]) + bias[...]
        expo = jnp.exp(score - jnp.max(score, axis=1, keepdims=True))
        p = (expo * (1.0 / jnp.sum(expo, axis=1, keepdims=True))).astype(BF)
        probs[k, mine, :] = p
        o_heads[k, mine, :] = dot_nn(p, v_heads[k])
        return carry

    lax.fori_loop(0, 6, head, 0)
    dn.step(2)
    gu[0].step(1)
    gs.pass_on()
    b.corner(2)
    lax.fori_loop(6, 12, head, 0)
    dn.step(3)
    gu[0].step(2)
    lax.fori_loop(12, 18, head, 0)
    b.corner(3)
    b.take()
    for j in range(H // 2):
        att_all[d, :, 128 * j : 128 * j + 128] = joined(o_heads, j, tok).astype(BF)
    full = att_all[d]
    branch = [dot_nn(full, wb[j, :, 128:]) for j in range(4)] + [dot_nn(full, wb[3, :, :128])]
    mid = x_in[0].astype(F32) + scale_attn * jnp.concatenate(branch, axis=1)
    middle[...] = mid
    mn_all[d] = (mid * norm_scale(mid)).astype(BF)
    ms.start()
    gu[0].step(3)
    gu[1].start()
    gs.take()
    dn.give(1)
    gu[0].give(1)
    dn.give(2)
    ms.pass_on()
    gu[1].step(1)
    gu[0].give(2)
    dn.give(3)
    gu[0].give(3)
    gu[1].give(1)
    ms.take()
    dn.take()
    gu[0].take()
    ats.start()
    net.finish(a2a_gu, *a2a_qkv)

    def by_cols(send, land, width):
        return [
            Spread(
                net,
                lambda j, n=n: send.at[j, :, pl.ds(width * n, width)],
                lambda j, n=n: land.at[j, :, pl.ds(width * n, width)],
            )
            for n in range(dim // width)
        ]

    gn, br, gx = by_cols(gn_send, gn_land, 384), by_cols(br_send, br_land, dim), by_cols(gx_send, gx_land, 384)
    wgu_flat, wd_flat = wgu.reshape(dim, 2 * hid), wd.reshape(hid, dim)
    other = 1 - c
    halves = [pl.ds(hid * h, hid) for h in range(2)]
    gu_pair = [ToMate(net, wgu.at[:, other, :, cols], gu_mate.at[:, :, cols]) for cols in halves]
    dn_pair = [ToMate(net, wd.at[2 * h : 2 * h + 2, other], dn_mate.at[2 * h : 2 * h + 2]) for h in range(2)]

    def add_dn(block, slot):
        wd[block, c] = (wd[block, c].astype(F32) + dn_zone[slot].astype(F32)).astype(BF)

    def half_sum(cols):
        def add(block, slot):
            wgu[block, c, :, cols] = (wgu[block, c, :, cols].astype(F32) + gu_zone[slot, :, cols].astype(F32)).astype(BF)

        return ChainSum(net, lambda zz: wgu.at[zz, c, :, cols], lambda k: gu_zone.at[k, :, cols], add)

    gu_sum = [half_sum(cols) for cols in halves]
    dn_sum = ChainSum(net, lambda zz: wd.at[zz, c], lambda k: dn_zone.at[k], add_dn)

    def pair_gu(h):
        gu_pair[h].take()
        cols = halves[h]
        for k in range(4):
            wgu[k, c, :, cols] = (wgu[k, c, :, cols].astype(F32) + gu_mate[k, :, cols].astype(F32)).astype(BF)
        gu_sum[h].stage(0)

    turn_x[...] = mn_all[...].reshape(span, dim).T
    for h in range(2):
        base = hid * h
        gates, ups, downs = pl.ds(base, quad), pl.ds(base + quad, quad), pl.ds(quad * h, quad)
        if h == 1:
            gu[1].step(3)
            gu[1].give(3)
            gu[1].take()
        for pair in range(2):
            lines, two = pl.ds(2 * tok * pair, 2 * tok), slice(2 * pair, 2 * pair + 2)
            normed = mn_all[two].reshape(2 * tok, dim)
            gate = dot_nn(normed, wgu_flat[:, gates])
            up = dot_nn(normed, wgu_flat[:, ups])
            g_act = dot_nt(gd_all[two].reshape(2 * tok, dim), wd_flat[downs, :])
            sig = jax.nn.sigmoid(gate)
            swish = gate * sig
            act[lines, downs] = (swish * up).astype(BF)
            gboth[lines, gates] = (g_act * up * (sig * (1.0 + gate * (1.0 - sig)))).astype(BF)
            gboth[lines, ups] = (g_act * swish).astype(BF)
        for n in range(3):
            cols = pl.ds(384 * n, 384)
            part = dot_nt(gboth[:, halves[h]], wgu_flat[cols, halves[h]]).reshape(4, tok, 384)
            if h == 0:
                gn_send[:, :, cols] = part.astype(BF)
            else:
                gn_send[:, :, cols] = (gn_send[:, :, cols].astype(F32) + part).astype(BF)
                gn[n].start()
        if h == 0:
            gu[1].step(2)
            gu[1].give(2)
        net.finish(gu[h])
        for span_cols in (gates, ups):
            wgu_flat[:, span_cols] = dot_nn(turn_x[...], gboth[:, span_cols]).astype(BF)
        gu_pair[h].start()
        for n in range(3):
            cols = pl.ds(384 * n, 384)
            part = dot_nn(act[:, downs], wd_flat[downs, cols]).reshape(4, tok, 384)
            if h == 0:
                br_send[:, :, cols] = part.astype(BF)
            else:
                br_send[:, :, cols] = (br_send[:, :, cols].astype(F32) + part).astype(BF)
        turn_a[downs, :] = act[:, downs].T
        if h == 0:
            net.finish(dn)
        for n in range(3):
            cols = pl.ds(384 * n, 384)
            wd_flat[downs, cols] = dot_nn(turn_a[downs, :], gd_all[:, :, cols].reshape(span, 384)).astype(BF)
        dn_pair[h].start()
        if h == 0:
            pair_gu(0)
    pair_gu(1)
    for h in range(2):
        dn_pair[h].take()
        for k in (2 * h, 2 * h + 1):
            wd[k, c] = (wd[k, c].astype(F32) + dn_mate[k].astype(F32)).astype(BF)
    dn_sum.stage(0)
    gu_sum[0].stage(1)

    for n in range(3):
        gn[n].take()
    mid = middle[...]
    g_mid = cot_in[0].astype(F32) + norm_pull(plane_sum(net, gn_send, gn_land), mid)
    gmid[...] = g_mid
    gba = (scale_attn * g_mid).astype(BF)
    for j in range(4):
        cut_send[j, :, 512:768] = gba[:, 256 * j : 256 * j + 256]
    cut_send[3, :, 384:512] = gba[:, 1024:1152]
    cut = lambda cols: Spread(net, lambda j: cut_send.at[j, :, cols], lambda j: cut_land.at[j, :, cols])
    cut_o, cut_q, cut_l = cut(pl.ds(512, 256)), cut(pl.ds(0, 256)), cut(pl.ds(256, 256))
    cut_o.start()
    ats.pass_on()
    cut_land[d, :, 512:768] = cut_send[d, :, 512:768]
    g_att = dot_nt(gba[:, 1024:1152], wb[3, :, :128])
    for j in range(4):
        g_att = g_att + dot_nt(gba[:, 256 * j : 256 * j + 256], wb[j, :, 128:])
    for h in range(H):
        do_heads[h // groups, tok * (h % groups) : tok * (h % groups) + tok, :] = g_att[:, HD * h : HD * h + HD].astype(BF)
    net.finish(b, gs)

    kv_pair = [ToMate(net, dkv.at[n, :, other], kv_mate.at[n]) for n in range(2)]
    kv_sum = [ToOwners(net, lambda zz, n=n: dkv.at[n, zz, c], lambda k, n=n: kv_zone.at[n, k], True) for n in range(2)]

    def pull(k, carry):
        for g in range(groups):
            mine = pl.ds(tok * g, tok)
            p = probs[k, mine, :].astype(F32)
            t = p * dot_nt(do_heads[k, mine, :], v_heads[k])
            ds = (t - p * jnp.sum(t, axis=1, keepdims=True)).astype(BF)
            gs_heads[mine, :length] = ds
            o_heads[k, mine, :] = dot_nn(ds, k_heads[k]) * eighth
        half, kk = lax.div(k, 3), lax.rem(k, 3)
        for i, (left, right) in enumerate(((q_heads[k], gs_heads[: groups * tok, :length]), (do_heads[k], probs[k]))):
            turned_grad = dot_tn(left, right).astype(BF)
            at = pl.ds(pl.multiple_of(192 * i + HD * kk, HD), HD)
            for j in range(8):
                dkv[half, j // 2, j % 2, at, :] = turned_grad[:, tok * j : tok * j + tok]
        return carry

    def pair_sum(n):
        kv_pair[n].take()
        for k in range(4):
            dkv[n, k, c] = (dkv[n, k, c].astype(F32) + kv_mate[n, k].astype(F32)).astype(BF)
        kv_sum[n].start()

    def grads(p, parts):
        at = 0
        for part in parts:
            wb[p, :, at : at + part.shape[1]] = part.astype(BF)
            at += part.shape[1]
        pair = ToMate(net, m_att.at[p, :, other, :, quarter], ma_mate.at[p])
        pair.start()
        return pair

    def grads_pair(p, pair):
        pair.take()
        for k in range(4):
            m_att[p, k, c, :, quarter] = (m_att[p, k, c, :, quarter].astype(F32) + ma_mate[p, k].astype(F32)).astype(BF)

    def grads_chain(p, pair):
        def add(block, slot):
            m_att[p, block, c, :, quarter] = (
                m_att[p, block, c, :, quarter].astype(F32) + ma_zone[p, slot].astype(F32)
            ).astype(BF)

        grads_pair(p, pair)
        out = ChainSum(net, lambda zz: m_att.at[p, zz, c, :, quarter], lambda k: ma_zone.at[p, k], add)
        out.stage(0)
        return out

    def grads_straight(p, pair):
        grads_pair(p, pair)
        out = ToOwners(net, lambda zz: m_att.at[p, zz, c, :, quarter], lambda k: ma_zone.at[p, k])
        out.start()
        return out

    def grads_back(p, out):
        cols = pl.ds(256 * p, 256)
        if isinstance(out, ChainSum):
            out.own()
            total = m_att[p, z, c, :, quarter].astype(F32)
        else:
            out.take()
            total = m_att[p, z, c, :, quarter].astype(F32)
            for k in range(3):
                total = total + ma_zone[p, k].astype(F32)
        unsettle(total, wide, att_land, rows, cols)
        spread = Spread(net, lambda j: att_land.at[j, :, cols], lambda j: back_att.at[j, :, cols])
        spread.start()
        back_att[d, :, cols] = att_land[d, :, cols]
        return spread

    q_cols, l_cols, o_cols = pl.ds(0, 256), pl.ds(256, 256), pl.ds(512, 256)
    quarter = pl.ds(0, 256)
    lax.fori_loop(0, 3, pull, 0)
    kv_pair[0].start()
    gu_sum[0].stage(2)
    pair_sum(0)
    lax.fori_loop(3, 6, pull, 0)
    kv_pair[1].start()
    for t in range(9):
        j, col = (t // 2, (t % 2) * 128) if t < 8 else (2, 384)
        cut_send[j, :, col : col + 128] = turned(joined(o_heads, t, tok), cosine, -sine).astype(BF)
    cut_q.start()
    br[0].start()
    cut_land[d, :, q_cols] = cut_send[d, :, q_cols]
    pair_sum(1)
    gu_sum[1].stage(1)
    ats.take()
    cut_o.take()
    turn_x[...] = att_all[...].reshape(span, dim).T
    pair_o = grads(2, [dot_nn(turn_x[...], cut_land[:, :, o_cols].reshape(span, 256))])
    turn_n[...] = xn_all[...].reshape(span, dim).T
    cut_q.take()
    pair_q = grads(0, [dot_nn(turn_n[...], cut_land[:, :, q_cols].reshape(span, 256))])
    dn_sum.stage(1)
    gu_sum[1].stage(2)
    br[0].take()
    block_out[0] = (middle[...] + scale_mlp * plane_sum(net, br_send, br_land)).astype(BF)
    sum_o = grads_chain(2, pair_o)

    for n in range(2):
        kv_sum[n].take()
        kv_tot[n] = dkv[n, z, c].astype(F32)
        for k in (1, 2, 3):

            @pl.when(z + k <= 3)
            def _(n=n, k=k):
                kv_tot[n] += kv_zone[n, k - 1].astype(F32)

    keys = jnp.concatenate([kv_tot[0, :192, :], kv_tot[1, :192, :]], axis=0).T
    vals = jnp.concatenate([kv_tot[0, 192:, :], kv_tot[1, 192:, :]], axis=0).T
    late = [turned(keys[:, 128 * i : 128 * i + 128], cosine, -sine) for i in range(3)] + [vals[:, 128 * i : 128 * i + 128] for i in range(3)]
    for tile, (j, col) in zip(late, places):
        cut_send[j, :, col : col + 128] = tile.astype(BF)
    cut_l.start()
    cut_land[d, :, l_cols] = cut_send[d, :, l_cols]
    sum_q = grads_chain(0, pair_q)
    sum_o.stage(1)
    dn_sum.stage(2)
    cut_l.take()
    last = cut_land[:, :, 384:512].reshape(span, 128)
    cuts = cut_land[:, :, :512].reshape(span, 512)
    lane = lax.broadcasted_iota(jnp.int32, cuts.shape, 1)
    cuts = jnp.where((d == 3) & (lane >= 384), jnp.zeros_like(cuts), cuts)
    for n in range(3):
        part = dot_nt(cuts, wa[384 * n : 384 * n + 384, :]).astype(BF)
        gx_send[:, :, 384 * n : 384 * n + 384] = part.reshape(4, tok, 384)
        gx[n].start()
    second = jnp.where(d == 3, dot_nn(turn_x[...], last), dot_nn(turn_n[...], last))
    pair_l = grads(1, [dot_nn(turn_n[...], cut_land[:, :, 256:384].reshape(span, 128)), second])
    sum_l = grads_straight(1, pair_l)
    sum_q.stage(1)
    sum_o.stage(2)
    for k in range(2):
        gu_sum[k].own()
        unsettle(wgu[z, c, :, halves[k]].astype(F32), wide, gu_land, rows, halves[k])
    back_g = Spread(net, lambda j: gu_land.at[j], lambda j: back_gu.at[j])
    back_g.start()
    back_gu[d] = gu_land[d]
    sum_q.stage(2)
    dn_sum.own()
    back_down[...] = wd[z, c]
    back_o = grads_back(2, sum_o)
    back_l = grads_back(1, sum_l)
    back_q = grads_back(0, sum_q)
    for n in range(3):
        gx[n].take()
    input_grad[0] = gmid[...] + norm_pull(plane_sum(net, gx_send, gx_land), x_in[0].astype(F32))
    for spread in (back_o, back_q, back_g, back_l):
        spread.take()
    net.finish()


def layer(x, cot, weights, down, gains, freq, doc_starts, keep_mask, keep_rate, seq_order):
    tok, dim = x.shape[1:]
    ns = 8
    length = tok * ns
    ffr = down.shape[0]
    hid = ffr * ns
    blk = dim // ns
    span = 4 * tok
    vm = pl.BlockSpec(memory_space=pltpu.VMEM)
    sm = pl.BlockSpec(memory_space=pltpu.SMEM)
    padded = blk // 4 + -(blk // 4) % 16
    att_pack, gu_pack = ((4, padded, 768), BF), ((4, padded, 2 * hid), BF)
    outs = [((1, tok, dim), BF), ((1, tok, dim), F32), gu_pack, att_pack, (down.shape, BF)]
    plane = ((4, tok, dim), BF)
    wide_cut = ((4, tok, 512), BF)
    three = ((KV, 3 * tok, HD), BF)
    scratch = [
        att_pack,
        gu_pack,
        ((blk, hid), F32),
        wide_cut,
        ((4, 2, tok, 2 * KV * HD), BF),
        ((KV, 3 * tok, HD), F32),
        ((tok, length), F32),
        ((dim, 512), BF),
        ((4, dim, 384), BF),
        ((4, 2, blk, 2 * hid), BF),
        ((4, 2, ffr, dim), BF),
        plane,
        plane,
        plane,
        plane,
        three,
        ((KV, length, HD), BF),
        ((KV, length, HD), BF),
        ((KV, 3 * tok, length), BF),
        ((tok, dim), F32),
        ((span, hid), BF),
        ((span, 2 * hid), BF),
        ((dim, span), BF),
        ((dim, span), BF),
        ((hid, span), BF),
        plane,
        plane,
        plane,
        plane,
        ((4, blk, 2 * hid), BF),
        ((5, blk, 2 * hid), BF),
        ((4, ffr, dim), BF),
        ((5, ffr, dim), BF),
        ((tok, dim), F32),
        three,
        ((2, 4, 2, 384, tok), BF),
        ((2, 4, 384, tok), BF),
        ((2, 3, 384, tok), BF),
        ((2, 384, tok), F32),
        ((4, tok, 768), BF),
        ((3, 4, blk, 256), BF),
        ((3, 5, blk, 256), BF),
        plane,
    ]
    return pl.pallas_call(
        layer_kernel,
        out_shape=[jax.ShapeDtypeStruct(*o) for o in outs],
        in_specs=[vm] * 12 + [sm] * 4,
        out_specs=[vm] * len(outs),
        scratch_shapes=[pltpu.VMEM(*t) for t in scratch] + [pltpu.SemaphoreType.DMA((320,)), pltpu.SemaphoreType.DMA((256,))],
        compiler_params=pltpu.CompilerParams(collective_id=0, has_side_effects=True, vmem_limit_bytes=LIMIT),
        name="k_layer",
    )(x, cot, *weights, down, *gains, freq, doc_starts, keep_mask, keep_rate, seq_order)


def grads_kernel(
    query, key_w, value, gate_w, up_w, gain_one, gain_two, block_in, input_in, back_gu, back_att, back_down,
    block_out, input_out, norm_one, g_query, g_key, g_value, g_output, norm_two, g_gate, g_up, g_down,
):
    rows, ffr = query.shape[0], back_down.shape[0]
    hid = 8 * ffr
    block_out[...] = block_in[...]
    input_out[...] = input_in[...]
    g_down[...] = back_down[...].astype(F32)
    gain = column(gain_one[...])
    total = jnp.zeros((rows, 128), F32)
    for j in range(4):
        for i, t in enumerate((2 * j, 2 * j + 1, LATE[j][0], LATE[j][1])):
            m = back_att[j, :rows, 128 * i : 128 * i + 128].astype(F32)
            if t is None:
                g_output[:, 1024:1152] = m
                continue
            w, g, t = (query, g_query, t) if t < 9 else (key_w, g_key, t - 9) if t < 12 else (value, g_value, t - 12)
            cols = slice(128 * t, 128 * t + 128)
            total = total + w[:, cols].astype(F32) * m
            g[:, cols] = m * gain
        g_output[:, 256 * j : 256 * j + 256] = back_att[j, :rows, 512:768].astype(F32)
    norm_one[...] = row_of(jnp.sum(total, axis=1, keepdims=True))
    gain = column(gain_two[...])
    total = jnp.zeros((rows, 4 * ffr), F32)
    for i, (w, g) in enumerate(((gate_w, g_gate), (up_w, g_up))):
        for k in range(8):
            at = hid * (k // 4) + 4 * ffr * i + ffr * (k % 4)
            m = jnp.concatenate([back_gu[j, :rows, at : at + ffr].astype(F32) for j in range(4)], axis=1)
            cols = slice(4 * ffr * k, 4 * ffr * k + 4 * ffr)
            total = total + w[:, cols].astype(F32) * m
            g[:, cols] = m * gain
    norm_two[...] = row_of(jnp.sum(total, axis=1, keepdims=True))


def gradients(query, key_w, value, output, gate_w, up_w, gains, results):
    block, grad, back_gu, back_att, back_down = results
    shapes = [grad.shape, gains[0].shape] + [w.shape for w in (query, key_w, value, output)]
    shapes += [gains[1].shape, gate_w.shape, up_w.shape, back_down.shape]
    vm = pl.BlockSpec(memory_space=pltpu.VMEM)
    return pl.pallas_call(
        grads_kernel,
        out_shape=[jax.ShapeDtypeStruct(block.shape, BF)] + [jax.ShapeDtypeStruct(t, F32) for t in shapes],
        in_specs=[vm] * 12,
        out_specs=[vm] * 11,
        name="k_grads",
    )(query, key_w, value, gate_w, up_w, *gains, block, grad, back_gu, back_att, back_down)


def shards_by_kernel(
    hidden_in,
    attn_norm,
    query_weight,
    key_weight,
    value_weight,
    output_weight,
    mlp_norm,
    gate_weight,
    up_weight,
    down_weight,
    cotangent,
    doc_starts,
    keep_mask,
    keep_rate,
    seq_order,
):
    rows = query_weight.shape[0]
    freq = ROPE_BASE ** (-2.0 * jnp.arange(HD // 2, dtype=F32) / HD)
    freq = jnp.tile(freq, 128 // freq.shape[0])[None]
    gains = (attn_norm.reshape(1, rows), mlp_norm.reshape(1, rows))
    weights = (query_weight, key_weight, value_weight, output_weight, gate_weight, up_weight)
    results = layer(
        hidden_in, cotangent, weights, down_weight, gains, freq, doc_starts, keep_mask, keep_rate, seq_order
    )
    outs = list(gradients(*weights, gains, results))
    outs[2], outs[7] = outs[2].reshape(rows), outs[7].reshape(rows)
    return tuple(outs)


def solution(mesh):
    placed = (
        P("dp", "seq", None),
        P(("seq", "dp")),
        P(("seq", "dp"), None),
        P(("seq", "dp"), None),
        P(("seq", "dp"), None),
        P(("seq", "dp"), None),
        P(("seq", "dp")),
        P(("seq", "dp"), None),
        P(("seq", "dp"), None),
        P(("seq", "dp"), None),
        P("dp", "seq", None),
        P(),
        P(),
        P(),
        P(),
    )
    fits = mesh.shape["seq"] == 8 and mesh.shape["dp"] == 4
    return jax.shard_map(
        shards_by_kernel if fits else shards,
        mesh=mesh,
        in_specs=placed,
        out_specs=(
            P("dp", "seq", None),
            P("dp", "seq", None),
            P(("seq", "dp")),
            P(("seq", "dp"), None),
            P(("seq", "dp"), None),
            P(("seq", "dp"), None),
            P(("seq", "dp"), None),
            P(("seq", "dp")),
            P(("seq", "dp"), None),
            P(("seq", "dp"), None),
            P(("seq", "dp"), None),
        ),
        check_vma=False,
    )
```

```python
import math

import jax
import jax.numpy as jnp
from jax import lax
from jax.experimental import pallas as pl
from jax.experimental.pallas import tpu as pltpu
from jax.sharding import PartitionSpec as P

H = 18
KV = 6
HD = 64


EPSILON = 1e-05
ROPE_BASE = 10000.0
MASKED = -1e30


def contract_rows(left_rows, right_rows):
    return lax.dot_general(
        left_rows, right_rows, (((0,), (0,)), ((), ())), preferred_element_type=jnp.float32
    )


def contract_cols(left_mat, right_mat):
    return lax.dot_general(
        left_mat, right_mat, (((1,), (1,)), ((), ())), preferred_element_type=jnp.float32
    )


def low(v):
    return v.astype(jnp.bfloat16)


def dot(a, b):
    return jnp.dot(a, b, preferred_element_type=jnp.float32)


def swap_halves(vectors):
    half = HD // 2
    return jnp.concatenate([vectors[..., half:], vectors[..., :half]], axis=-1)


def shards(
    hidden_in,
    attn_norm,
    query_weight,
    key_weight,
    value_weight,
    output_weight,
    mlp_norm,
    gate_weight,
    up_weight,
    down_weight,
    cotangent,
    doc_starts,
    keep_mask,
    keep_rate,
    seq_order,
):
    tok = hidden_in.shape[1]
    ns, nd = lax.axis_size("seq"), lax.axis_size("dp")
    length = tok * ns
    rows = query_weight.shape[0]
    ffr = down_weight.shape[0]
    dim = hidden_in.shape[2]
    groups = H // KV
    nq, nk = H * HD, KV * HD
    score_scale = 1.0 / math.sqrt(HD)
    me_s, me_d = lax.axis_index("seq"), lax.axis_index("dp")
    sample = jnp.sum(jnp.where(jnp.arange(nd) == me_d, seq_order, 0))
    pick = jnp.arange(nd) == sample
    doc_begin = jnp.sum(jnp.where(pick[:, None], doc_starts, 0), axis=0)
    keep_flags = jnp.sum(jnp.where(pick[:, None], keep_mask, 0), axis=0).astype(jnp.float32)
    attn_scale = keep_flags[0] / keep_rate[0]
    mlp_scale = keep_flags[1] / keep_rate[1]
    positions = me_s * tok + jnp.arange(tok)
    first = jnp.max(jnp.where(doc_begin[None, :] <= positions[:, None], doc_begin[None, :], 0), axis=1)
    gain_one, gain_two = attn_norm[:, None], mlp_norm[:, None]

    qkv_rows = low(jnp.concatenate([query_weight, key_weight, value_weight], axis=1).astype(jnp.float32) * gain_one)
    w_qkv = lax.all_gather(qkv_rows, ("seq", "dp"), axis=0, tiled=True)
    w_out = lax.all_gather(output_weight, ("seq", "dp"), axis=0, tiled=True)

    def split_hidden(w):
        w = low(w.astype(jnp.float32) * gain_two).reshape(rows, ns, nd, ffr)
        w = jnp.transpose(w, (0, 2, 1, 3)).reshape(rows, nd * ns * ffr)
        return w

    gu = jnp.concatenate(
        [split_hidden(gate_weight).reshape(rows, nd, -1), split_hidden(up_weight).reshape(rows, nd, -1)], axis=2
    )
    gu = lax.all_to_all(gu, "dp", split_axis=1, concat_axis=0, tiled=True).reshape(nd * rows, -1)
    w_gu = lax.all_gather(gu, "seq", axis=0, tiled=True)
    w_down = lax.all_gather(down_weight, "seq", axis=0, tiled=True)
    hid = w_down.shape[0]

    x = hidden_in[0].astype(jnp.float32)
    r_one = lax.rsqrt(jnp.mean(x * x, axis=-1, keepdims=True) + EPSILON)
    xn = low(x * r_one)
    qkv = dot(xn, w_qkv)
    inverse_freq = ROPE_BASE ** (-2.0 * jnp.arange(HD // 2, dtype=jnp.float32) / HD)
    angles = positions.astype(jnp.float32)[:, None] * inverse_freq[None, :]
    cosine = jnp.tile(jnp.cos(angles), (1, 2))[:, None, :]
    sine = jnp.concatenate([-jnp.sin(angles), jnp.sin(angles)], axis=1)[:, None, :]

    def turn(v):
        return v * cosine + swap_halves(v) * sine

    def turn_back(v):
        return v * cosine - swap_halves(v) * sine

    queries = low(turn(qkv[:, :nq].reshape(tok, H, HD))).reshape(tok, KV, groups, HD)
    keys = low(turn(qkv[:, nq : nq + nk].reshape(tok, KV, HD)))
    kv = jnp.concatenate([keys.reshape(tok, nk), low(qkv[:, nq + nk :])], axis=1)
    kv_all = lax.all_gather(kv, "seq", axis=0, tiled=True)
    k_all, v_all = kv_all[:, :nk].reshape(length, KV, HD), kv_all[:, nk:].reshape(length, KV, HD)
    key_pos = jnp.arange(length)
    allowed = (key_pos[None, :] <= positions[:, None]) & (key_pos[None, :] >= first[:, None])
    scores = jnp.einsum("tkgd,skd->kgts", queries, k_all, preferred_element_type=jnp.float32) * score_scale
    scores = jnp.where(allowed, scores, MASKED)
    expo = jnp.exp(scores - jnp.max(scores, axis=-1, keepdims=True))
    probs = low(expo / jnp.sum(expo, axis=-1, keepdims=True))
    attended = jnp.einsum("kgts,skd->tkgd", probs, v_all, preferred_element_type=jnp.float32)
    att = low(attended.reshape(tok, nq))
    middle = x + attn_scale * dot(att, w_out)
    r_two = lax.rsqrt(jnp.mean(middle * middle, axis=-1, keepdims=True) + EPSILON)
    mn = low(middle * r_two)

    cot = cotangent[0].astype(jnp.float32)
    side = lax.all_gather(jnp.concatenate([xn, low(mlp_scale * cot), att], axis=1), "dp", axis=0, tiled=True)
    xn_all, gd_all, att_all = side[:, :dim], side[:, dim : 2 * dim], side[:, 2 * dim :]
    mn_all = lax.all_gather(mn, "dp", axis=0, tiled=True)
    gate, up = dot(mn_all, w_gu[:, :hid]), dot(mn_all, w_gu[:, hid:])
    sig = jax.nn.sigmoid(gate)
    act_gate = gate * sig
    act = low(act_gate * up)
    g_act = contract_cols(gd_all, w_down)
    gg = low(g_act * up * (sig * (1.0 + gate * (1.0 - sig))))
    gu_in = low(g_act * act_gate)
    gboth = jnp.concatenate([gg, gu_in], axis=1)
    g_mn = lax.psum_scatter(low(contract_cols(gboth, w_gu)), "dp", scatter_dimension=0, tiled=True).astype(jnp.float32)
    branch = lax.psum_scatter(low(dot(act, w_down)), "dp", scatter_dimension=0, tiled=True).astype(jnp.float32)
    block_output = low(middle + mlp_scale * branch)[None]
    m_gu = lax.psum_scatter(low(contract_rows(mn_all, gboth)), "seq", scatter_dimension=0, tiled=True)
    m_down = lax.psum_scatter(low(contract_rows(act, gd_all)), "seq", scatter_dimension=0, tiled=True)

    def norm_back(e, v, r):
        return r * e - v * (r * r * r) * jnp.mean(e * v, axis=-1, keepdims=True)

    g_mid = cot + norm_back(g_mn, middle, r_two)
    gba = low(attn_scale * g_mid)
    g_att = low(contract_cols(gba, w_out)).reshape(tok, KV, groups, HD)
    g_probs = jnp.einsum("tkgd,skd->kgts", g_att, v_all, preferred_element_type=jnp.float32)
    delta = jnp.einsum("tkgd,tkgd->kgt", g_att.astype(jnp.float32), attended)
    g_scores = low(probs.astype(jnp.float32) * (g_probs - delta[..., None]))
    g_q = jnp.einsum("kgts,skd->tkgd", g_scores, k_all, preferred_element_type=jnp.float32) * score_scale
    g_k = jnp.einsum("kgts,tkgd->skd", g_scores, queries, preferred_element_type=jnp.float32) * score_scale
    g_v = jnp.einsum("kgts,tkgd->skd", probs, g_att, preferred_element_type=jnp.float32)
    g_kv = low(jnp.concatenate([g_k.reshape(length, nk), g_v.reshape(length, nk)], axis=1))
    g_kv = lax.psum_scatter(g_kv, "seq", scatter_dimension=0, tiled=True).astype(jnp.float32)
    g_q_in = low(turn_back(g_q.reshape(tok, H, HD))).reshape(tok, nq)
    g_k_in = low(turn_back(g_kv[:, :nk].reshape(tok, KV, HD))).reshape(tok, nk)
    g_qkv = jnp.concatenate([g_q_in, g_k_in, low(g_kv[:, nk:])], axis=1)
    g_xn = contract_cols(g_qkv, w_qkv)
    input_grad = (g_mid + norm_back(g_xn, x, r_one))[None]

    cut = jnp.concatenate([g_qkv.reshape(tok, nd, -1), gba.reshape(tok, nd, -1)], axis=2)
    wq = g_qkv.shape[1] // nd
    cut = lax.all_to_all(cut, "dp", split_axis=1, concat_axis=0, tiled=True).reshape(nd * tok, -1)
    m_att = jnp.concatenate([contract_rows(xn_all, cut[:, :wq]), contract_rows(att_all, cut[:, wq:])], axis=1)
    m_att = lax.psum_scatter(low(m_att), "seq", scatter_dimension=0, tiled=True)

    back = jnp.concatenate([m_gu, m_att], axis=1)
    back = lax.all_to_all(back.reshape(nd, rows, 1, -1), "dp", split_axis=0, concat_axis=2, tiled=True)
    back = back.reshape(rows, nd, -1).astype(jnp.float32)

    def whole_hidden(m):
        return jnp.transpose(m.reshape(rows, nd, ns, ffr), (0, 2, 1, 3)).reshape(rows, -1)

    m_gate, m_up = whole_hidden(back[:, :, :hid]), whole_hidden(back[:, :, hid : 2 * hid])
    m_qkv = back[:, :, 2 * hid : 2 * hid + wq].reshape(rows, -1)
    g_out = back[:, :, 2 * hid + wq :].reshape(rows, -1)

    def weigh(w, m):
        return jnp.sum(w.astype(jnp.float32) * m, axis=1)

    m_q, m_k, m_v = m_qkv[:, :nq], m_qkv[:, nq : nq + nk], m_qkv[:, nq + nk :]
    g_norm_one = weigh(query_weight, m_q) + weigh(key_weight, m_k) + weigh(value_weight, m_v)
    g_norm_two = weigh(gate_weight, m_gate) + weigh(up_weight, m_up)
    return (
        block_output,
        input_grad,
        g_norm_one,
        m_q * gain_one,
        m_k * gain_one,
        m_v * gain_one,
        g_out,
        g_norm_two,
        m_gate * gain_two,
        m_up * gain_two,
        m_down.astype(jnp.float32),
    )


MESH = pl.DeviceIdType.MESH
LIMIT = 60 * 2**20
SENDS, RECVS = 120, 202
BF, F32 = jnp.bfloat16, jnp.float32


def dot_nn(a, b):
    return lax.dot_general(a, b, (((1,), (0,)), ((), ())), preferred_element_type=F32)


def dot_nt(a, b):
    return lax.dot_general(a, b, (((1,), (1,)), ((), ())), preferred_element_type=F32)


def dot_tn(a, b):
    return lax.dot_general(a, b, (((0,), (0,)), ((), ())), preferred_element_type=F32)


class Net:
    def __init__(self, sends, recvs):
        self.sends, self.recvs, self.open, self.used = sends, recvs, [], 0
        self.free = list(range(sends.shape[0]))
        self.s, self.d = lax.axis_index("seq"), lax.axis_index("dp")
        self.z, self.c = lax.div(self.s, 2), lax.rem(self.s, 2)
        y, x = lax.div(self.d, 2), lax.rem(self.d, 2)
        self.plane = (y * 2 + 1 - x, (1 - y) * 2 + x, 3 - self.d)
        self.mate = self.at(self.z, 1 - self.c)

    def room(self, count):
        base = self.used
        self.used += count
        return base

    def at(self, z, core):
        return {"seq": z * 2 + core, "dp": self.d}

    def across(self, kind):
        return {"seq": self.s, "dp": self.plane[kind]}

    def greet(self):
        barrier = pltpu.get_barrier_semaphore()
        peers = [self.mate] + [self.across(k) for k in range(3)]
        peers += [self.at(lax.rem(self.z + k, 4), self.c) for k in (1, 2, 3)]
        for peer in peers:
            pl.semaphore_signal(barrier, inc=1, device_id=peer, device_id_type=MESH)

    def greeted(self):
        pl.semaphore_wait(pltpu.get_barrier_semaphore(), 7)

    def copy(self, src, dst, send, recv, peer):
        return pltpu.make_async_remote_copy(
            src_ref=src,
            dst_ref=dst,
            send_sem=self.sends.at[send],
            recv_sem=self.recvs.at[recv],
            device_id=peer,
            device_id_type=MESH,
        )

    def push(self, owner, src, dst, recv, peer, when=None):
        send = self.free.pop(0)
        copy = self.copy(src, dst, send, recv, peer)
        if when is None:
            copy.start()
        else:
            pl.when(when)(copy.start)
        self.open.append((copy, when, owner, send))

    def arrive(self, dst, recv, when=None):
        copy = self.copy(dst, dst, 0, recv, self.mate)
        if when is None:
            copy.wait_recv()
        else:
            pl.when(when)(copy.wait_recv)

    def finish(self, *owners):
        kept = []
        for entry in self.open:
            copy, when, owner, send = entry
            if owners and owner not in owners:
                kept.append(entry)
                continue
            if when is None:
                copy.wait_send()
            else:
                pl.when(when)(copy.wait_send)
            self.free.append(send)
        self.open = kept

    def order(self, step):
        if step == 0:
            return self.z
        table = ((1, 0, 3, 2), (2, 2, 1, 1), (3, 3, 0, 0))[step - 1]
        z = self.z
        return jnp.where(z == 0, table[0], jnp.where(z == 1, table[1], jnp.where(z == 2, table[2], table[3])))


class Chain:
    def __init__(self, net, block, room=4):
        self.net, self.block, self.base = net, block, net.room(room)

    def start(self):
        net = self.net
        own = self.block(net.z, net.c)
        net.push(self, own, own, self.base + net.z, net.at(net.z + 1, net.c), net.z < 3)
        net.push(self, own, own, self.base + net.z, net.at(net.z - 1, net.c), net.z > 0)

    def step(self, k):
        net = self.net
        b = net.order(k)
        block = self.block(b, net.c)
        net.arrive(block, self.base + b)
        to = jnp.where(b < net.z, net.z + 1, net.z - 1)
        net.push(self, block, block, self.base + b, net.at(to, net.c), (to >= 0) & (to <= 3))


class Lines(Chain):
    def __init__(self, net, block):
        super().__init__(net, block, 8)

    def start(self, ends=None):
        net = self.net
        own = self.block(net.z, net.c)
        up, down, any_z = net.z < 3, net.z > 0, None
        if ends is not None:
            any_z = (net.z == 0) | (net.z == 3)
            any_z = any_z if ends else jnp.logical_not(any_z)
            up, down = up & any_z, down & any_z
        net.push(self, own, own, self.base + net.z, net.at(net.z + 1, net.c), up)
        net.push(self, own, own, self.base + net.z, net.at(net.z - 1, net.c), down)
        net.push(self, own, own, self.base + 4 + net.z, net.mate, any_z)

    def onward(self, b):
        to = jnp.where(b < self.net.z, self.net.z + 1, self.net.z - 1)
        return to, (to >= 0) & (to <= 3)

    def step(self, k):
        net = self.net
        b = net.order(k)
        block = self.block(b, net.c)
        to, on = self.onward(b)
        net.arrive(block, self.base + b, on)
        net.push(self, block, block, self.base + b, net.at(to, net.c), on)

    def give(self, k):
        net = self.net
        b = net.order(k)
        block = self.block(b, net.c)
        if k:
            net.arrive(block, self.base + b, jnp.logical_not(self.onward(b)[1]))
        net.push(self, block, block, self.base + 4 + b, net.mate)

    def take(self):
        net = self.net
        for b in range(4):
            net.arrive(self.block(b, 1 - net.c), self.base + 4 + b)


class Rising(Lines):
    def start(self):
        net = self.net
        own = self.block(net.z, net.c)
        net.push(self, own, own, self.base + net.z, net.at(net.z + 1, net.c), net.z < 3)
        net.push(self, own, own, self.base + 4 + net.z, net.mate)

    def step(self, k):
        net = self.net
        b = jnp.maximum(net.z - k, 0)
        block = self.block(b, net.c)
        net.arrive(block, self.base + b, net.z >= k)
        net.push(self, block, block, self.base + b, net.at(net.z + 1, net.c), (net.z >= k) & (net.z < 3))
        net.push(self, block, block, self.base + 4 + b, net.mate, net.z >= k)

    def take(self):
        net = self.net
        for b in range(4):
            net.arrive(self.block(b, 1 - net.c), self.base + 4 + b, net.z >= b)


class Slices(Chain):
    def __init__(self, net, full, rows):
        self.full, self.rows, self.half = full, rows, rows // 32 * 16
        super().__init__(net, lambda z, core: self.part(net.d, z, core), 36)

    def part(self, slot, z, core, half=None):
        first = pl.multiple_of((z * 2 + core) * self.rows, 16)
        if half is None:
            return self.full.at[slot, pl.ds(first, self.rows)]
        if half == 0:
            return self.full.at[slot, pl.ds(first, self.half)]
        return self.full.at[slot, pl.ds(pl.multiple_of(first + self.half, 16), self.rows - self.half)]

    def spread(self, k):
        net = self.net
        b = net.order(k)
        block = self.part(net.d, b, net.c)
        net.push(self, block, block, self.base + 4 + b, net.across(0))
        net.push(self, block, block, self.base + 8 + b, net.across(1))
        net.push(self, block, block, self.base + 20 + b, net.mate)

    def pass_on(self, k):
        net = self.net
        b = net.order(k)
        for kind in (0, 1):
            block = self.part(net.plane[kind], b, net.c)
            net.arrive(block, self.base + 4 + 4 * kind + b)
            half = self.part(net.plane[kind], b, net.c, kind)
            net.push(self, half, half, self.base + 12 + 4 * kind + b, net.across(1 - kind))
            net.push(self, block, block, self.base + 24 + 4 * kind + b, net.mate)

    def corner(self, k):
        net = self.net
        b = net.order(k)
        for kind in (0, 1):
            half = self.part(net.plane[2], b, net.c, kind)
            net.arrive(half, self.base + 12 + 4 * kind + b)
        block = self.part(net.plane[2], b, net.c)
        net.push(self, block, block, self.base + 32 + b, net.mate)

    def take(self):
        net = self.net
        for b in range(4):
            net.arrive(self.part(net.d, b, 1 - net.c), self.base + 20 + b)
            for kind in range(3):
                net.arrive(self.part(net.plane[kind], b, 1 - net.c), self.base + 24 + 4 * kind + b)


class Plane:
    def __init__(self, net, full):
        self.net, self.full, self.base = net, full, net.room(4)
        self.half = full.shape[1] // 2

    def start(self):
        net = self.net
        own = self.full.at[net.d]
        for kind in (0, 1):
            net.push(self, own, own, self.base + kind, net.across(kind))

    def pass_on(self):
        net = self.net
        for kind in (0, 1):
            net.arrive(self.full.at[net.plane[kind]], self.base + kind)
            half = self.full.at[net.plane[kind], pl.ds(kind * self.half, self.half)]
            net.push(self, half, half, self.base + 2 + kind, net.across(1 - kind))

    def take(self):
        net = self.net
        for kind in (0, 1):
            net.arrive(self.full.at[net.plane[2], pl.ds(kind * self.half, self.half)], self.base + 2 + kind)


class Spread:
    def __init__(self, net, send, land):
        self.net, self.send, self.land, self.base = net, send, land, net.room(3)

    def start(self):
        net = self.net
        for kind in (2, 0, 1):
            net.push(self, self.send(net.plane[kind]), self.land(net.d), self.base + kind, net.across(kind))

    def take(self):
        for kind in range(3):
            self.net.arrive(self.land(self.net.plane[kind]), self.base + kind)


class ToMate:
    def __init__(self, net, send, land):
        self.net, self.send, self.land, self.base = net, send, land, net.room(1)

    def start(self):
        self.net.push(self, self.send, self.land, self.base, self.net.mate)

    def take(self):
        self.net.arrive(self.land, self.base)


class ToOwners:
    def __init__(self, net, part, land, down=False):
        self.net, self.part, self.land, self.down, self.base = net, part, land, down, net.room(3)

    def start(self):
        net = self.net
        for k in (3, 2, 1):
            to = lax.rem(net.z - k + 4, 4)
            net.push(self, self.part(to), self.land(k - 1), self.base + k - 1, net.at(to, net.c), (net.z >= k) if self.down else None)

    def take(self):
        net = self.net
        for k in (1, 2, 3):
            net.arrive(self.land(k - 1), self.base + k - 1, (net.z + k <= 3) if self.down else None)


class DownSum:
    def __init__(self, net, part, land, add):
        self.net, self.part, self.land, self.add, self.base = net, part, land, add, net.room(3)

    def send(self, b, when):
        net = self.net
        net.push(self, self.part(b), self.land(b), self.base + b, net.at(net.z - 1, net.c), when)

    def start(self):
        for b in range(3):
            self.send(b, self.net.z == 3)

    def relay(self, b):
        net = self.net
        on = (net.z > b) & (net.z < 3)

        @pl.when(on)
        def _():
            net.arrive(self.land(b), self.base + b)
            self.add(b)

        self.send(b, on)

    def own(self):
        net = self.net
        for b in range(3):

            @pl.when(net.z == b)
            def _(b=b):
                net.arrive(self.land(b), self.base + b)
                self.add(b)


class ChainSum:
    def __init__(self, net, part, land, add):
        self.net, self.part, self.land, self.add, self.base = net, part, land, add, net.room(6)

    def stage(self, k):
        self.falling(k)
        self.rising(k)

    def falling(self, k):
        net, z = self.net, self.net.z
        i = k - 3 + z
        valid = (i >= 0) & (i < z)
        i = jnp.clip(i, 0, 3)

        @pl.when(valid & (z < 3))
        def _():
            net.arrive(self.land(i), self.base + i)
            self.add(i, i)

        net.push(self, self.part(i), self.land(i), self.base + i, net.at(z - 1, net.c), valid)

    def rising(self, k):
        net, z = self.net, self.net.z
        j = k - z
        valid = (j >= 0) & (3 - j > z)
        j = jnp.clip(j, 0, 3)

        @pl.when(valid & (z > 0))
        def _():
            net.arrive(self.land(4 - j), self.base + 3 + j)
            self.add(3 - j, 4 - j)

        net.push(self, self.part(3 - j), self.land(4 - j), self.base + 3 + j, net.at(z + 1, net.c), valid)

    def own(self):
        net, z = self.net, self.net.z

        @pl.when(z < 3)
        def _():
            net.arrive(self.land(z), self.base + z)
            self.add(z, z)

        @pl.when(z > 0)
        def _():
            net.arrive(self.land(1 + z), self.base + 6 - z)
            self.add(z, 1 + z)


def settle(land, wide, rows, cols=slice(None)):
    for j in range(4):
        wide[pl.ds(j * rows, rows), :] = land[j, :rows, cols].astype(F32)
    return wide[...].astype(BF)


def unsettle(block, wide, land, rows, cols):
    wide[:, : block.shape[1]] = block
    for j in range(4):
        land[j, :rows, cols] = wide[pl.ds(j * rows, rows), : block.shape[1]].astype(BF)


def turned(tile, cosine, sine):
    lane = lax.broadcasted_iota(jnp.int32, tile.shape, 1)
    other = jnp.where(lax.rem(lane, HD) < HD // 2, pltpu.roll(tile, 128 - HD // 2, 1), pltpu.roll(tile, HD // 2, 1))
    return tile * cosine + other * sine


def own_rows(index, rows):
    return pl.ds(pl.multiple_of(index * rows, 16), rows)


def norm_scale(v):
    return lax.rsqrt(jnp.mean(v * v, axis=1, keepdims=True) + EPSILON)


def norm_pull(e, v):
    r = norm_scale(v)
    return r * e - v * (r * r * r) * jnp.mean(e * v, axis=1, keepdims=True)


def joined(heads, j, tok):
    groups = H // KV
    pair = [heads[h // groups, tok * (h % groups) : tok * (h % groups) + tok, :] for h in (2 * j, 2 * j + 1)]
    return jnp.concatenate(pair, axis=1)


def plane_sum(net, send, land):
    total = send[net.d].astype(F32)
    for kind in range(3):
        total = total + land[net.plane[kind]].astype(F32)
    return total


LATE = ((9, 10), (11, 12), (13, 8), (14, None))


def column(row):
    n = row.shape[1]
    same = lax.broadcasted_iota(jnp.int32, (n, n), 0) == lax.broadcasted_iota(jnp.int32, (n, n), 1)
    return jnp.sum(jnp.where(same, row, 0.0), axis=1, keepdims=True)


def row_of(col):
    n = col.shape[0]
    same = lax.broadcasted_iota(jnp.int32, (n, n), 0) == lax.broadcasted_iota(jnp.int32, (n, n), 1)
    return jnp.sum(jnp.where(same, col, 0.0), axis=0, keepdims=True)


def layer_kernel(
    x_in, cot_in, query, key_w, value, output, gate_w, up_w, down, gain_one, gain_two,
    doc_starts, keep_mask, keep_rate, seq_order,
    block_out, input_grad, back_gu, back_att, back_down,
    att_land, gu_land, wide, qkv_land, kv_all, o_heads, bias, wa, wb, wgu, wd,
    xn_all, gd_all, mn_all, att_all, q_heads, k_heads, v_heads, probs, middle, act, gboth, turn_x, turn_n, turn_a,
    gn_send, gn_land, br_send, br_land, gu_mate, gu_zone, dn_mate, dn_zone, gmid, do_heads, dkv, kv_mate, kv_zone, kv_tot,
    cut_land, ma_mate, ma_zone, gx_land, sends, recvs,
):
    net = Net(sends, recvs)
    tok, dim = x_in.shape[1], x_in.shape[2]
    rows = dim // 32
    blk = 4 * rows
    ffr = down.shape[0]
    hid, quad = 8 * ffr, 4 * ffr
    d, z, c, s = net.d, net.z, net.c, net.s
    span, length = 4 * tok, 8 * tok
    groups = H // KV
    padded = att_land.shape[1]
    att_send = qkv_send = cut_send = act.reshape(4, tok, hid)
    gu_send = gboth.reshape(4, tok, 2 * hid)
    gx_send, gs_heads = gd_all, gboth
    m_att = wb.reshape(4, 4, 2, blk, 384)

    first_cols, late_cols = pl.ds(0, 256), pl.ds(256, 256)
    a2a_att = Spread(net, lambda j: att_send.at[j, pl.ds(0, padded)], lambda j: att_land.at[j])
    a2a_gu = Spread(net, lambda j: gu_send.at[j, pl.ds(0, padded)], lambda j: gu_land.at[j])
    a2a_qkv = [
        Spread(net, lambda j, cols=cols: qkv_send.at[j, :, cols], lambda j, cols=cols: qkv_land.at[j, :, cols])
        for cols in (late_cols, first_cols)
    ]
    a = [Lines(net, lambda zz, core, cols=cols: wa.at[own_rows(zz * 2 + core, blk), cols]) for cols in (late_cols, first_cols)]
    b = Slices(net, wb, blk)
    gu = [Lines(net, lambda zz, core, h=h: wgu.at[zz, core, :, pl.ds(hid * h, hid)]) for h in range(2)]
    dn = Lines(net, lambda zz, core: wd.at[zz, core])
    kv = Rising(net, lambda zz, core: kv_all.at[zz, core])
    xs = Plane(net, xn_all)
    gs = Plane(net, gd_all)
    ms = Plane(net, mn_all)
    ats = Plane(net, att_all)

    kv_all[...] = jnp.zeros_like(kv_all)
    net.greet()
    first_gain = column(gain_one[...])
    zero = jnp.zeros((padded - rows, 128), BF)
    weights = (query, key_w, value)

    def qkv_tile(t):
        ref, t = (query, t) if t < 9 else (key_w, t - 9) if t < 12 else (value, t - 12)
        return (ref[:, 128 * t : 128 * t + 128].astype(F32) * first_gain).astype(BF)

    for j in range(4):
        tiles = [qkv_tile(2 * j), qkv_tile(2 * j + 1), qkv_tile(LATE[j][0])]
        tiles.append(output[:, 1024:1152] if LATE[j][1] is None else qkv_tile(LATE[j][1]))
        tiles += [output[:, 256 * j : 256 * j + 128], output[:, 256 * j + 128 : 256 * j + 256]]
        for i, tile in enumerate(tiles):
            att_send[j, :rows, 128 * i : 128 * i + 128] = tile
            att_send[j, rows:padded, 128 * i : 128 * i + 128] = zero
    net.greeted()
    a2a_att.start()
    att_land[d] = att_send[d, :padded, :]
    x = x_in[0].astype(F32)
    xn_all[d] = (x * norm_scale(x)).astype(BF)
    xs.start()
    second_gain = column(gain_two[...])
    for i, ref in enumerate((gate_w, up_w)):
        scaled = ref[...].astype(F32) * second_gain
        for j in range(4):
            for h in range(2):
                part = [scaled[:, ffr * (4 * k + j) : ffr * (4 * k + j) + ffr] for k in range(4 * h, 4 * h + 4)]
                cols = slice(hid * h + quad * i, hid * h + quad * i + quad)
                gu_send[j, :rows, cols] = jnp.concatenate(part, axis=1).astype(BF)
                gu_send[j, rows:padded, cols] = jnp.zeros((padded - rows, quad), BF)
    gu_land[d] = gu_send[d, :padded, :]
    sample = seq_order[d]
    scale_attn, scale_mlp = [
        jnp.full((1, 1), keep_mask[2 * sample + i].astype(F32), F32) / jnp.full((1, 1), keep_rate[i], F32) for i in range(2)
    ]
    gd_all[d] = (cot_in[0].astype(F32) * scale_mlp).astype(BF)
    wd[z, c] = down[...]
    position = s * tok + lax.broadcasted_iota(jnp.int32, (tok, 1), 0)
    lane = lax.broadcasted_iota(jnp.int32, (tok, 128), 1)
    power = lax.rem(lane, HD // 2).astype(F32) * (-2.0 * math.log(ROPE_BASE) / HD)
    angle = position.astype(F32) * jnp.exp(power)
    cosine, sine = jnp.cos(angle), jnp.where(lax.rem(lane, HD) < HD // 2, -jnp.sin(angle), jnp.sin(angle))
    a2a_att.take()
    own = own_rows(s, blk)
    packed = settle(att_land, wide, rows)
    wa[own, :] = packed[:, :512]
    wb[d, own, :] = packed[:, 384:]
    for line in a:
        line.start()
    for k in (1, 2, 3):
        for line in a:
            line.step(k)
        for line in a:
            line.give(k)
        if k == 1:
            xs.pass_on()
            a2a_gu.start()
    b.start()
    dn.start()
    xs.take()
    a[0].take()

    eighth = 1.0 / math.sqrt(HD)

    def project(cols, kinds):
        part = dot_nn(xn_all[...].reshape(span, dim), wa[:, cols])
        for j in range(4):
            for i, kind in enumerate(kinds):
                tile = part[tok * j : tok * j + tok, 128 * i : 128 * i + 128]
                spun = turned(tile, cosine, sine)
                if kind == 1:
                    tile = jnp.where(d < 2, spun, tile)
                elif kind == 2:
                    tile = jnp.where(d == 0, spun, jnp.where(d == 2, spun * eighth, tile))
                else:
                    tile = spun * eighth
                qkv_send[j, :, pl.ds(cols.start + 128 * i, 128)] = tile.astype(BF)

    net.finish(a2a_att)
    project(late_cols, (1, 2))
    a2a_qkv[0].start()
    a[1].take()
    project(first_cols, (0, 0))
    a2a_qkv[1].start()
    qkv_land[d] = qkv_send[d, :, :512]
    b.spread(0)
    b.step(1)
    b.spread(1)
    a2a_qkv[0].take()
    places = [(0, 256), (0, 384), (1, 256), (1, 384), (2, 256), (3, 256)]
    for i, (j, col) in enumerate(places):
        kv_all[z, c, :, 128 * i : 128 * i + 128] = qkv_land[j, :, col : col + 128]
    kv.start()
    b.step(2)
    b.spread(2)
    a2a_gu.take()
    for h in range(2):
        wgu[z, c, :, hid * h : hid * h + hid] = settle(gu_land, wide, rows, slice(hid * h, hid * h + hid))
    b.step(3)
    b.spread(3)
    for half in gu:
        half.start(True)
    b.pass_on(0)
    b.pass_on(1)
    a2a_qkv[1].take()
    gs.start()
    for t in range(9):
        j, col = (t // 2, (t % 2) * 128) if t < 8 else (2, 384)
        for h in (2 * t, 2 * t + 1):
            at = col + HD * (h % 2)
            q_heads[h // groups, tok * (h % groups) : tok * (h % groups) + tok, :] = qkv_land[j, :, at : at + HD]
    first = jnp.zeros((tok, 1), jnp.int32)
    for j in range(doc_starts.shape[1]):
        start = doc_starts[sample, j]
        first = jnp.where(position >= start, jnp.maximum(first, start), first)
    key = lax.broadcasted_iota(jnp.int32, bias.shape, 1)
    bias[...] = jnp.where((key <= position) & (key >= first), 0.0, MASKED)

    kv.step(1)
    kv.step(2)
    gu[0].start(False)
    b.pass_on(2)
    b.pass_on(3)
    b.corner(0)
    b.corner(1)
    kv.step(3)
    dn.step(1)
    kv.take()
    for j in range(8):
        for k in range(KV):
            k_heads[k, pl.ds(tok * j, tok), :] = kv_all[j // 2, j % 2, :, HD * k : HD * k + HD]
            v_heads[k, pl.ds(tok * j, tok), :] = kv_all[j // 2, j % 2, :, HD * (KV + k) : HD * (KV + k) + HD]

    def head(h, carry):
        k = lax.div(h, groups)
        mine = pl.ds(pl.multiple_of(lax.rem(h, groups) * tok, tok), tok)
        score = dot_nt(q_heads[k, mine, :], k_heads[k]) + bias[...]
        expo = jnp.exp(score - jnp.max(score, axis=1, keepdims=True))
        p = (expo * (1.0 / jnp.sum(expo, axis=1, keepdims=True))).astype(BF)
        probs[k, mine, :] = p
        o_heads[k, mine, :] = dot_nn(p, v_heads[k])
        return carry

    net.finish(xs, *a, a2a_gu)
    lax.fori_loop(0, 6, head, 0)
    dn.step(2)
    gu[0].step(1)
    gs.pass_on()
    b.corner(2)
    lax.fori_loop(6, 12, head, 0)
    dn.step(3)
    gu[0].step(2)
    gu[1].step(1)
    lax.fori_loop(12, 18, head, 0)
    b.corner(3)
    b.take()
    for j in range(H // 2):
        att_all[d, :, 128 * j : 128 * j + 128] = joined(o_heads, j, tok).astype(BF)
    full = att_all[d]
    branch = [dot_nn(full, wb[j, :, 128:]) for j in range(4)] + [dot_nn(full, wb[3, :, :128])]
    mid = x_in[0].astype(F32) + scale_attn * jnp.concatenate(branch, axis=1)
    middle[...] = mid
    mn_all[d] = (mid * norm_scale(mid)).astype(BF)
    ms.start()
    gu[0].step(3)
    gu[1].start(False)
    gs.take()
    dn.give(1)
    gu[0].give(1)
    dn.give(2)
    ms.pass_on()
    gu[1].step(2)
    gu[0].give(2)
    dn.give(3)
    gu[0].give(3)
    ms.take()
    gu[1].step(3)
    dn.take()
    gu[0].take()
    ats.start()
    net.finish(b, kv, gs, *a2a_qkv)

    def by_cols(send, land, width):
        return [
            Spread(
                net,
                lambda j, n=n: send.at[j, :, pl.ds(width * n, width)],
                lambda j, n=n: land.at[j, :, pl.ds(width * n, width)],
            )
            for n in range(dim // width)
        ]

    gn, br, gx = by_cols(gn_send, gn_land, 384), by_cols(br_send, br_land, dim), by_cols(gx_send, gx_land, 384)
    wgu_flat, wd_flat = wgu.reshape(dim, 2 * hid), wd.reshape(hid, dim)
    other = 1 - c
    halves = [pl.ds(hid * h, hid) for h in range(2)]
    gu_pair = [ToMate(net, wgu.at[:, other, :, cols], gu_mate.at[:, :, cols]) for cols in halves]
    dn_pair = [ToMate(net, wd.at[2 * h : 2 * h + 2, other], dn_mate.at[2 * h : 2 * h + 2]) for h in range(2)]

    def add_dn(block, slot):
        wd[block, c] = (wd[block, c].astype(F32) + dn_zone[slot].astype(F32)).astype(BF)

    def half_sum(cols):
        def add(block, slot):
            wgu[block, c, :, cols] = (wgu[block, c, :, cols].astype(F32) + gu_zone[slot, :, cols].astype(F32)).astype(BF)

        return ChainSum(net, lambda zz: wgu.at[zz, c, :, cols], lambda k: gu_zone.at[k, :, cols], add)

    gu_sum = [half_sum(cols) for cols in halves]
    dn_sum = ChainSum(net, lambda zz: wd.at[zz, c], lambda k: dn_zone.at[k], add_dn)

    def pair_gu(h):
        gu_pair[h].take()
        cols = halves[h]
        for k in range(4):
            wgu[k, c, :, cols] = (wgu[k, c, :, cols].astype(F32) + gu_mate[k, :, cols].astype(F32)).astype(BF)
        gu_sum[h].stage(0)

    def branch_rows(h, downs):
        for n in range(3):
            cols = pl.ds(384 * n, 384)
            part = dot_nn(act[:, downs], wd_flat[downs, cols]).reshape(4, tok, 384)
            if h == 0:
                br_send[:, :, cols] = part.astype(BF)
            else:
                br_send[:, :, cols] = (br_send[:, :, cols].astype(F32) + part).astype(BF)
        turn_a[downs, :] = act[:, downs].T
        if h == 0:
            net.finish(dn)
        for n in range(3):
            cols = pl.ds(384 * n, 384)
            wd_flat[downs, cols] = dot_nn(turn_a[downs, :], gd_all[:, :, cols].reshape(span, 384)).astype(BF)
        dn_pair[h].start()

    def pair_dn(h):
        dn_pair[h].take()
        for k in (2 * h, 2 * h + 1):
            wd[k, c] = (wd[k, c].astype(F32) + dn_mate[k].astype(F32)).astype(BF)

    turn_x[...] = mn_all[...].reshape(span, dim).T
    for h in range(2):
        base = hid * h
        gates, ups, downs = pl.ds(base, quad), pl.ds(base + quad, quad), pl.ds(quad * h, quad)
        if h == 1:
            for k in (1, 2, 3):
                gu[1].give(k)
            gu[1].take()
            pair_gu(0)
        for pair in range(2):
            lines, two = pl.ds(2 * tok * pair, 2 * tok), slice(2 * pair, 2 * pair + 2)
            normed = mn_all[two].reshape(2 * tok, dim)
            gate = dot_nn(normed, wgu_flat[:, gates])
            up = dot_nn(normed, wgu_flat[:, ups])
            g_act = dot_nt(gd_all[two].reshape(2 * tok, dim), wd_flat[downs, :])
            sig = jax.nn.sigmoid(gate)
            swish = gate * sig
            act[lines, downs] = (swish * up).astype(BF)
            gboth[lines, gates] = (g_act * up * (sig * (1.0 + gate * (1.0 - sig)))).astype(BF)
            gboth[lines, ups] = (g_act * swish).astype(BF)
        if h == 0:
            branch_rows(h, downs)
        for n in range(3):
            cols = pl.ds(384 * n, 384)
            part = dot_nt(gboth[:, halves[h]], wgu_flat[cols, halves[h]]).reshape(4, tok, 384)
            if h == 0:
                gn_send[:, :, cols] = part.astype(BF)
            else:
                gn_send[:, :, cols] = (gn_send[:, :, cols].astype(F32) + part).astype(BF)
                gn[n].start()
        if h == 1:
            branch_rows(h, downs)
        net.finish(gu[h])
        for span_cols in (gates, ups):
            wgu_flat[:, span_cols] = dot_nn(turn_x[...], gboth[:, span_cols]).astype(BF)
        gu_pair[h].start()
        pair_dn(h)
        if h == 0:
            dn_sum.falling(0)
    dn_sum.rising(0)
    dn_sum.falling(1)
    pair_gu(1)
    gu_sum[0].stage(1)

    for n in range(3):
        gn[n].take()
    mid = middle[...]
    g_mid = cot_in[0].astype(F32) + norm_pull(plane_sum(net, gn_send, gn_land), mid)
    gmid[...] = g_mid
    gba = (scale_attn * g_mid).astype(BF)
    for j in range(4):
        cut_send[j, :, 512:768] = gba[:, 256 * j : 256 * j + 256]
    cut_send[3, :, 384:512] = gba[:, 1024:1152]
    cut = lambda cols: Spread(net, lambda j: cut_send.at[j, :, cols], lambda j: cut_land.at[j, :, cols])
    cut_o, cut_q, cut_l = cut(pl.ds(512, 256)), cut(pl.ds(0, 256)), cut(pl.ds(256, 256))
    cut_o.start()
    ats.pass_on()
    cut_land[d, :, 512:768] = cut_send[d, :, 512:768]
    g_att = dot_nt(gba[:, 1024:1152], wb[3, :, :128])
    for j in range(4):
        g_att = g_att + dot_nt(gba[:, 256 * j : 256 * j + 256], wb[j, :, 128:])
    for h in range(H):
        do_heads[h // groups, tok * (h % groups) : tok * (h % groups) + tok, :] = g_att[:, HD * h : HD * h + HD].astype(BF)

    dn_sum.falling(2)
    dn_sum.rising(1)

    kv_pair = [ToMate(net, dkv.at[n, :, other], kv_mate.at[n]) for n in range(2)]

    def kv_total(n):
        def add(block):
            dkv[n, block, c] = (dkv[n, block, c].astype(F32) + kv_zone[n, block].astype(F32)).astype(BF)

        return DownSum(net, lambda zz: dkv.at[n, zz, c], lambda k: kv_zone.at[n, k], add)

    kv_sum = [kv_total(n) for n in range(2)]

    def pull(k, carry):
        for g in range(groups):
            mine = pl.ds(tok * g, tok)
            p = probs[k, mine, :].astype(F32)
            t = p * dot_nt(do_heads[k, mine, :], v_heads[k])
            ds = (t - p * jnp.sum(t, axis=1, keepdims=True)).astype(BF)
            gs_heads[mine, :length] = ds
            o_heads[k, mine, :] = dot_nn(ds, k_heads[k]) * eighth
        half, kk = lax.div(k, 3), lax.rem(k, 3)
        for i, (left, right) in enumerate(((q_heads[k], gs_heads[: groups * tok, :length]), (do_heads[k], probs[k]))):
            turned_grad = dot_tn(left, right).astype(BF)
            at = pl.ds(pl.multiple_of(192 * i + HD * kk, HD), HD)
            for j in range(8):
                dkv[half, j // 2, j % 2, at, :] = turned_grad[:, tok * j : tok * j + tok]
        return carry

    def pair_sum(n):
        kv_pair[n].take()
        for k in range(4):
            dkv[n, k, c] = (dkv[n, k, c].astype(F32) + kv_mate[n, k].astype(F32)).astype(BF)
        kv_sum[n].start()

    def grads(p, parts):
        at = 0
        for part in parts:
            wb[p, :, at : at + part.shape[1]] = part.astype(BF)
            at += part.shape[1]
        pair = ToMate(net, m_att.at[p, :, other, :, quarter], ma_mate.at[p])
        pair.start()
        return pair

    def grads_pair(p, pair):
        pair.take()
        for k in range(4):
            m_att[p, k, c, :, quarter] = (m_att[p, k, c, :, quarter].astype(F32) + ma_mate[p, k].astype(F32)).astype(BF)

    def grads_chain(p, pair):
        def add(block, slot):
            m_att[p, block, c, :, quarter] = (
                m_att[p, block, c, :, quarter].astype(F32) + ma_zone[p, slot].astype(F32)
            ).astype(BF)

        grads_pair(p, pair)
        out = ChainSum(net, lambda zz: m_att.at[p, zz, c, :, quarter], lambda k: ma_zone.at[p, k], add)
        out.stage(0)
        return out

    def grads_straight(p, pair):
        grads_pair(p, pair)
        out = ToOwners(net, lambda zz: m_att.at[p, zz, c, :, quarter], lambda k: ma_zone.at[p, k])
        out.start()
        return out

    def grads_back(p, out):
        cols = pl.ds(256 * p, 256)
        if isinstance(out, ChainSum):
            out.own()
            total = m_att[p, z, c, :, quarter].astype(F32)
        else:
            out.take()
            total = m_att[p, z, c, :, quarter].astype(F32)
            for k in range(3):
                total = total + ma_zone[p, k].astype(F32)
        unsettle(total, wide, att_land, rows, cols)
        spread = Spread(net, lambda j: att_land.at[j, :, cols], lambda j: back_att.at[j, :, cols])
        spread.start()
        back_att[d, :, cols] = att_land[d, :, cols]
        return spread

    q_cols, l_cols, o_cols = pl.ds(0, 256), pl.ds(256, 256), pl.ds(512, 256)
    quarter = pl.ds(0, 256)
    lax.fori_loop(0, 3, pull, 0)
    kv_pair[0].start()
    lax.fori_loop(3, 4, pull, 0)
    pair_sum(0)
    lax.fori_loop(4, 6, pull, 0)
    kv_pair[1].start()
    for t in range(9):
        j, col = (t // 2, (t % 2) * 128) if t < 8 else (2, 384)
        cut_send[j, :, col : col + 128] = turned(joined(o_heads, t, tok), cosine, -sine).astype(BF)
    cut_q.start()
    br[0].start()
    cut_land[d, :, q_cols] = cut_send[d, :, q_cols]
    pair_sum(1)
    ats.take()
    cut_o.take()
    turn_x[...] = att_all[...].reshape(span, dim).T
    pair_o = grads(2, [dot_nn(turn_x[...], cut_land[:, :, o_cols].reshape(span, 256))])
    turn_n[...] = xn_all[...].reshape(span, dim).T
    for n in range(2):
        kv_sum[n].relay(0)
        kv_sum[n].relay(1)
    gu_sum[0].stage(2)
    gu_sum[1].stage(1)
    cut_q.take()
    pair_q = grads(0, [dot_nn(turn_n[...], cut_land[:, :, q_cols].reshape(span, 256))])
    sum_o = grads_chain(2, pair_o)
    gu_sum[1].stage(2)
    dn_sum.rising(2)

    for n in range(2):
        kv_sum[n].own()
        kv_tot[n] = dkv[n, z, c].astype(F32)
    keys = jnp.concatenate([kv_tot[0, :192, :], kv_tot[1, :192, :]], axis=0).T
    vals = jnp.concatenate([kv_tot[0, 192:, :], kv_tot[1, 192:, :]], axis=0).T
    late = [turned(keys[:, 128 * i : 128 * i + 128], cosine, -sine) for i in range(3)] + [vals[:, 128 * i : 128 * i + 128] for i in range(3)]
    for tile, (j, col) in zip(late, places):
        cut_send[j, :, col : col + 128] = tile.astype(BF)
    cut_l.start()
    cut_land[d, :, l_cols] = cut_send[d, :, l_cols]
    sum_q = grads_chain(0, pair_q)
    sum_o.stage(1)
    cut_l.take()
    last = cut_land[:, :, 384:512].reshape(span, 128)
    cuts = cut_land[:, :, :512].reshape(span, 512)
    lane = lax.broadcasted_iota(jnp.int32, cuts.shape, 1)
    cuts = jnp.where((d == 3) & (lane >= 384), jnp.zeros_like(cuts), cuts)
    for n in range(3):
        part = dot_nt(cuts, wa[384 * n : 384 * n + 384, :]).astype(BF)
        gx_send[:, :, 384 * n : 384 * n + 384] = part.reshape(4, tok, 384)
        gx[n].start()
    second = jnp.where(d == 3, dot_nn(turn_x[...], last), dot_nn(turn_n[...], last))
    pair_l = grads(1, [dot_nn(turn_n[...], cut_land[:, :, 256:384].reshape(span, 128)), second])
    sum_l = grads_straight(1, pair_l)
    br[0].take()
    block_out[0] = (middle[...] + scale_mlp * plane_sum(net, br_send, br_land)).astype(BF)
    sum_q.stage(1)
    sum_o.stage(2)
    for k in range(2):
        gu_sum[k].own()
        unsettle(wgu[z, c, :, halves[k]].astype(F32), wide, gu_land, rows, halves[k])
    back_g = Spread(net, lambda j: gu_land.at[j], lambda j: back_gu.at[j])
    back_g.start()
    back_gu[d] = gu_land[d]
    sum_q.stage(2)
    back_o = grads_back(2, sum_o)
    back_l = grads_back(1, sum_l)
    back_q = grads_back(0, sum_q)
    dn_sum.own()
    back_down[...] = wd[z, c]
    for n in range(3):
        gx[n].take()
    input_grad[0] = gmid[...] + norm_pull(plane_sum(net, gx_send, gx_land), x_in[0].astype(F32))
    for spread in (back_o, back_q, back_g, back_l):
        spread.take()
    net.finish()


def layer(x, cot, weights, down, gains, doc_starts, keep_mask, keep_rate, seq_order):
    tok, dim = x.shape[1:]
    ns = 8
    length = tok * ns
    ffr = down.shape[0]
    hid = ffr * ns
    blk = dim // ns
    span = 4 * tok
    vm = pl.BlockSpec(memory_space=pltpu.VMEM)
    sm = pl.BlockSpec(memory_space=pltpu.SMEM)
    padded = blk // 4 + -(blk // 4) % 16
    att_pack, gu_pack = ((4, padded, 768), BF), ((4, padded, 2 * hid), BF)
    outs = [((1, tok, dim), BF), ((1, tok, dim), F32), gu_pack, att_pack, (down.shape, BF)]
    plane = ((4, tok, dim), BF)
    wide_cut = ((4, tok, 512), BF)
    three = ((KV, 3 * tok, HD), BF)
    scratch = [
        att_pack,
        gu_pack,
        ((blk, hid), F32),
        wide_cut,
        ((4, 2, tok, 2 * KV * HD), BF),
        ((KV, 3 * tok, HD), F32),
        ((tok, length), F32),
        ((dim, 512), BF),
        ((4, dim, 384), BF),
        ((4, 2, blk, 2 * hid), BF),
        ((4, 2, ffr, dim), BF),
        plane,
        plane,
        plane,
        plane,
        three,
        ((KV, length, HD), BF),
        ((KV, length, HD), BF),
        ((KV, 3 * tok, length), BF),
        ((tok, dim), F32),
        ((span, hid), BF),
        ((span, 2 * hid), BF),
        ((dim, span), BF),
        ((dim, span), BF),
        ((hid, span), BF),
        plane,
        plane,
        plane,
        plane,
        ((4, blk, 2 * hid), BF),
        ((5, blk, 2 * hid), BF),
        ((4, ffr, dim), BF),
        ((5, ffr, dim), BF),
        ((tok, dim), F32),
        three,
        ((2, 4, 2, 384, tok), BF),
        ((2, 4, 384, tok), BF),
        ((2, 3, 384, tok), BF),
        ((2, 384, tok), F32),
        ((4, tok, 768), BF),
        ((3, 4, blk, 256), BF),
        ((3, 5, blk, 256), BF),
        plane,
    ]
    return pl.pallas_call(
        layer_kernel,
        out_shape=[jax.ShapeDtypeStruct(*o) for o in outs],
        in_specs=[vm] * 11 + [sm] * 4,
        out_specs=[vm] * len(outs),
        scratch_shapes=[pltpu.VMEM(*t) for t in scratch] + [pltpu.SemaphoreType.DMA((SENDS,)), pltpu.SemaphoreType.DMA((RECVS,))],
        compiler_params=pltpu.CompilerParams(collective_id=0, has_side_effects=True, vmem_limit_bytes=LIMIT),
        name="k_layer",
    )(x, cot, *weights, down, *gains, doc_starts, keep_mask, keep_rate, seq_order)


def grads_kernel(
    query, key_w, value, gate_w, up_w, gain_one, gain_two, block_in, input_in, back_gu, back_att, back_down,
    block_out, input_out, norm_one, g_query, g_key, g_value, g_output, norm_two, g_gate, g_up, g_down,
):
    rows, ffr = query.shape[0], back_down.shape[0]
    hid = 8 * ffr
    block_out[...] = block_in[...]
    input_out[...] = input_in[...]
    g_down[...] = back_down[...].astype(F32)
    gain = column(gain_one[...])
    total = jnp.zeros((rows, 128), F32)
    for j in range(4):
        for i, t in enumerate((2 * j, 2 * j + 1, LATE[j][0], LATE[j][1])):
            m = back_att[j, :rows, 128 * i : 128 * i + 128].astype(F32)
            if t is None:
                g_output[:, 1024:1152] = m
                continue
            w, g, t = (query, g_query, t) if t < 9 else (key_w, g_key, t - 9) if t < 12 else (value, g_value, t - 12)
            cols = slice(128 * t, 128 * t + 128)
            total = total + w[:, cols].astype(F32) * m
            g[:, cols] = m * gain
        g_output[:, 256 * j : 256 * j + 256] = back_att[j, :rows, 512:768].astype(F32)
    norm_one[...] = row_of(jnp.sum(total, axis=1, keepdims=True))
    gain = column(gain_two[...])
    total = jnp.zeros((rows, 4 * ffr), F32)
    for i, (w, g) in enumerate(((gate_w, g_gate), (up_w, g_up))):
        for k in range(8):
            at = hid * (k // 4) + 4 * ffr * i + ffr * (k % 4)
            m = jnp.concatenate([back_gu[j, :rows, at : at + ffr].astype(F32) for j in range(4)], axis=1)
            cols = slice(4 * ffr * k, 4 * ffr * k + 4 * ffr)
            total = total + w[:, cols].astype(F32) * m
            g[:, cols] = m * gain
    norm_two[...] = row_of(jnp.sum(total, axis=1, keepdims=True))


def gradients(query, key_w, value, output, gate_w, up_w, gains, results):
    block, grad, back_gu, back_att, back_down = results
    shapes = [grad.shape, gains[0].shape] + [w.shape for w in (query, key_w, value, output)]
    shapes += [gains[1].shape, gate_w.shape, up_w.shape, back_down.shape]
    vm = pl.BlockSpec(memory_space=pltpu.VMEM)
    return pl.pallas_call(
        grads_kernel,
        out_shape=[jax.ShapeDtypeStruct(block.shape, BF)] + [jax.ShapeDtypeStruct(t, F32) for t in shapes],
        in_specs=[vm] * 12,
        out_specs=[vm] * 11,
        name="k_grads",
    )(query, key_w, value, gate_w, up_w, *gains, block, grad, back_gu, back_att, back_down)


def shards_by_kernel(
    hidden_in,
    attn_norm,
    query_weight,
    key_weight,
    value_weight,
    output_weight,
    mlp_norm,
    gate_weight,
    up_weight,
    down_weight,
    cotangent,
    doc_starts,
    keep_mask,
    keep_rate,
    seq_order,
):
    rows = query_weight.shape[0]
    gains = (attn_norm.reshape(1, rows), mlp_norm.reshape(1, rows))
    weights = (query_weight, key_weight, value_weight, output_weight, gate_weight, up_weight)
    results = layer(
        hidden_in, cotangent, weights, down_weight, gains, doc_starts, keep_mask.reshape(-1), keep_rate, seq_order
    )
    outs = list(gradients(*weights, gains, results))
    outs[2], outs[7] = outs[2].reshape(rows), outs[7].reshape(rows)
    return tuple(outs)


def solution(mesh):
    placed = (
        P("dp", "seq", None),
        P(("seq", "dp")),
        P(("seq", "dp"), None),
        P(("seq", "dp"), None),
        P(("seq", "dp"), None),
        P(("seq", "dp"), None),
        P(("seq", "dp")),
        P(("seq", "dp"), None),
        P(("seq", "dp"), None),
        P(("seq", "dp"), None),
        P("dp", "seq", None),
        P(),
        P(),
        P(),
        P(),
    )
    fits = mesh.shape["seq"] == 8 and mesh.shape["dp"] == 4
    return jax.shard_map(
        shards_by_kernel if fits else shards,
        mesh=mesh,
        in_specs=placed,
        out_specs=(
            P("dp", "seq", None),
            P("dp", "seq", None),
            P(("seq", "dp")),
            P(("seq", "dp"), None),
            P(("seq", "dp"), None),
            P(("seq", "dp"), None),
            P(("seq", "dp"), None),
            P(("seq", "dp")),
            P(("seq", "dp"), None),
            P(("seq", "dp"), None),
            P(("seq", "dp"), None),
        ),
        check_vma=False,
    )
```

```python
import math

import jax
import jax.numpy as jnp
from jax import lax
from jax.experimental import pallas as pl
from jax.experimental.pallas import tpu as pltpu
from jax.sharding import PartitionSpec as P

H = 18
KV = 6
HD = 64


EPSILON = 1e-05
ROPE_BASE = 10000.0
MASKED = -1e30


def contract_rows(left_rows, right_rows):
    return lax.dot_general(
        left_rows, right_rows, (((0,), (0,)), ((), ())), preferred_element_type=jnp.float32
    )


def contract_cols(left_mat, right_mat):
    return lax.dot_general(
        left_mat, right_mat, (((1,), (1,)), ((), ())), preferred_element_type=jnp.float32
    )


def low(v):
    return v.astype(jnp.bfloat16)


def dot(a, b):
    return jnp.dot(a, b, preferred_element_type=jnp.float32)


def swap_halves(vectors):
    half = HD // 2
    return jnp.concatenate([vectors[..., half:], vectors[..., :half]], axis=-1)


def shards(
    hidden_in,
    attn_norm,
    query_weight,
    key_weight,
    value_weight,
    output_weight,
    mlp_norm,
    gate_weight,
    up_weight,
    down_weight,
    cotangent,
    doc_starts,
    keep_mask,
    keep_rate,
    seq_order,
):
    tok = hidden_in.shape[1]
    ns, nd = lax.axis_size("seq"), lax.axis_size("dp")
    length = tok * ns
    rows = query_weight.shape[0]
    ffr = down_weight.shape[0]
    dim = hidden_in.shape[2]
    groups = H // KV
    nq, nk = H * HD, KV * HD
    score_scale = 1.0 / math.sqrt(HD)
    me_s, me_d = lax.axis_index("seq"), lax.axis_index("dp")
    sample = jnp.sum(jnp.where(jnp.arange(nd) == me_d, seq_order, 0))
    pick = jnp.arange(nd) == sample
    doc_begin = jnp.sum(jnp.where(pick[:, None], doc_starts, 0), axis=0)
    keep_flags = jnp.sum(jnp.where(pick[:, None], keep_mask, 0), axis=0).astype(jnp.float32)
    attn_scale = keep_flags[0] / keep_rate[0]
    mlp_scale = keep_flags[1] / keep_rate[1]
    positions = me_s * tok + jnp.arange(tok)
    first = jnp.max(jnp.where(doc_begin[None, :] <= positions[:, None], doc_begin[None, :], 0), axis=1)
    gain_one, gain_two = attn_norm[:, None], mlp_norm[:, None]

    qkv_rows = low(jnp.concatenate([query_weight, key_weight, value_weight], axis=1).astype(jnp.float32) * gain_one)
    w_qkv = lax.all_gather(qkv_rows, ("seq", "dp"), axis=0, tiled=True)
    w_out = lax.all_gather(output_weight, ("seq", "dp"), axis=0, tiled=True)

    def split_hidden(w):
        w = low(w.astype(jnp.float32) * gain_two).reshape(rows, ns, nd, ffr)
        w = jnp.transpose(w, (0, 2, 1, 3)).reshape(rows, nd * ns * ffr)
        return w

    gu = jnp.concatenate(
        [split_hidden(gate_weight).reshape(rows, nd, -1), split_hidden(up_weight).reshape(rows, nd, -1)], axis=2
    )
    gu = lax.all_to_all(gu, "dp", split_axis=1, concat_axis=0, tiled=True).reshape(nd * rows, -1)
    w_gu = lax.all_gather(gu, "seq", axis=0, tiled=True)
    w_down = lax.all_gather(down_weight, "seq", axis=0, tiled=True)
    hid = w_down.shape[0]

    x = hidden_in[0].astype(jnp.float32)
    r_one = lax.rsqrt(jnp.mean(x * x, axis=-1, keepdims=True) + EPSILON)
    xn = low(x * r_one)
    qkv = dot(xn, w_qkv)
    inverse_freq = ROPE_BASE ** (-2.0 * jnp.arange(HD // 2, dtype=jnp.float32) / HD)
    angles = positions.astype(jnp.float32)[:, None] * inverse_freq[None, :]
    cosine = jnp.tile(jnp.cos(angles), (1, 2))[:, None, :]
    sine = jnp.concatenate([-jnp.sin(angles), jnp.sin(angles)], axis=1)[:, None, :]

    def turn(v):
        return v * cosine + swap_halves(v) * sine

    def turn_back(v):
        return v * cosine - swap_halves(v) * sine

    queries = low(turn(qkv[:, :nq].reshape(tok, H, HD))).reshape(tok, KV, groups, HD)
    keys = low(turn(qkv[:, nq : nq + nk].reshape(tok, KV, HD)))
    kv = jnp.concatenate([keys.reshape(tok, nk), low(qkv[:, nq + nk :])], axis=1)
    kv_all = lax.all_gather(kv, "seq", axis=0, tiled=True)
    k_all, v_all = kv_all[:, :nk].reshape(length, KV, HD), kv_all[:, nk:].reshape(length, KV, HD)
    key_pos = jnp.arange(length)
    allowed = (key_pos[None, :] <= positions[:, None]) & (key_pos[None, :] >= first[:, None])
    scores = jnp.einsum("tkgd,skd->kgts", queries, k_all, preferred_element_type=jnp.float32) * score_scale
    scores = jnp.where(allowed, scores, MASKED)
    expo = jnp.exp(scores - jnp.max(scores, axis=-1, keepdims=True))
    probs = low(expo / jnp.sum(expo, axis=-1, keepdims=True))
    attended = jnp.einsum("kgts,skd->tkgd", probs, v_all, preferred_element_type=jnp.float32)
    att = low(attended.reshape(tok, nq))
    middle = x + attn_scale * dot(att, w_out)
    r_two = lax.rsqrt(jnp.mean(middle * middle, axis=-1, keepdims=True) + EPSILON)
    mn = low(middle * r_two)

    cot = cotangent[0].astype(jnp.float32)
    side = lax.all_gather(jnp.concatenate([xn, low(mlp_scale * cot), att], axis=1), "dp", axis=0, tiled=True)
    xn_all, gd_all, att_all = side[:, :dim], side[:, dim : 2 * dim], side[:, 2 * dim :]
    mn_all = lax.all_gather(mn, "dp", axis=0, tiled=True)
    gate, up = dot(mn_all, w_gu[:, :hid]), dot(mn_all, w_gu[:, hid:])
    sig = jax.nn.sigmoid(gate)
    act_gate = gate * sig
    act = low(act_gate * up)
    g_act = contract_cols(gd_all, w_down)
    gg = low(g_act * up * (sig * (1.0 + gate * (1.0 - sig))))
    gu_in = low(g_act * act_gate)
    gboth = jnp.concatenate([gg, gu_in], axis=1)
    g_mn = lax.psum_scatter(low(contract_cols(gboth, w_gu)), "dp", scatter_dimension=0, tiled=True).astype(jnp.float32)
    branch = lax.psum_scatter(low(dot(act, w_down)), "dp", scatter_dimension=0, tiled=True).astype(jnp.float32)
    block_output = low(middle + mlp_scale * branch)[None]
    m_gu = lax.psum_scatter(low(contract_rows(mn_all, gboth)), "seq", scatter_dimension=0, tiled=True)
    m_down = lax.psum_scatter(low(contract_rows(act, gd_all)), "seq", scatter_dimension=0, tiled=True)

    def norm_back(e, v, r):
        return r * e - v * (r * r * r) * jnp.mean(e * v, axis=-1, keepdims=True)

    g_mid = cot + norm_back(g_mn, middle, r_two)
    gba = low(attn_scale * g_mid)
    g_att = low(contract_cols(gba, w_out)).reshape(tok, KV, groups, HD)
    g_probs = jnp.einsum("tkgd,skd->kgts", g_att, v_all, preferred_element_type=jnp.float32)
    delta = jnp.einsum("tkgd,tkgd->kgt", g_att.astype(jnp.float32), attended)
    g_scores = low(probs.astype(jnp.float32) * (g_probs - delta[..., None]))
    g_q = jnp.einsum("kgts,skd->tkgd", g_scores, k_all, preferred_element_type=jnp.float32) * score_scale
    g_k = jnp.einsum("kgts,tkgd->skd", g_scores, queries, preferred_element_type=jnp.float32) * score_scale
    g_v = jnp.einsum("kgts,tkgd->skd", probs, g_att, preferred_element_type=jnp.float32)
    g_kv = low(jnp.concatenate([g_k.reshape(length, nk), g_v.reshape(length, nk)], axis=1))
    g_kv = lax.psum_scatter(g_kv, "seq", scatter_dimension=0, tiled=True).astype(jnp.float32)
    g_q_in = low(turn_back(g_q.reshape(tok, H, HD))).reshape(tok, nq)
    g_k_in = low(turn_back(g_kv[:, :nk].reshape(tok, KV, HD))).reshape(tok, nk)
    g_qkv = jnp.concatenate([g_q_in, g_k_in, low(g_kv[:, nk:])], axis=1)
    g_xn = contract_cols(g_qkv, w_qkv)
    input_grad = (g_mid + norm_back(g_xn, x, r_one))[None]

    cut = jnp.concatenate([g_qkv.reshape(tok, nd, -1), gba.reshape(tok, nd, -1)], axis=2)
    wq = g_qkv.shape[1] // nd
    cut = lax.all_to_all(cut, "dp", split_axis=1, concat_axis=0, tiled=True).reshape(nd * tok, -1)
    m_att = jnp.concatenate([contract_rows(xn_all, cut[:, :wq]), contract_rows(att_all, cut[:, wq:])], axis=1)
    m_att = lax.psum_scatter(low(m_att), "seq", scatter_dimension=0, tiled=True)

    back = jnp.concatenate([m_gu, m_att], axis=1)
    back = lax.all_to_all(back.reshape(nd, rows, 1, -1), "dp", split_axis=0, concat_axis=2, tiled=True)
    back = back.reshape(rows, nd, -1).astype(jnp.float32)

    def whole_hidden(m):
        return jnp.transpose(m.reshape(rows, nd, ns, ffr), (0, 2, 1, 3)).reshape(rows, -1)

    m_gate, m_up = whole_hidden(back[:, :, :hid]), whole_hidden(back[:, :, hid : 2 * hid])
    m_qkv = back[:, :, 2 * hid : 2 * hid + wq].reshape(rows, -1)
    g_out = back[:, :, 2 * hid + wq :].reshape(rows, -1)

    def weigh(w, m):
        return jnp.sum(w.astype(jnp.float32) * m, axis=1)

    m_q, m_k, m_v = m_qkv[:, :nq], m_qkv[:, nq : nq + nk], m_qkv[:, nq + nk :]
    g_norm_one = weigh(query_weight, m_q) + weigh(key_weight, m_k) + weigh(value_weight, m_v)
    g_norm_two = weigh(gate_weight, m_gate) + weigh(up_weight, m_up)
    return (
        block_output,
        input_grad,
        g_norm_one,
        m_q * gain_one,
        m_k * gain_one,
        m_v * gain_one,
        g_out,
        g_norm_two,
        m_gate * gain_two,
        m_up * gain_two,
        m_down.astype(jnp.float32),
    )


MESH = pl.DeviceIdType.MESH
LIMIT = 60 * 2**20
SENDS, RECVS = 120, 202
BF, F32 = jnp.bfloat16, jnp.float32


def dot_nn(a, b):
    return lax.dot_general(a, b, (((1,), (0,)), ((), ())), preferred_element_type=F32)


def dot_nt(a, b):
    return lax.dot_general(a, b, (((1,), (1,)), ((), ())), preferred_element_type=F32)


def dot_tn(a, b):
    return lax.dot_general(a, b, (((0,), (0,)), ((), ())), preferred_element_type=F32)


class Net:
    def __init__(self, sends, recvs):
        self.sends, self.recvs, self.open, self.used = sends, recvs, [], 0
        self.free = list(range(sends.shape[0]))
        self.s, self.d = lax.axis_index("seq"), lax.axis_index("dp")
        self.z, self.c = lax.div(self.s, 2), lax.rem(self.s, 2)
        y, x = lax.div(self.d, 2), lax.rem(self.d, 2)
        self.plane = (y * 2 + 1 - x, (1 - y) * 2 + x, 3 - self.d)
        self.mate = self.at(self.z, 1 - self.c)

    def room(self, count):
        base = self.used
        self.used += count
        return base

    def at(self, z, core):
        return {"seq": z * 2 + core, "dp": self.d}

    def across(self, kind):
        return {"seq": self.s, "dp": self.plane[kind]}

    def greet(self):
        barrier = pltpu.get_barrier_semaphore()
        peers = [self.mate] + [self.across(k) for k in range(3)]
        peers += [self.at(lax.rem(self.z + k, 4), self.c) for k in (1, 2, 3)]
        for peer in peers:
            pl.semaphore_signal(barrier, inc=1, device_id=peer, device_id_type=MESH)

    def greeted(self):
        pl.semaphore_wait(pltpu.get_barrier_semaphore(), 7)

    def copy(self, src, dst, send, recv, peer):
        return pltpu.make_async_remote_copy(
            src_ref=src,
            dst_ref=dst,
            send_sem=self.sends.at[send],
            recv_sem=self.recvs.at[recv],
            device_id=peer,
            device_id_type=MESH,
        )

    def push(self, owner, src, dst, recv, peer, when=None):
        send = self.free.pop(0)
        copy = self.copy(src, dst, send, recv, peer)
        if when is None:
            copy.start()
        else:
            pl.when(when)(copy.start)
        self.open.append((copy, when, owner, send))

    def arrive(self, dst, recv, when=None):
        copy = self.copy(dst, dst, 0, recv, self.mate)
        if when is None:
            copy.wait_recv()
        else:
            pl.when(when)(copy.wait_recv)

    def finish(self, *owners):
        kept = []
        for entry in self.open:
            copy, when, owner, send = entry
            if owners and owner not in owners:
                kept.append(entry)
                continue
            if when is None:
                copy.wait_send()
            else:
                pl.when(when)(copy.wait_send)
            self.free.append(send)
        self.open = kept

    def order(self, step):
        if step == 0:
            return self.z
        table = ((1, 0, 3, 2), (2, 2, 1, 1), (3, 3, 0, 0))[step - 1]
        z = self.z
        return jnp.where(z == 0, table[0], jnp.where(z == 1, table[1], jnp.where(z == 2, table[2], table[3])))


class Chain:
    def __init__(self, net, block, room=4):
        self.net, self.block, self.base = net, block, net.room(room)

    def start(self):
        net = self.net
        own = self.block(net.z, net.c)
        net.push(self, own, own, self.base + net.z, net.at(net.z + 1, net.c), net.z < 3)
        net.push(self, own, own, self.base + net.z, net.at(net.z - 1, net.c), net.z > 0)

    def step(self, k):
        net = self.net
        b = net.order(k)
        block = self.block(b, net.c)
        net.arrive(block, self.base + b)
        to = jnp.where(b < net.z, net.z + 1, net.z - 1)
        net.push(self, block, block, self.base + b, net.at(to, net.c), (to >= 0) & (to <= 3))


class Lines(Chain):
    def __init__(self, net, block):
        super().__init__(net, block, 8)

    def start(self, ends=None):
        net = self.net
        own = self.block(net.z, net.c)
        up, down, any_z = net.z < 3, net.z > 0, None
        if ends is not None:
            any_z = (net.z == 0) | (net.z == 3)
            any_z = any_z if ends else jnp.logical_not(any_z)
            up, down = up & any_z, down & any_z
        net.push(self, own, own, self.base + net.z, net.at(net.z + 1, net.c), up)
        net.push(self, own, own, self.base + net.z, net.at(net.z - 1, net.c), down)
        net.push(self, own, own, self.base + 4 + net.z, net.mate, any_z)

    def onward(self, b):
        to = jnp.where(b < self.net.z, self.net.z + 1, self.net.z - 1)
        return to, (to >= 0) & (to <= 3)

    def step(self, k):
        net = self.net
        b = net.order(k)
        block = self.block(b, net.c)
        to, on = self.onward(b)
        net.arrive(block, self.base + b, on)
        net.push(self, block, block, self.base + b, net.at(to, net.c), on)

    def give(self, k):
        net = self.net
        b = net.order(k)
        block = self.block(b, net.c)
        if k:
            net.arrive(block, self.base + b, jnp.logical_not(self.onward(b)[1]))
        net.push(self, block, block, self.base + 4 + b, net.mate)

    def take(self):
        net = self.net
        for b in range(4):
            net.arrive(self.block(b, 1 - net.c), self.base + 4 + b)


class Rising(Lines):
    def start(self):
        net = self.net
        own = self.block(net.z, net.c)
        net.push(self, own, own, self.base + net.z, net.at(net.z + 1, net.c), net.z < 3)
        net.push(self, own, own, self.base + 4 + net.z, net.mate)

    def step(self, k):
        net = self.net
        b = jnp.maximum(net.z - k, 0)
        block = self.block(b, net.c)
        net.arrive(block, self.base + b, net.z >= k)
        net.push(self, block, block, self.base + b, net.at(net.z + 1, net.c), (net.z >= k) & (net.z < 3))
        net.push(self, block, block, self.base + 4 + b, net.mate, net.z >= k)

    def take(self):
        net = self.net
        for b in range(4):
            net.arrive(self.block(b, 1 - net.c), self.base + 4 + b, net.z >= b)


class Slices(Chain):
    def __init__(self, net, full, rows):
        self.full, self.rows, self.half = full, rows, rows // 32 * 16
        super().__init__(net, lambda z, core: self.part(net.d, z, core), 36)

    def part(self, slot, z, core, half=None):
        first = pl.multiple_of((z * 2 + core) * self.rows, 16)
        if half is None:
            return self.full.at[slot, pl.ds(first, self.rows)]
        if half == 0:
            return self.full.at[slot, pl.ds(first, self.half)]
        return self.full.at[slot, pl.ds(pl.multiple_of(first + self.half, 16), self.rows - self.half)]

    def spread(self, k):
        net = self.net
        b = net.order(k)
        block = self.part(net.d, b, net.c)
        net.push(self, block, block, self.base + 4 + b, net.across(0))
        net.push(self, block, block, self.base + 8 + b, net.across(1))
        net.push(self, block, block, self.base + 20 + b, net.mate)

    def pass_on(self, k):
        net = self.net
        b = net.order(k)
        for kind in (0, 1):
            block = self.part(net.plane[kind], b, net.c)
            net.arrive(block, self.base + 4 + 4 * kind + b)
            half = self.part(net.plane[kind], b, net.c, kind)
            net.push(self, half, half, self.base + 12 + 4 * kind + b, net.across(1 - kind))
            net.push(self, block, block, self.base + 24 + 4 * kind + b, net.mate)

    def corner(self, k):
        net = self.net
        b = net.order(k)
        for kind in (0, 1):
            half = self.part(net.plane[2], b, net.c, kind)
            net.arrive(half, self.base + 12 + 4 * kind + b)
        block = self.part(net.plane[2], b, net.c)
        net.push(self, block, block, self.base + 32 + b, net.mate)

    def take(self):
        net = self.net
        for b in range(4):
            net.arrive(self.part(net.d, b, 1 - net.c), self.base + 20 + b)
            for kind in range(3):
                net.arrive(self.part(net.plane[kind], b, 1 - net.c), self.base + 24 + 4 * kind + b)


class Plane:
    def __init__(self, net, full):
        self.net, self.full, self.base = net, full, net.room(4)
        self.half = full.shape[1] // 2

    def start(self):
        net = self.net
        own = self.full.at[net.d]
        for kind in (0, 1):
            net.push(self, own, own, self.base + kind, net.across(kind))

    def pass_on(self):
        net = self.net
        for kind in (0, 1):
            net.arrive(self.full.at[net.plane[kind]], self.base + kind)
            half = self.full.at[net.plane[kind], pl.ds(kind * self.half, self.half)]
            net.push(self, half, half, self.base + 2 + kind, net.across(1 - kind))

    def take(self):
        net = self.net
        for kind in (0, 1):
            net.arrive(self.full.at[net.plane[2], pl.ds(kind * self.half, self.half)], self.base + 2 + kind)


class Spread:
    def __init__(self, net, send, land):
        self.net, self.send, self.land, self.base = net, send, land, net.room(3)

    def start(self):
        net = self.net
        for kind in (2, 0, 1):
            net.push(self, self.send(net.plane[kind]), self.land(net.d), self.base + kind, net.across(kind))

    def take(self):
        for kind in range(3):
            self.net.arrive(self.land(self.net.plane[kind]), self.base + kind)


class ToMate:
    def __init__(self, net, send, land):
        self.net, self.send, self.land, self.base = net, send, land, net.room(1)

    def start(self):
        self.net.push(self, self.send, self.land, self.base, self.net.mate)

    def take(self):
        self.net.arrive(self.land, self.base)


class ToOwners:
    def __init__(self, net, part, land, down=False):
        self.net, self.part, self.land, self.down, self.base = net, part, land, down, net.room(3)

    def start(self):
        net = self.net
        for k in (3, 2, 1):
            to = lax.rem(net.z - k + 4, 4)
            net.push(self, self.part(to), self.land(k - 1), self.base + k - 1, net.at(to, net.c), (net.z >= k) if self.down else None)

    def take(self):
        net = self.net
        for k in (1, 2, 3):
            net.arrive(self.land(k - 1), self.base + k - 1, (net.z + k <= 3) if self.down else None)


class DownSum:
    def __init__(self, net, part, land, add):
        self.net, self.part, self.land, self.add, self.base = net, part, land, add, net.room(3)

    def send(self, b, when):
        net = self.net
        net.push(self, self.part(b), self.land(b), self.base + b, net.at(net.z - 1, net.c), when)

    def start(self):
        for b in range(3):
            self.send(b, self.net.z == 3)

    def relay(self, b):
        net = self.net
        on = (net.z > b) & (net.z < 3)

        @pl.when(on)
        def _():
            net.arrive(self.land(b), self.base + b)
            self.add(b)

        self.send(b, on)

    def own(self):
        net = self.net
        for b in range(3):

            @pl.when(net.z == b)
            def _(b=b):
                net.arrive(self.land(b), self.base + b)
                self.add(b)


class ChainSum:
    def __init__(self, net, part, land, add):
        self.net, self.part, self.land, self.add, self.base = net, part, land, add, net.room(6)

    def stage(self, k):
        self.falling(k)
        self.rising(k)

    def falling(self, k, top=None):
        net, z = self.net, self.net.z
        i = k - 3 + z
        valid = (i >= 0) & (i < z)
        if top is not None:
            valid = valid & ((z == 3) if top else (z < 3))
        i = jnp.clip(i, 0, 3)

        @pl.when(valid & (z < 3))
        def _():
            net.arrive(self.land(i), self.base + i)
            self.add(i, i)

        net.push(self, self.part(i), self.land(i), self.base + i, net.at(z - 1, net.c), valid)

    def last(self):
        self.falling(2, True)
        self.rising(2, True)

    def between(self, k):
        self.falling(k, False)
        self.rising(k, False)

    def rising(self, k, end=None):
        net, z = self.net, self.net.z
        j = k - z
        valid = (j >= 0) & (3 - j > z)
        if end is not None:
            valid = valid & ((z == 0) if end else (z > 0))
        j = jnp.clip(j, 0, 3)

        @pl.when(valid & (z > 0))
        def _():
            net.arrive(self.land(4 - j), self.base + 3 + j)
            self.add(3 - j, 4 - j)

        net.push(self, self.part(3 - j), self.land(4 - j), self.base + 3 + j, net.at(z + 1, net.c), valid)

    def own(self):
        net, z = self.net, self.net.z

        @pl.when(z < 3)
        def _():
            net.arrive(self.land(z), self.base + z)
            self.add(z, z)

        @pl.when(z > 0)
        def _():
            net.arrive(self.land(1 + z), self.base + 6 - z)
            self.add(z, 1 + z)


def settle(land, wide, rows, cols=slice(None)):
    for j in range(4):
        wide[pl.ds(j * rows, rows), :] = land[j, :rows, cols].astype(F32)
    return wide[...].astype(BF)


def unsettle(block, wide, land, rows, cols):
    wide[:, : block.shape[1]] = block
    for j in range(4):
        land[j, :rows, cols] = wide[pl.ds(j * rows, rows), : block.shape[1]].astype(BF)


def turned(tile, cosine, sine):
    lane = lax.broadcasted_iota(jnp.int32, tile.shape, 1)
    other = jnp.where(lax.rem(lane, HD) < HD // 2, pltpu.roll(tile, 128 - HD // 2, 1), pltpu.roll(tile, HD // 2, 1))
    return tile * cosine + other * sine


def own_rows(index, rows):
    return pl.ds(pl.multiple_of(index * rows, 16), rows)


def norm_scale(v):
    return lax.rsqrt(jnp.mean(v * v, axis=1, keepdims=True) + EPSILON)


def norm_pull(e, v):
    r = norm_scale(v)
    return r * e - v * (r * r * r) * jnp.mean(e * v, axis=1, keepdims=True)


def joined(heads, j, tok):
    groups = H // KV
    pair = [heads[h // groups, tok * (h % groups) : tok * (h % groups) + tok, :] for h in (2 * j, 2 * j + 1)]
    return jnp.concatenate(pair, axis=1)


def plane_sum(net, send, land):
    total = send[net.d].astype(F32)
    for kind in range(3):
        total = total + land[net.plane[kind]].astype(F32)
    return total


LATE = ((9, 10), (11, 12), (13, 8), (14, None))


def column(row):
    n = row.shape[1]
    same = lax.broadcasted_iota(jnp.int32, (n, n), 0) == lax.broadcasted_iota(jnp.int32, (n, n), 1)
    return jnp.sum(jnp.where(same, row, 0.0), axis=1, keepdims=True)


def row_of(col):
    n = col.shape[0]
    same = lax.broadcasted_iota(jnp.int32, (n, n), 0) == lax.broadcasted_iota(jnp.int32, (n, n), 1)
    return jnp.sum(jnp.where(same, col, 0.0), axis=0, keepdims=True)


def layer_kernel(
    x_in, cot_in, query, key_w, value, output, gate_w, up_w, down, gain_one, gain_two,
    doc_starts, keep_mask, keep_rate, seq_order,
    block_out, input_grad, back_gu, back_att, back_down,
    att_land, gu_land, wide, qkv_land, kv_all, o_heads, bias, wa, wb, wgu, wd,
    xn_all, gd_all, mn_all, att_all, q_heads, k_heads, v_heads, probs, middle, act, gboth, turn_x, turn_n, turn_a,
    gn_send, gn_land, br_send, br_land, gu_mate, gu_zone, dn_mate, dn_zone, gmid, do_heads, dkv, kv_mate, kv_zone, kv_tot,
    cut_land, ma_mate, ma_zone, gx_land, sends, recvs,
):
    net = Net(sends, recvs)
    tok, dim = x_in.shape[1], x_in.shape[2]
    rows = dim // 32
    blk = 4 * rows
    ffr = down.shape[0]
    hid, quad = 8 * ffr, 4 * ffr
    d, z, c, s = net.d, net.z, net.c, net.s
    span, length = 4 * tok, 8 * tok
    groups = H // KV
    padded = att_land.shape[1]
    att_send = qkv_send = cut_send = act.reshape(4, tok, hid)
    gu_send = gboth.reshape(4, tok, 2 * hid)
    gx_send, gs_heads = gd_all, gboth
    m_att = wb.reshape(4, 4, 2, blk, 384)

    first_cols, late_cols = pl.ds(0, 256), pl.ds(256, 256)
    a2a_att = Spread(net, lambda j: att_send.at[j, pl.ds(0, padded)], lambda j: att_land.at[j])
    a2a_gu = Spread(net, lambda j: gu_send.at[j, pl.ds(0, padded)], lambda j: gu_land.at[j])
    a2a_qkv = [
        Spread(net, lambda j, cols=cols: qkv_send.at[j, :, cols], lambda j, cols=cols: qkv_land.at[j, :, cols])
        for cols in (late_cols, first_cols)
    ]
    a = [Lines(net, lambda zz, core, cols=cols: wa.at[own_rows(zz * 2 + core, blk), cols]) for cols in (late_cols, first_cols)]
    b = Slices(net, wb, blk)
    gu = [Lines(net, lambda zz, core, h=h: wgu.at[zz, core, :, pl.ds(hid * h, hid)]) for h in range(2)]
    dn = Lines(net, lambda zz, core: wd.at[zz, core])
    kv = Rising(net, lambda zz, core: kv_all.at[zz, core])
    xs = Plane(net, xn_all)
    gs = Plane(net, gd_all)
    ms = Plane(net, mn_all)
    ats = Plane(net, att_all)

    kv_all[...] = jnp.zeros_like(kv_all)
    net.greet()
    first_gain = column(gain_one[...])
    zero = jnp.zeros((padded - rows, 128), BF)
    weights = (query, key_w, value)

    def qkv_tile(t):
        ref, t = (query, t) if t < 9 else (key_w, t - 9) if t < 12 else (value, t - 12)
        return (ref[:, 128 * t : 128 * t + 128].astype(F32) * first_gain).astype(BF)

    for j in range(4):
        tiles = [qkv_tile(2 * j), qkv_tile(2 * j + 1), qkv_tile(LATE[j][0])]
        tiles.append(output[:, 1024:1152] if LATE[j][1] is None else qkv_tile(LATE[j][1]))
        tiles += [output[:, 256 * j : 256 * j + 128], output[:, 256 * j + 128 : 256 * j + 256]]
        for i, tile in enumerate(tiles):
            att_send[j, :rows, 128 * i : 128 * i + 128] = tile
            att_send[j, rows:padded, 128 * i : 128 * i + 128] = zero
    net.greeted()
    a2a_att.start()
    att_land[d] = att_send[d, :padded, :]
    x = x_in[0].astype(F32)
    xn_all[d] = (x * norm_scale(x)).astype(BF)
    xs.start()
    second_gain = column(gain_two[...])
    for i, ref in enumerate((gate_w, up_w)):
        scaled = ref[...].astype(F32) * second_gain
        for j in range(4):
            for h in range(2):
                part = [scaled[:, ffr * (4 * k + j) : ffr * (4 * k + j) + ffr] for k in range(4 * h, 4 * h + 4)]
                cols = slice(hid * h + quad * i, hid * h + quad * i + quad)
                gu_send[j, :rows, cols] = jnp.concatenate(part, axis=1).astype(BF)
                gu_send[j, rows:padded, cols] = jnp.zeros((padded - rows, quad), BF)
    gu_land[d] = gu_send[d, :padded, :]
    sample = seq_order[d]
    scale_attn, scale_mlp = [
        jnp.full((1, 1), keep_mask[2 * sample + i].astype(F32), F32) / jnp.full((1, 1), keep_rate[i], F32) for i in range(2)
    ]
    gd_all[d] = (cot_in[0].astype(F32) * scale_mlp).astype(BF)
    wd[z, c] = down[...]
    position = s * tok + lax.broadcasted_iota(jnp.int32, (tok, 1), 0)
    lane = lax.broadcasted_iota(jnp.int32, (tok, 128), 1)
    power = lax.rem(lane, HD // 2).astype(F32) * (-2.0 * math.log(ROPE_BASE) / HD)
    angle = position.astype(F32) * jnp.exp(power)
    cosine, sine = jnp.cos(angle), jnp.where(lax.rem(lane, HD) < HD // 2, -jnp.sin(angle), jnp.sin(angle))
    a2a_att.take()
    own = own_rows(s, blk)
    packed = settle(att_land, wide, rows)
    wa[own, :] = packed[:, :512]
    wb[d, own, :] = packed[:, 384:]
    for line in a:
        line.start()
    for k in (1, 2, 3):
        for line in a:
            line.step(k)
        for line in a:
            line.give(k)
        if k == 1:
            xs.pass_on()
            a2a_gu.start()
    b.start()
    dn.start()
    xs.take()
    a[0].take()

    eighth = 1.0 / math.sqrt(HD)

    def project(cols, kinds):
        part = dot_nn(xn_all[...].reshape(span, dim), wa[:, cols])
        for j in range(4):
            for i, kind in enumerate(kinds):
                tile = part[tok * j : tok * j + tok, 128 * i : 128 * i + 128]
                spun = turned(tile, cosine, sine)
                if kind == 1:
                    tile = jnp.where(d < 2, spun, tile)
                elif kind == 2:
                    tile = jnp.where(d == 0, spun, jnp.where(d == 2, spun * eighth, tile))
                else:
                    tile = spun * eighth
                qkv_send[j, :, pl.ds(cols.start + 128 * i, 128)] = tile.astype(BF)

    net.finish(a2a_att)
    project(late_cols, (1, 2))
    a2a_qkv[0].start()
    a[1].take()
    project(first_cols, (0, 0))
    a2a_qkv[1].start()
    qkv_land[d] = qkv_send[d, :, :512]
    b.spread(0)
    b.step(1)
    b.spread(1)
    a2a_qkv[0].take()
    places = [(0, 256), (0, 384), (1, 256), (1, 384), (2, 256), (3, 256)]
    for i, (j, col) in enumerate(places):
        kv_all[z, c, :, 128 * i : 128 * i + 128] = qkv_land[j, :, col : col + 128]
    kv.start()
    b.step(2)
    b.spread(2)
    a2a_gu.take()
    for h in range(2):
        wgu[z, c, :, hid * h : hid * h + hid] = settle(gu_land, wide, rows, slice(hid * h, hid * h + hid))
    b.step(3)
    b.spread(3)
    for half in gu:
        half.start(True)
    kv.step(1)
    b.pass_on(0)
    b.pass_on(1)
    a2a_qkv[1].take()
    gs.start()
    for t in range(9):
        j, col = (t // 2, (t % 2) * 128) if t < 8 else (2, 384)
        for h in (2 * t, 2 * t + 1):
            at = col + HD * (h % 2)
            q_heads[h // groups, tok * (h % groups) : tok * (h % groups) + tok, :] = qkv_land[j, :, at : at + HD]
    first = jnp.zeros((tok, 1), jnp.int32)
    for j in range(doc_starts.shape[1]):
        start = doc_starts[sample, j]
        first = jnp.where(position >= start, jnp.maximum(first, start), first)
    key = lax.broadcasted_iota(jnp.int32, bias.shape, 1)
    bias[...] = jnp.where((key <= position) & (key >= first), 0.0, MASKED)

    kv.step(2)
    gu[0].start(False)
    b.pass_on(2)
    b.pass_on(3)
    b.corner(0)
    b.corner(1)
    kv.step(3)
    dn.step(1)
    kv.take()
    for j in range(8):
        for k in range(KV):
            k_heads[k, pl.ds(tok * j, tok), :] = kv_all[j // 2, j % 2, :, HD * k : HD * k + HD]
            v_heads[k, pl.ds(tok * j, tok), :] = kv_all[j // 2, j % 2, :, HD * (KV + k) : HD * (KV + k) + HD]

    def attend(k, carry):
        for g in range(groups):
            mine = pl.ds(tok * g, tok)
            score = dot_nt(q_heads[k, mine, :], k_heads[k]) + bias[...]
            expo = jnp.exp(score - jnp.max(score, axis=1, keepdims=True))
            p = (expo * (1.0 / jnp.sum(expo, axis=1, keepdims=True))).astype(BF)
            probs[k, mine, :] = p
            o_heads[k, mine, :] = dot_nn(p, v_heads[k])
        return carry

    net.finish(xs, *a, a2a_gu)
    lax.fori_loop(0, 2, attend, 0)
    dn.step(2)
    gu[0].step(1)
    gs.pass_on()
    b.corner(2)
    lax.fori_loop(2, 4, attend, 0)
    dn.step(3)
    gu[0].step(2)
    gu[1].step(1)
    lax.fori_loop(4, 6, attend, 0)
    b.corner(3)
    b.take()
    for j in range(H // 2):
        att_all[d, :, 128 * j : 128 * j + 128] = joined(o_heads, j, tok).astype(BF)
    full = att_all[d]
    branch = [dot_nn(full, wb[j, :, 128:]) for j in range(4)] + [dot_nn(full, wb[3, :, :128])]
    mid = x_in[0].astype(F32) + scale_attn * jnp.concatenate(branch, axis=1)
    middle[...] = mid
    mn_all[d] = (mid * norm_scale(mid)).astype(BF)
    ms.start()
    gu[0].step(3)
    gu[1].start(False)
    gs.take()
    dn.give(1)
    gu[0].give(1)
    dn.give(2)
    ms.pass_on()
    gu[1].step(2)
    gu[0].give(2)
    dn.give(3)
    gu[0].give(3)
    ms.take()
    gu[1].step(3)
    dn.take()
    gu[0].take()
    ats.start()
    net.finish(b, kv, gs, *a2a_qkv)

    def by_cols(send, land, width):
        return [
            Spread(
                net,
                lambda j, n=n: send.at[j, :, pl.ds(width * n, width)],
                lambda j, n=n: land.at[j, :, pl.ds(width * n, width)],
            )
            for n in range(dim // width)
        ]

    gn, br, gx = by_cols(gn_send, gn_land, 384), by_cols(br_send, br_land, dim), by_cols(gx_send, gx_land, 384)
    wgu_flat, wd_flat = wgu.reshape(dim, 2 * hid), wd.reshape(hid, dim)
    other = 1 - c
    halves = [pl.ds(hid * h, hid) for h in range(2)]
    gu_pair = [ToMate(net, wgu.at[:, other, :, cols], gu_mate.at[:, :, cols]) for cols in halves]
    dn_pair = [ToMate(net, wd.at[2 * h : 2 * h + 2, other], dn_mate.at[2 * h : 2 * h + 2]) for h in range(2)]

    def add_dn(block, slot):
        wd[block, c] = (wd[block, c].astype(F32) + dn_zone[slot].astype(F32)).astype(BF)

    def half_sum(cols):
        def add(block, slot):
            wgu[block, c, :, cols] = (wgu[block, c, :, cols].astype(F32) + gu_zone[slot, :, cols].astype(F32)).astype(BF)

        return ChainSum(net, lambda zz: wgu.at[zz, c, :, cols], lambda k: gu_zone.at[k, :, cols], add)

    gu_sum = [half_sum(cols) for cols in halves]
    dn_sum = ChainSum(net, lambda zz: wd.at[zz, c], lambda k: dn_zone.at[k], add_dn)

    def pair_gu(h):
        gu_pair[h].take()
        cols = halves[h]
        for k in range(4):
            wgu[k, c, :, cols] = (wgu[k, c, :, cols].astype(F32) + gu_mate[k, :, cols].astype(F32)).astype(BF)
        gu_sum[h].stage(0)

    def branch_rows(h, downs):
        for n in range(3):
            cols = pl.ds(384 * n, 384)
            part = dot_nn(act[:, downs], wd_flat[downs, cols]).reshape(4, tok, 384)
            if h == 0:
                br_send[:, :, cols] = part.astype(BF)
            else:
                br_send[:, :, cols] = (br_send[:, :, cols].astype(F32) + part).astype(BF)
        turn_a[downs, :] = act[:, downs].T
        if h == 0:
            net.finish(dn)
        for n in range(3):
            cols = pl.ds(384 * n, 384)
            wd_flat[downs, cols] = dot_nn(turn_a[downs, :], gd_all[:, :, cols].reshape(span, 384)).astype(BF)
        dn_pair[h].start()

    def pair_dn(h):
        dn_pair[h].take()
        for k in (2 * h, 2 * h + 1):
            wd[k, c] = (wd[k, c].astype(F32) + dn_mate[k].astype(F32)).astype(BF)

    turn_x[...] = mn_all[...].reshape(span, dim).T
    for h in range(2):
        base = hid * h
        gates, ups, downs = pl.ds(base, quad), pl.ds(base + quad, quad), pl.ds(quad * h, quad)
        if h == 1:
            for k in (1, 2, 3):
                gu[1].give(k)
            gu[1].take()
        for pair in range(2):
            lines, two = pl.ds(2 * tok * pair, 2 * tok), slice(2 * pair, 2 * pair + 2)
            normed = mn_all[two].reshape(2 * tok, dim)
            gate = dot_nn(normed, wgu_flat[:, gates])
            up = dot_nn(normed, wgu_flat[:, ups])
            g_act = dot_nt(gd_all[two].reshape(2 * tok, dim), wd_flat[downs, :])
            sig = jax.nn.sigmoid(gate)
            swish = gate * sig
            act[lines, downs] = (swish * up).astype(BF)
            gboth[lines, gates] = (g_act * up * (sig * (1.0 + gate * (1.0 - sig)))).astype(BF)
            gboth[lines, ups] = (g_act * swish).astype(BF)
        if h == 0:
            branch_rows(h, downs)
        for n in range(3):
            cols = pl.ds(384 * n, 384)
            part = dot_nt(gboth[:, halves[h]], wgu_flat[cols, halves[h]]).reshape(4, tok, 384)
            if h == 0:
                gn_send[:, :, cols] = part.astype(BF)
            else:
                gn_send[:, :, cols] = (gn_send[:, :, cols].astype(F32) + part).astype(BF)
                gn[n].start()
        if h == 0:
            pair_dn(h)
            dn_sum.falling(0)
            dn_sum.falling(1, True)

    def grads_gu(h):
        net.finish(gu[h])
        for base in (hid * h, hid * h + quad):
            cols = pl.ds(base, quad)
            wgu_flat[:, cols] = dot_nn(turn_x[...], gboth[:, cols]).astype(BF)
        gu_pair[h].start()

    grads_gu(0)
    branch_rows(1, pl.ds(quad, quad))
    pair_gu(0)
    grads_gu(1)
    pair_dn(1)
    dn_sum.rising(0)
    dn_sum.falling(1, False)
    pair_gu(1)
    gu_sum[0].stage(1)

    for n in range(3):
        gn[n].take()
    mid = middle[...]
    g_mid = cot_in[0].astype(F32) + norm_pull(plane_sum(net, gn_send, gn_land), mid)
    gmid[...] = g_mid
    gba = (scale_attn * g_mid).astype(BF)
    for j in range(4):
        cut_send[j, :, 512:768] = gba[:, 256 * j : 256 * j + 256]
    cut_send[3, :, 384:512] = gba[:, 1024:1152]
    cut = lambda cols: Spread(net, lambda j: cut_send.at[j, :, cols], lambda j: cut_land.at[j, :, cols])
    cut_o, cut_q, cut_l = cut(pl.ds(512, 256)), cut(pl.ds(0, 256)), cut(pl.ds(256, 256))
    cut_o.start()
    ats.pass_on()
    cut_land[d, :, 512:768] = cut_send[d, :, 512:768]
    g_att = dot_nt(gba[:, 1024:1152], wb[3, :, :128])
    for j in range(4):
        g_att = g_att + dot_nt(gba[:, 256 * j : 256 * j + 256], wb[j, :, 128:])
    for h in range(H):
        do_heads[h // groups, tok * (h % groups) : tok * (h % groups) + tok, :] = g_att[:, HD * h : HD * h + HD].astype(BF)

    dn_sum.falling(2, False)
    dn_sum.rising(1)

    kv_pair = [ToMate(net, dkv.at[n, :, other], kv_mate.at[n]) for n in range(2)]

    def kv_total(n):
        def add(block):
            dkv[n, block, c] = (dkv[n, block, c].astype(F32) + kv_zone[n, block].astype(F32)).astype(BF)

        return DownSum(net, lambda zz: dkv.at[n, zz, c], lambda k: kv_zone.at[n, k], add)

    kv_sum = [kv_total(n) for n in range(2)]

    def pull(k, carry):
        for g in range(groups):
            mine = pl.ds(tok * g, tok)
            p = probs[k, mine, :].astype(F32)
            t = p * dot_nt(do_heads[k, mine, :], v_heads[k])
            ds = (t - p * jnp.sum(t, axis=1, keepdims=True)).astype(BF)
            gs_heads[mine, :length] = ds
            o_heads[k, mine, :] = dot_nn(ds, k_heads[k]) * eighth
        half, kk = lax.div(k, 3), lax.rem(k, 3)
        for i, (left, right) in enumerate(((q_heads[k], gs_heads[: groups * tok, :length]), (do_heads[k], probs[k]))):
            turned_grad = dot_tn(left, right).astype(BF)
            at = pl.ds(pl.multiple_of(192 * i + HD * kk, HD), HD)
            for j in range(8):
                dkv[half, j // 2, j % 2, at, :] = turned_grad[:, tok * j : tok * j + tok]
        return carry

    def pair_sum(n):
        kv_pair[n].take()
        for k in range(4):
            dkv[n, k, c] = (dkv[n, k, c].astype(F32) + kv_mate[n, k].astype(F32)).astype(BF)
        kv_sum[n].start()

    def grads(p, parts):
        at = 0
        for part in parts:
            wb[p, :, at : at + part.shape[1]] = part.astype(BF)
            at += part.shape[1]
        pair = ToMate(net, m_att.at[p, :, other, :, quarter], ma_mate.at[p])
        pair.start()
        return pair

    def grads_pair(p, pair):
        pair.take()
        for k in range(4):
            m_att[p, k, c, :, quarter] = (m_att[p, k, c, :, quarter].astype(F32) + ma_mate[p, k].astype(F32)).astype(BF)

    def grads_chain(p, pair):
        def add(block, slot):
            m_att[p, block, c, :, quarter] = (
                m_att[p, block, c, :, quarter].astype(F32) + ma_zone[p, slot].astype(F32)
            ).astype(BF)

        grads_pair(p, pair)
        out = ChainSum(net, lambda zz: m_att.at[p, zz, c, :, quarter], lambda k: ma_zone.at[p, k], add)
        out.stage(0)
        return out

    def grads_straight(p, pair):
        grads_pair(p, pair)
        out = ToOwners(net, lambda zz: m_att.at[p, zz, c, :, quarter], lambda k: ma_zone.at[p, k])
        out.start()
        return out

    def grads_back(p, out):
        cols = pl.ds(256 * p, 256)
        if isinstance(out, ChainSum):
            out.own()
            total = m_att[p, z, c, :, quarter].astype(F32)
        else:
            out.take()
            total = m_att[p, z, c, :, quarter].astype(F32)
            for k in range(3):
                total = total + ma_zone[p, k].astype(F32)
        unsettle(total, wide, att_land, rows, cols)
        spread = Spread(net, lambda j: att_land.at[j, :, cols], lambda j: back_att.at[j, :, cols])
        spread.start()
        back_att[d, :, cols] = att_land[d, :, cols]
        return spread

    q_cols, l_cols, o_cols = pl.ds(0, 256), pl.ds(256, 256), pl.ds(512, 256)
    quarter = pl.ds(0, 256)
    lax.fori_loop(0, 3, pull, 0)
    kv_pair[0].start()
    lax.fori_loop(3, 4, pull, 0)
    pair_sum(0)
    lax.fori_loop(4, 6, pull, 0)
    kv_pair[1].start()
    for t in range(9):
        j, col = (t // 2, (t % 2) * 128) if t < 8 else (2, 384)
        cut_send[j, :, col : col + 128] = turned(joined(o_heads, t, tok), cosine, -sine).astype(BF)
    cut_q.start()
    br[0].start()
    cut_land[d, :, q_cols] = cut_send[d, :, q_cols]
    pair_sum(1)
    ats.take()
    cut_o.take()
    turn_x[...] = att_all[...].reshape(span, dim).T
    pair_o = grads(2, [dot_nn(turn_x[...], cut_land[:, :, o_cols].reshape(span, 256))])
    turn_n[...] = xn_all[...].reshape(span, dim).T
    for n in range(2):
        kv_sum[n].relay(0)
        kv_sum[n].relay(1)
    cut_q.take()
    pair_q = grads(0, [dot_nn(turn_n[...], cut_land[:, :, q_cols].reshape(span, 256))])
    gu_sum[1].stage(1)
    sum_o = grads_chain(2, pair_o)
    sum_q = grads_chain(0, pair_q)
    gu_sum[0].between(2)

    for n in range(2):
        kv_sum[n].own()
        kv_tot[n] = dkv[n, z, c].astype(F32)
    keys = jnp.concatenate([kv_tot[0, :192, :], kv_tot[1, :192, :]], axis=0).T
    vals = jnp.concatenate([kv_tot[0, 192:, :], kv_tot[1, 192:, :]], axis=0).T
    late = [turned(keys[:, 128 * i : 128 * i + 128], cosine, -sine) for i in range(3)] + [vals[:, 128 * i : 128 * i + 128] for i in range(3)]
    for tile, (j, col) in zip(late, places):
        cut_send[j, :, col : col + 128] = tile.astype(BF)
    cut_l.start()
    cut_land[d, :, l_cols] = cut_send[d, :, l_cols]
    sum_o.stage(1)
    sum_q.stage(1)
    gu_sum[1].between(2)
    gu_sum[0].last()
    cut_l.take()
    gu_sum[1].last()
    dn_sum.rising(2, False)
    last = cut_land[:, :, 384:512].reshape(span, 128)
    cuts = cut_land[:, :, :512].reshape(span, 512)
    lane = lax.broadcasted_iota(jnp.int32, cuts.shape, 1)
    cuts = jnp.where((d == 3) & (lane >= 384), jnp.zeros_like(cuts), cuts)
    for n in range(3):
        part = dot_nt(cuts, wa[384 * n : 384 * n + 384, :]).astype(BF)
        gx_send[:, :, 384 * n : 384 * n + 384] = part.reshape(4, tok, 384)
        gx[n].start()
    second = jnp.where(d == 3, dot_nn(turn_x[...], last), dot_nn(turn_n[...], last))
    pair_l = grads(1, [dot_nn(turn_n[...], cut_land[:, :, 256:384].reshape(span, 128)), second])
    sum_l = grads_straight(1, pair_l)
    br[0].take()
    block_out[0] = (middle[...] + scale_mlp * plane_sum(net, br_send, br_land)).astype(BF)
    dn_sum.last()
    sum_o.stage(2)
    sum_q.stage(2)
    for k in range(2):
        gu_sum[k].own()
        unsettle(wgu[z, c, :, halves[k]].astype(F32), wide, gu_land, rows, halves[k])
    back_g = Spread(net, lambda j: gu_land.at[j], lambda j: back_gu.at[j])
    back_g.start()
    back_gu[d] = gu_land[d]
    back_o = grads_back(2, sum_o)
    back_l = grads_back(1, sum_l)
    back_q = grads_back(0, sum_q)
    dn_sum.own()
    back_down[...] = wd[z, c]
    for n in range(3):
        gx[n].take()
    input_grad[0] = gmid[...] + norm_pull(plane_sum(net, gx_send, gx_land), x_in[0].astype(F32))
    for spread in (back_o, back_q, back_g, back_l):
        spread.take()
    net.finish()


def layer(x, cot, weights, down, gains, doc_starts, keep_mask, keep_rate, seq_order):
    tok, dim = x.shape[1:]
    ns = 8
    length = tok * ns
    ffr = down.shape[0]
    hid = ffr * ns
    blk = dim // ns
    span = 4 * tok
    vm = pl.BlockSpec(memory_space=pltpu.VMEM)
    sm = pl.BlockSpec(memory_space=pltpu.SMEM)
    padded = blk // 4 + -(blk // 4) % 16
    att_pack, gu_pack = ((4, padded, 768), BF), ((4, padded, 2 * hid), BF)
    outs = [((1, tok, dim), BF), ((1, tok, dim), F32), gu_pack, att_pack, (down.shape, BF)]
    plane = ((4, tok, dim), BF)
    wide_cut = ((4, tok, 512), BF)
    three = ((KV, 3 * tok, HD), BF)
    scratch = [
        att_pack,
        gu_pack,
        ((blk, hid), F32),
        wide_cut,
        ((4, 2, tok, 2 * KV * HD), BF),
        ((KV, 3 * tok, HD), F32),
        ((tok, length), F32),
        ((dim, 512), BF),
        ((4, dim, 384), BF),
        ((4, 2, blk, 2 * hid), BF),
        ((4, 2, ffr, dim), BF),
        plane,
        plane,
        plane,
        plane,
        three,
        ((KV, length, HD), BF),
        ((KV, length, HD), BF),
        ((KV, 3 * tok, length), BF),
        ((tok, dim), F32),
        ((span, hid), BF),
        ((span, 2 * hid), BF),
        ((dim, span), BF),
        ((dim, span), BF),
        ((hid, span), BF),
        plane,
        plane,
        plane,
        plane,
        ((4, blk, 2 * hid), BF),
        ((5, blk, 2 * hid), BF),
        ((4, ffr, dim), BF),
        ((5, ffr, dim), BF),
        ((tok, dim), F32),
        three,
        ((2, 4, 2, 384, tok), BF),
        ((2, 4, 384, tok), BF),
        ((2, 3, 384, tok), BF),
        ((2, 384, tok), F32),
        ((4, tok, 768), BF),
        ((3, 4, blk, 256), BF),
        ((3, 5, blk, 256), BF),
        plane,
    ]
    return pl.pallas_call(
        layer_kernel,
        out_shape=[jax.ShapeDtypeStruct(*o) for o in outs],
        in_specs=[vm] * 11 + [sm] * 4,
        out_specs=[vm] * len(outs),
        scratch_shapes=[pltpu.VMEM(*t) for t in scratch] + [pltpu.SemaphoreType.DMA((SENDS,)), pltpu.SemaphoreType.DMA((RECVS,))],
        compiler_params=pltpu.CompilerParams(collective_id=0, has_side_effects=True, vmem_limit_bytes=LIMIT),
        name="k_layer",
    )(x, cot, *weights, down, *gains, doc_starts, keep_mask, keep_rate, seq_order)


def grads_kernel(
    query, key_w, value, gate_w, up_w, gain_one, gain_two, block_in, input_in, back_gu, back_att, back_down,
    block_out, input_out, norm_one, g_query, g_key, g_value, g_output, norm_two, g_gate, g_up, g_down,
):
    rows, ffr = query.shape[0], back_down.shape[0]
    hid = 8 * ffr
    block_out[...] = block_in[...]
    input_out[...] = input_in[...]
    g_down[...] = back_down[...].astype(F32)
    gain = column(gain_one[...])
    total = jnp.zeros((rows, 128), F32)
    for j in range(4):
        for i, t in enumerate((2 * j, 2 * j + 1, LATE[j][0], LATE[j][1])):
            m = back_att[j, :rows, 128 * i : 128 * i + 128].astype(F32)
            if t is None:
                g_output[:, 1024:1152] = m
                continue
            w, g, t = (query, g_query, t) if t < 9 else (key_w, g_key, t - 9) if t < 12 else (value, g_value, t - 12)
            cols = slice(128 * t, 128 * t + 128)
            total = total + w[:, cols].astype(F32) * m
            g[:, cols] = m * gain
        g_output[:, 256 * j : 256 * j + 256] = back_att[j, :rows, 512:768].astype(F32)
    norm_one[...] = row_of(jnp.sum(total, axis=1, keepdims=True))
    gain = column(gain_two[...])
    total = jnp.zeros((rows, 4 * ffr), F32)
    for i, (w, g) in enumerate(((gate_w, g_gate), (up_w, g_up))):
        for k in range(8):
            at = hid * (k // 4) + 4 * ffr * i + ffr * (k % 4)
            m = jnp.concatenate([back_gu[j, :rows, at : at + ffr].astype(F32) for j in range(4)], axis=1)
            cols = slice(4 * ffr * k, 4 * ffr * k + 4 * ffr)
            total = total + w[:, cols].astype(F32) * m
            g[:, cols] = m * gain
    norm_two[...] = row_of(jnp.sum(total, axis=1, keepdims=True))


def gradients(query, key_w, value, output, gate_w, up_w, gains, results):
    block, grad, back_gu, back_att, back_down = results
    shapes = [grad.shape, gains[0].shape] + [w.shape for w in (query, key_w, value, output)]
    shapes += [gains[1].shape, gate_w.shape, up_w.shape, back_down.shape]
    vm = pl.BlockSpec(memory_space=pltpu.VMEM)
    return pl.pallas_call(
        grads_kernel,
        out_shape=[jax.ShapeDtypeStruct(block.shape, BF)] + [jax.ShapeDtypeStruct(t, F32) for t in shapes],
        in_specs=[vm] * 12,
        out_specs=[vm] * 11,
        name="k_grads",
    )(query, key_w, value, gate_w, up_w, *gains, block, grad, back_gu, back_att, back_down)


def shards_by_kernel(
    hidden_in,
    attn_norm,
    query_weight,
    key_weight,
    value_weight,
    output_weight,
    mlp_norm,
    gate_weight,
    up_weight,
    down_weight,
    cotangent,
    doc_starts,
    keep_mask,
    keep_rate,
    seq_order,
):
    rows = query_weight.shape[0]
    gains = (attn_norm.reshape(1, rows), mlp_norm.reshape(1, rows))
    weights = (query_weight, key_weight, value_weight, output_weight, gate_weight, up_weight)
    results = layer(
        hidden_in, cotangent, weights, down_weight, gains, doc_starts, keep_mask.reshape(-1), keep_rate, seq_order
    )
    outs = list(gradients(*weights, gains, results))
    outs[2], outs[7] = outs[2].reshape(rows), outs[7].reshape(rows)
    return tuple(outs)


def solution(mesh):
    placed = (
        P("dp", "seq", None),
        P(("seq", "dp")),
        P(("seq", "dp"), None),
        P(("seq", "dp"), None),
        P(("seq", "dp"), None),
        P(("seq", "dp"), None),
        P(("seq", "dp")),
        P(("seq", "dp"), None),
        P(("seq", "dp"), None),
        P(("seq", "dp"), None),
        P("dp", "seq", None),
        P(),
        P(),
        P(),
        P(),
    )
    fits = mesh.shape["seq"] == 8 and mesh.shape["dp"] == 4
    return jax.shard_map(
        shards_by_kernel if fits else shards,
        mesh=mesh,
        in_specs=placed,
        out_specs=(
            P("dp", "seq", None),
            P("dp", "seq", None),
            P(("seq", "dp")),
            P(("seq", "dp"), None),
            P(("seq", "dp"), None),
            P(("seq", "dp"), None),
            P(("seq", "dp"), None),
            P(("seq", "dp")),
            P(("seq", "dp"), None),
            P(("seq", "dp"), None),
            P(("seq", "dp"), None),
        ),
        check_vma=False,
    )
```

```python
import math

import jax
import jax.numpy as jnp
from jax import lax
from jax.experimental import pallas as pl
from jax.experimental.pallas import tpu as pltpu
from jax.sharding import PartitionSpec as P

H = 18
KV = 6
HD = 64


EPSILON = 1e-05
ROPE_BASE = 10000.0
MASKED = -1e30


def contract_rows(left_rows, right_rows):
    return lax.dot_general(
        left_rows, right_rows, (((0,), (0,)), ((), ())), preferred_element_type=jnp.float32
    )


def contract_cols(left_mat, right_mat):
    return lax.dot_general(
        left_mat, right_mat, (((1,), (1,)), ((), ())), preferred_element_type=jnp.float32
    )


def low(v):
    return v.astype(jnp.bfloat16)


def dot(a, b):
    return jnp.dot(a, b, preferred_element_type=jnp.float32)


def swap_halves(vectors):
    half = HD // 2
    return jnp.concatenate([vectors[..., half:], vectors[..., :half]], axis=-1)


def shards(
    hidden_in,
    attn_norm,
    query_weight,
    key_weight,
    value_weight,
    output_weight,
    mlp_norm,
    gate_weight,
    up_weight,
    down_weight,
    cotangent,
    doc_starts,
    keep_mask,
    keep_rate,
    seq_order,
):
    tok = hidden_in.shape[1]
    ns, nd = lax.axis_size("seq"), lax.axis_size("dp")
    length = tok * ns
    rows = query_weight.shape[0]
    ffr = down_weight.shape[0]
    dim = hidden_in.shape[2]
    groups = H // KV
    nq, nk = H * HD, KV * HD
    score_scale = 1.0 / math.sqrt(HD)
    me_s, me_d = lax.axis_index("seq"), lax.axis_index("dp")
    sample = jnp.sum(jnp.where(jnp.arange(nd) == me_d, seq_order, 0))
    pick = jnp.arange(nd) == sample
    doc_begin = jnp.sum(jnp.where(pick[:, None], doc_starts, 0), axis=0)
    keep_flags = jnp.sum(jnp.where(pick[:, None], keep_mask, 0), axis=0).astype(jnp.float32)
    attn_scale = keep_flags[0] / keep_rate[0]
    mlp_scale = keep_flags[1] / keep_rate[1]
    positions = me_s * tok + jnp.arange(tok)
    first = jnp.max(jnp.where(doc_begin[None, :] <= positions[:, None], doc_begin[None, :], 0), axis=1)
    gain_one, gain_two = attn_norm[:, None], mlp_norm[:, None]

    qkv_rows = low(jnp.concatenate([query_weight, key_weight, value_weight], axis=1).astype(jnp.float32) * gain_one)
    w_qkv = lax.all_gather(qkv_rows, ("seq", "dp"), axis=0, tiled=True)
    w_out = lax.all_gather(output_weight, ("seq", "dp"), axis=0, tiled=True)

    def split_hidden(w):
        w = low(w.astype(jnp.float32) * gain_two).reshape(rows, ns, nd, ffr)
        w = jnp.transpose(w, (0, 2, 1, 3)).reshape(rows, nd * ns * ffr)
        return w

    gu = jnp.concatenate(
        [split_hidden(gate_weight).reshape(rows, nd, -1), split_hidden(up_weight).reshape(rows, nd, -1)], axis=2
    )
    gu = lax.all_to_all(gu, "dp", split_axis=1, concat_axis=0, tiled=True).reshape(nd * rows, -1)
    w_gu = lax.all_gather(gu, "seq", axis=0, tiled=True)
    w_down = lax.all_gather(down_weight, "seq", axis=0, tiled=True)
    hid = w_down.shape[0]

    x = hidden_in[0].astype(jnp.float32)
    r_one = lax.rsqrt(jnp.mean(x * x, axis=-1, keepdims=True) + EPSILON)
    xn = low(x * r_one)
    qkv = dot(xn, w_qkv)
    inverse_freq = ROPE_BASE ** (-2.0 * jnp.arange(HD // 2, dtype=jnp.float32) / HD)
    angles = positions.astype(jnp.float32)[:, None] * inverse_freq[None, :]
    cosine = jnp.tile(jnp.cos(angles), (1, 2))[:, None, :]
    sine = jnp.concatenate([-jnp.sin(angles), jnp.sin(angles)], axis=1)[:, None, :]

    def turn(v):
        return v * cosine + swap_halves(v) * sine

    def turn_back(v):
        return v * cosine - swap_halves(v) * sine

    queries = low(turn(qkv[:, :nq].reshape(tok, H, HD))).reshape(tok, KV, groups, HD)
    keys = low(turn(qkv[:, nq : nq + nk].reshape(tok, KV, HD)))
    kv = jnp.concatenate([keys.reshape(tok, nk), low(qkv[:, nq + nk :])], axis=1)
    kv_all = lax.all_gather(kv, "seq", axis=0, tiled=True)
    k_all, v_all = kv_all[:, :nk].reshape(length, KV, HD), kv_all[:, nk:].reshape(length, KV, HD)
    key_pos = jnp.arange(length)
    allowed = (key_pos[None, :] <= positions[:, None]) & (key_pos[None, :] >= first[:, None])
    scores = jnp.einsum("tkgd,skd->kgts", queries, k_all, preferred_element_type=jnp.float32) * score_scale
    scores = jnp.where(allowed, scores, MASKED)
    expo = jnp.exp(scores - jnp.max(scores, axis=-1, keepdims=True))
    probs = low(expo / jnp.sum(expo, axis=-1, keepdims=True))
    attended = jnp.einsum("kgts,skd->tkgd", probs, v_all, preferred_element_type=jnp.float32)
    att = low(attended.reshape(tok, nq))
    middle = x + attn_scale * dot(att, w_out)
    r_two = lax.rsqrt(jnp.mean(middle * middle, axis=-1, keepdims=True) + EPSILON)
    mn = low(middle * r_two)

    cot = cotangent[0].astype(jnp.float32)
    side = lax.all_gather(jnp.concatenate([xn, low(mlp_scale * cot), att], axis=1), "dp", axis=0, tiled=True)
    xn_all, gd_all, att_all = side[:, :dim], side[:, dim : 2 * dim], side[:, 2 * dim :]
    mn_all = lax.all_gather(mn, "dp", axis=0, tiled=True)
    gate, up = dot(mn_all, w_gu[:, :hid]), dot(mn_all, w_gu[:, hid:])
    sig = jax.nn.sigmoid(gate)
    act_gate = gate * sig
    act = low(act_gate * up)
    g_act = contract_cols(gd_all, w_down)
    gg = low(g_act * up * (sig * (1.0 + gate * (1.0 - sig))))
    gu_in = low(g_act * act_gate)
    gboth = jnp.concatenate([gg, gu_in], axis=1)
    g_mn = lax.psum_scatter(low(contract_cols(gboth, w_gu)), "dp", scatter_dimension=0, tiled=True).astype(jnp.float32)
    branch = lax.psum_scatter(low(dot(act, w_down)), "dp", scatter_dimension=0, tiled=True).astype(jnp.float32)
    block_output = low(middle + mlp_scale * branch)[None]
    m_gu = lax.psum_scatter(low(contract_rows(mn_all, gboth)), "seq", scatter_dimension=0, tiled=True)
    m_down = lax.psum_scatter(low(contract_rows(act, gd_all)), "seq", scatter_dimension=0, tiled=True)

    def norm_back(e, v, r):
        return r * e - v * (r * r * r) * jnp.mean(e * v, axis=-1, keepdims=True)

    g_mid = cot + norm_back(g_mn, middle, r_two)
    gba = low(attn_scale * g_mid)
    g_att = low(contract_cols(gba, w_out)).reshape(tok, KV, groups, HD)
    g_probs = jnp.einsum("tkgd,skd->kgts", g_att, v_all, preferred_element_type=jnp.float32)
    delta = jnp.einsum("tkgd,tkgd->kgt", g_att.astype(jnp.float32), attended)
    g_scores = low(probs.astype(jnp.float32) * (g_probs - delta[..., None]))
    g_q = jnp.einsum("kgts,skd->tkgd", g_scores, k_all, preferred_element_type=jnp.float32) * score_scale
    g_k = jnp.einsum("kgts,tkgd->skd", g_scores, queries, preferred_element_type=jnp.float32) * score_scale
    g_v = jnp.einsum("kgts,tkgd->skd", probs, g_att, preferred_element_type=jnp.float32)
    g_kv = low(jnp.concatenate([g_k.reshape(length, nk), g_v.reshape(length, nk)], axis=1))
    g_kv = lax.psum_scatter(g_kv, "seq", scatter_dimension=0, tiled=True).astype(jnp.float32)
    g_q_in = low(turn_back(g_q.reshape(tok, H, HD))).reshape(tok, nq)
    g_k_in = low(turn_back(g_kv[:, :nk].reshape(tok, KV, HD))).reshape(tok, nk)
    g_qkv = jnp.concatenate([g_q_in, g_k_in, low(g_kv[:, nk:])], axis=1)
    g_xn = contract_cols(g_qkv, w_qkv)
    input_grad = (g_mid + norm_back(g_xn, x, r_one))[None]

    cut = jnp.concatenate([g_qkv.reshape(tok, nd, -1), gba.reshape(tok, nd, -1)], axis=2)
    wq = g_qkv.shape[1] // nd
    cut = lax.all_to_all(cut, "dp", split_axis=1, concat_axis=0, tiled=True).reshape(nd * tok, -1)
    m_att = jnp.concatenate([contract_rows(xn_all, cut[:, :wq]), contract_rows(att_all, cut[:, wq:])], axis=1)
    m_att = lax.psum_scatter(low(m_att), "seq", scatter_dimension=0, tiled=True)

    back = jnp.concatenate([m_gu, m_att], axis=1)
    back = lax.all_to_all(back.reshape(nd, rows, 1, -1), "dp", split_axis=0, concat_axis=2, tiled=True)
    back = back.reshape(rows, nd, -1).astype(jnp.float32)

    def whole_hidden(m):
        return jnp.transpose(m.reshape(rows, nd, ns, ffr), (0, 2, 1, 3)).reshape(rows, -1)

    m_gate, m_up = whole_hidden(back[:, :, :hid]), whole_hidden(back[:, :, hid : 2 * hid])
    m_qkv = back[:, :, 2 * hid : 2 * hid + wq].reshape(rows, -1)
    g_out = back[:, :, 2 * hid + wq :].reshape(rows, -1)

    def weigh(w, m):
        return jnp.sum(w.astype(jnp.float32) * m, axis=1)

    m_q, m_k, m_v = m_qkv[:, :nq], m_qkv[:, nq : nq + nk], m_qkv[:, nq + nk :]
    g_norm_one = weigh(query_weight, m_q) + weigh(key_weight, m_k) + weigh(value_weight, m_v)
    g_norm_two = weigh(gate_weight, m_gate) + weigh(up_weight, m_up)
    return (
        block_output,
        input_grad,
        g_norm_one,
        m_q * gain_one,
        m_k * gain_one,
        m_v * gain_one,
        g_out,
        g_norm_two,
        m_gate * gain_two,
        m_up * gain_two,
        m_down.astype(jnp.float32),
    )


MESH = pl.DeviceIdType.MESH
LIMIT = 60 * 2**20
SENDS, RECVS = 120, 204
BF, F32 = jnp.bfloat16, jnp.float32


def dot_nn(a, b):
    return lax.dot_general(a, b, (((1,), (0,)), ((), ())), preferred_element_type=F32)


def dot_nt(a, b):
    return lax.dot_general(a, b, (((1,), (1,)), ((), ())), preferred_element_type=F32)


def dot_tn(a, b):
    return lax.dot_general(a, b, (((0,), (0,)), ((), ())), preferred_element_type=F32)


class Net:
    def __init__(self, sends, recvs):
        self.sends, self.recvs, self.open, self.used = sends, recvs, [], 0
        self.free = list(range(sends.shape[0]))
        self.s, self.d = lax.axis_index("seq"), lax.axis_index("dp")
        self.z, self.c = lax.div(self.s, 2), lax.rem(self.s, 2)
        y, x = lax.div(self.d, 2), lax.rem(self.d, 2)
        self.plane = (y * 2 + 1 - x, (1 - y) * 2 + x, 3 - self.d)
        self.mate = self.at(self.z, 1 - self.c)

    def room(self, count):
        base = self.used
        self.used += count
        return base

    def at(self, z, core):
        return {"seq": z * 2 + core, "dp": self.d}

    def across(self, kind):
        return {"seq": self.s, "dp": self.plane[kind]}

    def greet(self):
        barrier = pltpu.get_barrier_semaphore()
        peers = [self.mate] + [self.across(k) for k in range(3)]
        peers += [self.at(lax.rem(self.z + k, 4), self.c) for k in (1, 2, 3)]
        for peer in peers:
            pl.semaphore_signal(barrier, inc=1, device_id=peer, device_id_type=MESH)

    def greeted(self):
        pl.semaphore_wait(pltpu.get_barrier_semaphore(), 7)

    def copy(self, src, dst, send, recv, peer):
        return pltpu.make_async_remote_copy(
            src_ref=src,
            dst_ref=dst,
            send_sem=self.sends.at[send],
            recv_sem=self.recvs.at[recv],
            device_id=peer,
            device_id_type=MESH,
        )

    def push(self, owner, src, dst, recv, peer, when=None):
        send = self.free.pop(0)
        copy = self.copy(src, dst, send, recv, peer)
        if when is None:
            copy.start()
        else:
            pl.when(when)(copy.start)
        self.open.append((copy, when, owner, send))

    def arrive(self, dst, recv, when=None):
        copy = self.copy(dst, dst, 0, recv, self.mate)
        if when is None:
            copy.wait_recv()
        else:
            pl.when(when)(copy.wait_recv)

    def finish(self, *owners):
        kept = []
        for entry in self.open:
            copy, when, owner, send = entry
            if owners and owner not in owners:
                kept.append(entry)
                continue
            if when is None:
                copy.wait_send()
            else:
                pl.when(when)(copy.wait_send)
            self.free.append(send)
        self.open = kept

    def order(self, step):
        if step == 0:
            return self.z
        table = ((1, 0, 3, 2), (2, 2, 1, 1), (3, 3, 0, 0))[step - 1]
        z = self.z
        return jnp.where(z == 0, table[0], jnp.where(z == 1, table[1], jnp.where(z == 2, table[2], table[3])))


class Chain:
    def __init__(self, net, block, room=4):
        self.net, self.block, self.base = net, block, net.room(room)

    def start(self):
        net = self.net
        own = self.block(net.z, net.c)
        net.push(self, own, own, self.base + net.z, net.at(net.z + 1, net.c), net.z < 3)
        net.push(self, own, own, self.base + net.z, net.at(net.z - 1, net.c), net.z > 0)

    def step(self, k):
        net = self.net
        b = net.order(k)
        block = self.block(b, net.c)
        net.arrive(block, self.base + b)
        to = jnp.where(b < net.z, net.z + 1, net.z - 1)
        net.push(self, block, block, self.base + b, net.at(to, net.c), (to >= 0) & (to <= 3))


class Lines(Chain):
    def __init__(self, net, block):
        super().__init__(net, block, 8)

    def start(self, ends=None):
        net = self.net
        own = self.block(net.z, net.c)
        up, down, any_z = net.z < 3, net.z > 0, None
        if ends is not None:
            any_z = (net.z == 0) | (net.z == 3)
            any_z = any_z if ends else jnp.logical_not(any_z)
            up, down = up & any_z, down & any_z
        net.push(self, own, own, self.base + net.z, net.at(net.z + 1, net.c), up)
        net.push(self, own, own, self.base + net.z, net.at(net.z - 1, net.c), down)
        net.push(self, own, own, self.base + 4 + net.z, net.mate, any_z)

    def onward(self, b):
        to = jnp.where(b < self.net.z, self.net.z + 1, self.net.z - 1)
        return to, (to >= 0) & (to <= 3)

    def step(self, k):
        net = self.net
        b = net.order(k)
        block = self.block(b, net.c)
        to, on = self.onward(b)
        net.arrive(block, self.base + b, on)
        net.push(self, block, block, self.base + b, net.at(to, net.c), on)

    def give(self, k):
        net = self.net
        b = net.order(k)
        block = self.block(b, net.c)
        if k:
            net.arrive(block, self.base + b, jnp.logical_not(self.onward(b)[1]))
        net.push(self, block, block, self.base + 4 + b, net.mate)

    def take(self):
        net = self.net
        for b in range(4):
            net.arrive(self.block(b, 1 - net.c), self.base + 4 + b)


class FromLast:
    def __init__(self, net, source, full):
        self.net, self.source, self.full, self.base = net, source, full, net.room(2)

    def start(self):
        net = self.net
        for kind in range(3):
            part = self.full.at[:, net.c]
            net.push(self, self.source.at[:, net.c, :, pl.ds(384, 128)], part, self.base, net.across(kind), net.d == 3)

        @pl.when(net.d == 3)
        def _():
            self.full[...] = self.source[:, :, :, 384:512]

    def pass_on(self):
        net = self.net
        part = self.full.at[:, net.c]
        net.arrive(part, self.base, net.d < 3)
        net.push(self, part, part, self.base + 1, net.mate, net.d < 3)

    def take(self):
        self.net.arrive(self.full.at[:, 1 - self.net.c], self.base + 1, self.net.d < 3)


class Rising(Lines):
    def start(self):
        net = self.net
        own = self.block(net.z, net.c)
        net.push(self, own, own, self.base + net.z, net.at(net.z + 1, net.c), net.z < 3)
        net.push(self, own, own, self.base + 4 + net.z, net.mate)

    def step(self, k):
        net = self.net
        b = jnp.maximum(net.z - k, 0)
        block = self.block(b, net.c)
        net.arrive(block, self.base + b, net.z >= k)
        net.push(self, block, block, self.base + b, net.at(net.z + 1, net.c), (net.z >= k) & (net.z < 3))
        net.push(self, block, block, self.base + 4 + b, net.mate, net.z >= k)

    def take(self):
        net = self.net
        for b in range(4):
            net.arrive(self.block(b, 1 - net.c), self.base + 4 + b, net.z >= b)


class Slices(Chain):
    def __init__(self, net, full, rows):
        self.full, self.rows, self.half = full, rows, rows // 32 * 16
        super().__init__(net, lambda z, core: self.part(net.d, z, core), 36)

    def part(self, slot, z, core, half=None):
        first = pl.multiple_of((z * 2 + core) * self.rows, 16)
        if half is None:
            return self.full.at[slot, pl.ds(first, self.rows)]
        if half == 0:
            return self.full.at[slot, pl.ds(first, self.half)]
        return self.full.at[slot, pl.ds(pl.multiple_of(first + self.half, 16), self.rows - self.half)]

    def spread(self, k):
        net = self.net
        b = net.order(k)
        block = self.part(net.d, b, net.c)
        net.push(self, block, block, self.base + 4 + b, net.across(0))
        net.push(self, block, block, self.base + 8 + b, net.across(1))
        net.push(self, block, block, self.base + 20 + b, net.mate)

    def pass_on(self, k):
        net = self.net
        b = net.order(k)
        for kind in (0, 1):
            block = self.part(net.plane[kind], b, net.c)
            net.arrive(block, self.base + 4 + 4 * kind + b)
            half = self.part(net.plane[kind], b, net.c, kind)
            net.push(self, half, half, self.base + 12 + 4 * kind + b, net.across(1 - kind))
            net.push(self, block, block, self.base + 24 + 4 * kind + b, net.mate)

    def corner(self, k):
        net = self.net
        b = net.order(k)
        for kind in (0, 1):
            half = self.part(net.plane[2], b, net.c, kind)
            net.arrive(half, self.base + 12 + 4 * kind + b)
        block = self.part(net.plane[2], b, net.c)
        net.push(self, block, block, self.base + 32 + b, net.mate)

    def take(self):
        net = self.net
        for b in range(4):
            net.arrive(self.part(net.d, b, 1 - net.c), self.base + 20 + b)
            for kind in range(3):
                net.arrive(self.part(net.plane[kind], b, 1 - net.c), self.base + 24 + 4 * kind + b)


class Plane:
    def __init__(self, net, full):
        self.net, self.full, self.base = net, full, net.room(4)
        self.half = full.shape[1] // 2

    def start(self):
        net = self.net
        own = self.full.at[net.d]
        for kind in (0, 1):
            net.push(self, own, own, self.base + kind, net.across(kind))

    def pass_on(self):
        net = self.net
        for kind in (0, 1):
            net.arrive(self.full.at[net.plane[kind]], self.base + kind)
            half = self.full.at[net.plane[kind], pl.ds(kind * self.half, self.half)]
            net.push(self, half, half, self.base + 2 + kind, net.across(1 - kind))

    def take(self):
        net = self.net
        for kind in (0, 1):
            net.arrive(self.full.at[net.plane[2], pl.ds(kind * self.half, self.half)], self.base + 2 + kind)


class Spread:
    def __init__(self, net, send, land):
        self.net, self.send, self.land, self.base = net, send, land, net.room(3)

    def start(self):
        net = self.net
        for kind in (2, 0, 1):
            net.push(self, self.send(net.plane[kind]), self.land(net.d), self.base + kind, net.across(kind))

    def take(self):
        for kind in range(3):
            self.net.arrive(self.land(self.net.plane[kind]), self.base + kind)


class ToMate:
    def __init__(self, net, send, land):
        self.net, self.send, self.land, self.base = net, send, land, net.room(1)

    def start(self):
        self.net.push(self, self.send, self.land, self.base, self.net.mate)

    def take(self):
        self.net.arrive(self.land, self.base)


class ToOwners:
    def __init__(self, net, part, land, down=False):
        self.net, self.part, self.land, self.down, self.base = net, part, land, down, net.room(3)

    def start(self):
        net = self.net
        for k in (3, 2, 1):
            to = lax.rem(net.z - k + 4, 4)
            net.push(self, self.part(to), self.land(k - 1), self.base + k - 1, net.at(to, net.c), (net.z >= k) if self.down else None)

    def take(self):
        net = self.net
        for k in (1, 2, 3):
            net.arrive(self.land(k - 1), self.base + k - 1, (net.z + k <= 3) if self.down else None)


class DownSum:
    def __init__(self, net, part, land, add):
        self.net, self.part, self.land, self.add, self.base = net, part, land, add, net.room(3)

    def send(self, b, when):
        net = self.net
        net.push(self, self.part(b), self.land(b), self.base + b, net.at(net.z - 1, net.c), when)

    def start(self):
        for b in range(3):
            self.send(b, self.net.z == 3)

    def relay(self, b):
        net = self.net
        on = (net.z > b) & (net.z < 3)

        @pl.when(on)
        def _():
            net.arrive(self.land(b), self.base + b)
            self.add(b)

        self.send(b, on)

    def own(self):
        net = self.net
        for b in range(3):

            @pl.when(net.z == b)
            def _(b=b):
                net.arrive(self.land(b), self.base + b)
                self.add(b)


class ChainSum:
    def __init__(self, net, part, land, add):
        self.net, self.part, self.land, self.add, self.base = net, part, land, add, net.room(6)

    def stage(self, k):
        self.falling(k)
        self.rising(k)

    def falling(self, k, top=None):
        net, z = self.net, self.net.z
        i = k - 3 + z
        valid = (i >= 0) & (i < z)
        if top is not None:
            valid = valid & ((z == 3) if top else (z < 3))
        i = jnp.clip(i, 0, 3)

        @pl.when(valid & (z < 3))
        def _():
            net.arrive(self.land(i), self.base + i)
            self.add(i, i)

        net.push(self, self.part(i), self.land(i), self.base + i, net.at(z - 1, net.c), valid)

    def last(self):
        self.falling(2, True)
        self.rising(2, True)

    def between(self, k):
        self.falling(k, False)
        self.rising(k, False)

    def rising(self, k, end=None):
        net, z = self.net, self.net.z
        j = k - z
        valid = (j >= 0) & (3 - j > z)
        if end is not None:
            valid = valid & ((z == 0) if end else (z > 0))
        j = jnp.clip(j, 0, 3)

        @pl.when(valid & (z > 0))
        def _():
            net.arrive(self.land(4 - j), self.base + 3 + j)
            self.add(3 - j, 4 - j)

        net.push(self, self.part(3 - j), self.land(4 - j), self.base + 3 + j, net.at(z + 1, net.c), valid)

    def own(self):
        net, z = self.net, self.net.z

        @pl.when(z < 3)
        def _():
            net.arrive(self.land(z), self.base + z)
            self.add(z, z)

        @pl.when(z > 0)
        def _():
            net.arrive(self.land(1 + z), self.base + 6 - z)
            self.add(z, 1 + z)


def settle(land, wide, rows, cols=slice(None)):
    for j in range(4):
        wide[pl.ds(j * rows, rows), :] = land[j, :rows, cols].astype(F32)
    return wide[...].astype(BF)


def unsettle(block, wide, land, rows, cols):
    wide[:, : block.shape[1]] = block
    for j in range(4):
        land[j, :rows, cols] = wide[pl.ds(j * rows, rows), : block.shape[1]].astype(BF)


def turned(tile, cosine, sine):
    lane = lax.broadcasted_iota(jnp.int32, tile.shape, 1)
    other = jnp.where(lax.rem(lane, HD) < HD // 2, pltpu.roll(tile, 128 - HD // 2, 1), pltpu.roll(tile, HD // 2, 1))
    return tile * cosine + other * sine


def own_rows(index, rows):
    return pl.ds(pl.multiple_of(index * rows, 16), rows)


def norm_scale(v):
    return lax.rsqrt(jnp.mean(v * v, axis=1, keepdims=True) + EPSILON)


def norm_pull(e, v):
    r = norm_scale(v)
    return r * e - v * (r * r * r) * jnp.mean(e * v, axis=1, keepdims=True)


def joined(heads, j, tok):
    groups = H // KV
    pair = [heads[h // groups, tok * (h % groups) : tok * (h % groups) + tok, :] for h in (2 * j, 2 * j + 1)]
    return jnp.concatenate(pair, axis=1)


def plane_sum(net, send, land):
    total = send[net.d].astype(F32)
    for kind in range(3):
        total = total + land[net.plane[kind]].astype(F32)
    return total


LATE = ((9, 10), (11, 12), (13, 8), (14, None))


def column(row):
    n = row.shape[1]
    same = lax.broadcasted_iota(jnp.int32, (n, n), 0) == lax.broadcasted_iota(jnp.int32, (n, n), 1)
    return jnp.sum(jnp.where(same, row, 0.0), axis=1, keepdims=True)


def row_of(col):
    n = col.shape[0]
    same = lax.broadcasted_iota(jnp.int32, (n, n), 0) == lax.broadcasted_iota(jnp.int32, (n, n), 1)
    return jnp.sum(jnp.where(same, col, 0.0), axis=0, keepdims=True)


def layer_kernel(
    x_in, cot_in, query, key_w, value, output, gate_w, up_w, down, gain_one, gain_two,
    doc_starts, keep_mask, keep_rate, seq_order,
    block_out, input_grad, back_gu, back_att, back_down,
    att_land, gu_land, wide, qkv_land, kv_all, o_heads, bias, wa, wb, wlast, wgu, wd,
    xn_all, gd_all, mn_all, att_all, q_heads, k_heads, v_heads, probs, middle, act, gboth, turn_x, turn_n, turn_a,
    gn_send, gn_land, br_send, br_land, gu_mate, gu_zone, dn_mate, dn_zone, gmid, do_heads, dkv, kv_mate, kv_zone, kv_tot,
    cut_land, ma_mate, ma_zone, gx_land, sends, recvs,
):
    net = Net(sends, recvs)
    tok, dim = x_in.shape[1], x_in.shape[2]
    rows = dim // 32
    blk = 4 * rows
    ffr = down.shape[0]
    hid, quad = 8 * ffr, 4 * ffr
    d, z, c, s = net.d, net.z, net.c, net.s
    span, length = 4 * tok, 8 * tok
    groups = H // KV
    padded = att_land.shape[1]
    att_send = qkv_send = cut_send = act.reshape(4, tok, hid)
    gu_send = gboth.reshape(4, tok, 2 * hid)
    gx_send, gs_heads = gd_all, gboth
    m_att = wb.reshape(4, 4, 2, blk, 256)

    first_cols, late_cols = pl.ds(0, 256), pl.ds(256, 256)
    a2a_att = Spread(net, lambda j: att_send.at[j, pl.ds(0, padded)], lambda j: att_land.at[j])
    a2a_gu = Spread(net, lambda j: gu_send.at[j, pl.ds(0, padded)], lambda j: gu_land.at[j])
    a2a_qkv = [
        Spread(net, lambda j, cols=cols: qkv_send.at[j, :, cols], lambda j, cols=cols: qkv_land.at[j, :, cols])
        for cols in (late_cols, first_cols)
    ]
    a = [Lines(net, lambda zz, core, cols=cols: wa.at[own_rows(zz * 2 + core, blk), cols]) for cols in (late_cols, first_cols)]
    b = Slices(net, wb, blk)
    tail = FromLast(net, wa.reshape(4, 2, blk, 512), wlast.reshape(4, 2, blk, 128))
    gu = [Lines(net, lambda zz, core, h=h: wgu.at[zz, core, :, pl.ds(hid * h, hid)]) for h in range(2)]
    dn = Lines(net, lambda zz, core: wd.at[zz, core])
    kv = Rising(net, lambda zz, core: kv_all.at[zz, core])
    xs = Plane(net, xn_all)
    gs = Plane(net, gd_all)
    ms = Plane(net, mn_all)
    ats = Plane(net, att_all)

    kv_all[...] = jnp.zeros_like(kv_all)
    net.greet()
    first_gain = column(gain_one[...])
    zero = jnp.zeros((padded - rows, 128), BF)
    weights = (query, key_w, value)

    def qkv_tile(t):
        ref, t = (query, t) if t < 9 else (key_w, t - 9) if t < 12 else (value, t - 12)
        return (ref[:, 128 * t : 128 * t + 128].astype(F32) * first_gain).astype(BF)

    for j in range(4):
        tiles = [qkv_tile(2 * j), qkv_tile(2 * j + 1), qkv_tile(LATE[j][0])]
        tiles.append(output[:, 1024:1152] if LATE[j][1] is None else qkv_tile(LATE[j][1]))
        tiles += [output[:, 256 * j : 256 * j + 128], output[:, 256 * j + 128 : 256 * j + 256]]
        for i, tile in enumerate(tiles):
            att_send[j, :rows, 128 * i : 128 * i + 128] = tile
            att_send[j, rows:padded, 128 * i : 128 * i + 128] = zero
    net.greeted()
    a2a_att.start()
    att_land[d] = att_send[d, :padded, :]
    x = x_in[0].astype(F32)
    xn_all[d] = (x * norm_scale(x)).astype(BF)
    xs.start()
    second_gain = column(gain_two[...])
    for i, ref in enumerate((gate_w, up_w)):
        scaled = ref[...].astype(F32) * second_gain
        for j in range(4):
            for h in range(2):
                part = [scaled[:, ffr * (4 * k + j) : ffr * (4 * k + j) + ffr] for k in range(4 * h, 4 * h + 4)]
                cols = slice(hid * h + quad * i, hid * h + quad * i + quad)
                gu_send[j, :rows, cols] = jnp.concatenate(part, axis=1).astype(BF)
                gu_send[j, rows:padded, cols] = jnp.zeros((padded - rows, quad), BF)
    gu_land[d] = gu_send[d, :padded, :]
    sample = seq_order[d]
    scale_attn, scale_mlp = [
        jnp.full((1, 1), keep_mask[2 * sample + i].astype(F32), F32) / jnp.full((1, 1), keep_rate[i], F32) for i in range(2)
    ]
    gd_all[d] = (cot_in[0].astype(F32) * scale_mlp).astype(BF)
    wd[z, c] = down[...]
    position = s * tok + lax.broadcasted_iota(jnp.int32, (tok, 1), 0)
    lane = lax.broadcasted_iota(jnp.int32, (tok, 128), 1)
    power = lax.rem(lane, HD // 2).astype(F32) * (-2.0 * math.log(ROPE_BASE) / HD)
    angle = position.astype(F32) * jnp.exp(power)
    cosine, sine = jnp.cos(angle), jnp.where(lax.rem(lane, HD) < HD // 2, -jnp.sin(angle), jnp.sin(angle))
    a2a_att.take()
    own = own_rows(s, blk)
    packed = settle(att_land, wide, rows)
    wa[own, :] = packed[:, :512]
    wb[d, own, :] = packed[:, 512:]
    for line in a:
        line.start()
    for k in (1, 2, 3):
        for line in a:
            line.step(k)
        for line in a:
            line.give(k)
        if k == 1:
            xs.pass_on()
            a2a_gu.start()
    b.start()
    dn.start()
    xs.take()
    a[0].take()

    eighth = 1.0 / math.sqrt(HD)

    def project(cols, kinds):
        part = dot_nn(xn_all[...].reshape(span, dim), wa[:, cols])
        for j in range(4):
            for i, kind in enumerate(kinds):
                tile = part[tok * j : tok * j + tok, 128 * i : 128 * i + 128]
                spun = turned(tile, cosine, sine)
                if kind == 1:
                    tile = jnp.where(d < 2, spun, tile)
                elif kind == 2:
                    tile = jnp.where(d == 0, spun, jnp.where(d == 2, spun * eighth, tile))
                else:
                    tile = spun * eighth
                qkv_send[j, :, pl.ds(cols.start + 128 * i, 128)] = tile.astype(BF)

    net.finish(a2a_att)
    project(late_cols, (1, 2))
    a2a_qkv[0].start()
    a[1].take()
    project(first_cols, (0, 0))
    a2a_qkv[1].start()
    qkv_land[d] = qkv_send[d, :, :512]
    b.spread(0)
    b.step(1)
    b.spread(1)
    a2a_qkv[0].take()
    places = [(0, 256), (0, 384), (1, 256), (1, 384), (2, 256), (3, 256)]
    for i, (j, col) in enumerate(places):
        kv_all[z, c, :, 128 * i : 128 * i + 128] = qkv_land[j, :, col : col + 128]
    kv.start()
    b.step(2)
    b.spread(2)
    a2a_gu.take()
    for h in range(2):
        wgu[z, c, :, hid * h : hid * h + hid] = settle(gu_land, wide, rows, slice(hid * h, hid * h + hid))
    b.step(3)
    b.spread(3)
    for half in gu:
        half.start(True)
    kv.step(1)
    b.pass_on(0)
    b.pass_on(1)
    a2a_qkv[1].take()
    gs.start()
    for t in range(9):
        j, col = (t // 2, (t % 2) * 128) if t < 8 else (2, 384)
        for h in (2 * t, 2 * t + 1):
            at = col + HD * (h % 2)
            q_heads[h // groups, tok * (h % groups) : tok * (h % groups) + tok, :] = qkv_land[j, :, at : at + HD]
    first = jnp.zeros((tok, 1), jnp.int32)
    for j in range(doc_starts.shape[1]):
        start = doc_starts[sample, j]
        first = jnp.where(position >= start, jnp.maximum(first, start), first)
    key = lax.broadcasted_iota(jnp.int32, bias.shape, 1)
    bias[...] = jnp.where((key <= position) & (key >= first), 0.0, MASKED)

    kv.step(2)
    gu[0].start(False)
    b.pass_on(2)
    b.pass_on(3)
    b.corner(0)
    b.corner(1)
    kv.step(3)
    dn.step(1)
    kv.take()
    for j in range(8):
        for k in range(KV):
            k_heads[k, pl.ds(tok * j, tok), :] = kv_all[j // 2, j % 2, :, HD * k : HD * k + HD]
            v_heads[k, pl.ds(tok * j, tok), :] = kv_all[j // 2, j % 2, :, HD * (KV + k) : HD * (KV + k) + HD]

    def attend(k, carry):
        for g in range(groups):
            mine = pl.ds(tok * g, tok)
            score = dot_nt(q_heads[k, mine, :], k_heads[k]) + bias[...]
            expo = jnp.exp(score - jnp.max(score, axis=1, keepdims=True))
            p = (expo * (1.0 / jnp.sum(expo, axis=1, keepdims=True))).astype(BF)
            probs[k, mine, :] = p
            o_heads[k, mine, :] = dot_nn(p, v_heads[k])
        return carry

    net.finish(xs, *a, a2a_gu)
    tail.start()
    lax.fori_loop(0, 2, attend, 0)
    dn.step(2)
    gu[0].step(1)
    gs.pass_on()
    b.corner(2)
    lax.fori_loop(2, 4, attend, 0)
    dn.step(3)
    gu[0].step(2)
    gu[1].step(1)
    tail.pass_on()
    lax.fori_loop(4, 6, attend, 0)
    b.corner(3)
    b.take()
    tail.take()
    for j in range(H // 2):
        att_all[d, :, 128 * j : 128 * j + 128] = joined(o_heads, j, tok).astype(BF)
    full = att_all[d]
    branch = [dot_nn(full, wb[j]) for j in range(4)] + [dot_nn(full, wlast[...])]
    mid = x_in[0].astype(F32) + scale_attn * jnp.concatenate(branch, axis=1)
    middle[...] = mid
    mn_all[d] = (mid * norm_scale(mid)).astype(BF)
    ms.start()
    gu[0].step(3)
    gu[1].start(False)
    gs.take()
    dn.give(1)
    gu[0].give(1)
    dn.give(2)
    ms.pass_on()
    gu[1].step(2)
    gu[0].give(2)
    dn.give(3)
    gu[0].give(3)
    ms.take()
    gu[1].step(3)
    dn.take()
    gu[0].take()
    ats.start()
    net.finish(b, tail, kv, gs, *a2a_qkv)

    def by_cols(send, land, width):
        return [
            Spread(
                net,
                lambda j, n=n: send.at[j, :, pl.ds(width * n, width)],
                lambda j, n=n: land.at[j, :, pl.ds(width * n, width)],
            )
            for n in range(dim // width)
        ]

    gn, br, gx = by_cols(gn_send, gn_land, 384), by_cols(br_send, br_land, dim), by_cols(gx_send, gx_land, 384)
    wgu_flat, wd_flat = wgu.reshape(dim, 2 * hid), wd.reshape(hid, dim)
    other = 1 - c
    halves = [pl.ds(hid * h, hid) for h in range(2)]
    gu_pair = [ToMate(net, wgu.at[:, other, :, cols], gu_mate.at[:, :, cols]) for cols in halves]
    dn_pair = [ToMate(net, wd.at[2 * h : 2 * h + 2, other], dn_mate.at[2 * h : 2 * h + 2]) for h in range(2)]

    def add_dn(block, slot):
        wd[block, c] = (wd[block, c].astype(F32) + dn_zone[slot].astype(F32)).astype(BF)

    def half_sum(cols):
        def add(block, slot):
            wgu[block, c, :, cols] = (wgu[block, c, :, cols].astype(F32) + gu_zone[slot, :, cols].astype(F32)).astype(BF)

        return ChainSum(net, lambda zz: wgu.at[zz, c, :, cols], lambda k: gu_zone.at[k, :, cols], add)

    gu_sum = [half_sum(cols) for cols in halves]
    dn_sum = ChainSum(net, lambda zz: wd.at[zz, c], lambda k: dn_zone.at[k], add_dn)

    def pair_gu(h):
        gu_pair[h].take()
        cols = halves[h]
        for k in range(4):
            wgu[k, c, :, cols] = (wgu[k, c, :, cols].astype(F32) + gu_mate[k, :, cols].astype(F32)).astype(BF)
        gu_sum[h].stage(0)

    def branch_rows(h, downs):
        for n in range(3):
            cols = pl.ds(384 * n, 384)
            part = dot_nn(act[:, downs], wd_flat[downs, cols]).reshape(4, tok, 384)
            if h == 0:
                br_send[:, :, cols] = part.astype(BF)
            else:
                br_send[:, :, cols] = (br_send[:, :, cols].astype(F32) + part).astype(BF)
        turn_a[downs, :] = act[:, downs].T
        if h == 0:
            net.finish(dn)
        for n in range(3):
            cols = pl.ds(384 * n, 384)
            wd_flat[downs, cols] = dot_nn(turn_a[downs, :], gd_all[:, :, cols].reshape(span, 384)).astype(BF)
        dn_pair[h].start()

    def pair_dn(h):
        dn_pair[h].take()
        for k in (2 * h, 2 * h + 1):
            wd[k, c] = (wd[k, c].astype(F32) + dn_mate[k].astype(F32)).astype(BF)

    turn_x[...] = mn_all[...].reshape(span, dim).T
    for h in range(2):
        base = hid * h
        gates, ups, downs = pl.ds(base, quad), pl.ds(base + quad, quad), pl.ds(quad * h, quad)
        if h == 1:
            for k in (1, 2, 3):
                gu[1].give(k)
            gu[1].take()
        for pair in range(2):
            lines, two = pl.ds(2 * tok * pair, 2 * tok), slice(2 * pair, 2 * pair + 2)
            normed = mn_all[two].reshape(2 * tok, dim)
            gate = dot_nn(normed, wgu_flat[:, gates])
            up = dot_nn(normed, wgu_flat[:, ups])
            g_act = dot_nt(gd_all[two].reshape(2 * tok, dim), wd_flat[downs, :])
            sig = jax.nn.sigmoid(gate)
            swish = gate * sig
            act[lines, downs] = (swish * up).astype(BF)
            gboth[lines, gates] = (g_act * up * (sig * (1.0 + gate * (1.0 - sig)))).astype(BF)
            gboth[lines, ups] = (g_act * swish).astype(BF)
        if h == 0:
            branch_rows(h, downs)
        for n in range(3):
            cols = pl.ds(384 * n, 384)
            part = dot_nt(gboth[:, halves[h]], wgu_flat[cols, halves[h]]).reshape(4, tok, 384)
            if h == 0:
                gn_send[:, :, cols] = part.astype(BF)
                if n == 1:
                    pair_dn(h)
                    dn_sum.falling(0)
                    dn_sum.falling(1, True)
            else:
                gn_send[:, :, cols] = (gn_send[:, :, cols].astype(F32) + part).astype(BF)
                gn[n].start()

    def grads_gu(h):
        net.finish(gu[h])
        for base in (hid * h, hid * h + quad):
            cols = pl.ds(base, quad)
            wgu_flat[:, cols] = dot_nn(turn_x[...], gboth[:, cols]).astype(BF)
        gu_pair[h].start()

    grads_gu(0)
    branch_rows(1, pl.ds(quad, quad))
    pair_gu(0)
    grads_gu(1)
    pair_dn(1)
    dn_sum.rising(0)
    dn_sum.falling(1, False)
    pair_gu(1)
    gu_sum[0].stage(1)

    for n in range(3):
        gn[n].take()
    mid = middle[...]
    g_mid = cot_in[0].astype(F32) + norm_pull(plane_sum(net, gn_send, gn_land), mid)
    gmid[...] = g_mid
    gba = (scale_attn * g_mid).astype(BF)
    for j in range(4):
        cut_send[j, :, 512:768] = gba[:, 256 * j : 256 * j + 256]
    cut_send[3, :, 384:512] = gba[:, 1024:1152]
    cut = lambda cols: Spread(net, lambda j: cut_send.at[j, :, cols], lambda j: cut_land.at[j, :, cols])
    cut_o, cut_q, cut_l = cut(pl.ds(512, 256)), cut(pl.ds(0, 256)), cut(pl.ds(256, 256))
    cut_o.start()
    ats.pass_on()
    cut_land[d, :, 512:768] = cut_send[d, :, 512:768]
    g_att = dot_nt(gba[:, 1024:1152], wlast[...])
    for j in range(4):
        g_att = g_att + dot_nt(gba[:, 256 * j : 256 * j + 256], wb[j])
    for h in range(H):
        do_heads[h // groups, tok * (h % groups) : tok * (h % groups) + tok, :] = g_att[:, HD * h : HD * h + HD].astype(BF)

    dn_sum.falling(2, False)
    dn_sum.rising(1)

    kv_pair = [ToMate(net, dkv.at[n, :, other], kv_mate.at[n]) for n in range(2)]

    def kv_total(n):
        def add(block):
            dkv[n, block, c] = (dkv[n, block, c].astype(F32) + kv_zone[n, block].astype(F32)).astype(BF)

        return DownSum(net, lambda zz: dkv.at[n, zz, c], lambda k: kv_zone.at[n, k], add)

    kv_sum = [kv_total(n) for n in range(2)]

    def pull(k, carry):
        for g in range(groups):
            mine = pl.ds(tok * g, tok)
            p = probs[k, mine, :].astype(F32)
            t = p * dot_nt(do_heads[k, mine, :], v_heads[k])
            ds = (t - p * jnp.sum(t, axis=1, keepdims=True)).astype(BF)
            gs_heads[mine, :length] = ds
            o_heads[k, mine, :] = dot_nn(ds, k_heads[k]) * eighth
        half, kk = lax.div(k, 3), lax.rem(k, 3)
        for i, (left, right) in enumerate(((q_heads[k], gs_heads[: groups * tok, :length]), (do_heads[k], probs[k]))):
            turned_grad = dot_tn(left, right).astype(BF)
            at = pl.ds(pl.multiple_of(192 * i + HD * kk, HD), HD)
            for j in range(8):
                dkv[half, j // 2, j % 2, at, :] = turned_grad[:, tok * j : tok * j + tok]
        return carry

    def pair_sum(n):
        kv_pair[n].take()
        for k in range(4):
            dkv[n, k, c] = (dkv[n, k, c].astype(F32) + kv_mate[n, k].astype(F32)).astype(BF)
        kv_sum[n].start()

    def grads(p, parts):
        at = 0
        for part in parts:
            wb[p, :, at : at + part.shape[1]] = part.astype(BF)
            at += part.shape[1]
        pair = ToMate(net, m_att.at[p, :, other, :, quarter], ma_mate.at[p])
        pair.start()
        return pair

    def grads_pair(p, pair):
        pair.take()
        for k in range(4):
            m_att[p, k, c, :, quarter] = (m_att[p, k, c, :, quarter].astype(F32) + ma_mate[p, k].astype(F32)).astype(BF)

    def grads_chain(p, pair):
        def add(block, slot):
            m_att[p, block, c, :, quarter] = (
                m_att[p, block, c, :, quarter].astype(F32) + ma_zone[p, slot].astype(F32)
            ).astype(BF)

        grads_pair(p, pair)
        out = ChainSum(net, lambda zz: m_att.at[p, zz, c, :, quarter], lambda k: ma_zone.at[p, k], add)
        out.stage(0)
        return out

    def grads_straight(p, pair):
        grads_pair(p, pair)
        out = ToOwners(net, lambda zz: m_att.at[p, zz, c, :, quarter], lambda k: ma_zone.at[p, k])
        out.start()
        return out

    def grads_back(p, out):
        cols = pl.ds(256 * p, 256)
        if isinstance(out, ChainSum):
            out.own()
            total = m_att[p, z, c, :, quarter].astype(F32)
        else:
            out.take()
            total = m_att[p, z, c, :, quarter].astype(F32)
            for k in range(3):
                total = total + ma_zone[p, k].astype(F32)
        unsettle(total, wide, att_land, rows, cols)
        spread = Spread(net, lambda j: att_land.at[j, :, cols], lambda j: back_att.at[j, :, cols])
        spread.start()
        back_att[d, :, cols] = att_land[d, :, cols]
        return spread

    q_cols, l_cols, o_cols = pl.ds(0, 256), pl.ds(256, 256), pl.ds(512, 256)
    quarter = pl.ds(0, 256)
    lax.fori_loop(0, 3, pull, 0)
    kv_pair[0].start()
    lax.fori_loop(3, 4, pull, 0)
    pair_sum(0)
    lax.fori_loop(4, 6, pull, 0)
    kv_pair[1].start()
    for t in range(9):
        j, col = (t // 2, (t % 2) * 128) if t < 8 else (2, 384)
        cut_send[j, :, col : col + 128] = turned(joined(o_heads, t, tok), cosine, -sine).astype(BF)
    cut_q.start()
    br[0].start()
    cut_land[d, :, q_cols] = cut_send[d, :, q_cols]
    pair_sum(1)
    ats.take()
    cut_o.take()
    turn_x[...] = att_all[...].reshape(span, dim).T
    pair_o = grads(2, [dot_nn(turn_x[...], cut_land[:, :, o_cols].reshape(span, 256))])
    turn_n[...] = xn_all[...].reshape(span, dim).T
    dn_sum.rising(2, False)
    gu_sum[0].rising(2, False)
    for n in range(2):
        kv_sum[n].relay(0)
        kv_sum[n].relay(1)
    cut_q.take()
    pair_q = grads(0, [dot_nn(turn_n[...], cut_land[:, :, q_cols].reshape(span, 256))])
    gu_sum[1].stage(1)
    sum_o = grads_chain(2, pair_o)
    sum_q = grads_chain(0, pair_q)
    gu_sum[0].falling(2, False)

    for n in range(2):
        kv_sum[n].own()
        kv_tot[n] = dkv[n, z, c].astype(F32)
    keys = jnp.concatenate([kv_tot[0, :192, :], kv_tot[1, :192, :]], axis=0).T
    vals = jnp.concatenate([kv_tot[0, 192:, :], kv_tot[1, 192:, :]], axis=0).T
    late = [turned(keys[:, 128 * i : 128 * i + 128], cosine, -sine) for i in range(3)] + [vals[:, 128 * i : 128 * i + 128] for i in range(3)]
    for tile, (j, col) in zip(late, places):
        cut_send[j, :, col : col + 128] = tile.astype(BF)
    cut_l.start()
    cut_land[d, :, l_cols] = cut_send[d, :, l_cols]
    sum_o.stage(1)
    sum_q.stage(1)
    gu_sum[1].between(2)
    gu_sum[0].last()
    gu_sum[1].last()
    cut_l.take()
    last = cut_land[:, :, 384:512].reshape(span, 128)
    cuts = cut_land[:, :, :512].reshape(span, 512)
    lane = lax.broadcasted_iota(jnp.int32, cuts.shape, 1)
    cuts = jnp.where((d == 3) & (lane >= 384), jnp.zeros_like(cuts), cuts)
    for n in range(3):
        part = dot_nt(cuts, wa[384 * n : 384 * n + 384, :]).astype(BF)
        gx_send[:, :, 384 * n : 384 * n + 384] = part.reshape(4, tok, 384)
        gx[n].start()
    second = jnp.where(d == 3, dot_nn(turn_x[...], last), dot_nn(turn_n[...], last))
    pair_l = grads(1, [dot_nn(turn_n[...], cut_land[:, :, 256:384].reshape(span, 128)), second])
    sum_l = grads_straight(1, pair_l)
    br[0].take()
    block_out[0] = (middle[...] + scale_mlp * plane_sum(net, br_send, br_land)).astype(BF)
    sum_o.stage(2)
    sum_q.stage(2)
    dn_sum.last()
    for k in range(2):
        gu_sum[k].own()
        unsettle(wgu[z, c, :, halves[k]].astype(F32), wide, gu_land, rows, halves[k])
    back_g = Spread(net, lambda j: gu_land.at[j], lambda j: back_gu.at[j])
    back_g.start()
    back_gu[d] = gu_land[d]
    back_o = grads_back(2, sum_o)
    back_l = grads_back(1, sum_l)
    back_q = grads_back(0, sum_q)
    dn_sum.own()
    back_down[...] = wd[z, c]
    for n in range(3):
        gx[n].take()
    input_grad[0] = gmid[...] + norm_pull(plane_sum(net, gx_send, gx_land), x_in[0].astype(F32))
    for spread in (back_o, back_q, back_g, back_l):
        spread.take()
    net.finish()


def layer(x, cot, weights, down, gains, doc_starts, keep_mask, keep_rate, seq_order):
    tok, dim = x.shape[1:]
    ns = 8
    length = tok * ns
    ffr = down.shape[0]
    hid = ffr * ns
    blk = dim // ns
    span = 4 * tok
    vm = pl.BlockSpec(memory_space=pltpu.VMEM)
    sm = pl.BlockSpec(memory_space=pltpu.SMEM)
    padded = blk // 4 + -(blk // 4) % 16
    att_pack, gu_pack = ((4, padded, 768), BF), ((4, padded, 2 * hid), BF)
    outs = [((1, tok, dim), BF), ((1, tok, dim), F32), gu_pack, att_pack, (down.shape, BF)]
    plane = ((4, tok, dim), BF)
    wide_cut = ((4, tok, 512), BF)
    three = ((KV, 3 * tok, HD), BF)
    scratch = [
        att_pack,
        gu_pack,
        ((blk, hid), F32),
        wide_cut,
        ((4, 2, tok, 2 * KV * HD), BF),
        ((KV, 3 * tok, HD), F32),
        ((tok, length), F32),
        ((dim, 512), BF),
        ((4, dim, 256), BF),
        ((dim, 128), BF),
        ((4, 2, blk, 2 * hid), BF),
        ((4, 2, ffr, dim), BF),
        plane,
        plane,
        plane,
        plane,
        three,
        ((KV, length, HD), BF),
        ((KV, length, HD), BF),
        ((KV, 3 * tok, length), BF),
        ((tok, dim), F32),
        ((span, hid), BF),
        ((span, 2 * hid), BF),
        ((dim, span), BF),
        ((dim, span), BF),
        ((hid, span), BF),
        plane,
        plane,
        plane,
        plane,
        ((4, blk, 2 * hid), BF),
        ((5, blk, 2 * hid), BF),
        ((4, ffr, dim), BF),
        ((5, ffr, dim), BF),
        ((tok, dim), F32),
        three,
        ((2, 4, 2, 384, tok), BF),
        ((2, 4, 384, tok), BF),
        ((2, 3, 384, tok), BF),
        ((2, 384, tok), F32),
        ((4, tok, 768), BF),
        ((3, 4, blk, 256), BF),
        ((3, 5, blk, 256), BF),
        plane,
    ]
    return pl.pallas_call(
        layer_kernel,
        out_shape=[jax.ShapeDtypeStruct(*o) for o in outs],
        in_specs=[vm] * 11 + [sm] * 4,
        out_specs=[vm] * len(outs),
        scratch_shapes=[pltpu.VMEM(*t) for t in scratch] + [pltpu.SemaphoreType.DMA((SENDS,)), pltpu.SemaphoreType.DMA((RECVS,))],
        compiler_params=pltpu.CompilerParams(collective_id=0, has_side_effects=True, vmem_limit_bytes=LIMIT),
        name="k_layer",
    )(x, cot, *weights, down, *gains, doc_starts, keep_mask, keep_rate, seq_order)


def grads_kernel(
    query, key_w, value, gate_w, up_w, gain_one, gain_two, block_in, input_in, back_gu, back_att, back_down,
    block_out, input_out, norm_one, g_query, g_key, g_value, g_output, norm_two, g_gate, g_up, g_down,
):
    rows, ffr = query.shape[0], back_down.shape[0]
    hid = 8 * ffr
    block_out[...] = block_in[...]
    input_out[...] = input_in[...]
    g_down[...] = back_down[...].astype(F32)
    gain = column(gain_one[...])
    total = jnp.zeros((rows, 128), F32)
    for j in range(4):
        for i, t in enumerate((2 * j, 2 * j + 1, LATE[j][0], LATE[j][1])):
            m = back_att[j, :rows, 128 * i : 128 * i + 128].astype(F32)
            if t is None:
                g_output[:, 1024:1152] = m
                continue
            w, g, t = (query, g_query, t) if t < 9 else (key_w, g_key, t - 9) if t < 12 else (value, g_value, t - 12)
            cols = slice(128 * t, 128 * t + 128)
            total = total + w[:, cols].astype(F32) * m
            g[:, cols] = m * gain
        g_output[:, 256 * j : 256 * j + 256] = back_att[j, :rows, 512:768].astype(F32)
    norm_one[...] = row_of(jnp.sum(total, axis=1, keepdims=True))
    gain = column(gain_two[...])
    total = jnp.zeros((rows, 4 * ffr), F32)
    for i, (w, g) in enumerate(((gate_w, g_gate), (up_w, g_up))):
        for k in range(8):
            at = hid * (k // 4) + 4 * ffr * i + ffr * (k % 4)
            m = jnp.concatenate([back_gu[j, :rows, at : at + ffr].astype(F32) for j in range(4)], axis=1)
            cols = slice(4 * ffr * k, 4 * ffr * k + 4 * ffr)
            total = total + w[:, cols].astype(F32) * m
            g[:, cols] = m * gain
    norm_two[...] = row_of(jnp.sum(total, axis=1, keepdims=True))


def gradients(query, key_w, value, output, gate_w, up_w, gains, results):
    block, grad, back_gu, back_att, back_down = results
    shapes = [grad.shape, gains[0].shape] + [w.shape for w in (query, key_w, value, output)]
    shapes += [gains[1].shape, gate_w.shape, up_w.shape, back_down.shape]
    vm = pl.BlockSpec(memory_space=pltpu.VMEM)
    return pl.pallas_call(
        grads_kernel,
        out_shape=[jax.ShapeDtypeStruct(block.shape, BF)] + [jax.ShapeDtypeStruct(t, F32) for t in shapes],
        in_specs=[vm] * 12,
        out_specs=[vm] * 11,
        name="k_grads",
    )(query, key_w, value, gate_w, up_w, *gains, block, grad, back_gu, back_att, back_down)


def shards_by_kernel(
    hidden_in,
    attn_norm,
    query_weight,
    key_weight,
    value_weight,
    output_weight,
    mlp_norm,
    gate_weight,
    up_weight,
    down_weight,
    cotangent,
    doc_starts,
    keep_mask,
    keep_rate,
    seq_order,
):
    rows = query_weight.shape[0]
    gains = (attn_norm.reshape(1, rows), mlp_norm.reshape(1, rows))
    weights = (query_weight, key_weight, value_weight, output_weight, gate_weight, up_weight)
    results = layer(
        hidden_in, cotangent, weights, down_weight, gains, doc_starts, keep_mask.reshape(-1), keep_rate, seq_order
    )
    outs = list(gradients(*weights, gains, results))
    outs[2], outs[7] = outs[2].reshape(rows), outs[7].reshape(rows)
    return tuple(outs)


def solution(mesh):
    placed = (
        P("dp", "seq", None),
        P(("seq", "dp")),
        P(("seq", "dp"), None),
        P(("seq", "dp"), None),
        P(("seq", "dp"), None),
        P(("seq", "dp"), None),
        P(("seq", "dp")),
        P(("seq", "dp"), None),
        P(("seq", "dp"), None),
        P(("seq", "dp"), None),
        P("dp", "seq", None),
        P(),
        P(),
        P(),
        P(),
    )
    fits = mesh.shape["seq"] == 8 and mesh.shape["dp"] == 4
    return jax.shard_map(
        shards_by_kernel if fits else shards,
        mesh=mesh,
        in_specs=placed,
        out_specs=(
            P("dp", "seq", None),
            P("dp", "seq", None),
            P(("seq", "dp")),
            P(("seq", "dp"), None),
            P(("seq", "dp"), None),
            P(("seq", "dp"), None),
            P(("seq", "dp"), None),
            P(("seq", "dp")),
            P(("seq", "dp"), None),
            P(("seq", "dp"), None),
            P(("seq", "dp"), None),
        ),
        check_vma=False,
    )
```

```python
import math

import jax
import jax.numpy as jnp
from jax import lax
from jax.experimental import pallas as pl
from jax.experimental.pallas import tpu as pltpu
from jax.sharding import PartitionSpec as P

H = 18
KV = 6
HD = 64


EPSILON = 1e-05
ROPE_BASE = 10000.0
MASKED = -1e30


def contract_rows(left_rows, right_rows):
    return lax.dot_general(
        left_rows, right_rows, (((0,), (0,)), ((), ())), preferred_element_type=jnp.float32
    )


def contract_cols(left_mat, right_mat):
    return lax.dot_general(
        left_mat, right_mat, (((1,), (1,)), ((), ())), preferred_element_type=jnp.float32
    )


def low(v):
    return v.astype(jnp.bfloat16)


def dot(a, b):
    return jnp.dot(a, b, preferred_element_type=jnp.float32)


def swap_halves(vectors):
    half = HD // 2
    return jnp.concatenate([vectors[..., half:], vectors[..., :half]], axis=-1)


def shards(
    hidden_in,
    attn_norm,
    query_weight,
    key_weight,
    value_weight,
    output_weight,
    mlp_norm,
    gate_weight,
    up_weight,
    down_weight,
    cotangent,
    doc_starts,
    keep_mask,
    keep_rate,
    seq_order,
):
    tok = hidden_in.shape[1]
    ns, nd = lax.axis_size("seq"), lax.axis_size("dp")
    length = tok * ns
    rows = query_weight.shape[0]
    ffr = down_weight.shape[0]
    dim = hidden_in.shape[2]
    groups = H // KV
    nq, nk = H * HD, KV * HD
    score_scale = 1.0 / math.sqrt(HD)
    me_s, me_d = lax.axis_index("seq"), lax.axis_index("dp")
    sample = jnp.sum(jnp.where(jnp.arange(nd) == me_d, seq_order, 0))
    pick = jnp.arange(nd) == sample
    doc_begin = jnp.sum(jnp.where(pick[:, None], doc_starts, 0), axis=0)
    keep_flags = jnp.sum(jnp.where(pick[:, None], keep_mask, 0), axis=0).astype(jnp.float32)
    attn_scale = keep_flags[0] / keep_rate[0]
    mlp_scale = keep_flags[1] / keep_rate[1]
    positions = me_s * tok + jnp.arange(tok)
    first = jnp.max(jnp.where(doc_begin[None, :] <= positions[:, None], doc_begin[None, :], 0), axis=1)
    gain_one, gain_two = attn_norm[:, None], mlp_norm[:, None]

    qkv_rows = low(jnp.concatenate([query_weight, key_weight, value_weight], axis=1).astype(jnp.float32) * gain_one)
    w_qkv = lax.all_gather(qkv_rows, ("seq", "dp"), axis=0, tiled=True)
    w_out = lax.all_gather(output_weight, ("seq", "dp"), axis=0, tiled=True)

    def split_hidden(w):
        w = low(w.astype(jnp.float32) * gain_two).reshape(rows, ns, nd, ffr)
        w = jnp.transpose(w, (0, 2, 1, 3)).reshape(rows, nd * ns * ffr)
        return w

    gu = jnp.concatenate(
        [split_hidden(gate_weight).reshape(rows, nd, -1), split_hidden(up_weight).reshape(rows, nd, -1)], axis=2
    )
    gu = lax.all_to_all(gu, "dp", split_axis=1, concat_axis=0, tiled=True).reshape(nd * rows, -1)
    w_gu = lax.all_gather(gu, "seq", axis=0, tiled=True)
    w_down = lax.all_gather(down_weight, "seq", axis=0, tiled=True)
    hid = w_down.shape[0]

    x = hidden_in[0].astype(jnp.float32)
    r_one = lax.rsqrt(jnp.mean(x * x, axis=-1, keepdims=True) + EPSILON)
    xn = low(x * r_one)
    qkv = dot(xn, w_qkv)
    inverse_freq = ROPE_BASE ** (-2.0 * jnp.arange(HD // 2, dtype=jnp.float32) / HD)
    angles = positions.astype(jnp.float32)[:, None] * inverse_freq[None, :]
    cosine = jnp.tile(jnp.cos(angles), (1, 2))[:, None, :]
    sine = jnp.concatenate([-jnp.sin(angles), jnp.sin(angles)], axis=1)[:, None, :]

    def turn(v):
        return v * cosine + swap_halves(v) * sine

    def turn_back(v):
        return v * cosine - swap_halves(v) * sine

    queries = low(turn(qkv[:, :nq].reshape(tok, H, HD))).reshape(tok, KV, groups, HD)
    keys = low(turn(qkv[:, nq : nq + nk].reshape(tok, KV, HD)))
    kv = jnp.concatenate([keys.reshape(tok, nk), low(qkv[:, nq + nk :])], axis=1)
    kv_all = lax.all_gather(kv, "seq", axis=0, tiled=True)
    k_all, v_all = kv_all[:, :nk].reshape(length, KV, HD), kv_all[:, nk:].reshape(length, KV, HD)
    key_pos = jnp.arange(length)
    allowed = (key_pos[None, :] <= positions[:, None]) & (key_pos[None, :] >= first[:, None])
    scores = jnp.einsum("tkgd,skd->kgts", queries, k_all, preferred_element_type=jnp.float32) * score_scale
    scores = jnp.where(allowed, scores, MASKED)
    expo = jnp.exp(scores - jnp.max(scores, axis=-1, keepdims=True))
    probs = low(expo / jnp.sum(expo, axis=-1, keepdims=True))
    attended = jnp.einsum("kgts,skd->tkgd", probs, v_all, preferred_element_type=jnp.float32)
    att = low(attended.reshape(tok, nq))
    middle = x + attn_scale * dot(att, w_out)
    r_two = lax.rsqrt(jnp.mean(middle * middle, axis=-1, keepdims=True) + EPSILON)
    mn = low(middle * r_two)

    cot = cotangent[0].astype(jnp.float32)
    side = lax.all_gather(jnp.concatenate([xn, low(mlp_scale * cot), att], axis=1), "dp", axis=0, tiled=True)
    xn_all, gd_all, att_all = side[:, :dim], side[:, dim : 2 * dim], side[:, 2 * dim :]
    mn_all = lax.all_gather(mn, "dp", axis=0, tiled=True)
    gate, up = dot(mn_all, w_gu[:, :hid]), dot(mn_all, w_gu[:, hid:])
    sig = jax.nn.sigmoid(gate)
    act_gate = gate * sig
    act = low(act_gate * up)
    g_act = contract_cols(gd_all, w_down)
    gg = low(g_act * up * (sig * (1.0 + gate * (1.0 - sig))))
    gu_in = low(g_act * act_gate)
    gboth = jnp.concatenate([gg, gu_in], axis=1)
    g_mn = lax.psum_scatter(low(contract_cols(gboth, w_gu)), "dp", scatter_dimension=0, tiled=True).astype(jnp.float32)
    branch = lax.psum_scatter(low(dot(act, w_down)), "dp", scatter_dimension=0, tiled=True).astype(jnp.float32)
    block_output = low(middle + mlp_scale * branch)[None]
    m_gu = lax.psum_scatter(low(contract_rows(mn_all, gboth)), "seq", scatter_dimension=0, tiled=True)
    m_down = lax.psum_scatter(low(contract_rows(act, gd_all)), "seq", scatter_dimension=0, tiled=True)

    def norm_back(e, v, r):
        return r * e - v * (r * r * r) * jnp.mean(e * v, axis=-1, keepdims=True)

    g_mid = cot + norm_back(g_mn, middle, r_two)
    gba = low(attn_scale * g_mid)
    g_att = low(contract_cols(gba, w_out)).reshape(tok, KV, groups, HD)
    g_probs = jnp.einsum("tkgd,skd->kgts", g_att, v_all, preferred_element_type=jnp.float32)
    delta = jnp.einsum("tkgd,tkgd->kgt", g_att.astype(jnp.float32), attended)
    g_scores = low(probs.astype(jnp.float32) * (g_probs - delta[..., None]))
    g_q = jnp.einsum("kgts,skd->tkgd", g_scores, k_all, preferred_element_type=jnp.float32) * score_scale
    g_k = jnp.einsum("kgts,tkgd->skd", g_scores, queries, preferred_element_type=jnp.float32) * score_scale
    g_v = jnp.einsum("kgts,tkgd->skd", probs, g_att, preferred_element_type=jnp.float32)
    g_kv = low(jnp.concatenate([g_k.reshape(length, nk), g_v.reshape(length, nk)], axis=1))
    g_kv = lax.psum_scatter(g_kv, "seq", scatter_dimension=0, tiled=True).astype(jnp.float32)
    g_q_in = low(turn_back(g_q.reshape(tok, H, HD))).reshape(tok, nq)
    g_k_in = low(turn_back(g_kv[:, :nk].reshape(tok, KV, HD))).reshape(tok, nk)
    g_qkv = jnp.concatenate([g_q_in, g_k_in, low(g_kv[:, nk:])], axis=1)
    g_xn = contract_cols(g_qkv, w_qkv)
    input_grad = (g_mid + norm_back(g_xn, x, r_one))[None]

    cut = jnp.concatenate([g_qkv.reshape(tok, nd, -1), gba.reshape(tok, nd, -1)], axis=2)
    wq = g_qkv.shape[1] // nd
    cut = lax.all_to_all(cut, "dp", split_axis=1, concat_axis=0, tiled=True).reshape(nd * tok, -1)
    m_att = jnp.concatenate([contract_rows(xn_all, cut[:, :wq]), contract_rows(att_all, cut[:, wq:])], axis=1)
    m_att = lax.psum_scatter(low(m_att), "seq", scatter_dimension=0, tiled=True)

    back = jnp.concatenate([m_gu, m_att], axis=1)
    back = lax.all_to_all(back.reshape(nd, rows, 1, -1), "dp", split_axis=0, concat_axis=2, tiled=True)
    back = back.reshape(rows, nd, -1).astype(jnp.float32)

    def whole_hidden(m):
        return jnp.transpose(m.reshape(rows, nd, ns, ffr), (0, 2, 1, 3)).reshape(rows, -1)

    m_gate, m_up = whole_hidden(back[:, :, :hid]), whole_hidden(back[:, :, hid : 2 * hid])
    m_qkv = back[:, :, 2 * hid : 2 * hid + wq].reshape(rows, -1)
    g_out = back[:, :, 2 * hid + wq :].reshape(rows, -1)

    def weigh(w, m):
        return jnp.sum(w.astype(jnp.float32) * m, axis=1)

    m_q, m_k, m_v = m_qkv[:, :nq], m_qkv[:, nq : nq + nk], m_qkv[:, nq + nk :]
    g_norm_one = weigh(query_weight, m_q) + weigh(key_weight, m_k) + weigh(value_weight, m_v)
    g_norm_two = weigh(gate_weight, m_gate) + weigh(up_weight, m_up)
    return (
        block_output,
        input_grad,
        g_norm_one,
        m_q * gain_one,
        m_k * gain_one,
        m_v * gain_one,
        g_out,
        g_norm_two,
        m_gate * gain_two,
        m_up * gain_two,
        m_down.astype(jnp.float32),
    )


MESH = pl.DeviceIdType.MESH
LIMIT = 60 * 2**20
SENDS, RECVS = 92, 204
BF, F32 = jnp.bfloat16, jnp.float32


def dot_nn(a, b):
    return lax.dot_general(a, b, (((1,), (0,)), ((), ())), preferred_element_type=F32)


def dot_nt(a, b):
    return lax.dot_general(a, b, (((1,), (1,)), ((), ())), preferred_element_type=F32)


def dot_tn(a, b):
    return lax.dot_general(a, b, (((0,), (0,)), ((), ())), preferred_element_type=F32)


class Net:
    def __init__(self, sends, recvs):
        self.sends, self.recvs, self.open, self.used = sends, recvs, [], 0
        self.free = list(range(sends.shape[0]))
        self.s, self.d = lax.axis_index("seq"), lax.axis_index("dp")
        self.z, self.c = lax.div(self.s, 2), lax.rem(self.s, 2)
        y, x = lax.div(self.d, 2), lax.rem(self.d, 2)
        self.plane = (y * 2 + 1 - x, (1 - y) * 2 + x, 3 - self.d)
        self.mate = self.at(self.z, 1 - self.c)

    def room(self, count):
        base = self.used
        self.used += count
        return base

    def at(self, z, core):
        return {"seq": z * 2 + core, "dp": self.d}

    def across(self, kind):
        return {"seq": self.s, "dp": self.plane[kind]}

    def greet(self):
        barrier = pltpu.get_barrier_semaphore()
        peers = [self.mate] + [self.across(k) for k in range(3)]
        peers += [self.at(lax.rem(self.z + k, 4), self.c) for k in (1, 2, 3)]
        for peer in peers:
            pl.semaphore_signal(barrier, inc=1, device_id=peer, device_id_type=MESH)

    def greeted(self):
        pl.semaphore_wait(pltpu.get_barrier_semaphore(), 7)

    def copy(self, src, dst, send, recv, peer):
        return pltpu.make_async_remote_copy(
            src_ref=src,
            dst_ref=dst,
            send_sem=self.sends.at[send],
            recv_sem=self.recvs.at[recv],
            device_id=peer,
            device_id_type=MESH,
        )

    def push(self, owner, src, dst, recv, peer, when=None):
        send = self.free.pop(0)
        copy = self.copy(src, dst, send, recv, peer)
        if when is None:
            copy.start()
        else:
            pl.when(when)(copy.start)
        self.open.append((copy, when, owner, send))

    def arrive(self, dst, recv, when=None):
        copy = self.copy(dst, dst, 0, recv, self.mate)
        if when is None:
            copy.wait_recv()
        else:
            pl.when(when)(copy.wait_recv)

    def finish(self, *owners):
        kept = []
        for entry in self.open:
            copy, when, owner, send = entry
            if owners and owner not in owners:
                kept.append(entry)
                continue
            if when is None:
                copy.wait_send()
            else:
                pl.when(when)(copy.wait_send)
            self.free.append(send)
        self.open = kept

    def order(self, step):
        if step == 0:
            return self.z
        table = ((1, 0, 3, 2), (2, 2, 1, 1), (3, 3, 0, 0))[step - 1]
        z = self.z
        return jnp.where(z == 0, table[0], jnp.where(z == 1, table[1], jnp.where(z == 2, table[2], table[3])))


class Chain:
    def __init__(self, net, block, room=4):
        self.net, self.block, self.base = net, block, net.room(room)

    def start(self):
        net = self.net
        own = self.block(net.z, net.c)
        net.push(self, own, own, self.base + net.z, net.at(net.z + 1, net.c), net.z < 3)
        net.push(self, own, own, self.base + net.z, net.at(net.z - 1, net.c), net.z > 0)

    def step(self, k):
        net = self.net
        b = net.order(k)
        block = self.block(b, net.c)
        net.arrive(block, self.base + b)
        to = jnp.where(b < net.z, net.z + 1, net.z - 1)
        net.push(self, block, block, self.base + b, net.at(to, net.c), (to >= 0) & (to <= 3))


class Lines(Chain):
    def __init__(self, net, block):
        super().__init__(net, block, 8)

    def start(self, ends=None):
        net = self.net
        own = self.block(net.z, net.c)
        up, down, any_z = net.z < 3, net.z > 0, None
        if ends is not None:
            any_z = (net.z == 0) | (net.z == 3)
            any_z = any_z if ends else jnp.logical_not(any_z)
            up, down = up & any_z, down & any_z
        net.push(self, own, own, self.base + net.z, net.at(net.z + 1, net.c), up)
        net.push(self, own, own, self.base + net.z, net.at(net.z - 1, net.c), down)
        net.push(self, own, own, self.base + 4 + net.z, net.mate, any_z)

    def onward(self, b):
        to = jnp.where(b < self.net.z, self.net.z + 1, self.net.z - 1)
        return to, (to >= 0) & (to <= 3)

    def step(self, k):
        net = self.net
        b = net.order(k)
        block = self.block(b, net.c)
        to, on = self.onward(b)
        net.arrive(block, self.base + b, on)
        net.push(self, block, block, self.base + b, net.at(to, net.c), on)

    def give(self, k):
        net = self.net
        b = net.order(k)
        block = self.block(b, net.c)
        if k:
            net.arrive(block, self.base + b, jnp.logical_not(self.onward(b)[1]))
        net.push(self, block, block, self.base + 4 + b, net.mate)

    def take(self):
        net = self.net
        for b in range(4):
            net.arrive(self.block(b, 1 - net.c), self.base + 4 + b)


class FromLast:
    def __init__(self, net, source, full):
        self.net, self.source, self.full, self.base = net, source, full, net.room(2)

    def start(self):
        net = self.net
        for kind in range(3):
            part = self.full.at[:, net.c]
            net.push(self, self.source.at[:, net.c, :, pl.ds(384, 128)], part, self.base, net.across(kind), net.d == 3)

        @pl.when(net.d == 3)
        def _():
            self.full[...] = self.source[:, :, :, 384:512]

    def pass_on(self):
        net = self.net
        part = self.full.at[:, net.c]
        net.arrive(part, self.base, net.d < 3)
        net.push(self, part, part, self.base + 1, net.mate, net.d < 3)

    def take(self):
        self.net.arrive(self.full.at[:, 1 - self.net.c], self.base + 1, self.net.d < 3)


class Rising(Lines):
    def start(self):
        net = self.net
        own = self.block(net.z, net.c)
        net.push(self, own, own, self.base + net.z, net.at(net.z + 1, net.c), net.z < 3)
        net.push(self, own, own, self.base + 4 + net.z, net.mate)

    def step(self, k):
        net = self.net
        b = jnp.maximum(net.z - k, 0)
        block = self.block(b, net.c)
        net.arrive(block, self.base + b, net.z >= k)
        net.push(self, block, block, self.base + b, net.at(net.z + 1, net.c), (net.z >= k) & (net.z < 3))
        net.push(self, block, block, self.base + 4 + b, net.mate, net.z >= k)

    def take(self):
        net = self.net
        for b in range(4):
            net.arrive(self.block(b, 1 - net.c), self.base + 4 + b, net.z >= b)


class Slices(Chain):
    def __init__(self, net, full, rows):
        self.full, self.rows, self.half = full, rows, rows // 32 * 16
        super().__init__(net, lambda z, core: self.part(net.d, z, core), 36)

    def part(self, slot, z, core, half=None):
        first = pl.multiple_of((z * 2 + core) * self.rows, 16)
        if half is None:
            return self.full.at[slot, pl.ds(first, self.rows)]
        if half == 0:
            return self.full.at[slot, pl.ds(first, self.half)]
        return self.full.at[slot, pl.ds(pl.multiple_of(first + self.half, 16), self.rows - self.half)]

    def spread(self, k):
        net = self.net
        b = net.order(k)
        block = self.part(net.d, b, net.c)
        net.push(self, block, block, self.base + 4 + b, net.across(0))
        net.push(self, block, block, self.base + 8 + b, net.across(1))
        net.push(self, block, block, self.base + 20 + b, net.mate)

    def pass_on(self, k):
        net = self.net
        b = net.order(k)
        for kind in (0, 1):
            block = self.part(net.plane[kind], b, net.c)
            net.arrive(block, self.base + 4 + 4 * kind + b)
            half = self.part(net.plane[kind], b, net.c, kind)
            net.push(self, half, half, self.base + 12 + 4 * kind + b, net.across(1 - kind))
            net.push(self, block, block, self.base + 24 + 4 * kind + b, net.mate)

    def corner(self, k):
        net = self.net
        b = net.order(k)
        for kind in (0, 1):
            half = self.part(net.plane[2], b, net.c, kind)
            net.arrive(half, self.base + 12 + 4 * kind + b)
        block = self.part(net.plane[2], b, net.c)
        net.push(self, block, block, self.base + 32 + b, net.mate)

    def take(self):
        net = self.net
        for b in range(4):
            net.arrive(self.part(net.d, b, 1 - net.c), self.base + 20 + b)
            for kind in range(3):
                net.arrive(self.part(net.plane[kind], b, 1 - net.c), self.base + 24 + 4 * kind + b)


class Plane:
    def __init__(self, net, full):
        self.net, self.full, self.base = net, full, net.room(4)
        self.half = full.shape[1] // 2

    def start(self):
        net = self.net
        own = self.full.at[net.d]
        for kind in (0, 1):
            net.push(self, own, own, self.base + kind, net.across(kind))

    def pass_on(self):
        net = self.net
        for kind in (0, 1):
            net.arrive(self.full.at[net.plane[kind]], self.base + kind)
            half = self.full.at[net.plane[kind], pl.ds(kind * self.half, self.half)]
            net.push(self, half, half, self.base + 2 + kind, net.across(1 - kind))

    def take(self):
        net = self.net
        for kind in (0, 1):
            net.arrive(self.full.at[net.plane[2], pl.ds(kind * self.half, self.half)], self.base + 2 + kind)


class Spread:
    def __init__(self, net, send, land):
        self.net, self.send, self.land, self.base = net, send, land, net.room(3)

    def start(self):
        net = self.net
        for kind in (2, 0, 1):
            net.push(self, self.send(net.plane[kind]), self.land(net.d), self.base + kind, net.across(kind))

    def take(self):
        for kind in range(3):
            self.net.arrive(self.land(self.net.plane[kind]), self.base + kind)


class ToMate:
    def __init__(self, net, send, land):
        self.net, self.send, self.land, self.base = net, send, land, net.room(1)

    def start(self):
        self.net.push(self, self.send, self.land, self.base, self.net.mate)

    def take(self):
        self.net.arrive(self.land, self.base)


class ToOwners:
    def __init__(self, net, part, land, down=False):
        self.net, self.part, self.land, self.down, self.base = net, part, land, down, net.room(3)

    def start(self):
        net = self.net
        for k in (3, 2, 1):
            to = lax.rem(net.z - k + 4, 4)
            net.push(self, self.part(to), self.land(k - 1), self.base + k - 1, net.at(to, net.c), (net.z >= k) if self.down else None)

    def take(self):
        net = self.net
        for k in (1, 2, 3):
            net.arrive(self.land(k - 1), self.base + k - 1, (net.z + k <= 3) if self.down else None)


class DownSum:
    def __init__(self, net, part, land, add):
        self.net, self.part, self.land, self.add, self.base = net, part, land, add, net.room(3)

    def send(self, b, when):
        net = self.net
        net.push(self, self.part(b), self.land(b), self.base + b, net.at(net.z - 1, net.c), when)

    def start(self):
        for b in range(3):
            self.send(b, self.net.z == 3)

    def relay(self, b):
        net = self.net
        on = (net.z > b) & (net.z < 3)

        @pl.when(on)
        def _():
            net.arrive(self.land(b), self.base + b)
            self.add(b)

        self.send(b, on)

    def own(self):
        net = self.net
        for b in range(3):

            @pl.when(net.z == b)
            def _(b=b):
                net.arrive(self.land(b), self.base + b)
                self.add(b)


class ChainSum:
    def __init__(self, net, part, land, add):
        self.net, self.part, self.land, self.add, self.base = net, part, land, add, net.room(6)

    def stage(self, k):
        self.falling(k)
        self.rising(k)

    def falling(self, k, top=None):
        net, z = self.net, self.net.z
        i = k - 3 + z
        valid = (i >= 0) & (i < z)
        if top is not None:
            valid = valid & ((z == 3) if top else (z < 3))
        i = jnp.clip(i, 0, 3)

        @pl.when(valid & (z < 3))
        def _():
            net.arrive(self.land(i), self.base + i)
            self.add(i, i)

        net.push(self, self.part(i), self.land(i), self.base + i, net.at(z - 1, net.c), valid)

    def last(self):
        self.falling(2, True)
        self.rising(2, True)

    def between(self, k):
        self.falling(k, False)
        self.rising(k, False)

    def rising(self, k, end=None):
        net, z = self.net, self.net.z
        j = k - z
        valid = (j >= 0) & (3 - j > z)
        if end is not None:
            valid = valid & ((z == 0) if end else (z > 0))
        j = jnp.clip(j, 0, 3)

        @pl.when(valid & (z > 0))
        def _():
            net.arrive(self.land(4 - j), self.base + 3 + j)
            self.add(3 - j, 4 - j)

        net.push(self, self.part(3 - j), self.land(4 - j), self.base + 3 + j, net.at(z + 1, net.c), valid)

    def own(self):
        net, z = self.net, self.net.z

        @pl.when(z < 3)
        def _():
            net.arrive(self.land(z), self.base + z)
            self.add(z, z)

        @pl.when(z > 0)
        def _():
            net.arrive(self.land(1 + z), self.base + 6 - z)
            self.add(z, 1 + z)


def settle(land, wide, rows, cols=slice(None)):
    for j in range(4):
        wide[pl.ds(j * rows, rows), :] = land[j, :rows, cols].astype(F32)
    return wide[...].astype(BF)


def unsettle(block, wide, land, rows, cols):
    wide[:, : block.shape[1]] = block
    for j in range(4):
        land[j, :rows, cols] = wide[pl.ds(j * rows, rows), : block.shape[1]].astype(BF)


def turned(tile, cosine, sine):
    lane = lax.broadcasted_iota(jnp.int32, tile.shape, 1)
    other = jnp.where(lax.rem(lane, HD) < HD // 2, pltpu.roll(tile, 128 - HD // 2, 1), pltpu.roll(tile, HD // 2, 1))
    return tile * cosine + other * sine


def own_rows(index, rows):
    return pl.ds(pl.multiple_of(index * rows, 16), rows)


def norm_scale(v):
    return lax.rsqrt(jnp.mean(v * v, axis=1, keepdims=True) + EPSILON)


def norm_pull(e, v):
    r = norm_scale(v)
    return r * e - v * (r * r * r) * jnp.mean(e * v, axis=1, keepdims=True)


def joined(heads, j, tok):
    groups = H // KV
    pair = [heads[h // groups, tok * (h % groups) : tok * (h % groups) + tok, :] for h in (2 * j, 2 * j + 1)]
    return jnp.concatenate(pair, axis=1)


def plane_sum(net, send, land):
    total = send[net.d].astype(F32)
    for kind in range(3):
        total = total + land[net.plane[kind]].astype(F32)
    return total


LATE = ((9, 10), (11, 12), (13, 8), (14, None))


def column(row):
    n = row.shape[1]
    same = lax.broadcasted_iota(jnp.int32, (n, n), 0) == lax.broadcasted_iota(jnp.int32, (n, n), 1)
    return jnp.sum(jnp.where(same, row, 0.0), axis=1, keepdims=True)


def row_of(col):
    n = col.shape[0]
    same = lax.broadcasted_iota(jnp.int32, (n, n), 0) == lax.broadcasted_iota(jnp.int32, (n, n), 1)
    return jnp.sum(jnp.where(same, col, 0.0), axis=0, keepdims=True)


def layer_kernel(
    x_in, cot_in, query, key_w, value, output, gate_w, up_w, down, gain_one, gain_two,
    doc_starts, keep_mask, keep_rate, seq_order,
    block_out, input_grad, back_gu, back_att, back_down,
    att_land, gu_land, wide, qkv_land, kv_all, o_heads, bias, wa, wb, wlast, wgu, wd,
    xn_all, gd_all, mn_all, att_all, q_heads, k_heads, v_heads, probs, middle, act, gboth, turn_x, turn_n, turn_a,
    gn_send, gn_land, br_send, br_land, gu_mate, gu_zone, dn_mate, dn_zone, gmid, do_heads, dkv, kv_mate, kv_zone, kv_tot,
    cut_land, ma_mate, ma_zone, gx_land, sends, recvs,
):
    net = Net(sends, recvs)
    tok, dim = x_in.shape[1], x_in.shape[2]
    rows = dim // 32
    blk = 4 * rows
    ffr = down.shape[0]
    hid, quad = 8 * ffr, 4 * ffr
    d, z, c, s = net.d, net.z, net.c, net.s
    span, length = 4 * tok, 8 * tok
    groups = H // KV
    padded = att_land.shape[1]
    att_send = qkv_send = cut_send = act.reshape(4, tok, hid)
    gu_send = gboth.reshape(4, tok, 2 * hid)
    gx_send, gs_heads = gd_all, gboth
    m_att = wb.reshape(4, 4, 2, blk, 256)

    first_cols, late_cols = pl.ds(0, 256), pl.ds(256, 256)
    a2a_att = Spread(net, lambda j: att_send.at[j, pl.ds(0, padded)], lambda j: att_land.at[j])
    a2a_gu = Spread(net, lambda j: gu_send.at[j, pl.ds(0, padded)], lambda j: gu_land.at[j])
    a2a_qkv = [
        Spread(net, lambda j, cols=cols: qkv_send.at[j, :, cols], lambda j, cols=cols: qkv_land.at[j, :, cols])
        for cols in (late_cols, first_cols)
    ]
    a = [Lines(net, lambda zz, core, cols=cols: wa.at[own_rows(zz * 2 + core, blk), cols]) for cols in (late_cols, first_cols)]
    b = Slices(net, wb, blk)
    tail = FromLast(net, wa.reshape(4, 2, blk, 512), wlast.reshape(4, 2, blk, 128))
    gu = [Lines(net, lambda zz, core, h=h: wgu.at[zz, core, :, pl.ds(hid * h, hid)]) for h in range(2)]
    dn = Lines(net, lambda zz, core: wd.at[zz, core])
    kv = Rising(net, lambda zz, core: kv_all.at[zz, core])
    xs = Plane(net, xn_all)
    gs = Plane(net, gd_all)
    ms = Plane(net, mn_all)
    ats = Plane(net, att_all)

    kv_all[...] = jnp.zeros_like(kv_all)
    net.greet()
    first_gain = column(gain_one[...])
    zero = jnp.zeros((padded - rows, 128), BF)
    weights = (query, key_w, value)

    def qkv_tile(t):
        ref, t = (query, t) if t < 9 else (key_w, t - 9) if t < 12 else (value, t - 12)
        return (ref[:, 128 * t : 128 * t + 128].astype(F32) * first_gain).astype(BF)

    for j in range(4):
        tiles = [qkv_tile(2 * j), qkv_tile(2 * j + 1), qkv_tile(LATE[j][0])]
        tiles.append(output[:, 1024:1152] if LATE[j][1] is None else qkv_tile(LATE[j][1]))
        tiles += [output[:, 256 * j : 256 * j + 128], output[:, 256 * j + 128 : 256 * j + 256]]
        for i, tile in enumerate(tiles):
            att_send[j, :rows, 128 * i : 128 * i + 128] = tile
            att_send[j, rows:padded, 128 * i : 128 * i + 128] = zero
    net.greeted()
    a2a_att.start()
    att_land[d] = att_send[d, :padded, :]
    x = x_in[0].astype(F32)
    xn_all[d] = (x * norm_scale(x)).astype(BF)
    xs.start()
    second_gain = column(gain_two[...])
    for i, ref in enumerate((gate_w, up_w)):
        scaled = ref[...].astype(F32) * second_gain
        for j in range(4):
            for h in range(2):
                part = [scaled[:, ffr * (4 * k + j) : ffr * (4 * k + j) + ffr] for k in range(4 * h, 4 * h + 4)]
                cols = slice(hid * h + quad * i, hid * h + quad * i + quad)
                gu_send[j, :rows, cols] = jnp.concatenate(part, axis=1).astype(BF)
                gu_send[j, rows:padded, cols] = jnp.zeros((padded - rows, quad), BF)
    gu_land[d] = gu_send[d, :padded, :]
    sample = seq_order[d]
    scale_attn, scale_mlp = [
        jnp.full((1, 1), keep_mask[i, sample].astype(F32), F32) / jnp.full((1, 1), keep_rate[i], F32) for i in range(2)
    ]
    gd_all[d] = (cot_in[0].astype(F32) * scale_mlp).astype(BF)
    wd[z, c] = down[...]
    position = s * tok + lax.broadcasted_iota(jnp.int32, (tok, 1), 0)
    lane = lax.broadcasted_iota(jnp.int32, (tok, 128), 1)
    power = lax.rem(lane, HD // 2).astype(F32) * (-2.0 * math.log(ROPE_BASE) / HD)
    angle = position.astype(F32) * jnp.exp(power)
    cosine, sine = jnp.cos(angle), jnp.where(lax.rem(lane, HD) < HD // 2, -jnp.sin(angle), jnp.sin(angle))
    a2a_att.take()
    own = own_rows(s, blk)
    packed = settle(att_land, wide, rows)
    wa[own, :] = packed[:, :512]
    wb[d, own, :] = packed[:, 512:]
    for line in a:
        line.start()
    for k in (1, 2, 3):
        for line in a:
            line.step(k)
        for line in a:
            line.give(k)
        if k == 1:
            xs.pass_on()
            a2a_gu.start()
    b.start()
    dn.start()
    xs.take()
    a[0].take()

    eighth = 1.0 / math.sqrt(HD)

    def project(cols, kinds):
        part = dot_nn(xn_all[...].reshape(span, dim), wa[:, cols])
        for j in range(4):
            for i, kind in enumerate(kinds):
                tile = part[tok * j : tok * j + tok, 128 * i : 128 * i + 128]
                spun = turned(tile, cosine, sine)
                if kind == 1:
                    tile = jnp.where(d < 2, spun, tile)
                elif kind == 2:
                    tile = jnp.where(d == 0, spun, jnp.where(d == 2, spun * eighth, tile))
                else:
                    tile = spun * eighth
                qkv_send[j, :, pl.ds(cols.start + 128 * i, 128)] = tile.astype(BF)

    net.finish(a2a_att)
    project(late_cols, (1, 2))
    a2a_qkv[0].start()
    a[1].take()
    project(first_cols, (0, 0))
    a2a_qkv[1].start()
    qkv_land[d] = qkv_send[d, :, :512]
    b.spread(0)
    b.step(1)
    b.spread(1)
    a2a_qkv[0].take()
    places = [(0, 256), (0, 384), (1, 256), (1, 384), (2, 256), (3, 256)]
    for i, (j, col) in enumerate(places):
        kv_all[z, c, :, 128 * i : 128 * i + 128] = qkv_land[j, :, col : col + 128]
    kv.start()
    b.step(2)
    b.spread(2)
    a2a_gu.take()
    for h in range(2):
        wgu[z, c, :, hid * h : hid * h + hid] = settle(gu_land, wide, rows, slice(hid * h, hid * h + hid))
    b.step(3)
    b.spread(3)
    for half in gu:
        half.start(True)
    kv.step(1)
    b.pass_on(0)
    b.pass_on(1)
    a2a_qkv[1].take()
    gs.start()
    for t in range(9):
        j, col = (t // 2, (t % 2) * 128) if t < 8 else (2, 384)
        for h in (2 * t, 2 * t + 1):
            at = col + HD * (h % 2)
            q_heads[h // groups, tok * (h % groups) : tok * (h % groups) + tok, :] = qkv_land[j, :, at : at + HD]
    first = jnp.zeros((tok, 1), jnp.int32)
    for j in range(doc_starts.shape[1]):
        start = doc_starts[sample, j]
        first = jnp.where(position >= start, jnp.maximum(first, start), first)
    key = lax.broadcasted_iota(jnp.int32, bias.shape, 1)
    bias[...] = jnp.where((key <= position) & (key >= first), 0.0, MASKED)

    kv.step(2)
    gu[0].start(False)
    b.pass_on(2)
    b.pass_on(3)
    b.corner(0)
    b.corner(1)
    kv.step(3)
    dn.step(1)
    kv.take()
    for j in range(8):
        for k in range(KV):
            k_heads[k, pl.ds(tok * j, tok), :] = kv_all[j // 2, j % 2, :, HD * k : HD * k + HD]
            v_heads[k, pl.ds(tok * j, tok), :] = kv_all[j // 2, j % 2, :, HD * (KV + k) : HD * (KV + k) + HD]

    def attend(k, carry):
        for g in range(groups):
            mine = pl.ds(tok * g, tok)
            score = dot_nt(q_heads[k, mine, :], k_heads[k]) + bias[...]
            expo = jnp.exp(score - jnp.max(score, axis=1, keepdims=True))
            p = (expo * (1.0 / jnp.sum(expo, axis=1, keepdims=True))).astype(BF)
            probs[k, mine, :] = p
            o_heads[k, mine, :] = dot_nn(p, v_heads[k])
        return carry

    net.finish(xs, *a, a2a_gu)
    tail.start()
    lax.fori_loop(0, 2, attend, 0)
    dn.step(2)
    gu[0].step(1)
    gs.pass_on()
    b.corner(2)
    lax.fori_loop(2, 4, attend, 0)
    dn.step(3)
    gu[0].step(2)
    gu[1].step(1)
    tail.pass_on()
    lax.fori_loop(4, 6, attend, 0)
    b.corner(3)
    b.take()
    tail.take()
    net.finish(b, tail, kv, *a2a_qkv)
    for j in range(H // 2):
        att_all[d, :, 128 * j : 128 * j + 128] = joined(o_heads, j, tok).astype(BF)
    full = att_all[d]
    branch = [dot_nn(full, wb[j]) for j in range(4)] + [dot_nn(full, wlast[...])]
    mid = x_in[0].astype(F32) + scale_attn * jnp.concatenate(branch, axis=1)
    middle[...] = mid
    mn_all[d] = (mid * norm_scale(mid)).astype(BF)
    ms.start()
    gu[0].step(3)
    gu[1].start(False)
    gs.take()
    dn.give(1)
    gu[0].give(1)
    dn.give(2)
    ms.pass_on()
    gu[1].step(2)
    gu[0].give(2)
    dn.give(3)
    gu[0].give(3)
    ms.take()
    gu[1].step(3)
    dn.take()
    gu[0].take()
    ats.start()
    net.finish(gs)

    def by_cols(send, land, width):
        return [
            Spread(
                net,
                lambda j, n=n: send.at[j, :, pl.ds(width * n, width)],
                lambda j, n=n: land.at[j, :, pl.ds(width * n, width)],
            )
            for n in range(dim // width)
        ]

    gn, br, gx = by_cols(gn_send, gn_land, 384), by_cols(br_send, br_land, dim), by_cols(gx_send, gx_land, 384)
    wgu_flat, wd_flat = wgu.reshape(dim, 2 * hid), wd.reshape(hid, dim)
    other = 1 - c
    halves = [pl.ds(hid * h, hid) for h in range(2)]
    gu_pair = [ToMate(net, wgu.at[:, other, :, cols], gu_mate.at[:, :, cols]) for cols in halves]
    dn_pair = [ToMate(net, wd.at[2 * h : 2 * h + 2, other], dn_mate.at[2 * h : 2 * h + 2]) for h in range(2)]

    def add_dn(block, slot):
        wd[block, c] = (wd[block, c].astype(F32) + dn_zone[slot].astype(F32)).astype(BF)

    def half_sum(cols):
        def add(block, slot):
            wgu[block, c, :, cols] = (wgu[block, c, :, cols].astype(F32) + gu_zone[slot, :, cols].astype(F32)).astype(BF)

        return ChainSum(net, lambda zz: wgu.at[zz, c, :, cols], lambda k: gu_zone.at[k, :, cols], add)

    gu_sum = [half_sum(cols) for cols in halves]
    dn_sum = ChainSum(net, lambda zz: wd.at[zz, c], lambda k: dn_zone.at[k], add_dn)

    def pair_gu(h):
        gu_pair[h].take()
        cols = halves[h]
        for k in range(4):
            wgu[k, c, :, cols] = (wgu[k, c, :, cols].astype(F32) + gu_mate[k, :, cols].astype(F32)).astype(BF)
        gu_sum[h].stage(0)

    def branch_rows(h, downs):
        for n in range(3):
            cols = pl.ds(384 * n, 384)
            part = dot_nn(act[:, downs], wd_flat[downs, cols]).reshape(4, tok, 384)
            if h == 0:
                br_send[:, :, cols] = part.astype(BF)
            else:
                br_send[:, :, cols] = (br_send[:, :, cols].astype(F32) + part).astype(BF)
        turn_a[downs, :] = act[:, downs].T
        if h == 0:
            net.finish(dn)
        for n in range(3):
            cols = pl.ds(384 * n, 384)
            wd_flat[downs, cols] = dot_nn(turn_a[downs, :], gd_all[:, :, cols].reshape(span, 384)).astype(BF)
        dn_pair[h].start()

    def pair_dn(h):
        dn_pair[h].take()
        for k in (2 * h, 2 * h + 1):
            wd[k, c] = (wd[k, c].astype(F32) + dn_mate[k].astype(F32)).astype(BF)

    turn_x[...] = mn_all[...].reshape(span, dim).T
    for h in range(2):
        base = hid * h
        gates, ups, downs = pl.ds(base, quad), pl.ds(base + quad, quad), pl.ds(quad * h, quad)
        if h == 1:
            for k in (1, 2, 3):
                gu[1].give(k)
            gu[1].take()
        for pair in range(2):
            lines, two = pl.ds(2 * tok * pair, 2 * tok), slice(2 * pair, 2 * pair + 2)
            normed = mn_all[two].reshape(2 * tok, dim)
            gate = dot_nn(normed, wgu_flat[:, gates])
            up = dot_nn(normed, wgu_flat[:, ups])
            g_act = dot_nt(gd_all[two].reshape(2 * tok, dim), wd_flat[downs, :])
            sig = jax.nn.sigmoid(gate)
            swish = gate * sig
            act[lines, downs] = (swish * up).astype(BF)
            gboth[lines, gates] = (g_act * up * (sig * (1.0 + gate * (1.0 - sig)))).astype(BF)
            gboth[lines, ups] = (g_act * swish).astype(BF)
        if h == 0:
            branch_rows(h, downs)
        for n in range(3):
            cols = pl.ds(384 * n, 384)
            part = dot_nt(gboth[:, halves[h]], wgu_flat[cols, halves[h]]).reshape(4, tok, 384)
            if h == 0:
                gn_send[:, :, cols] = part.astype(BF)
                if n == 1:
                    pair_dn(h)
                    dn_sum.falling(0)
                    dn_sum.falling(1, True)
            else:
                gn_send[:, :, cols] = (gn_send[:, :, cols].astype(F32) + part).astype(BF)
                gn[n].start()

    def grads_gu(h):
        net.finish(gu[h])
        for base in (hid * h, hid * h + quad):
            cols = pl.ds(base, quad)
            wgu_flat[:, cols] = dot_nn(turn_x[...], gboth[:, cols]).astype(BF)
        gu_pair[h].start()

    grads_gu(0)
    branch_rows(1, pl.ds(quad, quad))
    pair_gu(0)
    grads_gu(1)
    pair_dn(1)
    dn_sum.rising(0)
    dn_sum.falling(1, False)
    pair_gu(1)
    gu_sum[0].stage(1)

    for n in range(3):
        gn[n].take()
    mid = middle[...]
    g_mid = cot_in[0].astype(F32) + norm_pull(plane_sum(net, gn_send, gn_land), mid)
    gmid[...] = g_mid
    gba = (scale_attn * g_mid).astype(BF)
    for j in range(4):
        cut_send[j, :, 512:768] = gba[:, 256 * j : 256 * j + 256]
    cut_send[3, :, 384:512] = gba[:, 1024:1152]
    cut = lambda cols: Spread(net, lambda j: cut_send.at[j, :, cols], lambda j: cut_land.at[j, :, cols])
    cut_o, cut_q, cut_l = cut(pl.ds(512, 256)), cut(pl.ds(0, 256)), cut(pl.ds(256, 256))
    cut_o.start()
    ats.pass_on()
    cut_land[d, :, 512:768] = cut_send[d, :, 512:768]
    g_att = dot_nt(gba[:, 1024:1152], wlast[...])
    for j in range(4):
        g_att = g_att + dot_nt(gba[:, 256 * j : 256 * j + 256], wb[j])
    for h in range(H):
        do_heads[h // groups, tok * (h % groups) : tok * (h % groups) + tok, :] = g_att[:, HD * h : HD * h + HD].astype(BF)

    dn_sum.falling(2, False)
    dn_sum.rising(1)

    kv_pair = [ToMate(net, dkv.at[n, :, other], kv_mate.at[n]) for n in range(2)]

    def kv_total(n):
        def add(block):
            dkv[n, block, c] = (dkv[n, block, c].astype(F32) + kv_zone[n, block].astype(F32)).astype(BF)

        return DownSum(net, lambda zz: dkv.at[n, zz, c], lambda k: kv_zone.at[n, k], add)

    kv_sum = [kv_total(n) for n in range(2)]

    def pull(k, carry):
        for g in range(groups):
            mine = pl.ds(tok * g, tok)
            p = probs[k, mine, :].astype(F32)
            t = p * dot_nt(do_heads[k, mine, :], v_heads[k])
            ds = (t - p * jnp.sum(t, axis=1, keepdims=True)).astype(BF)
            gs_heads[mine, :length] = ds
            o_heads[k, mine, :] = dot_nn(ds, k_heads[k]) * eighth
        half, kk = lax.div(k, 3), lax.rem(k, 3)
        for i, (left, right) in enumerate(((q_heads[k], gs_heads[: groups * tok, :length]), (do_heads[k], probs[k]))):
            turned_grad = dot_tn(left, right).astype(BF)
            at = pl.ds(pl.multiple_of(192 * i + HD * kk, HD), HD)
            for j in range(8):
                dkv[half, j // 2, j % 2, at, :] = turned_grad[:, tok * j : tok * j + tok]
        return carry

    def pair_sum(n):
        kv_pair[n].take()
        for k in range(4):
            dkv[n, k, c] = (dkv[n, k, c].astype(F32) + kv_mate[n, k].astype(F32)).astype(BF)
        kv_sum[n].start()

    def grads(p, parts):
        at = 0
        for part in parts:
            wb[p, :, at : at + part.shape[1]] = part.astype(BF)
            at += part.shape[1]
        pair = ToMate(net, m_att.at[p, :, other, :, quarter], ma_mate.at[p])
        pair.start()
        return pair

    def grads_pair(p, pair):
        pair.take()
        for k in range(4):
            m_att[p, k, c, :, quarter] = (m_att[p, k, c, :, quarter].astype(F32) + ma_mate[p, k].astype(F32)).astype(BF)

    def grads_chain(p, pair):
        def add(block, slot):
            m_att[p, block, c, :, quarter] = (
                m_att[p, block, c, :, quarter].astype(F32) + ma_zone[p, slot].astype(F32)
            ).astype(BF)

        grads_pair(p, pair)
        out = ChainSum(net, lambda zz: m_att.at[p, zz, c, :, quarter], lambda k: ma_zone.at[p, k], add)
        out.stage(0)
        return out

    def grads_straight(p, pair):
        grads_pair(p, pair)
        out = ToOwners(net, lambda zz: m_att.at[p, zz, c, :, quarter], lambda k: ma_zone.at[p, k])
        out.start()
        return out

    def grads_back(p, out):
        cols = pl.ds(256 * p, 256)
        if isinstance(out, ChainSum):
            out.own()
            total = m_att[p, z, c, :, quarter].astype(F32)
        else:
            out.take()
            total = m_att[p, z, c, :, quarter].astype(F32)
            for k in range(3):
                total = total + ma_zone[p, k].astype(F32)
        unsettle(total, wide, att_land, rows, cols)
        spread = Spread(net, lambda j: att_land.at[j, :, cols], lambda j: back_att.at[j, :, cols])
        spread.start()
        back_att[d, :, cols] = att_land[d, :, cols]
        return spread

    q_cols, l_cols, o_cols = pl.ds(0, 256), pl.ds(256, 256), pl.ds(512, 256)
    quarter = pl.ds(0, 256)
    net.finish(ms, *gn, *gu_pair, *dn_pair)
    lax.fori_loop(0, 3, pull, 0)
    kv_pair[0].start()
    lax.fori_loop(3, 4, pull, 0)
    pair_sum(0)
    lax.fori_loop(4, 6, pull, 0)
    kv_pair[1].start()
    for t in range(9):
        j, col = (t // 2, (t % 2) * 128) if t < 8 else (2, 384)
        cut_send[j, :, col : col + 128] = turned(joined(o_heads, t, tok), cosine, -sine).astype(BF)
    cut_q.start()
    br[0].start()
    cut_land[d, :, q_cols] = cut_send[d, :, q_cols]
    pair_sum(1)
    ats.take()
    cut_o.take()
    turn_x[...] = att_all[...].reshape(span, dim).T
    pair_o = grads(2, [dot_nn(turn_x[...], cut_land[:, :, o_cols].reshape(span, 256))])
    turn_n[...] = xn_all[...].reshape(span, dim).T
    dn_sum.rising(2, False)
    gu_sum[0].rising(2, False)
    for n in range(2):
        kv_sum[n].relay(0)
        kv_sum[n].relay(1)
    cut_q.take()
    pair_q = grads(0, [dot_nn(turn_n[...], cut_land[:, :, q_cols].reshape(span, 256))])
    gu_sum[1].stage(1)
    sum_o = grads_chain(2, pair_o)
    sum_q = grads_chain(0, pair_q)
    gu_sum[0].falling(2, False)

    for n in range(2):
        kv_sum[n].own()
        kv_tot[n] = dkv[n, z, c].astype(F32)
    keys = jnp.concatenate([kv_tot[0, :192, :], kv_tot[1, :192, :]], axis=0).T
    vals = jnp.concatenate([kv_tot[0, 192:, :], kv_tot[1, 192:, :]], axis=0).T
    late = [turned(keys[:, 128 * i : 128 * i + 128], cosine, -sine) for i in range(3)] + [vals[:, 128 * i : 128 * i + 128] for i in range(3)]
    for tile, (j, col) in zip(late, places):
        cut_send[j, :, col : col + 128] = tile.astype(BF)
    cut_l.start()
    cut_land[d, :, l_cols] = cut_send[d, :, l_cols]
    sum_o.stage(1)
    sum_q.stage(1)
    gu_sum[1].between(2)
    gu_sum[0].last()
    gu_sum[1].last()
    net.finish(ats, cut_o, cut_q, *kv_pair)
    cut_l.take()
    last = cut_land[:, :, 384:512].reshape(span, 128)
    cuts = cut_land[:, :, :512].reshape(span, 512)
    lane = lax.broadcasted_iota(jnp.int32, cuts.shape, 1)
    cuts = jnp.where((d == 3) & (lane >= 384), jnp.zeros_like(cuts), cuts)
    for n in range(3):
        part = dot_nt(cuts, wa[384 * n : 384 * n + 384, :]).astype(BF)
        gx_send[:, :, 384 * n : 384 * n + 384] = part.reshape(4, tok, 384)
        gx[n].start()
    second = jnp.where(d == 3, dot_nn(turn_x[...], last), dot_nn(turn_n[...], last))
    pair_l = grads(1, [dot_nn(turn_n[...], cut_land[:, :, 256:384].reshape(span, 128)), second])
    sum_l = grads_straight(1, pair_l)
    br[0].take()
    block_out[0] = (middle[...] + scale_mlp * plane_sum(net, br_send, br_land)).astype(BF)
    sum_o.stage(2)
    sum_q.stage(2)
    dn_sum.last()
    for k in range(2):
        gu_sum[k].own()
        unsettle(wgu[z, c, :, halves[k]].astype(F32), wide, gu_land, rows, halves[k])
    back_g = Spread(net, lambda j: gu_land.at[j], lambda j: back_gu.at[j])
    back_g.start()
    back_gu[d] = gu_land[d]
    back_o = grads_back(2, sum_o)
    back_l = grads_back(1, sum_l)
    back_q = grads_back(0, sum_q)
    dn_sum.own()
    back_down[...] = wd[z, c]
    for n in range(3):
        gx[n].take()
    input_grad[0] = gmid[...] + norm_pull(plane_sum(net, gx_send, gx_land), x_in[0].astype(F32))
    for spread in (back_o, back_q, back_g, back_l):
        spread.take()
    net.finish()


def layer(x, cot, weights, down, gains, doc_starts, keep_mask, keep_rate, seq_order):
    tok, dim = x.shape[1:]
    ns = 8
    length = tok * ns
    ffr = down.shape[0]
    hid = ffr * ns
    blk = dim // ns
    span = 4 * tok
    vm = pl.BlockSpec(memory_space=pltpu.VMEM)
    sm = pl.BlockSpec(memory_space=pltpu.SMEM)
    padded = blk // 4 + -(blk // 4) % 16
    att_pack, gu_pack = ((4, padded, 768), BF), ((4, padded, 2 * hid), BF)
    outs = [((1, tok, dim), BF), ((1, tok, dim), F32), gu_pack, att_pack, (down.shape, BF)]
    plane = ((4, tok, dim), BF)
    wide_cut = ((4, tok, 512), BF)
    three = ((KV, 3 * tok, HD), BF)
    scratch = [
        att_pack,
        gu_pack,
        ((blk, hid), F32),
        wide_cut,
        ((4, 2, tok, 2 * KV * HD), BF),
        ((KV, 3 * tok, HD), F32),
        ((tok, length), F32),
        ((dim, 512), BF),
        ((4, dim, 256), BF),
        ((dim, 128), BF),
        ((4, 2, blk, 2 * hid), BF),
        ((4, 2, ffr, dim), BF),
        plane,
        plane,
        plane,
        plane,
        three,
        ((KV, length, HD), BF),
        ((KV, length, HD), BF),
        ((KV, 3 * tok, length), BF),
        ((tok, dim), F32),
        ((span, hid), BF),
        ((span, 2 * hid), BF),
        ((dim, span), BF),
        ((dim, span), BF),
        ((hid, span), BF),
        plane,
        plane,
        plane,
        plane,
        ((4, blk, 2 * hid), BF),
        ((5, blk, 2 * hid), BF),
        ((4, ffr, dim), BF),
        ((5, ffr, dim), BF),
        ((tok, dim), F32),
        three,
        ((2, 4, 2, 384, tok), BF),
        ((2, 4, 384, tok), BF),
        ((2, 3, 384, tok), BF),
        ((2, 384, tok), F32),
        ((4, tok, 768), BF),
        ((3, 4, blk, 256), BF),
        ((3, 5, blk, 256), BF),
        plane,
    ]
    return pl.pallas_call(
        layer_kernel,
        out_shape=[jax.ShapeDtypeStruct(*o) for o in outs],
        in_specs=[vm] * 11 + [sm] * 4,
        out_specs=[vm] * len(outs),
        scratch_shapes=[pltpu.VMEM(*t) for t in scratch] + [pltpu.SemaphoreType.DMA((SENDS,)), pltpu.SemaphoreType.DMA((RECVS,))],
        compiler_params=pltpu.CompilerParams(collective_id=0, has_side_effects=True, vmem_limit_bytes=LIMIT),
        name="k_layer",
    )(x, cot, *weights, down, *gains, doc_starts, keep_mask, keep_rate, seq_order)


def grads_kernel(
    query, key_w, value, gate_w, up_w, gain_one, gain_two, block_in, input_in, back_gu, back_att, back_down,
    block_out, input_out, norm_one, g_query, g_key, g_value, g_output, norm_two, g_gate, g_up, g_down,
):
    rows, ffr = query.shape[0], back_down.shape[0]
    hid = 8 * ffr
    block_out[...] = block_in[...]
    input_out[...] = input_in[...]
    g_down[...] = back_down[...].astype(F32)
    gain = column(gain_one[...])
    total = jnp.zeros((rows, 128), F32)
    for j in range(4):
        for i, t in enumerate((2 * j, 2 * j + 1, LATE[j][0], LATE[j][1])):
            m = back_att[j, :rows, 128 * i : 128 * i + 128].astype(F32)
            if t is None:
                g_output[:, 1024:1152] = m
                continue
            w, g, t = (query, g_query, t) if t < 9 else (key_w, g_key, t - 9) if t < 12 else (value, g_value, t - 12)
            cols = slice(128 * t, 128 * t + 128)
            total = total + w[:, cols].astype(F32) * m
            g[:, cols] = m * gain
        g_output[:, 256 * j : 256 * j + 256] = back_att[j, :rows, 512:768].astype(F32)
    norm_one[...] = row_of(jnp.sum(total, axis=1, keepdims=True))
    gain = column(gain_two[...])
    total = jnp.zeros((rows, 4 * ffr), F32)
    for i, (w, g) in enumerate(((gate_w, g_gate), (up_w, g_up))):
        for k in range(8):
            at = hid * (k // 4) + 4 * ffr * i + ffr * (k % 4)
            m = jnp.concatenate([back_gu[j, :rows, at : at + ffr].astype(F32) for j in range(4)], axis=1)
            cols = slice(4 * ffr * k, 4 * ffr * k + 4 * ffr)
            total = total + w[:, cols].astype(F32) * m
            g[:, cols] = m * gain
    norm_two[...] = row_of(jnp.sum(total, axis=1, keepdims=True))


def gradients(query, key_w, value, output, gate_w, up_w, gains, results):
    block, grad, back_gu, back_att, back_down = results
    shapes = [grad.shape, gains[0].shape] + [w.shape for w in (query, key_w, value, output)]
    shapes += [gains[1].shape, gate_w.shape, up_w.shape, back_down.shape]
    vm = pl.BlockSpec(memory_space=pltpu.VMEM)
    return pl.pallas_call(
        grads_kernel,
        out_shape=[jax.ShapeDtypeStruct(block.shape, BF)] + [jax.ShapeDtypeStruct(t, F32) for t in shapes],
        in_specs=[vm] * 12,
        out_specs=[vm] * 11,
        name="k_grads",
    )(query, key_w, value, gate_w, up_w, *gains, block, grad, back_gu, back_att, back_down)


def shards_by_kernel(
    hidden_in,
    attn_norm,
    query_weight,
    key_weight,
    value_weight,
    output_weight,
    mlp_norm,
    gate_weight,
    up_weight,
    down_weight,
    cotangent,
    doc_starts,
    keep_mask,
    keep_rate,
    seq_order,
):
    rows = query_weight.shape[0]
    gains = (attn_norm.reshape(1, rows), mlp_norm.reshape(1, rows))
    weights = (query_weight, key_weight, value_weight, output_weight, gate_weight, up_weight)
    results = layer(
        hidden_in, cotangent, weights, down_weight, gains, doc_starts, keep_mask.T, keep_rate, seq_order
    )
    outs = list(gradients(*weights, gains, results))
    outs[2], outs[7] = outs[2].reshape(rows), outs[7].reshape(rows)
    return tuple(outs)


def solution(mesh):
    placed = (
        P("dp", "seq", None),
        P(("seq", "dp")),
        P(("seq", "dp"), None),
        P(("seq", "dp"), None),
        P(("seq", "dp"), None),
        P(("seq", "dp"), None),
        P(("seq", "dp")),
        P(("seq", "dp"), None),
        P(("seq", "dp"), None),
        P(("seq", "dp"), None),
        P("dp", "seq", None),
        P(),
        P(),
        P(),
        P(),
    )
    fits = mesh.shape["seq"] == 8 and mesh.shape["dp"] == 4
    return jax.shard_map(
        shards_by_kernel if fits else shards,
        mesh=mesh,
        in_specs=placed,
        out_specs=(
            P("dp", "seq", None),
            P("dp", "seq", None),
            P(("seq", "dp")),
            P(("seq", "dp"), None),
            P(("seq", "dp"), None),
            P(("seq", "dp"), None),
            P(("seq", "dp"), None),
            P(("seq", "dp")),
            P(("seq", "dp"), None),
            P(("seq", "dp"), None),
            P(("seq", "dp"), None),
        ),
        check_vma=False,
    )
```

```python
import math

import jax
import jax.numpy as jnp
from jax import lax
from jax.experimental import pallas as pl
from jax.experimental.pallas import tpu as pltpu
from jax.sharding import PartitionSpec as P

H = 18
KV = 6
HD = 64


EPSILON = 1e-05
ROPE_BASE = 10000.0
MASKED = -1e30


def contract_rows(left_rows, right_rows):
    return lax.dot_general(
        left_rows, right_rows, (((0,), (0,)), ((), ())), preferred_element_type=jnp.float32
    )


def contract_cols(left_mat, right_mat):
    return lax.dot_general(
        left_mat, right_mat, (((1,), (1,)), ((), ())), preferred_element_type=jnp.float32
    )


def low(v):
    return v.astype(jnp.bfloat16)


def dot(a, b):
    return jnp.dot(a, b, preferred_element_type=jnp.float32)


def swap_halves(vectors):
    half = HD // 2
    return jnp.concatenate([vectors[..., half:], vectors[..., :half]], axis=-1)


def shards(
    hidden_in,
    attn_norm,
    query_weight,
    key_weight,
    value_weight,
    output_weight,
    mlp_norm,
    gate_weight,
    up_weight,
    down_weight,
    cotangent,
    doc_starts,
    keep_mask,
    keep_rate,
    seq_order,
):
    tok = hidden_in.shape[1]
    ns, nd = lax.axis_size("seq"), lax.axis_size("dp")
    length = tok * ns
    rows = query_weight.shape[0]
    ffr = down_weight.shape[0]
    dim = hidden_in.shape[2]
    groups = H // KV
    nq, nk = H * HD, KV * HD
    score_scale = 1.0 / math.sqrt(HD)
    me_s, me_d = lax.axis_index("seq"), lax.axis_index("dp")
    sample = jnp.sum(jnp.where(jnp.arange(nd) == me_d, seq_order, 0))
    pick = jnp.arange(nd) == sample
    doc_begin = jnp.sum(jnp.where(pick[:, None], doc_starts, 0), axis=0)
    keep_flags = jnp.sum(jnp.where(pick[:, None], keep_mask, 0), axis=0).astype(jnp.float32)
    attn_scale = keep_flags[0] / keep_rate[0]
    mlp_scale = keep_flags[1] / keep_rate[1]
    positions = me_s * tok + jnp.arange(tok)
    first = jnp.max(jnp.where(doc_begin[None, :] <= positions[:, None], doc_begin[None, :], 0), axis=1)
    gain_one, gain_two = attn_norm[:, None], mlp_norm[:, None]

    qkv_rows = low(jnp.concatenate([query_weight, key_weight, value_weight], axis=1).astype(jnp.float32) * gain_one)
    w_qkv = lax.all_gather(qkv_rows, ("seq", "dp"), axis=0, tiled=True)
    w_out = lax.all_gather(output_weight, ("seq", "dp"), axis=0, tiled=True)

    def split_hidden(w):
        w = low(w.astype(jnp.float32) * gain_two).reshape(rows, ns, nd, ffr)
        w = jnp.transpose(w, (0, 2, 1, 3)).reshape(rows, nd * ns * ffr)
        return w

    gu = jnp.concatenate(
        [split_hidden(gate_weight).reshape(rows, nd, -1), split_hidden(up_weight).reshape(rows, nd, -1)], axis=2
    )
    gu = lax.all_to_all(gu, "dp", split_axis=1, concat_axis=0, tiled=True).reshape(nd * rows, -1)
    w_gu = lax.all_gather(gu, "seq", axis=0, tiled=True)
    w_down = lax.all_gather(down_weight, "seq", axis=0, tiled=True)
    hid = w_down.shape[0]

    x = hidden_in[0].astype(jnp.float32)
    r_one = lax.rsqrt(jnp.mean(x * x, axis=-1, keepdims=True) + EPSILON)
    xn = low(x * r_one)
    qkv = dot(xn, w_qkv)
    inverse_freq = ROPE_BASE ** (-2.0 * jnp.arange(HD // 2, dtype=jnp.float32) / HD)
    angles = positions.astype(jnp.float32)[:, None] * inverse_freq[None, :]
    cosine = jnp.tile(jnp.cos(angles), (1, 2))[:, None, :]
    sine = jnp.concatenate([-jnp.sin(angles), jnp.sin(angles)], axis=1)[:, None, :]

    def turn(v):
        return v * cosine + swap_halves(v) * sine

    def turn_back(v):
        return v * cosine - swap_halves(v) * sine

    queries = low(turn(qkv[:, :nq].reshape(tok, H, HD))).reshape(tok, KV, groups, HD)
    keys = low(turn(qkv[:, nq : nq + nk].reshape(tok, KV, HD)))
    kv = jnp.concatenate([keys.reshape(tok, nk), low(qkv[:, nq + nk :])], axis=1)
    kv_all = lax.all_gather(kv, "seq", axis=0, tiled=True)
    k_all, v_all = kv_all[:, :nk].reshape(length, KV, HD), kv_all[:, nk:].reshape(length, KV, HD)
    key_pos = jnp.arange(length)
    allowed = (key_pos[None, :] <= positions[:, None]) & (key_pos[None, :] >= first[:, None])
    scores = jnp.einsum("tkgd,skd->kgts", queries, k_all, preferred_element_type=jnp.float32) * score_scale
    scores = jnp.where(allowed, scores, MASKED)
    expo = jnp.exp(scores - jnp.max(scores, axis=-1, keepdims=True))
    probs = low(expo / jnp.sum(expo, axis=-1, keepdims=True))
    attended = jnp.einsum("kgts,skd->tkgd", probs, v_all, preferred_element_type=jnp.float32)
    att = low(attended.reshape(tok, nq))
    middle = x + attn_scale * dot(att, w_out)
    r_two = lax.rsqrt(jnp.mean(middle * middle, axis=-1, keepdims=True) + EPSILON)
    mn = low(middle * r_two)

    cot = cotangent[0].astype(jnp.float32)
    side = lax.all_gather(jnp.concatenate([xn, low(mlp_scale * cot), att], axis=1), "dp", axis=0, tiled=True)
    xn_all, gd_all, att_all = side[:, :dim], side[:, dim : 2 * dim], side[:, 2 * dim :]
    mn_all = lax.all_gather(mn, "dp", axis=0, tiled=True)
    gate, up = dot(mn_all, w_gu[:, :hid]), dot(mn_all, w_gu[:, hid:])
    sig = jax.nn.sigmoid(gate)
    act_gate = gate * sig
    act = low(act_gate * up)
    g_act = contract_cols(gd_all, w_down)
    gg = low(g_act * up * (sig * (1.0 + gate * (1.0 - sig))))
    gu_in = low(g_act * act_gate)
    gboth = jnp.concatenate([gg, gu_in], axis=1)
    g_mn = lax.psum_scatter(low(contract_cols(gboth, w_gu)), "dp", scatter_dimension=0, tiled=True).astype(jnp.float32)
    branch = lax.psum_scatter(low(dot(act, w_down)), "dp", scatter_dimension=0, tiled=True).astype(jnp.float32)
    block_output = low(middle + mlp_scale * branch)[None]
    m_gu = lax.psum_scatter(low(contract_rows(mn_all, gboth)), "seq", scatter_dimension=0, tiled=True)
    m_down = lax.psum_scatter(low(contract_rows(act, gd_all)), "seq", scatter_dimension=0, tiled=True)

    def norm_back(e, v, r):
        return r * e - v * (r * r * r) * jnp.mean(e * v, axis=-1, keepdims=True)

    g_mid = cot + norm_back(g_mn, middle, r_two)
    gba = low(attn_scale * g_mid)
    g_att = low(contract_cols(gba, w_out)).reshape(tok, KV, groups, HD)
    g_probs = jnp.einsum("tkgd,skd->kgts", g_att, v_all, preferred_element_type=jnp.float32)
    delta = jnp.einsum("tkgd,tkgd->kgt", g_att.astype(jnp.float32), attended)
    g_scores = low(probs.astype(jnp.float32) * (g_probs - delta[..., None]))
    g_q = jnp.einsum("kgts,skd->tkgd", g_scores, k_all, preferred_element_type=jnp.float32) * score_scale
    g_k = jnp.einsum("kgts,tkgd->skd", g_scores, queries, preferred_element_type=jnp.float32) * score_scale
    g_v = jnp.einsum("kgts,tkgd->skd", probs, g_att, preferred_element_type=jnp.float32)
    g_kv = low(jnp.concatenate([g_k.reshape(length, nk), g_v.reshape(length, nk)], axis=1))
    g_kv = lax.psum_scatter(g_kv, "seq", scatter_dimension=0, tiled=True).astype(jnp.float32)
    g_q_in = low(turn_back(g_q.reshape(tok, H, HD))).reshape(tok, nq)
    g_k_in = low(turn_back(g_kv[:, :nk].reshape(tok, KV, HD))).reshape(tok, nk)
    g_qkv = jnp.concatenate([g_q_in, g_k_in, low(g_kv[:, nk:])], axis=1)
    g_xn = contract_cols(g_qkv, w_qkv)
    input_grad = (g_mid + norm_back(g_xn, x, r_one))[None]

    cut = jnp.concatenate([g_qkv.reshape(tok, nd, -1), gba.reshape(tok, nd, -1)], axis=2)
    wq = g_qkv.shape[1] // nd
    cut = lax.all_to_all(cut, "dp", split_axis=1, concat_axis=0, tiled=True).reshape(nd * tok, -1)
    m_att = jnp.concatenate([contract_rows(xn_all, cut[:, :wq]), contract_rows(att_all, cut[:, wq:])], axis=1)
    m_att = lax.psum_scatter(low(m_att), "seq", scatter_dimension=0, tiled=True)

    back = jnp.concatenate([m_gu, m_att], axis=1)
    back = lax.all_to_all(back.reshape(nd, rows, 1, -1), "dp", split_axis=0, concat_axis=2, tiled=True)
    back = back.reshape(rows, nd, -1).astype(jnp.float32)

    def whole_hidden(m):
        return jnp.transpose(m.reshape(rows, nd, ns, ffr), (0, 2, 1, 3)).reshape(rows, -1)

    m_gate, m_up = whole_hidden(back[:, :, :hid]), whole_hidden(back[:, :, hid : 2 * hid])
    m_qkv = back[:, :, 2 * hid : 2 * hid + wq].reshape(rows, -1)
    g_out = back[:, :, 2 * hid + wq :].reshape(rows, -1)

    def weigh(w, m):
        return jnp.sum(w.astype(jnp.float32) * m, axis=1)

    m_q, m_k, m_v = m_qkv[:, :nq], m_qkv[:, nq : nq + nk], m_qkv[:, nq + nk :]
    g_norm_one = weigh(query_weight, m_q) + weigh(key_weight, m_k) + weigh(value_weight, m_v)
    g_norm_two = weigh(gate_weight, m_gate) + weigh(up_weight, m_up)
    return (
        block_output,
        input_grad,
        g_norm_one,
        m_q * gain_one,
        m_k * gain_one,
        m_v * gain_one,
        g_out,
        g_norm_two,
        m_gate * gain_two,
        m_up * gain_two,
        m_down.astype(jnp.float32),
    )


MESH = pl.DeviceIdType.MESH
LIMIT = 60 * 2**20
SENDS, RECVS = 100, 212
BF, F32 = jnp.bfloat16, jnp.float32


def dot_nn(a, b):
    return lax.dot_general(a, b, (((1,), (0,)), ((), ())), preferred_element_type=F32)


def dot_nt(a, b):
    return lax.dot_general(a, b, (((1,), (1,)), ((), ())), preferred_element_type=F32)


def dot_tn(a, b):
    return lax.dot_general(a, b, (((0,), (0,)), ((), ())), preferred_element_type=F32)


class Net:
    def __init__(self, sends, recvs):
        self.sends, self.recvs, self.open, self.used = sends, recvs, [], 0
        self.free = list(range(sends.shape[0]))
        self.s, self.d = lax.axis_index("seq"), lax.axis_index("dp")
        self.z, self.c = lax.div(self.s, 2), lax.rem(self.s, 2)
        y, x = lax.div(self.d, 2), lax.rem(self.d, 2)
        self.plane = (y * 2 + 1 - x, (1 - y) * 2 + x, 3 - self.d)
        self.mate = self.at(self.z, 1 - self.c)

    def room(self, count):
        base = self.used
        self.used += count
        return base

    def at(self, z, core):
        return {"seq": z * 2 + core, "dp": self.d}

    def across(self, kind):
        return {"seq": self.s, "dp": self.plane[kind]}

    def greet(self):
        barrier = pltpu.get_barrier_semaphore()
        peers = [self.mate] + [self.across(k) for k in range(3)]
        peers += [self.at(lax.rem(self.z + k, 4), self.c) for k in (1, 2, 3)]
        for peer in peers:
            pl.semaphore_signal(barrier, inc=1, device_id=peer, device_id_type=MESH)

    def greeted(self):
        pl.semaphore_wait(pltpu.get_barrier_semaphore(), 7)

    def copy(self, src, dst, send, recv, peer):
        return pltpu.make_async_remote_copy(
            src_ref=src,
            dst_ref=dst,
            send_sem=self.sends.at[send],
            recv_sem=self.recvs.at[recv],
            device_id=peer,
            device_id_type=MESH,
        )

    def push(self, owner, src, dst, recv, peer, when=None):
        send = self.free.pop(0)
        copy = self.copy(src, dst, send, recv, peer)
        if when is None:
            copy.start()
        else:
            pl.when(when)(copy.start)
        self.open.append((copy, when, owner, send))

    def arrive(self, dst, recv, when=None):
        copy = self.copy(dst, dst, 0, recv, self.mate)
        if when is None:
            copy.wait_recv()
        else:
            pl.when(when)(copy.wait_recv)

    def finish(self, *owners):
        kept = []
        for entry in self.open:
            copy, when, owner, send = entry
            if owners and owner not in owners:
                kept.append(entry)
                continue
            if when is None:
                copy.wait_send()
            else:
                pl.when(when)(copy.wait_send)
            self.free.append(send)
        self.open = kept

    def order(self, step):
        if step == 0:
            return self.z
        table = ((1, 0, 3, 2), (2, 2, 1, 1), (3, 3, 0, 0))[step - 1]
        z = self.z
        return jnp.where(z == 0, table[0], jnp.where(z == 1, table[1], jnp.where(z == 2, table[2], table[3])))


class Chain:
    def __init__(self, net, block, room=4):
        self.net, self.block, self.base = net, block, net.room(room)

    def start(self):
        net = self.net
        own = self.block(net.z, net.c)
        net.push(self, own, own, self.base + net.z, net.at(net.z + 1, net.c), net.z < 3)
        net.push(self, own, own, self.base + net.z, net.at(net.z - 1, net.c), net.z > 0)

    def step(self, k):
        net = self.net
        b = net.order(k)
        block = self.block(b, net.c)
        net.arrive(block, self.base + b)
        to = jnp.where(b < net.z, net.z + 1, net.z - 1)
        net.push(self, block, block, self.base + b, net.at(to, net.c), (to >= 0) & (to <= 3))


class Lines(Chain):
    def __init__(self, net, block):
        super().__init__(net, block, 8)

    def start(self, ends=None):
        net = self.net
        own = self.block(net.z, net.c)
        up, down, any_z = net.z < 3, net.z > 0, None
        if ends is not None:
            any_z = (net.z == 0) | (net.z == 3)
            any_z = any_z if ends else jnp.logical_not(any_z)
            up, down = up & any_z, down & any_z
        net.push(self, own, own, self.base + net.z, net.at(net.z + 1, net.c), up)
        net.push(self, own, own, self.base + net.z, net.at(net.z - 1, net.c), down)
        net.push(self, own, own, self.base + 4 + net.z, net.mate, any_z)

    def onward(self, b):
        to = jnp.where(b < self.net.z, self.net.z + 1, self.net.z - 1)
        return to, (to >= 0) & (to <= 3)

    def step(self, k):
        net = self.net
        b = net.order(k)
        block = self.block(b, net.c)
        to, on = self.onward(b)
        net.arrive(block, self.base + b, on)
        net.push(self, block, block, self.base + b, net.at(to, net.c), on)

    def give(self, k):
        net = self.net
        b = net.order(k)
        block = self.block(b, net.c)
        if k:
            net.arrive(block, self.base + b, jnp.logical_not(self.onward(b)[1]))
        net.push(self, block, block, self.base + 4 + b, net.mate)

    def take(self):
        net = self.net
        for b in range(4):
            net.arrive(self.block(b, 1 - net.c), self.base + 4 + b)


class FromLast:
    def __init__(self, net, source, full):
        self.net, self.source, self.full, self.base = net, source, full, net.room(2)

    def start(self):
        net = self.net
        for kind in range(3):
            part = self.full.at[:, net.c]
            net.push(self, self.source.at[:, net.c, :, pl.ds(384, 128)], part, self.base, net.across(kind), net.d == 3)

        @pl.when(net.d == 3)
        def _():
            self.full[...] = self.source[:, :, :, 384:512]

    def pass_on(self):
        net = self.net
        part = self.full.at[:, net.c]
        net.arrive(part, self.base, net.d < 3)
        net.push(self, part, part, self.base + 1, net.mate, net.d < 3)

    def take(self):
        self.net.arrive(self.full.at[:, 1 - self.net.c], self.base + 1, self.net.d < 3)


class Rising(Lines):
    def start(self):
        net = self.net
        own = self.block(net.z, net.c)
        net.push(self, own, own, self.base + net.z, net.at(net.z + 1, net.c), net.z < 3)
        net.push(self, own, own, self.base + 4 + net.z, net.mate)

    def step(self, k):
        net = self.net
        b = jnp.maximum(net.z - k, 0)
        block = self.block(b, net.c)
        net.arrive(block, self.base + b, net.z >= k)
        net.push(self, block, block, self.base + b, net.at(net.z + 1, net.c), (net.z >= k) & (net.z < 3))
        net.push(self, block, block, self.base + 4 + b, net.mate, net.z >= k)

    def take(self):
        net = self.net
        for b in range(4):
            net.arrive(self.block(b, 1 - net.c), self.base + 4 + b, net.z >= b)


class Slices(Chain):
    def __init__(self, net, full, rows):
        self.full, self.rows, self.half = full, rows, rows // 32 * 16
        super().__init__(net, lambda z, core: self.part(net.d, z, core), 36)

    def part(self, slot, z, core, half=None):
        first = pl.multiple_of((z * 2 + core) * self.rows, 16)
        if half is None:
            return self.full.at[slot, pl.ds(first, self.rows)]
        if half == 0:
            return self.full.at[slot, pl.ds(first, self.half)]
        return self.full.at[slot, pl.ds(pl.multiple_of(first + self.half, 16), self.rows - self.half)]

    def spread(self, k):
        net = self.net
        b = net.order(k)
        block = self.part(net.d, b, net.c)
        net.push(self, block, block, self.base + 4 + b, net.across(0))
        net.push(self, block, block, self.base + 8 + b, net.across(1))
        net.push(self, block, block, self.base + 20 + b, net.mate)

    def pass_on(self, k):
        net = self.net
        b = net.order(k)
        for kind in (0, 1):
            block = self.part(net.plane[kind], b, net.c)
            net.arrive(block, self.base + 4 + 4 * kind + b)
            half = self.part(net.plane[kind], b, net.c, kind)
            net.push(self, half, half, self.base + 12 + 4 * kind + b, net.across(1 - kind))
            net.push(self, block, block, self.base + 24 + 4 * kind + b, net.mate)

    def corner(self, k):
        net = self.net
        b = net.order(k)
        for kind in (0, 1):
            half = self.part(net.plane[2], b, net.c, kind)
            net.arrive(half, self.base + 12 + 4 * kind + b)
        block = self.part(net.plane[2], b, net.c)
        net.push(self, block, block, self.base + 32 + b, net.mate)

    def take(self):
        net = self.net
        for b in range(4):
            net.arrive(self.part(net.d, b, 1 - net.c), self.base + 20 + b)
            for kind in range(3):
                net.arrive(self.part(net.plane[kind], b, 1 - net.c), self.base + 24 + 4 * kind + b)


class Plane:
    def __init__(self, net, full):
        self.net, self.full, self.base = net, full, net.room(4)
        self.half = full.shape[1] // 2

    def start(self):
        net = self.net
        own = self.full.at[net.d]
        for kind in (0, 1):
            net.push(self, own, own, self.base + kind, net.across(kind))

    def pass_on(self):
        net = self.net
        for kind in (0, 1):
            net.arrive(self.full.at[net.plane[kind]], self.base + kind)
            half = self.full.at[net.plane[kind], pl.ds(kind * self.half, self.half)]
            net.push(self, half, half, self.base + 2 + kind, net.across(1 - kind))

    def take(self):
        net = self.net
        for kind in (0, 1):
            net.arrive(self.full.at[net.plane[2], pl.ds(kind * self.half, self.half)], self.base + 2 + kind)


class Spread:
    def __init__(self, net, send, land):
        self.net, self.send, self.land, self.base = net, send, land, net.room(3)

    def start(self):
        net = self.net
        for kind in (2, 0, 1):
            net.push(self, self.send(net.plane[kind]), self.land(net.d), self.base + kind, net.across(kind))

    def take(self):
        for kind in range(3):
            self.net.arrive(self.land(self.net.plane[kind]), self.base + kind)


class ToMate:
    def __init__(self, net, send, land):
        self.net, self.send, self.land, self.base = net, send, land, net.room(1)

    def start(self):
        self.net.push(self, self.send, self.land, self.base, self.net.mate)

    def take(self):
        self.net.arrive(self.land, self.base)


class ToOwners:
    def __init__(self, net, part, land, down=False):
        self.net, self.part, self.land, self.down, self.base = net, part, land, down, net.room(3)

    def start(self):
        net = self.net
        for k in (3, 2, 1):
            to = lax.rem(net.z - k + 4, 4)
            net.push(self, self.part(to), self.land(k - 1), self.base + k - 1, net.at(to, net.c), (net.z >= k) if self.down else None)

    def take(self):
        net = self.net
        for k in (1, 2, 3):
            net.arrive(self.land(k - 1), self.base + k - 1, (net.z + k <= 3) if self.down else None)


class DownSum:
    def __init__(self, net, part, land, add):
        self.net, self.part, self.land, self.add, self.base = net, part, land, add, net.room(3)

    def send(self, b, when):
        net = self.net
        net.push(self, self.part(b), self.land(b), self.base + b, net.at(net.z - 1, net.c), when)

    def start(self):
        for b in range(3):
            self.send(b, self.net.z == 3)

    def relay(self, b):
        net = self.net
        on = (net.z > b) & (net.z < 3)

        @pl.when(on)
        def _():
            net.arrive(self.land(b), self.base + b)
            self.add(b)

        self.send(b, on)

    def own(self):
        net = self.net
        for b in range(3):

            @pl.when(net.z == b)
            def _(b=b):
                net.arrive(self.land(b), self.base + b)
                self.add(b)


class ChainSum:
    def __init__(self, net, part, land, add):
        self.net, self.part, self.land, self.add, self.base = net, part, land, add, net.room(6)

    def stage(self, k):
        self.falling(k)
        self.rising(k)

    def falling(self, k, top=None):
        net, z = self.net, self.net.z
        i = k - 3 + z
        valid = (i >= 0) & (i < z)
        if top is not None:
            valid = valid & ((z == 3) if top else (z < 3))
        i = jnp.clip(i, 0, 3)

        @pl.when(valid & (z < 3))
        def _():
            net.arrive(self.land(i), self.base + i)
            self.add(i, i)

        net.push(self, self.part(i), self.land(i), self.base + i, net.at(z - 1, net.c), valid)

    def last(self):
        self.falling(2, True)
        self.rising(2, True)

    def between(self, k):
        self.falling(k, False)
        self.rising(k, False)

    def rising(self, k, end=None):
        net, z = self.net, self.net.z
        j = k - z
        valid = (j >= 0) & (3 - j > z)
        if end is not None:
            valid = valid & ((z == 0) if end else (z > 0))
        j = jnp.clip(j, 0, 3)

        @pl.when(valid & (z > 0))
        def _():
            net.arrive(self.land(4 - j), self.base + 3 + j)
            self.add(3 - j, 4 - j)

        net.push(self, self.part(3 - j), self.land(4 - j), self.base + 3 + j, net.at(z + 1, net.c), valid)

    def own(self):
        net, z = self.net, self.net.z

        @pl.when(z < 3)
        def _():
            net.arrive(self.land(z), self.base + z)
            self.add(z, z)

        @pl.when(z > 0)
        def _():
            net.arrive(self.land(1 + z), self.base + 6 - z)
            self.add(z, 1 + z)


def settle(land, wide, rows, cols=slice(None)):
    for j in range(4):
        wide[pl.ds(j * rows, rows), :] = land[j, :rows, cols].astype(F32)
    return wide[...].astype(BF)


def unsettle(block, wide, land, rows, cols):
    wide[:, : block.shape[1]] = block
    for j in range(4):
        land[j, :rows, cols] = wide[pl.ds(j * rows, rows), : block.shape[1]].astype(BF)


def turned(tile, cosine, sine):
    lane = lax.broadcasted_iota(jnp.int32, tile.shape, 1)
    other = jnp.where(lax.rem(lane, HD) < HD // 2, pltpu.roll(tile, 128 - HD // 2, 1), pltpu.roll(tile, HD // 2, 1))
    return tile * cosine + other * sine


def own_rows(index, rows):
    return pl.ds(pl.multiple_of(index * rows, 16), rows)


def norm_scale(v):
    return lax.rsqrt(jnp.mean(v * v, axis=1, keepdims=True) + EPSILON)


def norm_pull(e, v):
    r = norm_scale(v)
    return r * e - v * (r * r * r) * jnp.mean(e * v, axis=1, keepdims=True)


def joined(heads, j, tok):
    groups = H // KV
    pair = [heads[h // groups, tok * (h % groups) : tok * (h % groups) + tok, :] for h in (2 * j, 2 * j + 1)]
    return jnp.concatenate(pair, axis=1)


def plane_sum(net, send, land):
    total = send[net.d].astype(F32)
    for kind in range(3):
        total = total + land[net.plane[kind]].astype(F32)
    return total


LATE = ((9, 10), (11, 12), (13, 8), (14, None))


def column(row):
    n = row.shape[1]
    same = lax.broadcasted_iota(jnp.int32, (n, n), 0) == lax.broadcasted_iota(jnp.int32, (n, n), 1)
    return jnp.sum(jnp.where(same, row, 0.0), axis=1, keepdims=True)


def row_of(col):
    n = col.shape[0]
    same = lax.broadcasted_iota(jnp.int32, (n, n), 0) == lax.broadcasted_iota(jnp.int32, (n, n), 1)
    return jnp.sum(jnp.where(same, col, 0.0), axis=0, keepdims=True)


def layer_kernel(
    x_in, cot_in, query, key_w, value, output, gate_w, up_w, down, gain_one, gain_two,
    doc_starts, keep_mask, keep_rate, seq_order,
    block_out, input_grad, back_gu, back_att, back_down,
    att_land, gu_land, wide, qkv_land, kv_all, o_heads, bias, wa, wb, wlast, wgu, wd,
    xn_all, gd_all, mn_all, att_all, q_heads, k_heads, v_heads, probs, middle, act, gboth, turn_x, turn_n, turn_a,
    gn_send, gn_land, br_send, br_land, gu_mate, gu_zone, dn_mate, dn_zone, gmid, do_heads, dkv, kv_mate, kv_zone, kv_tot,
    cut_land, ma_mate, ma_zone, gx_land, sends, recvs,
):
    net = Net(sends, recvs)
    tok, dim = x_in.shape[1], x_in.shape[2]
    rows = dim // 32
    blk = 4 * rows
    ffr = down.shape[0]
    hid, quad = 8 * ffr, 4 * ffr
    d, z, c, s = net.d, net.z, net.c, net.s
    span, length = 4 * tok, 8 * tok
    groups = H // KV
    padded = att_land.shape[1]
    att_send = qkv_send = cut_send = act.reshape(4, tok, hid)
    gu_send = gboth.reshape(4, tok, 2 * hid)
    gx_send, gs_heads = gd_all, gboth
    m_att = wb.reshape(4, 4, 2, blk, 256)

    first_cols, late_cols = pl.ds(0, 256), pl.ds(256, 256)
    a2a_att = Spread(net, lambda j: att_send.at[j, pl.ds(0, padded)], lambda j: att_land.at[j])
    a2a_gu = Spread(net, lambda j: gu_send.at[j, pl.ds(0, padded)], lambda j: gu_land.at[j])
    a2a_qkv = [
        Spread(net, lambda j, cols=cols: qkv_send.at[j, :, cols], lambda j, cols=cols: qkv_land.at[j, :, cols])
        for cols in (late_cols, first_cols)
    ]
    a = [Lines(net, lambda zz, core, cols=cols: wa.at[own_rows(zz * 2 + core, blk), cols]) for cols in (late_cols, first_cols)]
    b = Slices(net, wb, blk)
    tail = FromLast(net, wa.reshape(4, 2, blk, 512), wlast.reshape(4, 2, blk, 128))
    gu = [Lines(net, lambda zz, core, h=h: wgu.at[zz, core, :, pl.ds(hid * h, hid)]) for h in range(2)]
    dn = Lines(net, lambda zz, core: wd.at[zz, core])
    kv = [
        Rising(net, lambda zz, core, i=i: kv_all.at[zz, core, :, pl.ds(KV * HD * i, KV * HD)]) for i in range(2)
    ]
    xs = Plane(net, xn_all)
    gs = Plane(net, gd_all)
    ms = Plane(net, mn_all)
    ats = Plane(net, att_all)

    kv_all[...] = jnp.zeros_like(kv_all)
    net.greet()
    first_gain = column(gain_one[...])
    zero = jnp.zeros((padded - rows, 128), BF)
    weights = (query, key_w, value)

    def qkv_tile(t):
        ref, t = (query, t) if t < 9 else (key_w, t - 9) if t < 12 else (value, t - 12)
        return (ref[:, 128 * t : 128 * t + 128].astype(F32) * first_gain).astype(BF)

    for j in range(4):
        tiles = [qkv_tile(2 * j), qkv_tile(2 * j + 1), qkv_tile(LATE[j][0])]
        tiles.append(output[:, 1024:1152] if LATE[j][1] is None else qkv_tile(LATE[j][1]))
        tiles += [output[:, 256 * j : 256 * j + 128], output[:, 256 * j + 128 : 256 * j + 256]]
        for i, tile in enumerate(tiles):
            att_send[j, :rows, 128 * i : 128 * i + 128] = tile
            att_send[j, rows:padded, 128 * i : 128 * i + 128] = zero
    net.greeted()
    a2a_att.start()
    att_land[d] = att_send[d, :padded, :]
    x = x_in[0].astype(F32)
    xn_all[d] = (x * norm_scale(x)).astype(BF)
    xs.start()
    second_gain = column(gain_two[...])
    for i, ref in enumerate((gate_w, up_w)):
        scaled = ref[...].astype(F32) * second_gain
        for j in range(4):
            for h in range(2):
                part = [scaled[:, ffr * (4 * k + j) : ffr * (4 * k + j) + ffr] for k in range(4 * h, 4 * h + 4)]
                cols = slice(hid * h + quad * i, hid * h + quad * i + quad)
                gu_send[j, :rows, cols] = jnp.concatenate(part, axis=1).astype(BF)
                gu_send[j, rows:padded, cols] = jnp.zeros((padded - rows, quad), BF)
    gu_land[d] = gu_send[d, :padded, :]
    sample = seq_order[d]
    scale_attn, scale_mlp = [
        jnp.full((1, 1), keep_mask[i, sample].astype(F32), F32) / jnp.full((1, 1), keep_rate[i], F32) for i in range(2)
    ]
    gd_all[d] = (cot_in[0].astype(F32) * scale_mlp).astype(BF)
    wd[z, c] = down[...]
    position = s * tok + lax.broadcasted_iota(jnp.int32, (tok, 1), 0)
    lane = lax.broadcasted_iota(jnp.int32, (tok, 128), 1)
    power = lax.rem(lane, HD // 2).astype(F32) * (-2.0 * math.log(ROPE_BASE) / HD)
    angle = position.astype(F32) * jnp.exp(power)
    cosine, sine = jnp.cos(angle), jnp.where(lax.rem(lane, HD) < HD // 2, -jnp.sin(angle), jnp.sin(angle))
    a2a_att.take()
    own = own_rows(s, blk)
    packed = settle(att_land, wide, rows)
    wa[own, :] = packed[:, :512]
    wb[d, own, :] = packed[:, 512:]
    for line in a:
        line.start()
    for k in (1, 2, 3):
        for line in a:
            line.step(k)
        for line in a:
            line.give(k)
        if k == 1:
            xs.pass_on()
            a2a_gu.start()
    b.start()
    dn.start()
    xs.take()
    a[0].take()

    eighth = 1.0 / math.sqrt(HD)

    def project(cols, kinds):
        part = dot_nn(xn_all[...].reshape(span, dim), wa[:, cols])
        for j in range(4):
            for i, kind in enumerate(kinds):
                tile = part[tok * j : tok * j + tok, 128 * i : 128 * i + 128]
                spun = turned(tile, cosine, sine)
                if kind == 1:
                    tile = jnp.where(d < 2, spun, tile)
                elif kind == 2:
                    tile = jnp.where(d == 0, spun, jnp.where(d == 2, spun * eighth, tile))
                else:
                    tile = spun * eighth
                qkv_send[j, :, pl.ds(cols.start + 128 * i, 128)] = tile.astype(BF)

    net.finish(a2a_att)
    project(late_cols, (1, 2))
    a2a_qkv[0].start()
    a[1].take()
    project(first_cols, (0, 0))
    a2a_qkv[1].start()
    qkv_land[d] = qkv_send[d, :, :512]
    b.spread(0)
    b.step(1)
    b.spread(1)
    a2a_qkv[0].take()
    places = [(0, 256), (0, 384), (1, 256), (1, 384), (2, 256), (3, 256)]
    for i, (j, col) in enumerate(places):
        kv_all[z, c, :, 128 * i : 128 * i + 128] = qkv_land[j, :, col : col + 128]
    for line in kv:
        line.start()
    b.step(2)
    b.spread(2)
    a2a_gu.take()
    for h in range(2):
        wgu[z, c, :, hid * h : hid * h + hid] = settle(gu_land, wide, rows, slice(hid * h, hid * h + hid))
    b.step(3)
    b.spread(3)
    for half in gu:
        half.start(True)
    for line in kv:
        line.step(1)
    b.pass_on(0)
    b.pass_on(1)
    a2a_qkv[1].take()
    gs.start()
    for t in range(9):
        j, col = (t // 2, (t % 2) * 128) if t < 8 else (2, 384)
        for h in (2 * t, 2 * t + 1):
            at = col + HD * (h % 2)
            q_heads[h // groups, tok * (h % groups) : tok * (h % groups) + tok, :] = qkv_land[j, :, at : at + HD]
    first = jnp.zeros((tok, 1), jnp.int32)
    for j in range(doc_starts.shape[1]):
        start = doc_starts[sample, j]
        first = jnp.where(position >= start, jnp.maximum(first, start), first)
    key = lax.broadcasted_iota(jnp.int32, bias.shape, 1)
    bias[...] = jnp.where((key <= position) & (key >= first), 0.0, MASKED)

    for line in kv:
        line.step(2)
    gu[0].start(False)
    b.pass_on(2)
    b.pass_on(3)
    b.corner(0)
    b.corner(1)
    for line in kv:
        line.step(3)
    dn.step(1)
    for line in kv:
        line.take()
    for j in range(8):
        for k in range(KV):
            k_heads[k, pl.ds(tok * j, tok), :] = kv_all[j // 2, j % 2, :, HD * k : HD * k + HD]
            v_heads[k, pl.ds(tok * j, tok), :] = kv_all[j // 2, j % 2, :, HD * (KV + k) : HD * (KV + k) + HD]

    def attend(k, carry):
        for g in range(groups):
            mine = pl.ds(tok * g, tok)
            score = dot_nt(q_heads[k, mine, :], k_heads[k]) + bias[...]
            expo = jnp.exp(score - jnp.max(score, axis=1, keepdims=True))
            p = (expo * (1.0 / jnp.sum(expo, axis=1, keepdims=True))).astype(BF)
            probs[k, mine, :] = p
            o_heads[k, mine, :] = dot_nn(p, v_heads[k])
        return carry

    net.finish(xs, *a, a2a_gu)
    tail.start()
    lax.fori_loop(0, 2, attend, 0)
    dn.step(2)
    gu[0].step(1)
    gs.pass_on()
    b.corner(2)
    lax.fori_loop(2, 4, attend, 0)
    dn.step(3)
    gu[0].step(2)
    gu[1].step(1)
    tail.pass_on()
    lax.fori_loop(4, 6, attend, 0)
    b.corner(3)
    b.take()
    tail.take()
    net.finish(b, tail, *kv, *a2a_qkv)
    for j in range(H // 2):
        att_all[d, :, 128 * j : 128 * j + 128] = joined(o_heads, j, tok).astype(BF)
    full = att_all[d]
    branch = [dot_nn(full, wb[j]) for j in range(4)] + [dot_nn(full, wlast[...])]
    mid = x_in[0].astype(F32) + scale_attn * jnp.concatenate(branch, axis=1)
    middle[...] = mid
    mn_all[d] = (mid * norm_scale(mid)).astype(BF)
    ms.start()
    gu[0].step(3)
    gu[1].start(False)
    gs.take()
    dn.give(1)
    gu[0].give(1)
    dn.give(2)
    ms.pass_on()
    gu[1].step(2)
    gu[0].give(2)
    dn.give(3)
    gu[0].give(3)
    ms.take()
    gu[1].step(3)
    dn.take()
    gu[0].take()
    ats.start()
    net.finish(gs)

    def by_cols(send, land, width):
        return [
            Spread(
                net,
                lambda j, n=n: send.at[j, :, pl.ds(width * n, width)],
                lambda j, n=n: land.at[j, :, pl.ds(width * n, width)],
            )
            for n in range(dim // width)
        ]

    gn, br, gx = by_cols(gn_send, gn_land, 384), by_cols(br_send, br_land, dim), by_cols(gx_send, gx_land, 384)
    wgu_flat, wd_flat = wgu.reshape(dim, 2 * hid), wd.reshape(hid, dim)
    other = 1 - c
    halves = [pl.ds(hid * h, hid) for h in range(2)]
    gu_pair = [ToMate(net, wgu.at[:, other, :, cols], gu_mate.at[:, :, cols]) for cols in halves]
    dn_pair = [ToMate(net, wd.at[2 * h : 2 * h + 2, other], dn_mate.at[2 * h : 2 * h + 2]) for h in range(2)]

    def add_dn(block, slot):
        wd[block, c] = (wd[block, c].astype(F32) + dn_zone[slot].astype(F32)).astype(BF)

    def half_sum(cols):
        def add(block, slot):
            wgu[block, c, :, cols] = (wgu[block, c, :, cols].astype(F32) + gu_zone[slot, :, cols].astype(F32)).astype(BF)

        return ChainSum(net, lambda zz: wgu.at[zz, c, :, cols], lambda k: gu_zone.at[k, :, cols], add)

    gu_sum = [half_sum(cols) for cols in halves]
    dn_sum = ChainSum(net, lambda zz: wd.at[zz, c], lambda k: dn_zone.at[k], add_dn)

    def pair_gu(h):
        gu_pair[h].take()
        cols = halves[h]
        for k in range(4):
            wgu[k, c, :, cols] = (wgu[k, c, :, cols].astype(F32) + gu_mate[k, :, cols].astype(F32)).astype(BF)
        gu_sum[h].stage(0)

    def branch_rows(h, downs):
        for n in range(3):
            cols = pl.ds(384 * n, 384)
            part = dot_nn(act[:, downs], wd_flat[downs, cols]).reshape(4, tok, 384)
            if h == 0:
                br_send[:, :, cols] = part.astype(BF)
            else:
                br_send[:, :, cols] = (br_send[:, :, cols].astype(F32) + part).astype(BF)
        turn_a[downs, :] = act[:, downs].T
        if h == 0:
            net.finish(dn)
        for n in range(3):
            cols = pl.ds(384 * n, 384)
            wd_flat[downs, cols] = dot_nn(turn_a[downs, :], gd_all[:, :, cols].reshape(span, 384)).astype(BF)
        dn_pair[h].start()

    def pair_dn(h):
        dn_pair[h].take()
        for k in (2 * h, 2 * h + 1):
            wd[k, c] = (wd[k, c].astype(F32) + dn_mate[k].astype(F32)).astype(BF)

    turn_x[...] = mn_all[...].reshape(span, dim).T
    for h in range(2):
        base = hid * h
        gates, ups, downs = pl.ds(base, quad), pl.ds(base + quad, quad), pl.ds(quad * h, quad)
        if h == 1:
            for k in (1, 2, 3):
                gu[1].give(k)
            gu[1].take()
        for pair in range(2):
            lines, two = pl.ds(2 * tok * pair, 2 * tok), slice(2 * pair, 2 * pair + 2)
            normed = mn_all[two].reshape(2 * tok, dim)
            gate = dot_nn(normed, wgu_flat[:, gates])
            up = dot_nn(normed, wgu_flat[:, ups])
            g_act = dot_nt(gd_all[two].reshape(2 * tok, dim), wd_flat[downs, :])
            sig = jax.nn.sigmoid(gate)
            swish = gate * sig
            act[lines, downs] = (swish * up).astype(BF)
            gboth[lines, gates] = (g_act * up * (sig * (1.0 + gate * (1.0 - sig)))).astype(BF)
            gboth[lines, ups] = (g_act * swish).astype(BF)
        if h == 0:
            branch_rows(h, downs)
        for n in range(3):
            cols = pl.ds(384 * n, 384)
            part = dot_nt(gboth[:, halves[h]], wgu_flat[cols, halves[h]]).reshape(4, tok, 384)
            if h == 0:
                gn_send[:, :, cols] = part.astype(BF)
                if n == 1:
                    pair_dn(h)
                    dn_sum.falling(0)
                    dn_sum.falling(1, True)
            else:
                gn_send[:, :, cols] = (gn_send[:, :, cols].astype(F32) + part).astype(BF)
                gn[n].start()

    def grads_gu(h):
        net.finish(gu[h])
        for base in (hid * h, hid * h + quad):
            cols = pl.ds(base, quad)
            wgu_flat[:, cols] = dot_nn(turn_x[...], gboth[:, cols]).astype(BF)
        gu_pair[h].start()

    grads_gu(0)
    branch_rows(1, pl.ds(quad, quad))
    pair_gu(0)
    grads_gu(1)
    pair_dn(1)
    dn_sum.rising(0)
    dn_sum.falling(1, False)
    pair_gu(1)
    gu_sum[0].stage(1)

    for n in range(3):
        gn[n].take()
    mid = middle[...]
    g_mid = cot_in[0].astype(F32) + norm_pull(plane_sum(net, gn_send, gn_land), mid)
    gmid[...] = g_mid
    gba = (scale_attn * g_mid).astype(BF)
    for j in range(4):
        cut_send[j, :, 512:768] = gba[:, 256 * j : 256 * j + 256]
    cut_send[3, :, 384:512] = gba[:, 1024:1152]
    cut = lambda cols: Spread(net, lambda j: cut_send.at[j, :, cols], lambda j: cut_land.at[j, :, cols])
    cut_o, cut_q, cut_l = cut(pl.ds(512, 256)), cut(pl.ds(0, 256)), cut(pl.ds(256, 256))
    cut_o.start()
    ats.pass_on()
    cut_land[d, :, 512:768] = cut_send[d, :, 512:768]
    g_att = dot_nt(gba[:, 1024:1152], wlast[...])
    for j in range(4):
        g_att = g_att + dot_nt(gba[:, 256 * j : 256 * j + 256], wb[j])
    for h in range(H):
        do_heads[h // groups, tok * (h % groups) : tok * (h % groups) + tok, :] = g_att[:, HD * h : HD * h + HD].astype(BF)

    dn_sum.falling(2, False)
    dn_sum.rising(1)

    kv_pair = [ToMate(net, dkv.at[n, :, other], kv_mate.at[n]) for n in range(2)]

    def kv_total(n):
        def add(block):
            dkv[n, block, c] = (dkv[n, block, c].astype(F32) + kv_zone[n, block].astype(F32)).astype(BF)

        return DownSum(net, lambda zz: dkv.at[n, zz, c], lambda k: kv_zone.at[n, k], add)

    kv_sum = [kv_total(n) for n in range(2)]

    def pull(k, carry):
        for g in range(groups):
            mine = pl.ds(tok * g, tok)
            p = probs[k, mine, :].astype(F32)
            t = p * dot_nt(do_heads[k, mine, :], v_heads[k])
            ds = (t - p * jnp.sum(t, axis=1, keepdims=True)).astype(BF)
            gs_heads[mine, :length] = ds
            o_heads[k, mine, :] = dot_nn(ds, k_heads[k]) * eighth
        half, kk = lax.div(k, 3), lax.rem(k, 3)
        for i, (left, right) in enumerate(((q_heads[k], gs_heads[: groups * tok, :length]), (do_heads[k], probs[k]))):
            turned_grad = dot_tn(left, right).astype(BF)
            at = pl.ds(pl.multiple_of(192 * i + HD * kk, HD), HD)
            for j in range(8):
                dkv[half, j // 2, j % 2, at, :] = turned_grad[:, tok * j : tok * j + tok]
        return carry

    def pair_sum(n):
        kv_pair[n].take()
        for k in range(4):
            dkv[n, k, c] = (dkv[n, k, c].astype(F32) + kv_mate[n, k].astype(F32)).astype(BF)
        kv_sum[n].start()

    def grads(p, parts):
        at = 0
        for part in parts:
            wb[p, :, at : at + part.shape[1]] = part.astype(BF)
            at += part.shape[1]
        pair = ToMate(net, m_att.at[p, :, other, :, quarter], ma_mate.at[p])
        pair.start()
        return pair

    def grads_pair(p, pair):
        pair.take()
        for k in range(4):
            m_att[p, k, c, :, quarter] = (m_att[p, k, c, :, quarter].astype(F32) + ma_mate[p, k].astype(F32)).astype(BF)

    def grads_chain(p, pair):
        def add(block, slot):
            m_att[p, block, c, :, quarter] = (
                m_att[p, block, c, :, quarter].astype(F32) + ma_zone[p, slot].astype(F32)
            ).astype(BF)

        grads_pair(p, pair)
        out = ChainSum(net, lambda zz: m_att.at[p, zz, c, :, quarter], lambda k: ma_zone.at[p, k], add)
        out.stage(0)
        return out

    def grads_straight(p, pair):
        grads_pair(p, pair)
        out = ToOwners(net, lambda zz: m_att.at[p, zz, c, :, quarter], lambda k: ma_zone.at[p, k])
        out.start()
        return out

    def grads_back(p, out):
        cols = pl.ds(256 * p, 256)
        if isinstance(out, ChainSum):
            out.own()
            total = m_att[p, z, c, :, quarter].astype(F32)
        else:
            out.take()
            total = m_att[p, z, c, :, quarter].astype(F32)
            for k in range(3):
                total = total + ma_zone[p, k].astype(F32)
        unsettle(total, wide, att_land, rows, cols)
        spread = Spread(net, lambda j: att_land.at[j, :, cols], lambda j: back_att.at[j, :, cols])
        spread.start()
        back_att[d, :, cols] = att_land[d, :, cols]
        return spread

    q_cols, l_cols, o_cols = pl.ds(0, 256), pl.ds(256, 256), pl.ds(512, 256)
    quarter = pl.ds(0, 256)
    net.finish(ms, *gn, *gu_pair, *dn_pair)
    lax.fori_loop(0, 3, pull, 0)
    kv_pair[0].start()
    lax.fori_loop(3, 4, pull, 0)
    pair_sum(0)
    lax.fori_loop(4, 6, pull, 0)
    kv_pair[1].start()
    for t in range(9):
        j, col = (t // 2, (t % 2) * 128) if t < 8 else (2, 384)
        cut_send[j, :, col : col + 128] = turned(joined(o_heads, t, tok), cosine, -sine).astype(BF)
    cut_q.start()
    br[0].start()
    cut_land[d, :, q_cols] = cut_send[d, :, q_cols]
    pair_sum(1)
    ats.take()
    cut_o.take()
    turn_x[...] = att_all[...].reshape(span, dim).T
    pair_o = grads(2, [dot_nn(turn_x[...], cut_land[:, :, o_cols].reshape(span, 256))])
    turn_n[...] = xn_all[...].reshape(span, dim).T
    dn_sum.rising(2, False)
    gu_sum[0].rising(2, False)
    for n in range(2):
        kv_sum[n].relay(0)
        kv_sum[n].relay(1)
    cut_q.take()
    pair_q = grads(0, [dot_nn(turn_n[...], cut_land[:, :, q_cols].reshape(span, 256))])
    gu_sum[1].stage(1)
    sum_o = grads_chain(2, pair_o)
    sum_q = grads_chain(0, pair_q)
    gu_sum[0].falling(2, False)

    for n in range(2):
        kv_sum[n].own()
        kv_tot[n] = dkv[n, z, c].astype(F32)
    keys = jnp.concatenate([kv_tot[0, :192, :], kv_tot[1, :192, :]], axis=0).T
    vals = jnp.concatenate([kv_tot[0, 192:, :], kv_tot[1, 192:, :]], axis=0).T
    late = [turned(keys[:, 128 * i : 128 * i + 128], cosine, -sine) for i in range(3)] + [vals[:, 128 * i : 128 * i + 128] for i in range(3)]
    for tile, (j, col) in zip(late, places):
        cut_send[j, :, col : col + 128] = tile.astype(BF)
    cut_l.start()
    cut_land[d, :, l_cols] = cut_send[d, :, l_cols]
    sum_o.stage(1)
    sum_q.stage(1)
    gu_sum[1].between(2)
    gu_sum[0].last()
    gu_sum[1].last()
    net.finish(ats, cut_o, cut_q, *kv_pair)
    cut_l.take()
    last = cut_land[:, :, 384:512].reshape(span, 128)
    cuts = cut_land[:, :, :512].reshape(span, 512)
    lane = lax.broadcasted_iota(jnp.int32, cuts.shape, 1)
    cuts = jnp.where((d == 3) & (lane >= 384), jnp.zeros_like(cuts), cuts)
    for n in range(3):
        part = dot_nt(cuts, wa[384 * n : 384 * n + 384, :]).astype(BF)
        gx_send[:, :, 384 * n : 384 * n + 384] = part.reshape(4, tok, 384)
        gx[n].start()
    second = jnp.where(d == 3, dot_nn(turn_x[...], last), dot_nn(turn_n[...], last))
    pair_l = grads(1, [dot_nn(turn_n[...], cut_land[:, :, 256:384].reshape(span, 128)), second])
    sum_l = grads_straight(1, pair_l)
    br[0].take()
    block_out[0] = (middle[...] + scale_mlp * plane_sum(net, br_send, br_land)).astype(BF)
    sum_o.stage(2)
    sum_q.stage(2)
    dn_sum.last()
    for k in range(2):
        gu_sum[k].own()
        unsettle(wgu[z, c, :, halves[k]].astype(F32), wide, gu_land, rows, halves[k])
    back_g = Spread(net, lambda j: gu_land.at[j], lambda j: back_gu.at[j])
    back_g.start()
    back_gu[d] = gu_land[d]
    back_o = grads_back(2, sum_o)
    back_l = grads_back(1, sum_l)
    back_q = grads_back(0, sum_q)
    dn_sum.own()
    back_down[...] = wd[z, c]
    for n in range(3):
        gx[n].take()
    input_grad[0] = gmid[...] + norm_pull(plane_sum(net, gx_send, gx_land), x_in[0].astype(F32))
    for spread in (back_o, back_q, back_g, back_l):
        spread.take()
    net.finish()


def layer(x, cot, weights, down, gains, doc_starts, keep_mask, keep_rate, seq_order):
    tok, dim = x.shape[1:]
    ns = 8
    length = tok * ns
    ffr = down.shape[0]
    hid = ffr * ns
    blk = dim // ns
    span = 4 * tok
    vm = pl.BlockSpec(memory_space=pltpu.VMEM)
    sm = pl.BlockSpec(memory_space=pltpu.SMEM)
    padded = blk // 4 + -(blk // 4) % 16
    att_pack, gu_pack = ((4, padded, 768), BF), ((4, padded, 2 * hid), BF)
    outs = [((1, tok, dim), BF), ((1, tok, dim), F32), gu_pack, att_pack, (down.shape, BF)]
    plane = ((4, tok, dim), BF)
    wide_cut = ((4, tok, 512), BF)
    three = ((KV, 3 * tok, HD), BF)
    scratch = [
        att_pack,
        gu_pack,
        ((blk, hid), F32),
        wide_cut,
        ((4, 2, tok, 2 * KV * HD), BF),
        ((KV, 3 * tok, HD), F32),
        ((tok, length), F32),
        ((dim, 512), BF),
        ((4, dim, 256), BF),
        ((dim, 128), BF),
        ((4, 2, blk, 2 * hid), BF),
        ((4, 2, ffr, dim), BF),
        plane,
        plane,
        plane,
        plane,
        three,
        ((KV, length, HD), BF),
        ((KV, length, HD), BF),
        ((KV, 3 * tok, length), BF),
        ((tok, dim), F32),
        ((span, hid), BF),
        ((span, 2 * hid), BF),
        ((dim, span), BF),
        ((dim, span), BF),
        ((hid, span), BF),
        plane,
        plane,
        plane,
        plane,
        ((4, blk, 2 * hid), BF),
        ((5, blk, 2 * hid), BF),
        ((4, ffr, dim), BF),
        ((5, ffr, dim), BF),
        ((tok, dim), F32),
        three,
        ((2, 4, 2, 384, tok), BF),
        ((2, 4, 384, tok), BF),
        ((2, 3, 384, tok), BF),
        ((2, 384, tok), F32),
        ((4, tok, 768), BF),
        ((3, 4, blk, 256), BF),
        ((3, 5, blk, 256), BF),
        plane,
    ]
    return pl.pallas_call(
        layer_kernel,
        out_shape=[jax.ShapeDtypeStruct(*o) for o in outs],
        in_specs=[vm] * 11 + [sm] * 4,
        out_specs=[vm] * len(outs),
        scratch_shapes=[pltpu.VMEM(*t) for t in scratch] + [pltpu.SemaphoreType.DMA((SENDS,)), pltpu.SemaphoreType.DMA((RECVS,))],
        compiler_params=pltpu.CompilerParams(collective_id=0, has_side_effects=True, vmem_limit_bytes=LIMIT),
        name="k_layer",
    )(x, cot, *weights, down, *gains, doc_starts, keep_mask, keep_rate, seq_order)


def grads_kernel(
    query, key_w, value, gate_w, up_w, gain_one, gain_two, block_in, input_in, back_gu, back_att, back_down,
    block_out, input_out, norm_one, g_query, g_key, g_value, g_output, norm_two, g_gate, g_up, g_down,
):
    rows, ffr = query.shape[0], back_down.shape[0]
    hid = 8 * ffr
    block_out[...] = block_in[...]
    input_out[...] = input_in[...]
    g_down[...] = back_down[...].astype(F32)
    gain = column(gain_one[...])
    total = jnp.zeros((rows, 128), F32)
    for j in range(4):
        for i, t in enumerate((2 * j, 2 * j + 1, LATE[j][0], LATE[j][1])):
            m = back_att[j, :rows, 128 * i : 128 * i + 128].astype(F32)
            if t is None:
                g_output[:, 1024:1152] = m
                continue
            w, g, t = (query, g_query, t) if t < 9 else (key_w, g_key, t - 9) if t < 12 else (value, g_value, t - 12)
            cols = slice(128 * t, 128 * t + 128)
            total = total + w[:, cols].astype(F32) * m
            g[:, cols] = m * gain
        g_output[:, 256 * j : 256 * j + 256] = back_att[j, :rows, 512:768].astype(F32)
    norm_one[...] = row_of(jnp.sum(total, axis=1, keepdims=True))
    gain = column(gain_two[...])
    total = jnp.zeros((rows, 4 * ffr), F32)
    for i, (w, g) in enumerate(((gate_w, g_gate), (up_w, g_up))):
        for k in range(8):
            at = hid * (k // 4) + 4 * ffr * i + ffr * (k % 4)
            m = jnp.concatenate([back_gu[j, :rows, at : at + ffr].astype(F32) for j in range(4)], axis=1)
            cols = slice(4 * ffr * k, 4 * ffr * k + 4 * ffr)
            total = total + w[:, cols].astype(F32) * m
            g[:, cols] = m * gain
    norm_two[...] = row_of(jnp.sum(total, axis=1, keepdims=True))


def gradients(query, key_w, value, output, gate_w, up_w, gains, results):
    block, grad, back_gu, back_att, back_down = results
    shapes = [grad.shape, gains[0].shape] + [w.shape for w in (query, key_w, value, output)]
    shapes += [gains[1].shape, gate_w.shape, up_w.shape, back_down.shape]
    vm = pl.BlockSpec(memory_space=pltpu.VMEM)
    return pl.pallas_call(
        grads_kernel,
        out_shape=[jax.ShapeDtypeStruct(block.shape, BF)] + [jax.ShapeDtypeStruct(t, F32) for t in shapes],
        in_specs=[vm] * 12,
        out_specs=[vm] * 11,
        name="k_grads",
    )(query, key_w, value, gate_w, up_w, *gains, block, grad, back_gu, back_att, back_down)


def shards_by_kernel(
    hidden_in,
    attn_norm,
    query_weight,
    key_weight,
    value_weight,
    output_weight,
    mlp_norm,
    gate_weight,
    up_weight,
    down_weight,
    cotangent,
    doc_starts,
    keep_mask,
    keep_rate,
    seq_order,
):
    rows = query_weight.shape[0]
    gains = (attn_norm.reshape(1, rows), mlp_norm.reshape(1, rows))
    weights = (query_weight, key_weight, value_weight, output_weight, gate_weight, up_weight)
    results = layer(
        hidden_in, cotangent, weights, down_weight, gains, doc_starts, keep_mask.T, keep_rate, seq_order
    )
    outs = list(gradients(*weights, gains, results))
    outs[2], outs[7] = outs[2].reshape(rows), outs[7].reshape(rows)
    return tuple(outs)


def solution(mesh):
    placed = (
        P("dp", "seq", None),
        P(("seq", "dp")),
        P(("seq", "dp"), None),
        P(("seq", "dp"), None),
        P(("seq", "dp"), None),
        P(("seq", "dp"), None),
        P(("seq", "dp")),
        P(("seq", "dp"), None),
        P(("seq", "dp"), None),
        P(("seq", "dp"), None),
        P("dp", "seq", None),
        P(),
        P(),
        P(),
        P(),
    )
    fits = mesh.shape["seq"] == 8 and mesh.shape["dp"] == 4
    return jax.shard_map(
        shards_by_kernel if fits else shards,
        mesh=mesh,
        in_specs=placed,
        out_specs=(
            P("dp", "seq", None),
            P("dp", "seq", None),
            P(("seq", "dp")),
            P(("seq", "dp"), None),
            P(("seq", "dp"), None),
            P(("seq", "dp"), None),
            P(("seq", "dp"), None),
            P(("seq", "dp")),
            P(("seq", "dp"), None),
            P(("seq", "dp"), None),
            P(("seq", "dp"), None),
        ),
        check_vma=False,
    )
```
